32 devices in a mesh: seq: 4 (over y, x), ctx: 8 (over z, core).
Axes of the slice: x: 2, y: 2, z: 4, core: 2. Of those that a mesh axis runs over, the one named last changes fastest.
Arguments:
- tokens: bfloat16 [4, 4096, 768], P('seq', 'ctx'), may hold values from -6 to 6
- segment_ids: int32 [4, 4096], P('seq', 'ctx'), may hold values from 0 to 34, as said below
- valid_tokens: int32 [4, 4096], P('seq', 'ctx'), may hold values from 0 to 1, as said below
- query_weight: float32 [768, 768], P(('seq', 'ctx')), may hold values from -0.21875 to 0.21875
- query_bias: float32 [768], P(('seq', 'ctx')), may hold values from -1.75 to 1.75
- key_weight: float32 [768, 768], P(('seq', 'ctx')), may hold values from -0.21875 to 0.21875
- value_weight: float32 [768, 768], P(('seq', 'ctx')), may hold values from -0.21875 to 0.21875
- value_bias: float32 [768], P(('seq', 'ctx')), may hold values from -1.75 to 1.75
- output_weight: float32 [768, 768], P(('seq', 'ctx')), may hold values from -0.875 to 0.875
- output_bias: float32 [768], P(('seq', 'ctx')), may hold values from -1.75 to 1.75
- attn_norm_gain: float32 [768], P(('seq', 'ctx')), may hold values from 0.5 to 1.5
- attn_norm_shift: float32 [768], P(('seq', 'ctx')), may hold values from -1.75 to 1.75
- up_weight: float32 [768, 3072], P(('seq', 'ctx')), may hold values from -0.21875 to 0.21875
- up_bias: float32 [3072], P(('seq', 'ctx')), may hold values from -1.75 to 1.75
- down_weight: float32 [3072, 768], P(('seq', 'ctx')), may hold values from -0.109375 to 0.109375
- down_bias: float32 [768], P(('seq', 'ctx')), may hold values from -1.75 to 1.75
- ffn_norm_gain: float32 [768], P(('seq', 'ctx')), may hold values from 0.5 to 1.5
- ffn_norm_shift: float32 [768], P(('seq', 'ctx')), may hold values from -1.75 to 1.75
- out_cotangent: bfloat16 [4, 4096, 768], P('seq', 'ctx'), may hold values from -6 to 6
Outputs:
- layer_output: float32 [4, 4096, 768], P('seq', 'ctx')
- input_grad: float32 [4, 4096, 768], P('seq', 'ctx')
- query_weight_grad: float32 [768, 768], P(('seq', 'ctx'))
- query_bias_grad: float32 [768], P(('seq', 'ctx'))
- key_weight_grad: float32 [768, 768], P(('seq', 'ctx'))
- value_weight_grad: float32 [768, 768], P(('seq', 'ctx'))
- value_bias_grad: float32 [768], P(('seq', 'ctx'))
- output_weight_grad: float32 [768, 768], P(('seq', 'ctx'))
- output_bias_grad: float32 [768], P(('seq', 'ctx'))
- attn_norm_gain_grad: float32 [768], P(('seq', 'ctx'))
- attn_norm_shift_grad: float32 [768], P(('seq', 'ctx'))
- up_weight_grad: float32 [768, 3072], P(('seq', 'ctx'))
- up_bias_grad: float32 [3072], P(('seq', 'ctx'))
- down_weight_grad: float32 [3072, 768], P(('seq', 'ctx'))
- down_bias_grad: float32 [768], P(('seq', 'ctx'))
- ffn_norm_gain_grad: float32 [768], P(('seq', 'ctx'))
- ffn_norm_shift_grad: float32 [768], P(('seq', 'ctx'))
The draws below stay inside these ranges and needn't reach their ends.
Inputs may be any that keep to these rules, and one draw needn't show every extreme that they name: `segment_ids`: within each sequence the numbers start at 0 and rise by 0 or 1 from one token to the next, so that documents are contiguous; every sequence holds exactly 35 documents. `valid_tokens`: each sequence ends in a run of padding; the first token of every document is 1.
All inputs are finite; a program needn't handle non-finite values.
Results may differ from the reference program's by a relative error of at most 0.025.
Values may be sent and summed in bfloat16 or wider, within the bound.
A program may use at most 192 MiB of HBM per device.

```python
import jax
import jax.numpy as jnp
from jax import lax

D = 768
H = 12
DH = 64
FF = 3072
TOK_DEV = 512
SEQ_LEN = 4096
SEQUENCES = 4


def layout(key):
    key_first, key_last, key_padding, key_breaks = jax.random.split(jax.random.fold_in(key, 7), 4)
    position = jnp.arange(SEQ_LEN, dtype=jnp.int32)[None, :]
    first_doc = jax.random.randint(key_first, (SEQUENCES, 1), TOK_DEV // 2, TOK_DEV)
    last_doc = SEQ_LEN - jax.random.randint(key_last, (SEQUENCES, 1), TOK_DEV // 2, TOK_DEV)
    padding = jax.random.randint(key_padding, (SEQUENCES, 1), 1, TOK_DEV // 4 + 1)
    inside = (position > 0) & (position < first_doc) | (position > last_doc) & (position < SEQ_LEN - padding)
    ranking = jax.random.randint(key_breaks, (SEQUENCES, SEQ_LEN), 0, 1024) * SEQ_LEN + position
    ranking = jnp.where(inside, ranking, -1)
    chosen = lax.top_k(ranking, TOK_DEV // 16)[1].astype(jnp.int32)
    breaks = jnp.any(position[:, :, None] == chosen[:, None, :], axis=2)
    starts = (position == 0) | (position == first_doc) | (position == last_doc) | breaks
    segment = jnp.cumsum(starts.astype(jnp.int32), axis=1) - 1
    validity = (position < SEQ_LEN - padding).astype(jnp.int32)
    return (segment.astype(jnp.int32), validity)


def draw_segment_ids(key, part):
    return layout(key)[0]


def draw_valid_tokens(key, part):
    return layout(key)[1]


def shard_levels(rng, shape, pieces, least, high):
    level = 1.0
    for dim, parts in pieces:
        draws = jax.random.uniform(jax.random.fold_in(jax.random.fold_in(rng, 6), dim), (parts,), jnp.float32, least / len(pieces), high / len(pieces))
        level = level * jnp.repeat(jnp.exp(draws), shape[dim] // parts).reshape((-1,) + (1,) * (len(shape) - 1 - dim))
    return level


def bell_draw(rng, extent, scale, reach, cuts=(), kind=jnp.bfloat16):
    result = jax.random.normal(rng, extent, jnp.float32) * scale
    if len(cuts) > 0:
        result = shard_levels(rng, extent, cuts, -0.22, 0.18) * result
    return jnp.clip(result, min=-reach, max=reach).astype(kind)


def setup_inputs(seed: int = 0) -> dict:
    keys = jax.random.split(jax.random.key(seed), 20)
    tokens = bell_draw(keys[0], (SEQUENCES, SEQ_LEN, D), 1.0, 6.0, ((0, 4), (1, 8)))
    segment_ids = draw_segment_ids(jax.random.fold_in(keys[19], 71), 0)
    valid_tokens = draw_valid_tokens(jax.random.fold_in(keys[19], 71), 0)
    query_weight = bell_draw(keys[3], (D, D), D ** -0.5, 0.21875, ((0, 32),), jnp.float32)
    query_bias = bell_draw(keys[4], (D,), 0.3, 1.75, ((0, 32),), jnp.float32)
    key_weight = bell_draw(keys[5], (D, D), D ** -0.5, 0.21875, ((0, 32),), jnp.float32)
    value_weight = bell_draw(keys[6], (D, D), D ** -0.5, 0.21875, ((0, 32),), jnp.float32)
    value_bias = bell_draw(keys[7], (D,), 0.3, 1.75, ((0, 32),), jnp.float32)
    output_weight = bell_draw(keys[8], (D, D), (D // 16) ** -0.5, 0.875, ((0, 32),), jnp.float32)
    output_bias = bell_draw(keys[9], (D,), 0.3, 1.75, ((0, 32),), jnp.float32)
    attn_norm_gain = jnp.clip(1.0 + 0.1 * jax.random.normal(keys[10], (D,), jnp.float32), 0.5, 1.5)
    attn_norm_shift = bell_draw(keys[11], (D,), 0.3, 1.75, ((0, 32),), jnp.float32)
    up_weight = bell_draw(keys[12], (D, FF), D ** -0.5, 0.21875, ((0, 32),), jnp.float32)
    up_bias = bell_draw(keys[13], (FF,), 0.3, 1.75, ((0, 32),), jnp.float32)
    down_weight = bell_draw(keys[14], (FF, D), FF ** -0.5, 0.109375, ((0, 32),), jnp.float32)
    down_bias = bell_draw(keys[15], (D,), 0.3, 1.75, ((0, 32),), jnp.float32)
    ffn_norm_gain = jnp.clip(1.0 + 0.1 * jax.random.normal(keys[16], (D,), jnp.float32), 0.5, 1.5)
    ffn_norm_shift = bell_draw(keys[17], (D,), 0.3, 1.75, ((0, 32),), jnp.float32)
    out_cotangent = bell_draw(keys[18], (SEQUENCES, SEQ_LEN, D), 1.0, 6.0, ((0, 4), (1, 8)))
    return dict(tokens=tokens, segment_ids=segment_ids, valid_tokens=valid_tokens, query_weight=query_weight, query_bias=query_bias, key_weight=key_weight, value_weight=value_weight, value_bias=value_bias, output_weight=output_weight, output_bias=output_bias, attn_norm_gain=attn_norm_gain, attn_norm_shift=attn_norm_shift, up_weight=up_weight, up_bias=up_bias, down_weight=down_weight, down_bias=down_bias, ffn_norm_gain=ffn_norm_gain, ffn_norm_shift=ffn_norm_shift, out_cotangent=out_cotangent)


@jax.custom_vjp
def low(v):
    return lax.optimization_barrier(v.astype(jnp.bfloat16)).astype(jnp.float32)

@jax.custom_vjp
def low_back(v):
    return v

def low_keep(v):
    return (low(v), None)

def low_pass(kept, grad):
    return (grad,)

def back_keep(v):
    return (v, None)

def back_low(kept, grad):
    return (low(grad),)
low.defvjp(low_keep, low_pass)
low_back.defvjp(back_keep, back_low)
precise = lax.Precision.HIGHEST
epsilon = 1e-12

def rounded_both(value):
    return low_back(low(value))

def matmul(left, right):
    return jnp.dot(left, right, precision=precise, preferred_element_type=jnp.float32)

def normalize(hidden, gain, shift):
    centred = hidden - lax.optimization_barrier(jnp.mean(hidden, axis=-1, keepdims=True))
    variance = lax.optimization_barrier(jnp.mean(centred * centred, axis=-1, keepdims=True))
    return centred * lax.rsqrt(variance + epsilon) * gain + shift

def sequence(inputs, token_codes, parameters):
    query_weight, query_bias, key_weight, value_weight, value_bias, output_weight, output_bias, attn_gain, attn_shift, up_weight, up_bias, down_weight, down_bias, ffn_gain, ffn_shift = parameters
    length = inputs.shape[0]
    lowered = low(inputs)
    queries = rounded_both(matmul(lowered, query_weight) + query_bias)
    key_rows = rounded_both(matmul(lowered, key_weight))
    values = rounded_both(matmul(lowered, value_weight) + value_bias)
    key_heads = key_rows.reshape(length, H, DH)
    value_heads = values.reshape(length, H, DH)
    targets = token_codes // 2 * 2 + 1
    block_rows = min(512, length)
    score_scale = DH ** (-0.5)

    def attend(block_pair):
        query_block, target_block = block_pair
        scores = jnp.einsum('qhd,khd->qhk', query_block, key_heads, precision=precise) * score_scale
        scores = low_back(scores)
        allowed = (token_codes[None, :] == target_block[:, None])[:, None, :]
        scores = jnp.where(allowed, scores, -1e+30)
        probability = low(jax.nn.softmax(scores, axis=-1))
        return jnp.einsum('qhk,khd->qhd', probability, value_heads, precision=precise)
    mixed_rows = lax.map(jax.checkpoint(attend), (queries.reshape(length // block_rows, block_rows, H, DH), targets.reshape(length // block_rows, block_rows)))
    mixed_rows = rounded_both(mixed_rows.reshape(length, D))
    attended = low_back(matmul(mixed_rows, output_weight) + output_bias)
    normed_attn = normalize(inputs + attended, attn_gain, attn_shift)
    hidden = low_back(matmul(low(normed_attn), up_weight) + up_bias)
    activated = low(jax.nn.gelu(hidden, approximate=False))
    branch = low_back(matmul(activated, down_weight) + down_bias)
    return normalize(normed_attn + branch, ffn_gain, ffn_shift)

def reference(tokens, segment_ids, valid_tokens, query_weight, query_bias, key_weight, value_weight, value_bias, output_weight, output_bias, attn_norm_gain, attn_norm_shift, up_weight, up_bias, down_weight, down_bias, ffn_norm_gain, ffn_norm_shift, out_cotangent):
    parameters = (query_weight, query_bias, key_weight, value_weight, value_bias, output_weight, output_bias, attn_norm_gain, attn_norm_shift, up_weight, up_bias, down_weight, down_bias, ffn_norm_gain, ffn_norm_shift)
    token_codes = segment_ids * 2 + valid_tokens
    inputs = tokens.astype(jnp.float32)

    def forward(layer_input, masters):
        rounded = jax.tree.map(low, masters)
        return lax.map(lambda block_pair: sequence(block_pair[0], block_pair[1], rounded), (layer_input, token_codes))
    output, backward = jax.vjp(forward, inputs, parameters)
    input_grad, gradients = backward(out_cotangent.astype(jnp.float32))
    return (output, input_grad, gradients[0], gradients[1], gradients[2], gradients[3], gradients[4], gradients[5], gradients[6], gradients[7], gradients[8], gradients[9], gradients[10], gradients[11], gradients[12], gradients[13], gradients[14])
```

```python
import math
from functools import partial

import jax
import jax.numpy as jnp
from jax import lax
from jax.experimental import pallas as pl
from jax.experimental.pallas import tpu as pltpu
from jax.sharding import PartitionSpec as P

H = 12
DH = 64
VMEM_LIMIT = 60 * 1024 * 1024

LOG2E = 1.4426950408889634
BQ = 512
BK = 512
HALF = BK // 2
PAD = BK + HALF
LANES = 128


def nt(a, b):
    return lax.dot_general(a, b, (((1,), (1,)), ((), ())), preferred_element_type=jnp.float32)


def nn(a, b):
    return lax.dot_general(a, b, (((1,), (0,)), ((), ())), preferred_element_type=jnp.float32)


def code_columns(seg_ref, val_ref, kcode, pad):
    count, width = seg_ref.shape
    for i in range(count):
        code = (seg_ref[i : i + 1, :] * 2 + val_ref[i : i + 1, :]).astype(jnp.float32)
        for j in range(width // LANES):
            piece = code[:, j * LANES : (j + 1) * LANES]
            at = i * width + j * LANES
            kcode[at : at + LANES, :] = jnp.broadcast_to(piece, (LANES, LANES)).T
    kcode[count * width :, :] = jnp.full((pad, LANES), -1.0, jnp.float32)


def total(values):
    return jnp.sum(values.astype(jnp.float32)).astype(jnp.int32)


def key_range(seg_ref, val_ref, block, start):
    seg = seg_ref[...]
    val = val_ref[...]
    count, width = seg.shape
    position = lax.broadcasted_iota(jnp.int32, (count, width), 0) * width + lax.broadcasted_iota(
        jnp.int32, (count, width), 1
    )
    in_block = (position >= start) & (position < start + block)
    low = jnp.min(jnp.where(in_block, seg, 1 << 20).astype(jnp.float32)).astype(jnp.int32)
    high = jnp.max(jnp.where(in_block, seg, -1).astype(jnp.float32)).astype(jnp.int32)
    length = count * width
    first = total(seg < low)
    end = total(seg <= high)
    last_valid = jnp.max(jnp.where(val == 1, position + 1, 0).astype(jnp.float32)).astype(jnp.int32)
    first_invalid = jnp.min(jnp.where(val == 1, length, position).astype(jnp.float32)).astype(jnp.int32)
    end = jnp.minimum(end, last_valid)
    origin = first // LANES * LANES
    blocks = (end - origin + BK - 1) // BK
    clear_end = jnp.minimum(end, first_invalid)
    clear_from = (first - origin + BK - 1) // BK
    clear_to = jnp.maximum(clear_end - origin, 0) // BK
    one_document = low == high
    clear_from = jnp.where(one_document, jnp.minimum(clear_from, blocks), blocks)
    clear_to = jnp.where(one_document, jnp.minimum(jnp.maximum(clear_to, clear_from), blocks), blocks)
    return origin, blocks, clear_from, clear_to


def attend_kernel(
    heads, chunks, ctx_axis, repeat,
    x_ref, w_ref, bias_ref, seg_ref, val_ref,
    k_out, v_out, q_out, of_out, ob_out, lse_out,
    kcode, q_ext, k_ext, v_ext, s_even, s_odd,
):
    width = heads * DH
    length = x_ref.shape[0]
    rows = length // (chunks * repeat)
    place = lax.rem(lax.axis_index(ctx_axis), repeat)
    code_columns(seg_ref, val_ref, kcode, PAD)
    wt = w_ref[...].astype(jnp.float32).T.astype(jnp.bfloat16)
    wq, wv = wt[:width], wt[2 * width : 3 * width]
    bias_q = bias_ref[0:width, 0:1]
    bias_v = bias_ref[width : 2 * width, 0:1]

    def keys(i, carry):
        at = pl.multiple_of(i * rows, LANES)
        x = x_ref[pl.ds(at, rows), :]
        k = nn(x, w_ref[:, width : 2 * width]).astype(jnp.bfloat16)
        v = (nt(wv, x) + bias_v).astype(jnp.bfloat16)
        v_out[:, pl.ds(at, rows)] = v
        for h in range(heads):
            one = k[:, h * DH : (h + 1) * DH]
            k_out[h, pl.ds(at, rows), :] = one
            k_ext[h, pl.ds(at, rows), :] = jnp.concatenate([one, one], axis=1)
            v_ext[h, 0:DH, pl.ds(at, rows)] = v[h * DH : (h + 1) * DH]
        return carry

    lax.fori_loop(0, chunks * repeat, keys, 0)
    k_out[:, length:, :] = jnp.zeros((heads, PAD, DH), jnp.bfloat16)
    k_ext[:, length:, :] = jnp.zeros((heads, PAD, 2 * DH), jnp.bfloat16)
    v_ext[:, 0:DH, length:] = jnp.zeros((heads, DH, PAD), jnp.bfloat16)
    v_ext[:, DH:, :] = jnp.ones((heads, 16, length + PAD), jnp.bfloat16)

    def queries(i, carry):
        at = pl.multiple_of((i * repeat + place) * rows, LANES)
        to = pl.ds(pl.multiple_of(i * rows, LANES), rows)
        q = (nt(wq, x_ref[pl.ds(at, rows), :]) + bias_q).astype(jnp.bfloat16)
        q_out[:, to] = q
        scaled = q.astype(jnp.float32) * (DH**-0.5 * LOG2E)
        high = scaled.astype(jnp.bfloat16)
        rest = (scaled - high.astype(jnp.float32)).astype(jnp.bfloat16)
        for h in range(heads):
            q_ext[h, 0:DH, to] = high[h * DH : (h + 1) * DH]
            q_ext[h, DH:, to] = rest[h * DH : (h + 1) * DH]
        return carry

    lax.fori_loop(0, chunks, queries, 0)
    per_chunk = rows // BQ

    def block(i, carry):
        chunk = i // per_chunk
        inner = pl.multiple_of((i - chunk * per_chunk) * BQ, LANES)
        start = (chunk * repeat + place) * rows + inner
        origin, blocks, clear_from, clear_to = key_range(seg_ref, val_ref, BQ, start)
        at = pl.multiple_of(i * BQ, LANES)
        which = chunk * repeat + place
        target = (seg_ref[pl.ds(which, 1), pl.ds(inner, BQ)] * 2 + 1).astype(jnp.float32)

        def scores(slot, key_at):
            for h in range(heads):
                slot[h] = nn(k_ext[h, pl.ds(key_at, HALF), :], q_ext[h, :, pl.ds(at, BQ)])

        def soften(masked, slot, key_at, state):
            if masked:
                code = kcode[pl.ds(key_at, HALF), :]
                allowed = jnp.concatenate([code] * (BQ // LANES), axis=1) == target
            fresh = []
            for h in range(heads):
                top, acc = state[2 * h : 2 * h + 2]
                s = slot[h]
                if masked:
                    s = jnp.where(allowed, s, -1e30)
                new = jnp.maximum(top, jnp.max(s, axis=0, keepdims=True))
                p = jnp.exp2(s - new).astype(jnp.bfloat16)
                acc = acc * jnp.exp2(top - new) + nn(v_ext[h, :, pl.ds(key_at, HALF)], p)
                fresh += [new, acc]
            return tuple(fresh)

        def step(masked, j, state):
            first = pl.multiple_of(origin + j * BK, LANES)
            second = pl.multiple_of(first + HALF, LANES)
            scores(s_odd, second)
            state = soften(masked, s_even, first, state)
            scores(s_even, pl.multiple_of(first + BK, LANES))
            return soften(masked, s_odd, second, state)

        state = ()
        for h in range(heads):
            state += (jnp.full((1, BQ), -1e30, jnp.float32), jnp.zeros((DH + 16, BQ), jnp.float32))
        scores(s_even, pl.multiple_of(origin, LANES))
        state = lax.fori_loop(0, clear_from, partial(step, True), state)
        state = lax.fori_loop(clear_from, clear_to, partial(step, False), state)
        state = lax.fori_loop(clear_to, blocks, partial(step, True), state)
        for h in range(heads):
            top, acc = state[2 * h : 2 * h + 2]
            low = acc[DH : DH + 1]
            out = acc[0:DH] / low
            of_out[h * DH : (h + 1) * DH, pl.ds(at, BQ)] = out
            ob_out[chunk, h * DH : (h + 1) * DH, pl.ds(inner, BQ)] = out.astype(jnp.bfloat16)
            lse_out[h : h + 1, pl.ds(at, BQ)] = top + jnp.log2(low)
        return carry

    lax.fori_loop(0, chunks * per_chunk, block, 0)


def attend(x, w, bias, seg, val, heads, chunks):
    length = x.shape[0]
    width = heads * DH
    count, rows = seg.shape
    repeat = count // chunks
    mine = chunks * rows
    shape = jax.ShapeDtypeStruct
    whole = pl.BlockSpec(memory_space=pltpu.VMEM)
    return pl.pallas_call(
        partial(attend_kernel, heads, chunks, "ctx", repeat),
        out_shape=(
            shape((heads, length + PAD, DH), jnp.bfloat16),
            shape((width, length), jnp.bfloat16),
            shape((width, mine), jnp.bfloat16),
            shape((width, mine), jnp.float32),
            shape((chunks, width, rows), jnp.bfloat16),
            shape((8, mine), jnp.float32),
        ),
        in_specs=[whole] * 5,
        out_specs=(whole,) * 6,
        scratch_shapes=[
            pltpu.VMEM((length + PAD, LANES), jnp.float32),
            pltpu.VMEM((heads, 2 * DH, mine), jnp.bfloat16),
            pltpu.VMEM((heads, length + PAD, 2 * DH), jnp.bfloat16),
            pltpu.VMEM((heads, DH + 16, length + PAD), jnp.bfloat16),
            pltpu.VMEM((heads, HALF, BQ), jnp.float32),
            pltpu.VMEM((heads, HALF, BQ), jnp.float32),
        ],
        compiler_params=pltpu.CompilerParams(vmem_limit_bytes=VMEM_LIMIT),
        name="attend",
    )(x, w, bias, seg, val)


def tn(a, b):
    return lax.dot_general(a, b, (((0,), (0,)), ((), ())), preferred_element_type=jnp.float32)


def flip(a):
    return a.astype(jnp.float32).T.astype(a.dtype)


def three_parts(row):
    high = row.astype(jnp.bfloat16)
    rest = row - high.astype(jnp.float32)
    middle = rest.astype(jnp.bfloat16)
    low = (rest - middle.astype(jnp.float32)).astype(jnp.bfloat16)
    empty = jnp.zeros((13, row.shape[1]), jnp.float32)
    return jnp.concatenate(
        [high.astype(jnp.float32), middle.astype(jnp.float32), low.astype(jnp.float32), empty], axis=0
    )


def retreat_kernel(
    heads, chunks, ctx_axis, repeat,
    x_ref, w_ref, k_ref, v_ref, q_ref, o_ref, lse_ref, do_ref, seg_ref, val_ref,
    dx_out, dw_out, db_out,
    krow, target, q_ext, kt_ext, v_ext, do_ext, do_rows, dq, dkv,
    s_even, s_odd, g_even, g_odd, dw, x_slot, dx_slot, in_sem, out_sem, v_sem,
):
    width = heads * DH
    length = x_ref.shape[0]
    count = chunks * repeat
    rows = length // (chunks * repeat)
    mine = chunks * rows
    place = lax.rem(lax.axis_index(ctx_axis), repeat)
    bf16 = jnp.bfloat16

    def fetch(i):
        slot = lax.rem(i, 2)
        source = x_ref.at[pl.ds(pl.multiple_of(i * rows, LANES), rows)]
        return pltpu.make_async_copy(source, x_slot.at[slot], in_sem.at[slot])

    def deliver(i):
        slot = lax.rem(i, 2)
        return pltpu.make_async_copy(dx_slot.at[slot], dx_out.at[i], out_sem.at[slot])

    fetch(0).start()
    values = [
        pltpu.make_async_copy(
            v_ref.at[pl.ds(h * DH, DH)], v_ext.at[h, pl.ds(0, DH), pl.ds(0, length)], v_sem.at[h]
        )
        for h in range(heads)
    ]
    for copy in values:
        copy.start()
    for i in range(chunks * repeat):
        code = (seg_ref[i : i + 1, :] * 2 + val_ref[i : i + 1, :]).astype(jnp.float32)
        krow[:, i * rows : (i + 1) * rows] = jnp.broadcast_to(code, (8, rows))
    krow[:, length:] = jnp.full((8, PAD), -1.0, jnp.float32)

    def keys(i, carry):
        at = pl.ds(pl.multiple_of(i * rows, LANES), rows)
        for h in range(heads):
            kt = flip(k_ref[h, at, :])
            kt_ext[h, 0:DH, at] = kt
            kt_ext[h, DH : 2 * DH, at] = kt
        return carry

    lax.fori_loop(0, chunks * repeat, keys, 0)
    kt_ext[:, 0 : 2 * DH, length:] = jnp.zeros((heads, 2 * DH, PAD), bf16)
    v_ext[:, 0:DH, length:] = jnp.zeros((heads, DH, PAD), bf16)
    kt_ext[:, 2 * DH :, :] = jnp.ones((heads, 16, length + PAD), bf16)
    v_ext[:, DH:, :] = jnp.ones((heads, 16, length + PAD), bf16)
    dkv[...] = jnp.zeros(dkv.shape, jnp.float32)
    dq[...] = jnp.zeros(dq.shape, jnp.float32)

    def queries(i, carry):
        at = pl.ds(pl.multiple_of(i * rows, LANES), rows)
        which = i * repeat + place
        code = (seg_ref[pl.ds(which, 1), :] * 2 + 1).astype(jnp.float32)
        for j in range(rows // LANES):
            piece = code[:, j * LANES : (j + 1) * LANES]
            target[pl.ds(pl.multiple_of(i * rows + j * LANES, LANES), LANES), :] = jnp.broadcast_to(
                piece, (LANES, LANES)
            ).T
        for h in range(heads):
            part = slice(h * DH, (h + 1) * DH)
            scaled = q_ref[part, at].astype(jnp.float32) * (DH**-0.5 * LOG2E)
            high = scaled.astype(bf16).astype(jnp.float32)
            extra = three_parts(-lse_ref[h : h + 1, at])
            full = jnp.concatenate([high, scaled - high, extra], axis=0)
            q_ext[h, at, :] = full.T.astype(bf16)
            grad = do_ref[i, part, :].astype(jnp.float32)
            delta = jnp.sum(grad * o_ref[part, at], axis=0, keepdims=True)
            do_rows[part, at] = do_ref[i, part, :]
            do_ext[h, at, :] = jnp.concatenate([grad, three_parts(-delta)], axis=0).T.astype(bf16)
        return carry

    lax.fori_loop(0, chunks, queries, 0)
    per_chunk = rows // BQ

    def block(i, carry):
        chunk = i // per_chunk
        inner = (i - chunk * per_chunk) * BQ
        start = (chunk * repeat + place) * rows + inner
        origin, blocks, clear_from, clear_to = key_range(seg_ref, val_ref, BQ, start)
        at = pl.ds(pl.multiple_of(i * BQ, LANES), BQ)

        def scores(s_slot, g_slot, key_at):
            key = pl.ds(key_at, HALF)
            for h in range(heads):
                s_slot[h] = nn(q_ext[h, at, :], kt_ext[h, :, key])
                g_slot[h] = nn(do_ext[h, at, :], v_ext[h, :, key])

        def absorb(masked, s_slot, g_slot, key_at):
            key = pl.ds(key_at, HALF)
            if masked:
                code = krow[0:1, key]
                wanted = jnp.concatenate([target[at, :]] * (HALF // LANES), axis=1)
                allowed = wanted == code
            for h in range(heads):
                part = slice(h * DH, (h + 1) * DH)
                p = jnp.exp2(s_slot[h])
                if masked:
                    p = jnp.where(allowed, p, 0.0)
                ds = (p * g_slot[h]).astype(bf16)
                dkv[width + h * DH : width + (h + 1) * DH, key] += nn(do_rows[part, at], p.astype(bf16))
                dkv[part, key] += nn(q_ref[part, at], ds)
                dq[h, at, :] += nn(ds, k_ref[h, key, :])

        def step(masked, j, carry):
            first = pl.multiple_of(origin + j * BK, LANES)
            second = pl.multiple_of(first + HALF, LANES)
            scores(s_odd, g_odd, second)
            absorb(masked, s_even, g_even, first)
            scores(s_even, g_even, pl.multiple_of(first + BK, LANES))
            absorb(masked, s_odd, g_odd, second)
            return carry

        scores(s_even, g_even, pl.multiple_of(origin, LANES))
        lax.fori_loop(0, clear_from, partial(step, True), 0)
        lax.fori_loop(clear_from, clear_to, partial(step, False), 0)
        lax.fori_loop(clear_to, blocks, partial(step, True), 0)
        return carry

    for copy in values:
        copy.wait()
    lax.fori_loop(0, chunks * per_chunk, block, 0)

    wt = w_ref[...].astype(jnp.float32).T.astype(bf16)
    scale = DH**-0.5
    one = jnp.ones((8, rows), bf16)
    dw[...] = jnp.zeros(dw.shape, jnp.float32)
    db_out[...] = jnp.zeros(db_out.shape, jnp.float32)

    def spread(i, carry):
        slot = lax.rem(i, 2)

        @pl.when(i + 1 < count)
        def _():
            fetch(i + 1).start()

        fetch(i).wait()

        @pl.when(i >= 2)
        def _():
            deliver(i - 2).wait()

        at = pl.ds(pl.multiple_of(i * rows, LANES), rows)
        dk = (dkv[0:width, at] * scale).astype(bf16)
        dv = dkv[width:, at].astype(bf16)
        both = jnp.concatenate([dk, dv], axis=0)
        dx_slot[slot] = tn(both, wt[width : 3 * width]).astype(bf16)
        dw[width : 3 * width, :] += nn(both, x_slot[slot])
        db_out[:, width:] += nt(one, dv)

        @pl.when(lax.rem(i, repeat) == place)
        def _():
            own = pl.ds(pl.multiple_of(i // repeat * rows, LANES), rows)
            grad = jnp.concatenate([dq[h, own, :] for h in range(heads)], axis=1) * scale
            grad = grad.astype(bf16)
            dx_slot[slot] = (dx_slot[slot].astype(jnp.float32) + nn(grad, wt[0:width])).astype(bf16)
            dw[0:width, :] += tn(grad, x_slot[slot])
            db_out[:, 0:width] += nn(one, grad)

        deliver(i).start()
        return carry

    lax.fori_loop(0, count, spread, 0)
    deliver(count - 2).wait()
    deliver(count - 1).wait()
    dw_out[...] = dw[...].T.astype(bf16)


def retreat(x, w, k, v, q, o, lse, do, seg, val, heads, chunks):
    length, model = x.shape
    width = heads * DH
    count, rows = seg.shape
    repeat = count // chunks
    mine = chunks * rows
    shape = jax.ShapeDtypeStruct
    whole = pl.BlockSpec(memory_space=pltpu.VMEM)
    f32, bf16 = jnp.float32, jnp.bfloat16
    return pl.pallas_call(
        partial(retreat_kernel, heads, chunks, "ctx", repeat),
        out_shape=(
            shape((count, rows, model), bf16),
            shape((model, w.shape[1]), bf16),
            shape((8, 2 * width), f32),
        ),
        in_specs=[whole if i not in (0, 3) else pl.BlockSpec(memory_space=pl.ANY) for i in range(10)],
        out_specs=(pl.BlockSpec(memory_space=pl.ANY), whole, whole),
        scratch_shapes=[
            pltpu.VMEM((8, length + PAD), f32),
            pltpu.VMEM((mine, LANES), f32),
            pltpu.VMEM((heads, mine, 2 * DH + 16), bf16),
            pltpu.VMEM((heads, 2 * DH + 16, length + PAD), bf16),
            pltpu.VMEM((heads, DH + 16, length + PAD), bf16),
            pltpu.VMEM((heads, mine, DH + 16), bf16),
            pltpu.VMEM((width, mine), bf16),
            pltpu.VMEM((heads, mine, DH), f32),
            pltpu.VMEM((2 * width, length + PAD), f32),
        ]
        + [pltpu.VMEM((heads, BQ, HALF), f32)] * 4
        + [
            pltpu.VMEM((w.shape[1], model), f32),
            pltpu.VMEM((2, rows, model), bf16),
            pltpu.VMEM((2, rows, model), bf16),
            pltpu.SemaphoreType.DMA((2,)),
            pltpu.SemaphoreType.DMA((2,)),
            pltpu.SemaphoreType.DMA((heads,)),
        ],
        compiler_params=pltpu.CompilerParams(vmem_limit_bytes=VMEM_LIMIT),
        name="retreat",
    )(x, w, k, v, q, o, lse, do, seg, val)


EPSILON = 1e-12
FF_BLOCK = 512


def gelu_pair(u):
    z = jnp.abs(u) * (0.5**0.5)
    t = 1.0 / (1.0 + 0.3275911 * z)
    bell = jnp.exp(-z * z)
    poly = t * (
        0.254829592 + t * (-0.284496736 + t * (1.421413741 + t * (-1.453152027 + t * 1.061405429)))
    )
    half = 0.5 * poly * bell
    below = jnp.where(u < 0.0, half, 1.0 - half)
    return u * below, below + u * bell * 0.3989422804014327


def standard(hidden):
    centred = hidden - jnp.mean(hidden, axis=-1, keepdims=True)
    scale = lax.rsqrt(jnp.mean(centred * centred, axis=-1, keepdims=True) + EPSILON)
    return centred * scale, scale


def norm_back(grad, gain, normal, scale):
    t = grad * gain
    return scale * (
        t
        - jnp.mean(t, axis=-1, keepdims=True)
        - normal * jnp.mean(t * normal, axis=-1, keepdims=True)
    )


def middle_kernel(
    o_ref, x_ref, cot_ref, wo_ref, w1_ref, w2_ref, small_ref, b1_ref,
    out_ref, e1_ref, do_ref, dwo_ref, dw1_ref, dw2_ref, dsmall_ref, db1_ref,
    act, slope, y1_ref, normal_ref, r2_ref, y1t_ref, grad_ref,
):
    bf16 = jnp.bfloat16
    groups, width, rows = o_ref.shape
    hidden_width = w1_ref.shape[1]
    steps = hidden_width // FF_BLOCK
    row = lambda i: small_ref[i : i + 1, :]
    ones = jnp.ones((8, rows), bf16)
    o = o_ref[...].reshape(groups * width, rows)
    n1 = x_ref[...].astype(jnp.float32) + (tn(o, wo_ref[...]) + row(0))
    normal, scale_one = standard(n1)
    normal_ref[...] = normal
    y1 = normal * row(1) + row(2)
    y1_ref[...] = y1
    y1_low = y1.astype(bf16)
    y1t_ref[...] = y1.T.astype(bf16)
    grad_ref[...] = jnp.zeros(grad_ref.shape, jnp.float32)

    def forward(i, carry):
        at = pl.ds(pl.multiple_of(i * FF_BLOCK, FF_BLOCK), FF_BLOCK)
        u = nn(y1_low, w1_ref[:, at]) + b1_ref[0:1, at]
        value, gradient = gelu_pair(u)
        value = value.astype(bf16)
        act[:, at] = value
        slope[:, at] = gradient
        grad_ref[...] += nn(value, w2_ref[at, :])
        return carry

    lax.fori_loop(0, steps, forward, 0)
    normal_two, scale_two = standard(y1_ref[...] + (grad_ref[...] + row(3)))
    out_ref[...] = normal_two * row(4) + row(5)
    cot = cot_ref[...].astype(jnp.float32)
    dsmall_ref[4:5, :] = jnp.sum(cot * normal_two, axis=0, keepdims=True)
    dsmall_ref[5:6, :] = jnp.sum(cot, axis=0, keepdims=True)
    e2 = norm_back(cot, row(4), normal_two, scale_two)
    grad_ref[...] = e2
    r2 = e2.astype(bf16)
    r2_ref[...] = r2
    dsmall_ref[3:4, :] = nn(ones, r2)[0:1]

    def backward(i, carry):
        at = pl.ds(pl.multiple_of(i * FF_BLOCK, FF_BLOCK), FF_BLOCK)
        dw2_ref[at, :] = tn(act[:, at], r2_ref[...]).astype(bf16)
        du = (nt(r2_ref[...], w2_ref[at, :]) * slope[:, at]).astype(bf16)
        db1_ref[:, at] = nn(ones, du)
        dw1_ref[:, at] = nn(y1t_ref[...], du).astype(bf16)
        grad_ref[...] += nt(du, w1_ref[:, at])
        return carry

    lax.fori_loop(0, steps, backward, 0)
    grad = grad_ref[...]
    normal = normal_ref[...]
    dsmall_ref[1:2, :] = jnp.sum(grad * normal, axis=0, keepdims=True)
    dsmall_ref[2:3, :] = jnp.sum(grad, axis=0, keepdims=True)
    e1 = norm_back(grad, row(1), normal, scale_one)
    e1_ref[...] = e1
    r1 = e1.astype(bf16)
    dsmall_ref[0:1, :] = nn(ones, r1)[0:1]
    dsmall_ref[6:8, :] = jnp.zeros((2, dsmall_ref.shape[1]), jnp.float32)
    dwo_ref[...] = nn(o, r1).astype(bf16)
    do_ref[...] = nt(wo_ref[...], r1).astype(bf16).reshape(groups, width, rows)


def middle(o, x, cot, wo, w1, w2, small, b1):
    groups, width, rows = o.shape
    model = x.shape[1]
    hidden_width = w1.shape[1]
    shape = jax.ShapeDtypeStruct
    whole = pl.BlockSpec(memory_space=pltpu.VMEM)
    f32, bf16 = jnp.float32, jnp.bfloat16
    return pl.pallas_call(
        middle_kernel,
        out_shape=(
            shape((rows, model), f32),
            shape((rows, model), f32),
            shape(o.shape, bf16),
            shape(wo.shape, bf16),
            shape(w1.shape, bf16),
            shape(w2.shape, bf16),
            shape((8, model), f32),
            shape((8, hidden_width), f32),
        ),
        in_specs=[whole] * 8,
        out_specs=(whole,) * 8,
        scratch_shapes=[
            pltpu.VMEM((rows, hidden_width), bf16),
            pltpu.VMEM((rows, hidden_width), f32),
            pltpu.VMEM((rows, model), f32),
            pltpu.VMEM((rows, model), f32),
            pltpu.VMEM((rows, model), bf16),
            pltpu.VMEM((model, rows), bf16),
            pltpu.VMEM((rows, model), f32),
        ],
        compiler_params=pltpu.CompilerParams(vmem_limit_bytes=VMEM_LIMIT),
        name="middle",
    )(o, x, cot, wo, w1, w2, small, b1)


def on_device(
    tokens, segment_ids, valid_tokens, query_weight, query_bias, key_weight, value_weight, value_bias,
    output_weight, output_bias, attn_norm_gain, attn_norm_shift, up_weight, up_bias, down_weight,
    down_bias, ffn_norm_gain, ffn_norm_shift, out_cotangent,
):
    both = ("seq", "ctx")
    bf16 = jnp.bfloat16
    count = lax.axis_size("ctx")
    chunks = math.gcd(H, count)
    repeat = count // chunks
    heads = H // chunks
    width = heads * DH
    x = tokens[0]
    rows, model = x.shape
    group = lax.axis_index("ctx") // repeat

    def gather(a):
        return lax.all_gather(a.astype(bf16), both, axis=0, tiled=True)

    def share(a):
        return lax.dynamic_slice_in_dim(a, group * width, width, a.ndim - 1)

    wq, wk, wv = gather(query_weight), gather(key_weight), gather(value_weight)
    wo, w1, w2 = gather(output_weight), gather(up_weight), gather(down_weight)
    small_parts = (output_bias, attn_norm_gain, attn_norm_shift, down_bias, ffn_norm_gain, ffn_norm_shift)
    small = [gather(a).astype(jnp.float32) for a in small_parts]
    small = jnp.stack(small + [jnp.zeros_like(small[0])] * 2)
    b1 = jnp.broadcast_to(gather(up_bias).astype(jnp.float32)[None], (8, up_bias.shape[0] * lax.axis_size(both)))
    bias = jnp.concatenate([share(gather(query_bias)), share(gather(value_bias))]).astype(jnp.float32)
    bias = jnp.broadcast_to(bias[:, None], (2 * width, LANES))
    padded = -(-3 * width // LANES) * LANES
    w = jnp.concatenate(
        [share(wq), share(wk), share(wv), jnp.zeros((model, padded - 3 * width), bf16)], axis=1
    )
    x_all = lax.all_gather(x, "ctx", axis=0, tiled=True)
    seg = lax.all_gather(segment_ids[0], "ctx", axis=0)
    val = lax.all_gather(valid_tokens[0], "ctx", axis=0)
    k, v, q, o_float, o_send, lse = attend(x_all, w, bias, seg, val, heads, chunks)
    groups = [[g * repeat + r for g in range(chunks)] for r in range(repeat)]

    def exchange(a):
        return lax.all_to_all(a, "ctx", 0, 0, axis_index_groups=groups, tiled=True)

    output, e1, do, dwo, dw1, dw2, dsmall, db1 = middle(
        exchange(o_send), x, out_cotangent[0], wo, w1, w2, small, b1
    )
    dx, dw, db = retreat(x_all, w, k, v, q, o_float, lse, exchange(do), seg, val, heads, chunks)
    dx = lax.psum_scatter(dx, "ctx", scatter_dimension=0, tiled=True)[0]

    def place(a, wide):
        return lax.dynamic_update_slice_in_dim(
            jnp.zeros(a.shape[:-1] + (wide,), a.dtype), a, group * width, a.ndim - 1
        )

    def scatter(a):
        return lax.psum_scatter(a, both, scatter_dimension=0, tiled=True).astype(jnp.float32)

    dwq, dwk, dwv = [scatter(place(dw[:, i * width : (i + 1) * width], model)) for i in range(3)]
    dbq, dbv = [scatter(place(db[0, i * width : (i + 1) * width], model)) for i in range(2)]
    dbo, dg1, dc1, db2, dg2, dc2 = [scatter(dsmall[i]) for i in range(6)]
    return (
        output[None],
        (e1 + dx.astype(jnp.float32))[None],
        dwq, dbq, dwk, dwv, dbv,
        scatter(dwo), dbo, dg1, dc1,
        scatter(dw1), scatter(db1[0]), scatter(dw2), db2, dg2, dc2,
    )


def solution(mesh):
    in_specs = (
        P("seq", "ctx", None),
        P("seq", "ctx"),
        P("seq", "ctx"),
        P(("seq", "ctx"), None),
        P(("seq", "ctx")),
        P(("seq", "ctx"), None),
        P(("seq", "ctx"), None),
        P(("seq", "ctx")),
        P(("seq", "ctx"), None),
        P(("seq", "ctx")),
        P(("seq", "ctx")),
        P(("seq", "ctx")),
        P(("seq", "ctx"), None),
        P(("seq", "ctx")),
        P(("seq", "ctx"), None),
        P(("seq", "ctx")),
        P(("seq", "ctx")),
        P(("seq", "ctx")),
        P("seq", "ctx", None),
    )
    out_specs = (
        P("seq", "ctx", None),
        P("seq", "ctx", None),
        P(("seq", "ctx"), None),
        P(("seq", "ctx")),
        P(("seq", "ctx"), None),
        P(("seq", "ctx"), None),
        P(("seq", "ctx")),
        P(("seq", "ctx"), None),
        P(("seq", "ctx")),
        P(("seq", "ctx")),
        P(("seq", "ctx")),
        P(("seq", "ctx"), None),
        P(("seq", "ctx")),
        P(("seq", "ctx"), None),
        P(("seq", "ctx")),
        P(("seq", "ctx")),
        P(("seq", "ctx")),
    )
    return jax.shard_map(
        on_device, mesh=mesh, in_specs=in_specs, out_specs=out_specs, check_vma=False
    )
```

```python
import math
from functools import partial

import jax
import jax.numpy as jnp
from jax import lax
from jax.experimental import pallas as pl
from jax.experimental.pallas import tpu as pltpu
from jax.sharding import PartitionSpec as P

H = 12
DH = 64
VMEM_LIMIT = 60 * 1024 * 1024

LOG2E = 1.4426950408889634
BQ = 512
BK = 512
HALF = BK // 2
PAD = BK + HALF
LANES = 128


def nt(a, b):
    return lax.dot_general(a, b, (((1,), (1,)), ((), ())), preferred_element_type=jnp.float32)


def nn(a, b):
    return lax.dot_general(a, b, (((1,), (0,)), ((), ())), preferred_element_type=jnp.float32)


def code_columns(code_ref, kcode, pad):
    count, width = code_ref.shape
    for i in range(count):
        code = code_ref[i : i + 1, :].astype(jnp.float32)
        for j in range(width // LANES):
            piece = code[:, j * LANES : (j + 1) * LANES]
            at = i * width + j * LANES
            kcode[at : at + LANES, :] = jnp.broadcast_to(piece, (LANES, LANES)).T
    kcode[count * width :, :] = jnp.full((pad, LANES), -1.0, jnp.float32)


def unshard(vec, at, each):
    devices = vec.shape[0]
    shard = vec[:, at : at + each].astype(jnp.bfloat16)
    size = devices * each
    owner = lambda shape, axis: jnp.floor(
        (lax.broadcasted_iota(jnp.int32, shape, axis).astype(jnp.float32) + 0.5) / each
    )
    column = lax.broadcasted_iota(jnp.int32, (each, size), 1).astype(jnp.float32)
    inner = column - owner((each, size), 1) * each
    place = lax.broadcasted_iota(jnp.int32, (each, size), 0).astype(jnp.float32)
    repeated = nn(shard, (inner == place).astype(jnp.bfloat16))
    device = lax.broadcasted_iota(jnp.int32, (devices, size), 0).astype(jnp.float32)
    return jnp.sum(jnp.where(owner((devices, size), 1) == device, repeated, 0.0), axis=0, keepdims=True)


def total(values):
    return jnp.sum(values.astype(jnp.float32)).astype(jnp.int32)


def key_range(code_ref, block, start):
    code = code_ref[...]
    seg = lax.shift_right_logical(code, 1)
    val = code & 1
    count, width = seg.shape
    position = lax.broadcasted_iota(jnp.int32, (count, width), 0) * width + lax.broadcasted_iota(
        jnp.int32, (count, width), 1
    )
    in_block = (position >= start) & (position < start + block)
    low = jnp.min(jnp.where(in_block, seg, 1 << 20).astype(jnp.float32)).astype(jnp.int32)
    high = jnp.max(jnp.where(in_block, seg, -1).astype(jnp.float32)).astype(jnp.int32)
    length = count * width
    first = total(seg < low)
    end = total(seg <= high)
    last_valid = jnp.max(jnp.where(val == 1, position + 1, 0).astype(jnp.float32)).astype(jnp.int32)
    first_invalid = jnp.min(jnp.where(val == 1, length, position).astype(jnp.float32)).astype(jnp.int32)
    end = jnp.minimum(end, last_valid)
    origin = first // LANES * LANES
    blocks = (end - origin + BK - 1) // BK
    clear_end = jnp.minimum(end, first_invalid)
    clear_from = (first - origin + BK - 1) // BK
    clear_to = jnp.maximum(clear_end - origin, 0) // BK
    one_document = low == high
    clear_from = jnp.where(one_document, jnp.minimum(clear_from, blocks), blocks)
    clear_to = jnp.where(one_document, jnp.minimum(jnp.maximum(clear_to, clear_from), blocks), blocks)
    return origin, blocks, clear_from, clear_to


def attend_kernel(
    heads, chunks, ctx_axis, repeat,
    x_ref, w_ref, vec_ref, codes_ref,
    k_out, v_out, q_out, of_out, ob_out, lse_out, code_ref,
    kcode, q_ext, k_ext, v_ext, s_even, s_odd,
):
    width = heads * DH
    length = x_ref.shape[0]
    rows = length // (chunks * repeat)
    place = lax.rem(lax.axis_index(ctx_axis), repeat)
    code_ref[...] = codes_ref[:, 0, :]
    code_columns(code_ref, kcode, PAD)
    wt = w_ref[...].astype(jnp.float32).T.astype(jnp.bfloat16)
    wq, wv = wt[:width], wt[2 * width : 3 * width]
    vec = vec_ref[:, 0, :]
    each = x_ref.shape[1] // vec.shape[0]
    group = lax.axis_index(ctx_axis) // repeat

    def bias_column(which):
        whole = unshard(vec, which * each, each)
        row = jnp.zeros((1, width), jnp.float32)
        for k in range(chunks):
            row = row + jnp.where(group == k, whole[:, k * width : (k + 1) * width], 0.0)
        extra = -width % LANES
        row = jnp.concatenate([row, jnp.zeros((1, extra), jnp.float32)], axis=1)
        return jnp.broadcast_to(row, (LANES, width + extra)).T[0:width, 0:1]

    bias_q, bias_v = bias_column(6), bias_column(7)

    def keys(i, carry):
        at = pl.multiple_of(i * rows, LANES)
        x = x_ref[pl.ds(at, rows), :]
        k = nn(x, w_ref[:, width : 2 * width]).astype(jnp.bfloat16)
        v = (nt(wv, x) + bias_v).astype(jnp.bfloat16)
        v_out[:, pl.ds(at, rows)] = v
        for h in range(heads):
            one = k[:, h * DH : (h + 1) * DH]
            k_out[h, pl.ds(at, rows), :] = one
            k_ext[h, pl.ds(at, rows), :] = jnp.concatenate([one, one], axis=1)
            v_ext[h, 0:DH, pl.ds(at, rows)] = v[h * DH : (h + 1) * DH]
        return carry

    lax.fori_loop(0, chunks * repeat, keys, 0)
    k_out[:, length:, :] = jnp.zeros((heads, PAD, DH), jnp.bfloat16)
    k_ext[:, length:, :] = jnp.zeros((heads, PAD, 2 * DH), jnp.bfloat16)
    v_ext[:, 0:DH, length:] = jnp.zeros((heads, DH, PAD), jnp.bfloat16)
    v_ext[:, DH:, :] = jnp.ones((heads, 16, length + PAD), jnp.bfloat16)

    def queries(i, carry):
        at = pl.multiple_of((i * repeat + place) * rows, LANES)
        to = pl.ds(pl.multiple_of(i * rows, LANES), rows)
        q = (nt(wq, x_ref[pl.ds(at, rows), :]) + bias_q).astype(jnp.bfloat16)
        q_out[:, to] = q
        scaled = q.astype(jnp.float32) * (DH**-0.5 * LOG2E)
        high = scaled.astype(jnp.bfloat16)
        rest = (scaled - high.astype(jnp.float32)).astype(jnp.bfloat16)
        for h in range(heads):
            q_ext[h, 0:DH, to] = high[h * DH : (h + 1) * DH]
            q_ext[h, DH:, to] = rest[h * DH : (h + 1) * DH]
        return carry

    lax.fori_loop(0, chunks, queries, 0)
    per_chunk = rows // BQ

    def block(i, carry):
        chunk = i // per_chunk
        inner = pl.multiple_of((i - chunk * per_chunk) * BQ, LANES)
        start = (chunk * repeat + place) * rows + inner
        origin, blocks, clear_from, clear_to = key_range(code_ref, BQ, start)
        at = pl.multiple_of(i * BQ, LANES)
        which = chunk * repeat + place
        target = (code_ref[pl.ds(which, 1), pl.ds(inner, BQ)] | 1).astype(jnp.float32)

        def scores(slot, key_at):
            for h in range(heads):
                slot[h] = nn(k_ext[h, pl.ds(key_at, HALF), :], q_ext[h, :, pl.ds(at, BQ)])

        def soften(masked, slot, key_at, state):
            if masked:
                code = kcode[pl.ds(key_at, HALF), :]
                allowed = jnp.concatenate([code] * (BQ // LANES), axis=1) == target
            fresh = []
            for h in range(heads):
                top, acc = state[2 * h : 2 * h + 2]
                s = slot[h]
                if masked:
                    s = jnp.where(allowed, s, -1e30)
                new = jnp.maximum(top, jnp.max(s, axis=0, keepdims=True))
                p = jnp.exp2(s - new).astype(jnp.bfloat16)
                acc = acc * jnp.exp2(top - new) + nn(v_ext[h, :, pl.ds(key_at, HALF)], p)
                fresh += [new, acc]
            return tuple(fresh)

        def step(masked, j, state):
            first = pl.multiple_of(origin + j * BK, LANES)
            second = pl.multiple_of(first + HALF, LANES)
            scores(s_odd, second)
            state = soften(masked, s_even, first, state)
            scores(s_even, pl.multiple_of(first + BK, LANES))
            return soften(masked, s_odd, second, state)

        state = ()
        for h in range(heads):
            state += (jnp.full((1, BQ), -1e30, jnp.float32), jnp.zeros((DH + 16, BQ), jnp.float32))
        scores(s_even, pl.multiple_of(origin, LANES))
        state = lax.fori_loop(0, clear_from, partial(step, True), state)
        state = lax.fori_loop(clear_from, clear_to, partial(step, False), state)
        state = lax.fori_loop(clear_to, blocks, partial(step, True), state)
        for h in range(heads):
            top, acc = state[2 * h : 2 * h + 2]
            low = acc[DH : DH + 1]
            out = acc[0:DH] / low
            of_out[h * DH : (h + 1) * DH, pl.ds(at, BQ)] = out
            ob_out[chunk, h * DH : (h + 1) * DH, pl.ds(inner, BQ)] = out.astype(jnp.bfloat16)
            lse_out[h : h + 1, pl.ds(at, BQ)] = top + jnp.log2(low)
        return carry

    lax.fori_loop(0, chunks * per_chunk, block, 0)


def attend(x, w, vec, codes, heads, chunks):
    length = x.shape[0]
    width = heads * DH
    count, _, rows = codes.shape
    repeat = count // chunks
    mine = chunks * rows
    shape = jax.ShapeDtypeStruct
    whole = pl.BlockSpec(memory_space=pltpu.VMEM)
    return pl.pallas_call(
        partial(attend_kernel, heads, chunks, "ctx", repeat),
        out_shape=(
            shape((heads, length + PAD, DH), jnp.bfloat16),
            shape((width, length), jnp.bfloat16),
            shape((width, mine), jnp.bfloat16),
            shape((width, mine), jnp.float32),
            shape((chunks, width, rows), jnp.bfloat16),
            shape((8, mine), jnp.float32),
            shape((count, rows), jnp.int32),
        ),
        in_specs=[whole] * 4,
        out_specs=(whole,) * 7,
        scratch_shapes=[
            pltpu.VMEM((length + PAD, LANES), jnp.float32),
            pltpu.VMEM((heads, 2 * DH, mine), jnp.bfloat16),
            pltpu.VMEM((heads, length + PAD, 2 * DH), jnp.bfloat16),
            pltpu.VMEM((heads, DH + 16, length + PAD), jnp.bfloat16),
            pltpu.VMEM((heads, HALF, BQ), jnp.float32),
            pltpu.VMEM((heads, HALF, BQ), jnp.float32),
        ],
        compiler_params=pltpu.CompilerParams(vmem_limit_bytes=VMEM_LIMIT),
        name="attend",
    )(x, w, vec, codes)


def tn(a, b):
    return lax.dot_general(a, b, (((0,), (0,)), ((), ())), preferred_element_type=jnp.float32)


def flip(a):
    return a.astype(jnp.float32).T.astype(a.dtype)


def three_parts(row):
    high = row.astype(jnp.bfloat16)
    rest = row - high.astype(jnp.float32)
    middle = rest.astype(jnp.bfloat16)
    low = (rest - middle.astype(jnp.float32)).astype(jnp.bfloat16)
    empty = jnp.zeros((13, row.shape[1]), jnp.float32)
    return jnp.concatenate(
        [high.astype(jnp.float32), middle.astype(jnp.float32), low.astype(jnp.float32), empty], axis=0
    )


def retreat_kernel(
    heads, chunks, ctx_axis, repeat,
    x_ref, w_ref, k_ref, v_ref, q_ref, o_ref, lse_ref, do_ref, code_ref,
    dx_out, dw_out, db_out,
    krow, target, q_ext, kt_ext, v_ext, do_ext, do_rows, dq, dkv,
    s_even, s_odd, g_even, g_odd, dw, x_slot, dx_slot, in_sem, out_sem, v_sem,
):
    width = heads * DH
    length = x_ref.shape[0]
    count = chunks * repeat
    rows = length // (chunks * repeat)
    mine = chunks * rows
    place = lax.rem(lax.axis_index(ctx_axis), repeat)
    bf16 = jnp.bfloat16

    def fetch(i):
        slot = lax.rem(i, 2)
        source = x_ref.at[pl.ds(pl.multiple_of(i * rows, LANES), rows)]
        return pltpu.make_async_copy(source, x_slot.at[slot], in_sem.at[slot])

    def deliver(i):
        slot = lax.rem(i, 2)
        return pltpu.make_async_copy(dx_slot.at[slot], dx_out.at[i], out_sem.at[slot])

    fetch(0).start()
    values = [
        pltpu.make_async_copy(
            v_ref.at[pl.ds(h * DH, DH)], v_ext.at[h, pl.ds(0, DH), pl.ds(0, length)], v_sem.at[h]
        )
        for h in range(heads)
    ]
    for copy in values:
        copy.start()
    for i in range(chunks * repeat):
        code = code_ref[i : i + 1, :].astype(jnp.float32)
        krow[:, i * rows : (i + 1) * rows] = jnp.broadcast_to(code, (8, rows))
    krow[:, length:] = jnp.full((8, PAD), -1.0, jnp.float32)

    def keys(i, carry):
        at = pl.ds(pl.multiple_of(i * rows, LANES), rows)
        for h in range(heads):
            kt = flip(k_ref[h, at, :])
            kt_ext[h, 0:DH, at] = kt
            kt_ext[h, DH : 2 * DH, at] = kt
        return carry

    lax.fori_loop(0, chunks * repeat, keys, 0)
    kt_ext[:, 0 : 2 * DH, length:] = jnp.zeros((heads, 2 * DH, PAD), bf16)
    v_ext[:, 0:DH, length:] = jnp.zeros((heads, DH, PAD), bf16)
    kt_ext[:, 2 * DH :, :] = jnp.ones((heads, 16, length + PAD), bf16)
    v_ext[:, DH:, :] = jnp.ones((heads, 16, length + PAD), bf16)
    dkv[...] = jnp.zeros(dkv.shape, jnp.float32)
    dq[...] = jnp.zeros(dq.shape, jnp.float32)

    def queries(i, carry):
        at = pl.ds(pl.multiple_of(i * rows, LANES), rows)
        which = i * repeat + place
        code = (code_ref[pl.ds(which, 1), :] | 1).astype(jnp.float32)
        for j in range(rows // LANES):
            piece = code[:, j * LANES : (j + 1) * LANES]
            target[pl.ds(pl.multiple_of(i * rows + j * LANES, LANES), LANES), :] = jnp.broadcast_to(
                piece, (LANES, LANES)
            ).T
        for h in range(heads):
            part = slice(h * DH, (h + 1) * DH)
            scaled = q_ref[part, at].astype(jnp.float32) * (DH**-0.5 * LOG2E)
            high = scaled.astype(bf16).astype(jnp.float32)
            extra = three_parts(-lse_ref[h : h + 1, at])
            full = jnp.concatenate([high, scaled - high, extra], axis=0)
            q_ext[h, at, :] = full.T.astype(bf16)
            grad = do_ref[i, part, :].astype(jnp.float32)
            delta = jnp.sum(grad * o_ref[part, at], axis=0, keepdims=True)
            do_rows[part, at] = do_ref[i, part, :]
            do_ext[h, at, :] = jnp.concatenate([grad, three_parts(-delta)], axis=0).T.astype(bf16)
        return carry

    lax.fori_loop(0, chunks, queries, 0)
    per_chunk = rows // BQ

    def block(i, carry):
        chunk = i // per_chunk
        inner = (i - chunk * per_chunk) * BQ
        start = (chunk * repeat + place) * rows + inner
        origin, blocks, clear_from, clear_to = key_range(code_ref, BQ, start)
        at = pl.ds(pl.multiple_of(i * BQ, LANES), BQ)

        def scores(s_slot, g_slot, key_at):
            key = pl.ds(key_at, HALF)
            for h in range(heads):
                s_slot[h] = nn(q_ext[h, at, :], kt_ext[h, :, key])
                g_slot[h] = nn(do_ext[h, at, :], v_ext[h, :, key])

        def absorb(masked, s_slot, g_slot, key_at):
            key = pl.ds(key_at, HALF)
            if masked:
                code = krow[0:1, key]
                wanted = jnp.concatenate([target[at, :]] * (HALF // LANES), axis=1)
                allowed = wanted == code
            for h in range(heads):
                part = slice(h * DH, (h + 1) * DH)
                p = jnp.exp2(s_slot[h])
                if masked:
                    p = jnp.where(allowed, p, 0.0)
                ds = (p * g_slot[h]).astype(bf16)
                dkv[width + h * DH : width + (h + 1) * DH, key] += nn(do_rows[part, at], p.astype(bf16))
                dkv[part, key] += nn(q_ref[part, at], ds)
                dq[h, at, :] += nn(ds, k_ref[h, key, :])

        def step(masked, j, carry):
            first = pl.multiple_of(origin + j * BK, LANES)
            second = pl.multiple_of(first + HALF, LANES)
            scores(s_odd, g_odd, second)
            absorb(masked, s_even, g_even, first)
            scores(s_even, g_even, pl.multiple_of(first + BK, LANES))
            absorb(masked, s_odd, g_odd, second)
            return carry

        scores(s_even, g_even, pl.multiple_of(origin, LANES))
        lax.fori_loop(0, clear_from, partial(step, True), 0)
        lax.fori_loop(clear_from, clear_to, partial(step, False), 0)
        lax.fori_loop(clear_to, blocks, partial(step, True), 0)
        return carry

    for copy in values:
        copy.wait()
    lax.fori_loop(0, chunks * per_chunk, block, 0)

    wt = w_ref[...].astype(jnp.float32).T.astype(bf16)
    scale = DH**-0.5
    one = jnp.ones((8, rows), bf16)
    dw[...] = jnp.zeros(dw.shape, jnp.float32)
    db_out[...] = jnp.zeros(db_out.shape, jnp.float32)

    def spread(i, carry):
        slot = lax.rem(i, 2)

        @pl.when(i + 1 < count)
        def _():
            fetch(i + 1).start()

        fetch(i).wait()

        @pl.when(i >= 2)
        def _():
            deliver(i - 2).wait()

        at = pl.ds(pl.multiple_of(i * rows, LANES), rows)
        dk = (dkv[0:width, at] * scale).astype(bf16)
        dv = dkv[width:, at].astype(bf16)
        both = jnp.concatenate([dk, dv], axis=0)
        dx_slot[slot] = tn(both, wt[width : 3 * width]).astype(bf16)
        dw[width : 3 * width, :] += nn(both, x_slot[slot])
        db_out[:, width:] += nt(one, dv)

        @pl.when(lax.rem(i, repeat) == place)
        def _():
            own = pl.ds(pl.multiple_of(i // repeat * rows, LANES), rows)
            grad = jnp.concatenate([dq[h, own, :] for h in range(heads)], axis=1) * scale
            grad = grad.astype(bf16)
            dx_slot[slot] = (dx_slot[slot].astype(jnp.float32) + nn(grad, wt[0:width])).astype(bf16)
            dw[0:width, :] += tn(grad, x_slot[slot])
            db_out[:, 0:width] += nn(one, grad)

        deliver(i).start()
        return carry

    lax.fori_loop(0, count, spread, 0)
    deliver(count - 2).wait()
    deliver(count - 1).wait()
    dw_out[...] = dw[...].T.astype(bf16)


def retreat(x, w, k, v, q, o, lse, do, codes, heads, chunks):
    length, model = x.shape
    width = heads * DH
    count, rows = codes.shape
    repeat = count // chunks
    mine = chunks * rows
    shape = jax.ShapeDtypeStruct
    whole = pl.BlockSpec(memory_space=pltpu.VMEM)
    f32, bf16 = jnp.float32, jnp.bfloat16
    return pl.pallas_call(
        partial(retreat_kernel, heads, chunks, "ctx", repeat),
        out_shape=(
            shape((count, rows, model), bf16),
            shape((model, w.shape[1]), bf16),
            shape((8, 2 * width), f32),
        ),
        in_specs=[whole if i not in (0, 3) else pl.BlockSpec(memory_space=pl.ANY) for i in range(9)],
        out_specs=(pl.BlockSpec(memory_space=pl.ANY), whole, whole),
        scratch_shapes=[
            pltpu.VMEM((8, length + PAD), f32),
            pltpu.VMEM((mine, LANES), f32),
            pltpu.VMEM((heads, mine, 2 * DH + 16), bf16),
            pltpu.VMEM((heads, 2 * DH + 16, length + PAD), bf16),
            pltpu.VMEM((heads, DH + 16, length + PAD), bf16),
            pltpu.VMEM((heads, mine, DH + 16), bf16),
            pltpu.VMEM((width, mine), bf16),
            pltpu.VMEM((heads, mine, DH), f32),
            pltpu.VMEM((2 * width, length + PAD), f32),
        ]
        + [pltpu.VMEM((heads, BQ, HALF), f32)] * 4
        + [
            pltpu.VMEM((w.shape[1], model), f32),
            pltpu.VMEM((2, rows, model), bf16),
            pltpu.VMEM((2, rows, model), bf16),
            pltpu.SemaphoreType.DMA((2,)),
            pltpu.SemaphoreType.DMA((2,)),
            pltpu.SemaphoreType.DMA((heads,)),
        ],
        compiler_params=pltpu.CompilerParams(vmem_limit_bytes=VMEM_LIMIT),
        name="retreat",
    )(x, w, k, v, q, o, lse, do, codes)


EPSILON = 1e-12
FF_BLOCK = 512


def gelu_pair(u):
    z = jnp.abs(u) * (0.5**0.5)
    t = 1.0 / (1.0 + 0.3275911 * z)
    bell = jnp.exp(-z * z)
    poly = t * (
        0.254829592 + t * (-0.284496736 + t * (1.421413741 + t * (-1.453152027 + t * 1.061405429)))
    )
    half = 0.5 * poly * bell
    below = jnp.where(u < 0.0, half, 1.0 - half)
    return u * below, below + u * bell * 0.3989422804014327


def standard(hidden):
    centred = hidden - jnp.mean(hidden, axis=-1, keepdims=True)
    scale = lax.rsqrt(jnp.mean(centred * centred, axis=-1, keepdims=True) + EPSILON)
    return centred * scale, scale


def norm_back(grad, gain, normal, scale):
    t = grad * gain
    return scale * (
        t
        - jnp.mean(t, axis=-1, keepdims=True)
        - normal * jnp.mean(t * normal, axis=-1, keepdims=True)
    )


def middle_kernel(
    o_ref, x_ref, cot_ref, wo_ref, w1_ref, w2_ref, vec_ref,
    out_ref, e1_ref, do_ref, dwo_ref, dw1_ref, dw2_ref, dsmall_ref, db1_ref,
    act, slope, y1_ref, normal_ref, r2_ref, y1t_ref, grad_ref, small_ref, b1_ref,
):
    bf16 = jnp.bfloat16
    groups, width, rows = o_ref.shape
    hidden_width = w1_ref.shape[1]
    steps = hidden_width // FF_BLOCK
    vec = vec_ref[:, 0, :]
    each = x_ref.shape[1] // vec.shape[0]
    for i in range(6):
        small_ref[i : i + 1, :] = unshard(vec, i * each, each)
    b1_ref[0:1, :] = unshard(vec, 8 * each, hidden_width // vec.shape[0])
    row = lambda i: small_ref[i : i + 1, :]
    ones = jnp.ones((8, rows), bf16)
    o = o_ref[...].reshape(groups * width, rows)
    n1 = x_ref[...].astype(jnp.float32) + (tn(o, wo_ref[...]) + row(0))
    normal, scale_one = standard(n1)
    normal_ref[...] = normal
    y1 = normal * row(1) + row(2)
    y1_ref[...] = y1
    y1_low = y1.astype(bf16)
    y1t_ref[...] = y1.T.astype(bf16)
    grad_ref[...] = jnp.zeros(grad_ref.shape, jnp.float32)

    def forward(i, carry):
        at = pl.ds(pl.multiple_of(i * FF_BLOCK, FF_BLOCK), FF_BLOCK)
        u = nn(y1_low, w1_ref[:, at]) + b1_ref[0:1, at]
        value, gradient = gelu_pair(u)
        value = value.astype(bf16)
        act[:, at] = value
        slope[:, at] = gradient
        grad_ref[...] += nn(value, w2_ref[at, :])
        return carry

    lax.fori_loop(0, steps, forward, 0)
    normal_two, scale_two = standard(y1_ref[...] + (grad_ref[...] + row(3)))
    out_ref[...] = normal_two * row(4) + row(5)
    cot = cot_ref[...].astype(jnp.float32)
    dsmall_ref[4:5, :] = jnp.sum(cot * normal_two, axis=0, keepdims=True)
    dsmall_ref[5:6, :] = jnp.sum(cot, axis=0, keepdims=True)
    e2 = norm_back(cot, row(4), normal_two, scale_two)
    grad_ref[...] = e2
    r2 = e2.astype(bf16)
    r2_ref[...] = r2
    dsmall_ref[3:4, :] = nn(ones, r2)[0:1]

    def backward(i, carry):
        at = pl.ds(pl.multiple_of(i * FF_BLOCK, FF_BLOCK), FF_BLOCK)
        dw2_ref[at, :] = tn(act[:, at], r2_ref[...]).astype(bf16)
        du = (nt(r2_ref[...], w2_ref[at, :]) * slope[:, at]).astype(bf16)
        db1_ref[:, at] = nn(ones, du)
        dw1_ref[:, at] = nn(y1t_ref[...], du).astype(bf16)
        grad_ref[...] += nt(du, w1_ref[:, at])
        return carry

    lax.fori_loop(0, steps, backward, 0)
    grad = grad_ref[...]
    normal = normal_ref[...]
    dsmall_ref[1:2, :] = jnp.sum(grad * normal, axis=0, keepdims=True)
    dsmall_ref[2:3, :] = jnp.sum(grad, axis=0, keepdims=True)
    e1 = norm_back(grad, row(1), normal, scale_one)
    e1_ref[...] = e1
    r1 = e1.astype(bf16)
    dsmall_ref[0:1, :] = nn(ones, r1)[0:1]
    dsmall_ref[6:8, :] = jnp.zeros((2, dsmall_ref.shape[1]), jnp.float32)
    dwo_ref[...] = nn(o, r1).astype(bf16)
    do_ref[...] = nt(wo_ref[...], r1).astype(bf16).reshape(groups, width, rows)


def middle(o, x, cot, wo, w1, w2, vec):
    groups, width, rows = o.shape
    model = x.shape[1]
    hidden_width = w1.shape[1]
    shape = jax.ShapeDtypeStruct
    whole = pl.BlockSpec(memory_space=pltpu.VMEM)
    f32, bf16 = jnp.float32, jnp.bfloat16
    return pl.pallas_call(
        middle_kernel,
        out_shape=(
            shape((rows, model), f32),
            shape((rows, model), f32),
            shape(o.shape, bf16),
            shape(wo.shape, bf16),
            shape(w1.shape, bf16),
            shape(w2.shape, bf16),
            shape((8, model), f32),
            shape((8, hidden_width), f32),
        ),
        in_specs=[whole] * 7,
        out_specs=(whole,) * 8,
        scratch_shapes=[
            pltpu.VMEM((rows, hidden_width), bf16),
            pltpu.VMEM((rows, hidden_width), f32),
            pltpu.VMEM((rows, model), f32),
            pltpu.VMEM((rows, model), f32),
            pltpu.VMEM((rows, model), bf16),
            pltpu.VMEM((model, rows), bf16),
            pltpu.VMEM((rows, model), f32),
            pltpu.VMEM((8, model), f32),
            pltpu.VMEM((8, hidden_width), f32),
        ],
        compiler_params=pltpu.CompilerParams(vmem_limit_bytes=VMEM_LIMIT),
        name="middle",
    )(o, x, cot, wo, w1, w2, vec)


MESH = pl.DeviceIdType.MESH


class Sender:
    def __init__(self, send_sems, recv_sems):
        self.send_sems, self.recv_sems, self.used, self.open = send_sems, recv_sems, 0, []

    def copy(self, source, target, device, when=None, until=None):
        index = self.used
        self.used += 1
        one = pltpu.make_async_remote_copy(
            src_ref=source,
            dst_ref=target,
            send_sem=self.send_sems.at[index],
            recv_sem=self.recv_sems.at[index],
            device_id=device,
            device_id_type=MESH,
        )
        if when is None:
            one.start()
        else:
            pl.when(when)(one.start)
        self.open.append((one, when))

        def arrive():
            if until is None:
                one.wait_recv()
            else:
                pl.when(until)(one.wait_recv)

        return arrive

    def finish(self):
        for one, when in self.open:
            if when is None:
                one.wait_send()
            else:
                pl.when(when)(one.wait_send)


def greet(seqs, count):
    s, c = lax.axis_index("seq"), lax.axis_index("ctx")
    barrier = pltpu.get_barrier_semaphore()
    for d in range(1, count):
        pl.semaphore_signal(barrier, inc=1, device_id=(s, lax.rem(c + d, count)), device_id_type=MESH)
    for d in range(1, seqs):
        pl.semaphore_signal(barrier, inc=1, device_id=(lax.rem(s + d, seqs), c), device_id_type=MESH)
    pl.semaphore_wait(barrier, count - 1 + seqs - 1)


def cube_steps(seqs, turn):
    bits = seqs.bit_length() - 1
    masks = []
    for j in range(bits):
        bit = lax.rem(j + turn, bits)
        mask = 0
        for k in range(bits):
            mask = mask + jnp.where(bit == k, 1 << k, 0)
        masks.append(mask)
    return masks


def across(s, mask):
    return s + mask * (1 - 2 * lax.rem(s // mask, 2))


def block_mates(rows):
    mates = 1
    while (mates * rows) % 16:
        mates *= 2
    return mates


def collect_kernel(
    seqs, count, chunks, semaphores,
    wq_ref, wk_ref, wv_ref, wo_ref, w1_ref, w2_ref, x_ref, code_ref, vec_ref,
    w_out, wo_out, w1_out, w2_out, x_out, code_out, vec_out,
    stage4, stage1, stage2, flat4, flat1, flat2, low4, low1, low2, share4,
    send_sems, recv_sems, here_sems,
):
    s, c = lax.axis_index("seq"), lax.axis_index("ctx")
    bf16 = jnp.bfloat16
    small_rows, model = wq_ref.shape
    tall_rows = w2_ref.shape[0]
    wide = w1_ref.shape[1]
    mates = block_mates(small_rows)
    blocks = count // mates
    b, i = c // mates, lax.rem(c, mates)
    turn = lax.rem(c, 2)
    repeat = count // chunks
    g, r = c // repeat, lax.rem(c, repeat)
    group_width = model // chunks
    rows = x_ref.shape[0]
    block_rows, block_tall = mates * small_rows, mates * tall_rows
    sender = Sender(send_sems, recv_sems)
    here = []

    def move(source, target):
        one = pltpu.make_async_copy(source, target, here_sems.at[len(here)])
        one.start()
        here.append(one)

    greet(seqs, count)

    shards = []
    matrices = (wq_ref, wk_ref, wv_ref, wo_ref)
    for d in range(1, mates):
        other = (s, b * mates + lax.rem(i + d, mates))
        for m in range(4):
            shards.append(sender.copy(matrices[m], stage4.at[i, m], other))
        shards.append(sender.copy(w1_ref, stage1.at[i], other))
        shards.append(sender.copy(w2_ref, stage2.at[i], other))
    for m in range(4):
        stage4[i, m] = matrices[m][...]
    stage1[i] = w1_ref[...]
    stage2[i] = w2_ref[...]

    codes, vecs = [], []
    for d in range(1, count):
        other = (s, lax.rem(c + d, count))
        codes.append(sender.copy(code_ref, code_out.at[c], other))
        vecs.append(sender.copy(vec_ref, vec_out.at[s * count + c], other))
    move(code_ref, code_out.at[c])
    move(vec_ref, vec_out.at[s * count + c])

    def tokens_at(group, half):
        start = (group * repeat + r) * rows + half * (rows // 2)
        return pl.ds(pl.multiple_of(start, rows // 2), rows // 2)

    mate_waits = []

    def to_mates(source, group, half, when=None, until_group=None):
        for d in range(1, repeat):
            other = (s, g * repeat + lax.rem(r + d, repeat))
            mate_waits.append(
                sender.copy(source, x_out.at[tokens_at(group, half)], other, when, when)
            )

    half_rows = [pl.ds(h * (rows // 2), rows // 2) for h in range(2)]
    for h in range(2):
        to_mates(x_ref.at[half_rows[h]], g, h)
        move(x_ref.at[half_rows[h]], x_out.at[tokens_at(g, h)])

    for wait in shards:
        wait()
    for p in range(mates):
        for m in range(4):
            flat4[m, p * small_rows : (p + 1) * small_rows, :] = stage4[p, m]
        flat1[p * small_rows : (p + 1) * small_rows, :] = stage1[p]
        flat2[p * tall_rows : (p + 1) * tall_rows, :] = stage2[p]
    for k in range(chunks):
        part = slice(k * group_width, (k + 1) * group_width)
        pieces = [flat4[m, :, part] for m in range(3)]
        pieces.append(jnp.zeros((block_rows, w_out.shape[1] - 3 * group_width), jnp.float32))
        share4[k] = jnp.concatenate(pieces, axis=1).astype(bf16)
    low4[...] = flat4[3].astype(bf16)
    low1[...] = flat1[...].astype(bf16)
    low2[...] = flat2[...].astype(bf16)

    def w_rows(seq, block, size):
        start = (seq * blocks + block) * block_rows
        return pl.ds(pl.multiple_of(start, block_rows), size * block_rows)

    columns = []
    for d in range(1, blocks):
        to = lax.rem(b + d, blocks) * mates + i
        columns.append(
            sender.copy(share4.at[to // repeat], w_out.at[w_rows(s, b, 1)], (s, to))
        )
    move(share4.at[g], w_out.at[w_rows(s, b, 1)])

    half_wide, half_model = wide // 2, model // 2
    wide_at = pl.ds(pl.multiple_of(turn * half_wide, half_wide), half_wide)
    model_at = pl.ds(pl.multiple_of(turn * half_model, half_model), half_model)

    def tall_rows_at(seq, block, size):
        start = (seq * blocks + block) * block_tall
        return pl.ds(pl.multiple_of(start, block_tall), size * block_tall)

    def big(seq, block, size):
        return (
            w1_out.at[w_rows(seq, block, size), wide_at],
            w2_out.at[tall_rows_at(seq, block, size), model_at],
            wo_out.at[w_rows(seq, block, size), model_at],
        )

    own = (low1.at[:, wide_at], low2.at[:, model_at], low4.at[:, model_at])
    for source, target in zip(own, big(s, b, 1)):
        move(source, target)
    up, down = b * mates + mates + i, b * mates - mates + i
    line = []
    for t in range(blocks - 1):
        for wait in line:
            wait()
        line = []
        low_block, high_block = jnp.maximum(b - t, 0), jnp.minimum(b + t, blocks - 1)
        sources = (own, own) if t == 0 else (big(s, low_block, 1), big(s, high_block, 1))
        rising = (b - t >= 0) & (b + 1 < blocks)
        falling = (b + t < blocks) & (b >= 1)
        for source, target in zip(sources[0], big(s, low_block, 1)):
            line.append(
                sender.copy(source, target, (s, jnp.minimum(up, count - 1)), rising, b - 1 - t >= 0)
            )
        for source, target in zip(sources[1], big(s, high_block, 1)):
            line.append(
                sender.copy(source, target, (s, jnp.maximum(down, 0)), falling, b + 1 + t < blocks)
            )

    above, below = jnp.minimum((g + 1) * repeat + r, count - 1), jnp.maximum((g - 1) * repeat + r, 0)

    def pass_on(t):
        waits = []
        low_group, high_group = jnp.maximum(g - t, 0), jnp.minimum(g + t, chunks - 1)
        for h in range(2):
            rise = x_ref.at[half_rows[h]] if t == 0 else x_out.at[tokens_at(low_group, h)]
            fall = x_ref.at[half_rows[h]] if t == 0 else x_out.at[tokens_at(high_group, h)]
            rising = (g - t >= 0) & (g + 1 < chunks)
            falling = (g + t < chunks) & (g >= 1)
            waits.append((
                sender.copy(rise, x_out.at[tokens_at(low_group, h)], (s, above), rising, g - 1 - t >= 0),
                sender.copy(
                    fall, x_out.at[tokens_at(high_group, h)], (s, below), falling, g + 1 + t < chunks
                ),
            ))
        return waits

    def received(t, waits):
        low_group, high_group = jnp.maximum(g - 1 - t, 0), jnp.minimum(g + 1 + t, chunks - 1)
        for h in range(2):
            waits[h][0]()
            to_mates(x_out.at[tokens_at(low_group, h)], low_group, h, g - 1 - t >= 0)
            waits[h][1]()
            to_mates(x_out.at[tokens_at(high_group, h)], high_group, h, g + 1 + t < chunks)

    x_waits = pass_on(0)

    for wait in columns:
        wait()
    for one in here:
        one.wait()
    columns = []
    for d in range(1, seqs):
        to = (lax.rem(s + d, seqs), c)
        slab = w_out.at[w_rows(s, 0, blocks)]
        columns.append(sender.copy(slab, slab, to))
    for wait in vecs:
        wait()
    vecs = []
    for d in range(1, seqs):
        to = (lax.rem(s + d, seqs), c)
        slab = vec_out.at[pl.ds(s * count, count)]
        vecs.append(sender.copy(slab, slab, to))
    for wait in line:
        wait()

    sibling = (s, c + 1 - 2 * turn)
    sibling_waits = []

    def to_sibling(seq):
        for piece in big(seq, 0, blocks):
            sibling_waits.append(sender.copy(piece, piece, sibling))

    masks = cube_steps(seqs, turn)
    held = [s]
    step = 0
    for t in range(max(chunks - 1, len(masks) + 1)):
        if t <= len(masks):
            if t > 0:
                for wait in plane:
                    wait()
            fresh = held if t == 0 else held[len(held) // 2 :]
            plane = []
            if t < len(masks):
                partner = (across(s, masks[t]), c)
                for seq in held:
                    for piece in big(seq, 0, blocks):
                        plane.append(sender.copy(piece, piece, partner))
                held = held + [across(seq, masks[t]) for seq in held]
            for seq in fresh:
                to_sibling(seq)
        if t < chunks - 1:
            following = None
            if t + 1 < chunks - 1:
                for h in range(2):
                    pass
            received(t, x_waits)
            if t + 1 < chunks - 1:
                x_waits = pass_on(t + 1)
    for wait in codes + vecs + columns + sibling_waits + mate_waits:
        wait()
    sender.finish()


def collect(wq, wk, wv, wo, w1, w2, x, code, vec, chunks):
    seqs, count = lax.axis_size("seq"), lax.axis_size("ctx")
    small_rows, model = wq.shape
    tall_rows, wide = w2.shape[0], w1.shape[1]
    rows = x.shape[0]
    mates = block_mates(small_rows)
    blocks, repeat = count // mates, count // chunks
    semaphores = (
        6 * (mates - 1) + 2 * (count - 1) + 2 * (seqs - 1) + 7 * (blocks - 1)
        + 3 * (seqs - 1) + 3 * seqs + 4 * (chunks - 1) + 2 * (2 * chunks - 1) * (repeat - 1)
    )
    devices = seqs * count
    padded = -(-3 * (model // chunks) // LANES) * LANES
    shape = jax.ShapeDtypeStruct
    f32, bf16 = jnp.float32, jnp.bfloat16
    vmem, far = pl.BlockSpec(memory_space=pltpu.VMEM), pl.BlockSpec(memory_space=pl.ANY)
    block_rows, block_tall = mates * small_rows, mates * tall_rows
    return pl.pallas_call(
        partial(collect_kernel, seqs, count, chunks, semaphores),
        out_shape=(
            shape((model, padded), bf16),
            shape((model, model), bf16),
            shape((model, wide), bf16),
            shape((tall_rows * devices, model), bf16),
            shape((count * rows, model), bf16),
            shape((count, 1, rows), jnp.int32),
            shape((devices, 1, vec.shape[1]), f32),
        ),
        in_specs=[vmem] * 6 + [far] * 3,
        out_specs=(far,) * 7,
        scratch_shapes=[
            pltpu.VMEM((mates, 4, small_rows, model), f32),
            pltpu.VMEM((mates, small_rows, wide), f32),
            pltpu.VMEM((mates, tall_rows, model), f32),
            pltpu.VMEM((4, block_rows, model), f32),
            pltpu.VMEM((block_rows, wide), f32),
            pltpu.VMEM((block_tall, model), f32),
            pltpu.VMEM((block_rows, model), bf16),
            pltpu.VMEM((block_rows, wide), bf16),
            pltpu.VMEM((block_tall, model), bf16),
            pltpu.VMEM((chunks, block_rows, padded), bf16),
            pltpu.SemaphoreType.DMA((semaphores,)),
            pltpu.SemaphoreType.DMA((semaphores,)),
            pltpu.SemaphoreType.DMA((8,)),
        ],
        compiler_params=pltpu.CompilerParams(
            vmem_limit_bytes=VMEM_LIMIT, collective_id=1, has_side_effects=True
        ),
        name="collect",
    )(wq, wk, wv, wo, w1, w2, x, code, vec)


def added(*parts):
    sum_of = parts[0].astype(jnp.float32)
    for part in parts[1:]:
        sum_of = sum_of + part.astype(jnp.float32)
    return sum_of


class Line:
    def __init__(self, sender, place, size, device, pieces, landing):
        self.sender, self.place, self.size, self.device = sender, place, size, device
        self.pieces, self.landing = pieces, landing
        self.waits = None

    def send(self, t):
        self.waits = []
        for way in range(2):
            rank = self.place if way == 0 else self.size - 1 - self.place
            mirror = (lambda d: d) if way == 0 else (lambda d: self.size - 1 - d)
            goal = jnp.clip(mirror(self.size - 1 - t + rank), 0, self.size - 1)
            sends = rank <= t
            receives = (rank >= 1) & (rank - 1 <= t)
            to = jnp.clip(self.place + (1 - 2 * way), 0, self.size - 1)
            waits = []
            for source, target in zip(self.pieces(goal), self.landing(way, t)):
                waits.append(self.sender.copy(source, target, self.device(to), sends, receives))
            self.waits.append((receives, mirror, rank, waits))

    def receive(self, t):
        for way, (receives, mirror, rank, waits) in enumerate(self.waits):
            goal = jnp.clip(mirror(self.size - 2 - t + rank), 0, self.size - 1)
            pieces, landing = self.pieces(goal), self.landing(way, t)
            for wait, piece, arrived in zip(waits, pieces, landing):
                wait()

                @pl.when(receives)
                def _():
                    piece[...] = added(piece[...], arrived[...]).astype(piece.dtype)


def settle_kernel(
    seqs, count, chunks,
    dx_ref, dw_ref, dwo_ref, dw1_ref, dw2_ref, dsmall_ref, db1_ref, db_ref,
    dx_out, dw_out, dwo_out, dw1_out, dw2_out, dsmall_out, db1_out,
    dx_sum, dx_in, dx_line, sum1, sum2, sum4, in1, in2, in4, cube1, cube2, cube4,
    line1, line2, line4, last1, last2, last4, w_mine, w_seq, w_block, w_mates, w_tmp,
    small_in, b1_in, b_in, vec_seq,
    send_sems, recv_sems, here_sems,
):
    s, c = lax.axis_index("seq"), lax.axis_index("ctx")
    bf16 = jnp.bfloat16
    rows, model = dx_out.shape
    wide = dw1_ref.shape[1]
    repeat = count // chunks
    mates = w_mates.shape[0]
    blocks = count // mates
    block_rows, block_tall = dwo_out.shape[0], dw2_out.shape[0]
    width = model // chunks
    b, i = c // mates, lax.rem(c, mates)
    g, r = c // repeat, lax.rem(c, repeat)
    turn = lax.rem(c, 2)
    half_wide, half_model = wide // 2, model // 2
    slab_rows, slab_tall = blocks * block_rows, blocks * block_tall
    sender = Sender(send_sems, recv_sems)
    here = []

    def move(source, target):
        one = pltpu.make_async_copy(source, target, here_sems.at[len(here)])
        one.start()
        here.append(one)

    greet(seqs, count)

    dx_waits = []
    for d in range(1, repeat):
        to = lax.rem(r + d, repeat)
        for k in range(chunks):
            dx_waits.append(
                sender.copy(dx_ref.at[k * repeat + to], dx_in.at[d - 1, k], (s, g * repeat + to))
            )
    for k in range(chunks):
        move(dx_ref.at[k * repeat + r], dx_sum.at[k])

    sibling = (s, c + 1 - 2 * turn)

    def column_half(which):
        wide_at = pl.ds(pl.multiple_of(which * half_wide, half_wide), half_wide)
        model_at = pl.ds(pl.multiple_of(which * half_model, half_model), half_model)
        return dw1_ref.at[:, wide_at], dw2_ref.at[:, model_at], dwo_ref.at[:, model_at]

    half_waits = [
        sender.copy(source, target, sibling)
        for source, target in zip(column_half(1 - turn), (in1, in2, in4))
    ]
    for source, target in zip(column_half(turn), (sum1, sum2, sum4)):
        move(source, target)

    w_waits = []
    for d in range(1, seqs):
        to = lax.rem(s + d, seqs)
        source = dw_ref.at[pl.ds(pl.multiple_of(to * slab_rows, slab_rows), slab_rows)]
        w_waits.append(sender.copy(source, w_seq.at[d - 1], (to, c)))
    move(dw_ref.at[pl.ds(pl.multiple_of(s * slab_rows, slab_rows), slab_rows)], w_mine)

    vec_waits = []
    for d in range(1, count):
        to = (s, lax.rem(c + d, count))
        for source, target in ((dsmall_ref, small_in), (db1_ref, b1_in), (db_ref, b_in)):
            vec_waits.append(sender.copy(source, target.at[c], to))
    small_in[c] = dsmall_ref[...]
    b1_in[c] = db1_ref[...]
    b_in[c] = db_ref[...]

    for one in here:
        one.wait()
    for wait in dx_waits:
        wait()
    for k in range(chunks):
        dx_sum[k] = added(dx_sum[k], *[dx_in[d, k] for d in range(repeat - 1)]).astype(bf16)
    half_rows = rows // 2
    token_lines = []
    for h in range(2):
        at = pl.ds(h * half_rows, half_rows)
        token_lines.append(
            Line(
                sender, g, chunks, lambda to: (s, to * repeat + r),
                lambda goal, at=at: (dx_sum.at[goal, at],),
                lambda way, t, at=at: (dx_line.at[way, t, at],),
            )
        )
    for line in token_lines:
        line.send(0)

    for wait in half_waits:
        wait()
    quarter = sum1.shape[0] // 4
    for k in range(4):
        at = slice(k * quarter, (k + 1) * quarter)
        sum1[at] = added(sum1[at], in1[at]).astype(bf16)
    quarter = sum2.shape[0] // 4
    for k in range(4):
        at = slice(k * quarter, (k + 1) * quarter)
        sum2[at] = added(sum2[at], in2[at]).astype(bf16)
    sum4[...] = added(sum4[...], in4[...]).astype(bf16)

    def slab(seq):
        at = pl.ds(pl.multiple_of(seq * slab_rows, slab_rows), slab_rows)
        tall = pl.ds(pl.multiple_of(seq * slab_tall, slab_tall), slab_tall)
        return sum1.at[at], sum2.at[tall], sum4.at[at]

    masks = cube_steps(seqs, turn)

    def family(seq, rest):
        found = [seq]
        for mask in rest:
            found = found + [across(one, mask) for one in found]
        return found

    cube_waits, used = [], 0

    def cube_send(j):
        nonlocal used
        partner = across(s, masks[j])
        cube_waits.clear()
        mine = family(s, masks[j + 1 :])
        for k, seq in enumerate(family(partner, masks[j + 1 :])):
            landing = cube1.at[used + k], cube2.at[used + k], cube4.at[used + k]
            waits = [
                sender.copy(source, target, (partner, c)) for source, target in zip(slab(seq), landing)
            ]
            cube_waits.append((mine[k], landing, waits))
        used += len(cube_waits)

    def cube_receive():
        for seq, landing, waits in cube_waits:
            for wait, target, arrived in zip(waits, slab(seq), landing):
                wait()
                target[...] = added(target[...], arrived[...]).astype(bf16)

    cube_send(0)

    for wait in w_waits:
        wait()
    w_mine[...] = added(w_mine[...], *[w_seq[d] for d in range(seqs - 1)]).astype(bf16)
    w_waits = []
    for d in range(1, blocks):
        to = lax.rem(b + d, blocks)
        source = w_mine.at[pl.ds(pl.multiple_of(to * block_rows, block_rows), block_rows)]
        w_waits.append(sender.copy(source, w_block.at[b], (s, to * mates + i)))
    w_block[b] = w_mine[pl.ds(pl.multiple_of(b * block_rows, block_rows), block_rows), :]

    for wait in vec_waits:
        wait()
    vec_waits = []
    small = small_in[0]
    tall = b1_in[0]
    for k in range(1, count):
        small = small + small_in[k]
        tall = tall + b1_in[k]
    pair = []
    for k in range(chunks):
        one = b_in[k * repeat]
        for d in range(1, repeat):
            one = one + b_in[k * repeat + d]
        pair.append(one)
    for m in range(2):
        joined = jnp.concatenate([one[0:1, m * width : (m + 1) * width] for one in pair], axis=1)
        dsmall_out[6 + m : 7 + m, :] = joined
    vec_seq[s, 0:6, 0:model] = small[0:6]
    vec_seq[s, 6:8, 0:model] = dsmall_out[6:8, :]
    vec_seq[s, :, model:] = tall
    for d in range(1, seqs):
        vec_waits.append(sender.copy(vec_seq.at[s], vec_seq.at[s], (lax.rem(s + d, seqs), c)))

    for wait in w_waits:
        wait()
    w_waits = []
    w_mates[i] = w_block[...]
    for d in range(1, mates):
        to = (s, b * mates + lax.rem(i + d, mates))
        w_waits.append(sender.copy(w_block, w_mates.at[i], to))

    def block_slab(goal):
        row = s * slab_rows + goal * block_rows
        tall = s * slab_tall + goal * block_tall
        at = pl.ds(pl.multiple_of(row, block_rows), block_rows)
        tall_at = pl.ds(pl.multiple_of(tall, block_tall), block_tall)
        return sum1.at[at], sum2.at[tall_at], sum4.at[at]

    weight_line = Line(
        sender, b, blocks, lambda to: (s, to * mates + i),
        block_slab, lambda way, t: (line1.at[way, t], line2.at[way, t], line4.at[way, t]),
    )
    steps = len(masks)
    token_steps, weight_steps = chunks - 1, blocks - 1
    for t in range(max(token_steps, steps + weight_steps)):
        if t < token_steps:
            for line in token_lines:
                line.receive(t)
                if t + 1 < token_steps:
                    line.send(t + 1)
        if t < steps:
            cube_receive()
            if t + 1 < steps:
                cube_send(t + 1)
            elif weight_steps:
                weight_line.send(0)
        elif t - steps < weight_steps:
            weight_line.receive(t - steps)
            if t - steps + 1 < weight_steps:
                weight_line.send(t - steps + 1)

    last_waits = []
    for source, target in zip(block_slab(b), (last1, last2, last4)):
        target[i] = source[...]
        for d in range(1, mates):
            to = (s, b * mates + lax.rem(i + d, mates))
            last_waits.append(sender.copy(source, target.at[i], to))
    dx_out[...] = dx_sum[g]
    for wait in w_waits + vec_waits + last_waits:
        wait()
    for target, source in ((dw1_out, last1), (dw2_out, last2), (dwo_out, last4)):
        size = target.shape[1] // 2
        for which in range(2):
            target[:, which * size : (which + 1) * size] = added(
                *[source[k] for k in range(which, mates, 2)]
            )
    for k in range(chunks):
        terms = [
            w_mates[p, q]
            for p in range(mates)
            for q in range(blocks)
            if (q * mates + p) // repeat == k
        ]
        dw_out[k] = added(*terms)
    vec = vec_seq[0]
    for d in range(1, seqs):
        vec = vec + vec_seq[d]
    dsmall_out[...] = vec[:, 0:model]
    db1_out[...] = vec[:, model:]
    sender.finish()


def settle(dx, dw, dwo, dw1, dw2, dsmall, db1, db, chunks):
    seqs, count = lax.axis_size("seq"), lax.axis_size("ctx")
    _, rows, model = dx.shape
    wide, tall = dw1.shape[1], dw2.shape[0]
    devices = seqs * count
    mates = block_mates(model // devices)
    blocks, repeat = count // mates, count // chunks
    block_rows, block_tall = mates * (model // devices), mates * (tall // devices)
    slab_rows, slab_tall = blocks * block_rows, blocks * block_tall
    padded = dw.shape[1]
    semaphores = (
        chunks * (repeat - 1) + 3 + (seqs - 1) + 3 * (count - 1) + 4 * (chunks - 1)
        + 3 * (seqs - 1) + (blocks - 1) + (seqs - 1) + (mates - 1) + 6 * (blocks - 1) + 3 * (mates - 1)
    )
    shape = jax.ShapeDtypeStruct
    f32, bf16 = jnp.float32, jnp.bfloat16
    vmem, far = pl.BlockSpec(memory_space=pltpu.VMEM), pl.BlockSpec(memory_space=pl.ANY)
    half_wide, half_model = wide // 2, model // 2
    triple = lambda lead, a, t: [
        pltpu.VMEM(lead + (a, half_wide), bf16),
        pltpu.VMEM(lead + (t, half_model), bf16),
        pltpu.VMEM(lead + (a, half_model), bf16),
    ]
    return pl.pallas_call(
        partial(settle_kernel, seqs, count, chunks),
        out_shape=(
            shape((rows, model), bf16),
            shape((chunks, block_rows, padded), f32),
            shape((block_rows, model), f32),
            shape((block_rows, wide), f32),
            shape((block_tall, model), f32),
            shape((8, model), f32),
            shape((8, wide), f32),
        ),
        in_specs=[far] * 5 + [vmem] * 3,
        out_specs=(vmem,) * 7,
        scratch_shapes=[
            pltpu.VMEM((chunks, rows, model), bf16),
            pltpu.VMEM((repeat - 1, chunks, rows, model), bf16),
            pltpu.VMEM((2, chunks - 1, rows, model), bf16),
        ]
        + triple((), model, tall)
        + triple((), model, tall)
        + triple((seqs - 1,), slab_rows, slab_tall)
        + triple((2, blocks - 1), block_rows, block_tall)
        + triple((mates,), block_rows, block_tall)
        + [
            pltpu.VMEM((slab_rows, padded), bf16),
            pltpu.VMEM((seqs - 1, slab_rows, padded), bf16),
            pltpu.VMEM((blocks, block_rows, padded), bf16),
            pltpu.VMEM((mates, blocks, block_rows, padded), bf16),
            pltpu.VMEM((8, 128), f32),
            pltpu.VMEM((count, 8, model), f32),
            pltpu.VMEM((count, 8, wide), f32),
            pltpu.VMEM((count, 8, db.shape[1]), f32),
            pltpu.VMEM((seqs, 8, model + wide), f32),
            pltpu.SemaphoreType.DMA((semaphores,)),
            pltpu.SemaphoreType.DMA((semaphores,)),
            pltpu.SemaphoreType.DMA((chunks + 4,)),
        ],
        compiler_params=pltpu.CompilerParams(
            vmem_limit_bytes=VMEM_LIMIT, collective_id=2, has_side_effects=True
        ),
        name="settle",
    )(dx, dw, dwo, dw1, dw2, dsmall, db1, db)


def swap_kernel(chunks, repeat, a_ref, a_out, send_sems, recv_sems, here_sem):
    s, c = lax.axis_index("seq"), lax.axis_index("ctx")
    g, r = c // repeat, lax.rem(c, repeat)
    place = lambda d: lax.rem(g + d, chunks)
    barrier = pltpu.get_barrier_semaphore()
    for d in range(1, chunks):
        pl.semaphore_signal(
            barrier, inc=1, device_id=(s, place(d) * repeat + r), device_id_type=MESH
        )
    pl.semaphore_wait(barrier, chunks - 1)
    sender = Sender(send_sems, recv_sems)
    here = pltpu.make_async_copy(a_ref.at[g], a_out.at[g], here_sem)
    here.start()
    waits = [
        sender.copy(a_ref.at[place(d)], a_out.at[g], (s, place(d) * repeat + r))
        for d in range(1, chunks)
    ]
    for wait in waits:
        wait()
    here.wait()
    sender.finish()


def swap(a):
    chunks = a.shape[0]
    far = pl.BlockSpec(memory_space=pl.ANY)
    return pl.pallas_call(
        partial(swap_kernel, chunks, lax.axis_size("ctx") // chunks),
        out_shape=jax.ShapeDtypeStruct(a.shape, a.dtype),
        in_specs=[far],
        out_specs=far,
        scratch_shapes=[
            pltpu.SemaphoreType.DMA((chunks - 1,)),
            pltpu.SemaphoreType.DMA((chunks - 1,)),
            pltpu.SemaphoreType.DMA,
        ],
        compiler_params=pltpu.CompilerParams(collective_id=3, has_side_effects=True),
        name="swap",
    )(a)


def pick(values, size, device):
    wide = values.shape[1]
    row = lax.broadcasted_iota(jnp.int32, (wide, size), 0)
    column = lax.broadcasted_iota(jnp.int32, (wide, size), 1)
    chosen = (row == column + device * size).astype(jnp.bfloat16)
    high = values.astype(jnp.bfloat16)
    rest = values - high.astype(jnp.float32)
    middle_part = rest.astype(jnp.bfloat16)
    low = (rest - middle_part.astype(jnp.float32)).astype(jnp.bfloat16)
    return nn(high, chosen) + nn(middle_part, chosen) + nn(low, chosen)


def finish_kernel(
    count, mates,
    e1_ref, dx_ref, dw_ref, dwo_ref, dw1_ref, dw2_ref, small_ref, b1_ref,
    dx_out, dwq_out, dwk_out, dwv_out, dwo_out, dw1_out, dw2_out, small_out, b1_out,
):
    s, c = lax.axis_index("seq"), lax.axis_index("ctx")
    dx_out[...] = e1_ref[...] + dx_ref[...].astype(jnp.float32)
    each, tall = dwo_out.shape[0], dw2_out.shape[0]
    chunks = dw_ref.shape[0]
    width = dwq_out.shape[1] // chunks
    i = lax.rem(c, mates)
    for p in range(mates):
        rows = slice(p * each, (p + 1) * each)

        @pl.when(i == p)
        def _():
            for m, out in enumerate((dwq_out, dwk_out, dwv_out)):
                parts = [dw_ref[k, rows, m * width : (m + 1) * width] for k in range(chunks)]
                out[...] = jnp.concatenate(parts, axis=1)
            dwo_out[...] = dwo_ref[rows, :]
            dw1_out[...] = dw1_ref[rows, :]
            dw2_out[...] = dw2_ref[p * tall : (p + 1) * tall, :]

    device = s * count + c
    small_out[...] = pick(small_ref[...], each, device)
    b1_out[...] = pick(b1_ref[...], tall, device)


def finish(e1, dx, dw, dwo, dw1, dw2, small, b1):
    count = lax.axis_size("ctx")
    devices = count * lax.axis_size("seq")
    model, wide = dwo.shape[1], dw1.shape[1]
    each, tall = model // devices, wide // devices
    shape = jax.ShapeDtypeStruct
    f32 = jnp.float32
    vmem = pl.BlockSpec(memory_space=pltpu.VMEM)
    return pl.pallas_call(
        partial(finish_kernel, count, block_mates(each)),
        out_shape=(shape(e1.shape, f32),)
        + (shape((each, model), f32),) * 4
        + (shape((each, wide), f32), shape((tall, model), f32), shape((8, each), f32), shape((8, tall), f32)),
        in_specs=[vmem] * 8,
        out_specs=(vmem,) * 9,
        compiler_params=pltpu.CompilerParams(vmem_limit_bytes=VMEM_LIMIT),
        name="finish",
    )(e1, dx, dw, dwo, dw1, dw2, small, b1)


def on_device(
    tokens, segment_ids, valid_tokens, query_weight, query_bias, key_weight, value_weight, value_bias,
    output_weight, output_bias, attn_norm_gain, attn_norm_shift, up_weight, up_bias, down_weight,
    down_bias, ffn_norm_gain, ffn_norm_shift, out_cotangent,
):
    count = lax.axis_size("ctx")
    chunks = math.gcd(H, count)
    heads = H // chunks
    x = tokens[0]
    vec = jnp.concatenate([
        output_bias, attn_norm_gain, attn_norm_shift, down_bias, ffn_norm_gain, ffn_norm_shift,
        query_bias, value_bias, up_bias,
    ])
    vec = jnp.pad(vec, (0, -vec.shape[0] % LANES))[None]
    w, wo, w1, w2, x_all, codes, vecs = collect(
        query_weight, key_weight, value_weight, output_weight, up_weight, down_weight,
        x, segment_ids * 2 + valid_tokens, vec, chunks,
    )
    k, v, q, o_float, o_send, lse, codes = attend(x_all, w, vecs, codes, heads, chunks)
    output, e1, do, dwo, dw1, dw2, dsmall, db1 = middle(
        swap(o_send), x, out_cotangent[0], wo, w1, w2, vecs
    )
    dx, dw, db = retreat(x_all, w, k, v, q, o_float, lse, swap(do), codes, heads, chunks)
    summed = settle(dx, dw, dwo, dw1, dw2, dsmall, db1, db, chunks)
    grad, dwq, dwk, dwv, dwo, dw1, dw2, small, b1 = finish(e1, *summed)
    return (
        output[None], grad[None],
        dwq, small[6], dwk, dwv, small[7],
        dwo, small[0], small[1], small[2],
        dw1, b1[0], dw2, small[3], small[4], small[5],
    )


def solution(mesh):
    in_specs = (
        P("seq", "ctx", None),
        P("seq", "ctx"),
        P("seq", "ctx"),
        P(("seq", "ctx"), None),
        P(("seq", "ctx")),
        P(("seq", "ctx"), None),
        P(("seq", "ctx"), None),
        P(("seq", "ctx")),
        P(("seq", "ctx"), None),
        P(("seq", "ctx")),
        P(("seq", "ctx")),
        P(("seq", "ctx")),
        P(("seq", "ctx"), None),
        P(("seq", "ctx")),
        P(("seq", "ctx"), None),
        P(("seq", "ctx")),
        P(("seq", "ctx")),
        P(("seq", "ctx")),
        P("seq", "ctx", None),
    )
    out_specs = (
        P("seq", "ctx", None),
        P("seq", "ctx", None),
        P(("seq", "ctx"), None),
        P(("seq", "ctx")),
        P(("seq", "ctx"), None),
        P(("seq", "ctx"), None),
        P(("seq", "ctx")),
        P(("seq", "ctx"), None),
        P(("seq", "ctx")),
        P(("seq", "ctx")),
        P(("seq", "ctx")),
        P(("seq", "ctx"), None),
        P(("seq", "ctx")),
        P(("seq", "ctx"), None),
        P(("seq", "ctx")),
        P(("seq", "ctx")),
        P(("seq", "ctx")),
    )
    return jax.shard_map(
        on_device, mesh=mesh, in_specs=in_specs, out_specs=out_specs, check_vma=False
    )
```

```python
import math
from functools import partial

import jax
import jax.numpy as jnp
from jax import lax
from jax.experimental import pallas as pl
from jax.experimental.pallas import tpu as pltpu
from jax.sharding import PartitionSpec as P

H = 12
DH = 64
VMEM_LIMIT = 60 * 1024 * 1024

LOG2E = 1.4426950408889634
BQ = 512
BK = 512
HALF = BK // 2
PAD = BK + HALF
DOCS = 64
FAR = -(2.0**100)
LANES = 128


def nt(a, b):
    return lax.dot_general(a, b, (((1,), (1,)), ((), ())), preferred_element_type=jnp.float32)


def nn(a, b):
    return lax.dot_general(a, b, (((1,), (0,)), ((), ())), preferred_element_type=jnp.float32)


def unshard(vec, at, each):
    devices = vec.shape[0]
    shard = vec[:, at : at + each].astype(jnp.bfloat16)
    size = devices * each
    owner = lambda shape, axis: jnp.floor(
        (lax.broadcasted_iota(jnp.int32, shape, axis).astype(jnp.float32) + 0.5) / each
    )
    column = lax.broadcasted_iota(jnp.int32, (each, size), 1).astype(jnp.float32)
    inner = column - owner((each, size), 1) * each
    place = lax.broadcasted_iota(jnp.int32, (each, size), 0).astype(jnp.float32)
    repeated = nn(shard, (inner == place).astype(jnp.bfloat16))
    device = lax.broadcasted_iota(jnp.int32, (devices, size), 0).astype(jnp.float32)
    return jnp.sum(jnp.where(owner((devices, size), 1) == device, repeated, 0.0), axis=0, keepdims=True)


def total(values):
    return jnp.sum(values.astype(jnp.float32)).astype(jnp.int32)


def key_range(code_ref, block, start):
    code = code_ref[...]
    seg = lax.shift_right_logical(code, 1)
    val = code & 1
    count, width = seg.shape
    position = lax.broadcasted_iota(jnp.int32, (count, width), 0) * width + lax.broadcasted_iota(
        jnp.int32, (count, width), 1
    )
    in_block = (position >= start) & (position < start + block)
    low = jnp.min(jnp.where(in_block, seg, 1 << 20).astype(jnp.float32)).astype(jnp.int32)
    high = jnp.max(jnp.where(in_block, seg, -1).astype(jnp.float32)).astype(jnp.int32)
    length = count * width
    first = total(seg < low)
    end = total(seg <= high)
    last_valid = jnp.max(jnp.where(val == 1, position + 1, 0).astype(jnp.float32)).astype(jnp.int32)
    first_invalid = jnp.min(jnp.where(val == 1, length, position).astype(jnp.float32)).astype(jnp.int32)
    end = jnp.minimum(end, last_valid)
    origin = first // LANES * LANES
    blocks = (end - origin + BK - 1) // BK
    clear_end = jnp.minimum(end, first_invalid)
    clear_from = (first - origin + BK - 1) // BK
    clear_to = jnp.maximum(clear_end - origin, 0) // BK
    one_document = low == high
    clear_from = jnp.where(one_document, jnp.minimum(clear_from, blocks), blocks)
    clear_to = jnp.where(one_document, jnp.minimum(jnp.maximum(clear_to, clear_from), blocks), blocks)
    return origin, blocks, clear_from, clear_to


def tn(a, b):
    return lax.dot_general(a, b, (((0,), (0,)), ((), ())), preferred_element_type=jnp.float32)


def flip(a):
    return a.astype(jnp.float32).T.astype(a.dtype)


def three_parts(row):
    high = row.astype(jnp.bfloat16)
    rest = row - high.astype(jnp.float32)
    middle = rest.astype(jnp.bfloat16)
    low = (rest - middle.astype(jnp.float32)).astype(jnp.bfloat16)
    empty = jnp.zeros((13, row.shape[1]), jnp.float32)
    return jnp.concatenate(
        [high.astype(jnp.float32), middle.astype(jnp.float32), low.astype(jnp.float32), empty], axis=0
    )


def retreat_kernel(
    heads, chunks, ctx_axis, repeat,
    x_ref, w_ref, k_ref, v_ref, q_ref, o_ref, lse_ref, do_ref, code_ref,
    dx_out, dw_out, db_out,
    krow, target, q_ext, kt_ext, v_ext, do_ext, do_rows, dq, dkv,
    s_even, s_odd, g_even, g_odd, dw, x_slot, dx_slot, in_sem, out_sem, v_sem,
):
    width = heads * DH
    length = x_ref.shape[0]
    count = chunks * repeat
    rows = length // (chunks * repeat)
    mine = chunks * rows
    place = lax.rem(lax.axis_index(ctx_axis), repeat)
    bf16 = jnp.bfloat16

    def fetch(i):
        slot = lax.rem(i, 2)
        source = x_ref.at[pl.ds(pl.multiple_of(i * rows, LANES), rows)]
        return pltpu.make_async_copy(source, x_slot.at[slot], in_sem.at[slot])

    def deliver(i):
        slot = lax.rem(i, 2)
        return pltpu.make_async_copy(dx_slot.at[slot], dx_out.at[i], out_sem.at[slot])

    fetch(0).start()
    values = [
        pltpu.make_async_copy(
            v_ref.at[pl.ds(h * DH, DH)], v_ext.at[h, pl.ds(0, DH), pl.ds(0, length)], v_sem.at[h]
        )
        for h in range(heads)
    ]
    for copy in values:
        copy.start()
    for i in range(chunks * repeat):
        code = code_ref[i : i + 1, :].astype(jnp.float32)
        krow[:, i * rows : (i + 1) * rows] = jnp.broadcast_to(code, (8, rows))
    krow[:, length:] = jnp.full((8, PAD), -1.0, jnp.float32)

    def keys(i, carry):
        at = pl.ds(pl.multiple_of(i * rows, LANES), rows)
        for h in range(heads):
            kt = flip(k_ref[h, at, :])
            kt_ext[h, 0:DH, at] = kt
            kt_ext[h, DH : 2 * DH, at] = kt
        return carry

    lax.fori_loop(0, chunks * repeat, keys, 0)
    kt_ext[:, 0 : 2 * DH, length:] = jnp.zeros((heads, 2 * DH, PAD), bf16)
    v_ext[:, 0:DH, length:] = jnp.zeros((heads, DH, PAD), bf16)
    kt_ext[:, 2 * DH :, :] = jnp.ones((heads, 16, length + PAD), bf16)
    v_ext[:, DH:, :] = jnp.ones((heads, 16, length + PAD), bf16)
    dkv[...] = jnp.zeros(dkv.shape, jnp.float32)
    dq[...] = jnp.zeros(dq.shape, jnp.float32)

    def queries(i, carry):
        at = pl.ds(pl.multiple_of(i * rows, LANES), rows)
        which = i * repeat + place
        code = (code_ref[pl.ds(which, 1), :] | 1).astype(jnp.float32)
        for j in range(rows // LANES):
            piece = code[:, j * LANES : (j + 1) * LANES]
            target[pl.ds(pl.multiple_of(i * rows + j * LANES, LANES), LANES), :] = jnp.broadcast_to(
                piece, (LANES, LANES)
            ).T
        for h in range(heads):
            part = slice(h * DH, (h + 1) * DH)
            scaled = q_ref[part, at].astype(jnp.float32) * (DH**-0.5 * LOG2E)
            high = scaled.astype(bf16).astype(jnp.float32)
            extra = three_parts(-lse_ref[h : h + 1, at])
            full = jnp.concatenate([high, scaled - high, extra], axis=0)
            q_ext[h, at, :] = full.T.astype(bf16)
            grad = do_ref[i, part, :].astype(jnp.float32)
            delta = jnp.sum(grad * o_ref[part, at], axis=0, keepdims=True)
            do_rows[part, at] = do_ref[i, part, :]
            do_ext[h, at, :] = jnp.concatenate([grad, three_parts(-delta)], axis=0).T.astype(bf16)
        return carry

    lax.fori_loop(0, chunks, queries, 0)
    per_chunk = rows // BQ

    def block(i, carry):
        chunk = i // per_chunk
        inner = (i - chunk * per_chunk) * BQ
        start = (chunk * repeat + place) * rows + inner
        origin, blocks, clear_from, clear_to = key_range(code_ref, BQ, start)
        at = pl.ds(pl.multiple_of(i * BQ, LANES), BQ)

        def scores(s_slot, g_slot, key_at):
            key = pl.ds(key_at, HALF)
            for h in range(heads):
                s_slot[h] = nn(q_ext[h, at, :], kt_ext[h, :, key])
                g_slot[h] = nn(do_ext[h, at, :], v_ext[h, :, key])

        def absorb(masked, s_slot, g_slot, key_at):
            key = pl.ds(key_at, HALF)
            if masked:
                code = krow[0:1, key]
                wanted = jnp.concatenate([target[at, :]] * (HALF // LANES), axis=1)
                allowed = wanted == code
            for h in range(heads):
                part = slice(h * DH, (h + 1) * DH)
                p = jnp.exp2(s_slot[h])
                if masked:
                    p = jnp.where(allowed, p, 0.0)
                ds = (p * g_slot[h]).astype(bf16)
                dkv[width + h * DH : width + (h + 1) * DH, key] += nn(do_rows[part, at], p.astype(bf16))
                dkv[part, key] += nn(q_ref[part, at], ds)
                dq[h, at, :] += nn(ds, k_ref[h, key, :])

        def step(masked, j, carry):
            first = pl.multiple_of(origin + j * BK, LANES)
            second = pl.multiple_of(first + HALF, LANES)
            scores(s_odd, g_odd, second)
            absorb(masked, s_even, g_even, first)
            scores(s_even, g_even, pl.multiple_of(first + BK, LANES))
            absorb(masked, s_odd, g_odd, second)
            return carry

        scores(s_even, g_even, pl.multiple_of(origin, LANES))
        lax.fori_loop(0, clear_from, partial(step, True), 0)
        lax.fori_loop(clear_from, clear_to, partial(step, False), 0)
        lax.fori_loop(clear_to, blocks, partial(step, True), 0)
        return carry

    for copy in values:
        copy.wait()
    lax.fori_loop(0, chunks * per_chunk, block, 0)

    wt = w_ref[...].astype(jnp.float32).T.astype(bf16)
    scale = DH**-0.5
    one = jnp.ones((8, rows), bf16)
    dw[...] = jnp.zeros(dw.shape, jnp.float32)
    db_out[...] = jnp.zeros(db_out.shape, jnp.float32)

    def spread(i, carry):
        slot = lax.rem(i, 2)

        @pl.when(i + 1 < count)
        def _():
            fetch(i + 1).start()

        fetch(i).wait()

        @pl.when(i >= 2)
        def _():
            deliver(i - 2).wait()

        at = pl.ds(pl.multiple_of(i * rows, LANES), rows)
        dk = (dkv[0:width, at] * scale).astype(bf16)
        dv = dkv[width:, at].astype(bf16)
        both = jnp.concatenate([dk, dv], axis=0)
        dx_slot[slot] = tn(both, wt[width : 3 * width]).astype(bf16)
        dw[width : 3 * width, :] += nn(both, x_slot[slot])
        db_out[:, width:] += nt(one, dv)

        @pl.when(lax.rem(i, repeat) == place)
        def _():
            own = pl.ds(pl.multiple_of(i // repeat * rows, LANES), rows)
            grad = jnp.concatenate([dq[h, own, :] for h in range(heads)], axis=1) * scale
            grad = grad.astype(bf16)
            dx_slot[slot] = (dx_slot[slot].astype(jnp.float32) + nn(grad, wt[0:width])).astype(bf16)
            dw[0:width, :] += tn(grad, x_slot[slot])
            db_out[:, 0:width] += nn(one, grad)

        deliver(i).start()
        return carry

    lax.fori_loop(0, count, spread, 0)
    deliver(count - 2).wait()
    deliver(count - 1).wait()
    dw_out[...] = dw[...].T.astype(bf16)


def retreat(x, w, k, v, q, o, lse, do, codes, heads, chunks):
    length, model = x.shape
    width = heads * DH
    count, rows = codes.shape
    repeat = count // chunks
    mine = chunks * rows
    shape = jax.ShapeDtypeStruct
    whole = pl.BlockSpec(memory_space=pltpu.VMEM)
    f32, bf16 = jnp.float32, jnp.bfloat16
    return pl.pallas_call(
        partial(retreat_kernel, heads, chunks, "ctx", repeat),
        out_shape=(
            shape((count, rows, model), bf16),
            shape((model, w.shape[1]), bf16),
            shape((8, 2 * width), f32),
        ),
        in_specs=[whole if i not in (0, 3) else pl.BlockSpec(memory_space=pl.ANY) for i in range(9)],
        out_specs=(pl.BlockSpec(memory_space=pl.ANY), whole, whole),
        scratch_shapes=[
            pltpu.VMEM((8, length + PAD), f32),
            pltpu.VMEM((mine, LANES), f32),
            pltpu.VMEM((heads, mine, 2 * DH + 16), bf16),
            pltpu.VMEM((heads, 2 * DH + 16, length + PAD), bf16),
            pltpu.VMEM((heads, DH + 16, length + PAD), bf16),
            pltpu.VMEM((heads, mine, DH + 16), bf16),
            pltpu.VMEM((width, mine), bf16),
            pltpu.VMEM((heads, mine, DH), f32),
            pltpu.VMEM((2 * width, length + PAD), f32),
        ]
        + [pltpu.VMEM((heads, BQ, HALF), f32)] * 4
        + [
            pltpu.VMEM((w.shape[1], model), f32),
            pltpu.VMEM((2, rows, model), bf16),
            pltpu.VMEM((2, rows, model), bf16),
            pltpu.SemaphoreType.DMA((2,)),
            pltpu.SemaphoreType.DMA((2,)),
            pltpu.SemaphoreType.DMA((heads,)),
        ],
        compiler_params=pltpu.CompilerParams(vmem_limit_bytes=VMEM_LIMIT),
        name="retreat",
    )(x, w, k, v, q, o, lse, do, codes)


EPSILON = 1e-12
FF_BLOCK = 512


def gelu_pair(u):
    z = jnp.abs(u) * (0.5**0.5)
    t = 1.0 / (1.0 + 0.3275911 * z)
    bell = jnp.exp(-z * z)
    poly = t * (
        0.254829592 + t * (-0.284496736 + t * (1.421413741 + t * (-1.453152027 + t * 1.061405429)))
    )
    half = 0.5 * poly * bell
    below = jnp.where(u < 0.0, half, 1.0 - half)
    return u * below, below + u * bell * 0.3989422804014327


def standard(hidden):
    centred = hidden - jnp.mean(hidden, axis=-1, keepdims=True)
    scale = lax.rsqrt(jnp.mean(centred * centred, axis=-1, keepdims=True) + EPSILON)
    return centred * scale, scale


def norm_back(grad, gain, normal, scale):
    t = grad * gain
    return scale * (
        t
        - jnp.mean(t, axis=-1, keepdims=True)
        - normal * jnp.mean(t * normal, axis=-1, keepdims=True)
    )


def middle_kernel(
    o_ref, x_ref, cot_ref, wo_ref, w1_ref, w2_ref, vec_ref,
    out_ref, e1_ref, do_ref, dwo_ref, dw1_ref, dw2_ref, dsmall_ref, db1_ref,
    act, slope, y1_ref, normal_ref, r2_ref, y1t_ref, grad_ref, small_ref, b1_ref,
):
    bf16 = jnp.bfloat16
    groups, width, rows = o_ref.shape
    hidden_width = w1_ref.shape[1]
    steps = hidden_width // FF_BLOCK
    vec = vec_ref[:, 0, :]
    each = x_ref.shape[1] // vec.shape[0]
    for i in range(6):
        small_ref[i : i + 1, :] = unshard(vec, i * each, each)
    b1_ref[0:1, :] = unshard(vec, 8 * each, hidden_width // vec.shape[0])
    row = lambda i: small_ref[i : i + 1, :]
    ones = jnp.ones((8, rows), bf16)
    o = o_ref[...].reshape(groups * width, rows)
    n1 = x_ref[...].astype(jnp.float32) + (tn(o, wo_ref[...]) + row(0))
    normal, scale_one = standard(n1)
    normal_ref[...] = normal
    y1 = normal * row(1) + row(2)
    y1_ref[...] = y1
    y1_low = y1.astype(bf16)
    y1t_ref[...] = y1.T.astype(bf16)
    grad_ref[...] = jnp.zeros(grad_ref.shape, jnp.float32)

    def forward(i, carry):
        at = pl.ds(pl.multiple_of(i * FF_BLOCK, FF_BLOCK), FF_BLOCK)
        u = nn(y1_low, w1_ref[:, at]) + b1_ref[0:1, at]
        value, gradient = gelu_pair(u)
        value = value.astype(bf16)
        act[:, at] = value
        slope[:, at] = gradient
        grad_ref[...] += nn(value, w2_ref[at, :])
        return carry

    lax.fori_loop(0, steps, forward, 0)
    normal_two, scale_two = standard(y1_ref[...] + (grad_ref[...] + row(3)))
    out_ref[...] = normal_two * row(4) + row(5)
    cot = cot_ref[...].astype(jnp.float32)
    dsmall_ref[4:5, :] = jnp.sum(cot * normal_two, axis=0, keepdims=True)
    dsmall_ref[5:6, :] = jnp.sum(cot, axis=0, keepdims=True)
    e2 = norm_back(cot, row(4), normal_two, scale_two)
    grad_ref[...] = e2
    r2 = e2.astype(bf16)
    r2_ref[...] = r2
    dsmall_ref[3:4, :] = nn(ones, r2)[0:1]

    def backward(i, carry):
        at = pl.ds(pl.multiple_of(i * FF_BLOCK, FF_BLOCK), FF_BLOCK)
        dw2_ref[at, :] = tn(act[:, at], r2_ref[...]).astype(bf16)
        du = (nt(r2_ref[...], w2_ref[at, :]) * slope[:, at]).astype(bf16)
        db1_ref[:, at] = nn(ones, du)
        dw1_ref[:, at] = nn(y1t_ref[...], du).astype(bf16)
        grad_ref[...] += nt(du, w1_ref[:, at])
        return carry

    lax.fori_loop(0, steps, backward, 0)
    grad = grad_ref[...]
    normal = normal_ref[...]
    dsmall_ref[1:2, :] = jnp.sum(grad * normal, axis=0, keepdims=True)
    dsmall_ref[2:3, :] = jnp.sum(grad, axis=0, keepdims=True)
    e1 = norm_back(grad, row(1), normal, scale_one)
    e1_ref[...] = e1
    r1 = e1.astype(bf16)
    dsmall_ref[0:1, :] = nn(ones, r1)[0:1]
    dsmall_ref[6:8, :] = jnp.zeros((2, dsmall_ref.shape[1]), jnp.float32)
    dwo_ref[...] = nn(o, r1).astype(bf16)
    do_ref[...] = nt(wo_ref[...], r1).astype(bf16).reshape(groups, width, rows)


def middle(o, x, cot, wo, w1, w2, vec):
    groups, width, rows = o.shape
    model = x.shape[1]
    hidden_width = w1.shape[1]
    shape = jax.ShapeDtypeStruct
    whole = pl.BlockSpec(memory_space=pltpu.VMEM)
    f32, bf16 = jnp.float32, jnp.bfloat16
    return pl.pallas_call(
        middle_kernel,
        out_shape=(
            shape((rows, model), f32),
            shape((rows, model), f32),
            shape(o.shape, bf16),
            shape(wo.shape, bf16),
            shape(w1.shape, bf16),
            shape(w2.shape, bf16),
            shape((8, model), f32),
            shape((8, hidden_width), f32),
        ),
        in_specs=[whole] * 7,
        out_specs=(whole,) * 8,
        scratch_shapes=[
            pltpu.VMEM((rows, hidden_width), bf16),
            pltpu.VMEM((rows, hidden_width), f32),
            pltpu.VMEM((rows, model), f32),
            pltpu.VMEM((rows, model), f32),
            pltpu.VMEM((rows, model), bf16),
            pltpu.VMEM((model, rows), bf16),
            pltpu.VMEM((rows, model), f32),
            pltpu.VMEM((8, model), f32),
            pltpu.VMEM((8, hidden_width), f32),
        ],
        compiler_params=pltpu.CompilerParams(vmem_limit_bytes=VMEM_LIMIT),
        name="middle",
    )(o, x, cot, wo, w1, w2, vec)


MESH = pl.DeviceIdType.MESH


class Sender:
    def __init__(self, send_sems, recv_sems):
        self.send_sems, self.recv_sems, self.used, self.open = send_sems, recv_sems, 0, []

    def copy(self, source, target, device, when=None, until=None):
        index = self.used
        self.used += 1
        one = pltpu.make_async_remote_copy(
            src_ref=source,
            dst_ref=target,
            send_sem=self.send_sems.at[index],
            recv_sem=self.recv_sems.at[index],
            device_id=device,
            device_id_type=MESH,
        )
        if when is None:
            one.start()
        else:
            pl.when(when)(one.start)
        self.open.append((one, when))

        def arrive():
            if until is None:
                one.wait_recv()
            else:
                pl.when(until)(one.wait_recv)

        return arrive

    def finish(self):
        for one, when in self.open:
            if when is None:
                one.wait_send()
            else:
                pl.when(when)(one.wait_send)


def greet(seqs, count):
    s, c = lax.axis_index("seq"), lax.axis_index("ctx")
    barrier = pltpu.get_barrier_semaphore()
    for d in range(1, count):
        pl.semaphore_signal(barrier, inc=1, device_id=(s, lax.rem(c + d, count)), device_id_type=MESH)
    for d in range(1, seqs):
        pl.semaphore_signal(barrier, inc=1, device_id=(lax.rem(s + d, seqs), c), device_id_type=MESH)
    pl.semaphore_wait(barrier, count - 1 + seqs - 1)


def cube_steps(seqs, turn):
    bits = seqs.bit_length() - 1
    masks = []
    for j in range(bits):
        bit = lax.rem(j + turn, bits)
        mask = 0
        for k in range(bits):
            mask = mask + jnp.where(bit == k, 1 << k, 0)
        masks.append(mask)
    return masks


def across(s, mask):
    return s + mask * (1 - 2 * lax.rem(s // mask, 2))


def block_mates(rows):
    mates = 1
    while (mates * rows) % 16:
        mates *= 2
    return mates


def advance_kernel(
    seqs, count, chunks, heads,
    wq_ref, wk_ref, wv_ref, wo_ref, w1_ref, w2_ref, x_ref, code_ref, vec_ref,
    w_out, wo_out, w1_out, w2_out, x_out, code_out, vec_out,
    k_out, v_out, q_out, of_out, lse_out, o_out,
    stage4, stage1, stage2, flat4, flat1, flat2, low4, low1, low2, share4,
    w_all, x_all, codes, vecs, wt, k_ext, v_ext, q_ext, top_ref, acc_ref, s_even, s_odd, o_send,
    send_sems, recv_sems, here_sems, o_send_sems, o_recv_sems,
):
    s, c = lax.axis_index("seq"), lax.axis_index("ctx")
    f32, bf16 = jnp.float32, jnp.bfloat16
    small_rows, model = wq_ref.shape
    tall_rows, wide = w2_ref.shape[0], w1_ref.shape[1]
    mates = block_mates(small_rows)
    blocks = count // mates
    b, i = c // mates, lax.rem(c, mates)
    turn = lax.rem(c, 2)
    repeat = count // chunks
    g, r = c // repeat, lax.rem(c, repeat)
    width = heads * DH
    rows = x_ref.shape[0]
    length = count * rows
    block_rows, block_tall = mates * small_rows, mates * tall_rows
    sender = Sender(send_sems, recv_sems)
    here = []

    def move(source, target):
        one = pltpu.make_async_copy(source, target, here_sems.at[len(here)])
        one.start()
        here.append(one)

    greet(seqs, count)

    def tokens_at(place, half):
        start = pl.multiple_of(place * rows + half * (rows // 2), rows // 2)
        return pl.ds(start, rows // 2)

    mate_waits = {}

    def to_mates(source, group, half, when=None):
        waits = mate_waits.setdefault(half, [])
        for d in range(1, repeat):
            other = (s, g * repeat + lax.rem(r + d, repeat))
            waits.append(sender.copy(source, x_all.at[tokens_at(group * repeat + r, half)], other, when, when))

    half_rows = [pl.ds(h * (rows // 2), rows // 2) for h in range(2)]
    above, below = jnp.minimum((g + 1) * repeat + r, count - 1), jnp.maximum((g - 1) * repeat + r, 0)

    def pass_on(t):
        waits = []
        low_group, high_group = jnp.maximum(g - t, 0), jnp.minimum(g + t, chunks - 1)
        low_at = [tokens_at(low_group * repeat + r, h) for h in range(2)]
        high_at = [tokens_at(high_group * repeat + r, h) for h in range(2)]
        for h in range(2):
            rise = x_ref.at[half_rows[h]] if t == 0 else x_all.at[low_at[h]]
            fall = x_ref.at[half_rows[h]] if t == 0 else x_all.at[high_at[h]]
            rising = (g - t >= 0) & (g + 1 < chunks)
            falling = (g + t < chunks) & (g >= 1)
            waits.append((
                sender.copy(rise, x_all.at[low_at[h]], (s, above), rising, g - 1 - t >= 0),
                sender.copy(fall, x_all.at[high_at[h]], (s, below), falling, g + 1 + t < chunks),
            ))
        return waits

    def received(t, waits):
        low_group, high_group = jnp.maximum(g - 1 - t, 0), jnp.minimum(g + 1 + t, chunks - 1)
        for h in range(2):
            waits[h][0]()
            to_mates(x_all.at[tokens_at(low_group * repeat + r, h)], low_group, h, g - 1 - t >= 0)
            waits[h][1]()
            to_mates(x_all.at[tokens_at(high_group * repeat + r, h)], high_group, h, g + 1 + t < chunks)

    x_waits = pass_on(0)
    for h in range(2):
        to_mates(x_ref.at[half_rows[h]], g, h)

    shards = []
    matrices = (wq_ref, wk_ref, wv_ref, wo_ref)
    for d in range(1, mates):
        other = (s, b * mates + lax.rem(i + d, mates))
        for m in range(4):
            shards.append(sender.copy(matrices[m], stage4.at[i, m], other))
        shards.append(sender.copy(w1_ref, stage1.at[i], other))
        shards.append(sender.copy(w2_ref, stage2.at[i], other))
    for m in range(4):
        stage4[i, m] = matrices[m][...]
    stage1[i] = w1_ref[...]
    stage2[i] = w2_ref[...]

    small_waits = []
    for d in range(1, count):
        other = (s, lax.rem(c + d, count))
        small_waits.append(sender.copy(code_ref, codes.at[c], other))
        small_waits.append(sender.copy(vec_ref, vecs.at[s * count + c], other))
    codes[c] = code_ref[...]
    vecs[s * count + c] = vec_ref[...]
    x_all[tokens_at(c, 0), :] = x_ref[0 : rows // 2, :]
    x_all[tokens_at(c, 1), :] = x_ref[rows // 2 :, :]

    for wait in shards:
        wait()
    for p in range(mates):
        for m in range(4):
            flat4[m, p * small_rows : (p + 1) * small_rows, :] = stage4[p, m]
        flat1[p * small_rows : (p + 1) * small_rows, :] = stage1[p]
        flat2[p * tall_rows : (p + 1) * tall_rows, :] = stage2[p]
    for k in range(chunks):
        part = slice(k * width, (k + 1) * width)
        pieces = [flat4[m, :, part] for m in range(3)]
        pieces.append(jnp.zeros((block_rows, w_out.shape[1] - 3 * width), f32))
        share4[k] = jnp.concatenate(pieces, axis=1).astype(bf16)

    def w_rows(seq, block, size):
        start = (seq * blocks + block) * block_rows
        return pl.ds(pl.multiple_of(start, block_rows), size * block_rows)

    columns = []
    for d in range(1, blocks):
        to = lax.rem(b + d, blocks) * mates + i
        columns.append(sender.copy(share4.at[to // repeat], w_all.at[w_rows(s, b, 1)], (s, to)))
    w_all[w_rows(s, b, 1), :] = share4[g]

    low4[...] = flat4[3].astype(bf16)
    low1[...] = flat1[...].astype(bf16)
    low2[...] = flat2[...].astype(bf16)

    half_wide, half_model = wide // 2, model // 2
    wide_at = pl.ds(pl.multiple_of(turn * half_wide, half_wide), half_wide)
    model_at = pl.ds(pl.multiple_of(turn * half_model, half_model), half_model)

    def tall_rows_at(seq, block, size):
        start = (seq * blocks + block) * block_tall
        return pl.ds(pl.multiple_of(start, block_tall), size * block_tall)

    def big(seq, block, size=1):
        return (
            w1_out.at[w_rows(seq, block, size), wide_at],
            w2_out.at[tall_rows_at(seq, block, size), model_at],
            wo_out.at[w_rows(seq, block, size), model_at],
        )

    own = (low1.at[:, wide_at], low2.at[:, model_at], low4.at[:, model_at])
    for source, target in zip(own, big(s, b)):
        move(source, target)
    masks = cube_steps(seqs, turn)

    def families(seq):
        found = [(seq, -1)]
        for j, mask in enumerate(masks):
            found = found + [(across(one, mask), j) for one, _ in found]
        return found

    plane_waits = {}

    def spread(key, seq, step, block, sources, when):
        for j in range(step + 1, len(masks)):
            partner = (across(s, masks[j]), c)
            waits = plane_waits.setdefault((key, j), [])
            for source, target in zip(sources, big(seq, block)):
                waits.append((sender.copy(source, target, partner, when, when)))

    up, down = jnp.minimum((b + 1) * mates + i, count - 1), jnp.maximum((b - 1) * mates + i, 0)

    def line_send(t):
        waits = []
        low_block, high_block = jnp.maximum(b - t, 0), jnp.minimum(b + t, blocks - 1)
        rising = (b - t >= 0) & (b + 1 < blocks)
        falling = (b + t < blocks) & (b >= 1)
        rises = own if t == 0 else big(s, low_block)
        falls = own if t == 0 else big(s, high_block)
        for source, target in zip(rises, big(s, low_block)):
            waits.append(sender.copy(source, target, (s, up), rising, b - 1 - t >= 0))
        for source, target in zip(falls, big(s, high_block)):
            waits.append(sender.copy(source, target, (s, down), falling, b + 1 + t < blocks))
        return waits

    events = {("own",): (b, None)}
    for t in range(blocks - 1):
        events[(t, 0)] = (jnp.maximum(b - 1 - t, 0), b - 1 - t >= 0)
        events[(t, 1)] = (jnp.minimum(b + 1 + t, blocks - 1), b + 1 + t < blocks)

    spread(("own",), s, -1, b, own, None)
    line_waits = line_send(0)

    def token_service(t):
        nonlocal x_waits
        if t < chunks - 1:
            received(t, x_waits)
            if t + 1 < chunks - 1:
                x_waits = pass_on(t + 1)

    late = []

    def relay_event(key):
        block, when = events[key]
        queue = {j: list(plane_waits.get((key, j), [])) for j in range(len(masks))}
        for seq, j in families(s)[1:]:
            arriving, queue[j] = queue[j][:3], queue[j][3:]
            if j + 1 == len(masks):
                late.extend(arriving)
                continue
            for wait in arriving:
                wait()
            before = {k: len(plane_waits.get((key, k), [])) for k in range(j + 1, len(masks))}
            spread(key, seq, j, block, big(seq, block), when)
            for k in range(j + 1, len(masks)):
                queue[k] = queue[k] + plane_waits[(key, k)][before[k] :]

    def weight_service(t):
        nonlocal line_waits
        if t < blocks - 1:
            for wait in line_waits:
                wait()
            if t + 1 < blocks - 1:
                line_waits = line_send(t + 1)
            for way in range(2):
                block, when = events[(t, way)]
                spread((t, way), s, -1, block, big(s, block), when)
        if t == 0:
            relay_event(("own",))
        elif t - 1 < blocks - 1:
            relay_event((t - 1, 0))
            relay_event((t - 1, 1))

    for wait in columns:
        wait()
    columns = []
    for d in range(1, seqs):
        to = (lax.rem(s + d, seqs), c)
        slab = w_all.at[w_rows(s, 0, blocks)]
        columns.append(sender.copy(slab, slab, to))
    for wait in small_waits:
        wait()
    small_waits = []
    for d in range(1, seqs):
        to = (lax.rem(s + d, seqs), c)
        slab = vecs.at[pl.ds(s * count, count)]
        small_waits.append(sender.copy(slab, slab, to))

    top_ref[...] = jnp.full(top_ref.shape, FAR, f32)
    acc_ref[...] = jnp.zeros(acc_ref.shape, f32)
    k_ext[:, length:, :] = jnp.zeros((heads, PAD, k_ext.shape[2]), bf16)
    v_ext[:, 0:DH, length:] = jnp.zeros((heads, DH, PAD), bf16)
    v_ext[:, DH:, :] = jnp.ones((heads, 16, length + PAD), bf16)
    k_out[:, length:, :] = jnp.zeros((heads, PAD, DH), bf16)

    for wait in columns + small_waits:
        wait()
    move(w_all, w_out)
    move(vecs, vec_out)
    move(codes, code_out)
    wt[...] = w_all[...].astype(f32).T.astype(bf16)
    vec = vecs[:, 0, :]

    def bias_column(which):
        whole = unshard(vec, which * small_rows, small_rows)
        row = jnp.zeros((1, width), f32)
        for k in range(chunks):
            row = row + jnp.where(g == k, whole[:, k * width : (k + 1) * width], 0.0)
        extra = -width % LANES
        row = jnp.concatenate([row, jnp.zeros((1, extra), f32)], axis=1)
        return jnp.broadcast_to(row, (LANES, width + extra)).T[0:width, 0:1]

    bias_q, bias_v = bias_column(6), bias_column(7)

    def keys(chunk):
        at = pl.ds(pl.multiple_of(chunk * rows, rows), rows)
        x = x_all[at, :]
        k = nn(x, w_all[:, width : 2 * width]).astype(bf16)
        v = (nt(wt[2 * width : 3 * width, :], x) + bias_v).astype(bf16)
        v_out[:, at] = v
        code = codes[chunk].astype(f32)
        away = jnp.concatenate(
            [
                jnp.broadcast_to(code[:, j * LANES : (j + 1) * LANES], (LANES, LANES)).T[:, 0:DOCS]
                for j in range(rows // LANES)
            ],
            axis=0,
        )
        document = lax.broadcasted_iota(jnp.int32, (rows, DOCS), 1).astype(f32)
        away = jnp.where(away == 2.0 * document + 1.0, 0.0, 1.0).astype(bf16)
        for h in range(heads):
            one = k[:, h * DH : (h + 1) * DH]
            k_out[h, at, :] = one
            k_ext[h, at, :] = jnp.concatenate([one, one, away], axis=1)
            v_ext[h, 0:DH, at] = v[h * DH : (h + 1) * DH]

    def queries(group):
        chunk = group * repeat + r
        x = x_all[pl.ds(pl.multiple_of(chunk * rows, rows), rows), :]
        to = pl.ds(pl.multiple_of(group * rows, rows), rows)
        q = (nt(wt[0:width, :], x) + bias_q).astype(bf16)
        q_out[:, to] = q
        scaled = q.astype(f32) * (DH**-0.5 * LOG2E)
        high = scaled.astype(bf16)
        rest = (scaled - high.astype(f32)).astype(bf16)
        wanted = (codes[chunk] | 1).astype(f32)
        document = lax.broadcasted_iota(jnp.int32, (DOCS, rows), 0).astype(f32)
        away = jnp.where(wanted == 2.0 * document + 1.0, FAR, 0.0).astype(bf16)
        for h in range(heads):
            part = slice(h * DH, (h + 1) * DH)
            q_ext[h, :, to] = jnp.concatenate([high[part], rest[part], away], axis=0)

    def attend_to(group, first, last):
        at = pl.ds(pl.multiple_of(group * rows, rows), rows)

        def scores(slot, key_at):
            for h in range(heads):
                slot[h] = nn(k_ext[h, pl.ds(key_at, HALF), :], q_ext[h, :, at])

        def soften(slot, key_at):
            for h in range(heads):
                top = top_ref[group, h, 0:1, :]
                sc = slot[h]
                new = jnp.maximum(top, jnp.max(sc, axis=0, keepdims=True))
                p = jnp.exp2(sc - new).astype(bf16)
                acc_ref[group, h] = acc_ref[group, h] * jnp.exp2(top - new) + nn(
                    v_ext[h, :, pl.ds(key_at, HALF)], p
                )
                top_ref[group, h, 0:1, :] = new

        def step(j, carry):
            one = pl.multiple_of(j * BK, BK)
            two = pl.multiple_of(one + HALF, HALF)
            scores(s_odd, two)
            soften(s_even, one)
            scores(s_even, pl.multiple_of(one + BK, BK))
            soften(s_odd, two)
            return carry

        per = rows // BK
        scores(s_even, pl.multiple_of(first * rows, rows))
        lax.fori_loop(first * per, last * per, step, 0)

    def conclude(group):
        at = pl.ds(pl.multiple_of(group * rows, rows), rows)
        for h in range(heads):
            part = slice(h * DH, (h + 1) * DH)
            low = acc_ref[group, h, DH : DH + 1, :]
            out = acc_ref[group, h, 0:DH, :] / low
            of_out[part, at] = out
            o_send[group, part, :] = out.astype(bf16)
            lse_out[h : h + 1, at] = top_ref[group, h, 0:1, :] + jnp.log2(low)

        @pl.when(group != g)
        def _():
            o_copy(group).start()

    def o_copy(group):
        return pltpu.make_async_remote_copy(
            src_ref=o_send.at[group],
            dst_ref=o_out.at[g],
            send_sem=o_send_sems.at[group],
            recv_sem=o_recv_sems.at[g],
            device_id=(s, group * repeat + r),
            device_id_type=MESH,
        )

    def arrive(group, low, high):
        def make(j, carry):
            keys(group * repeat + j)
            return carry

        lax.fori_loop(0, repeat, make, 0)
        queries(group)
        whole = high - low + 1 == chunks

        def each(other, carry):
            same = other == group
            attend_to(
                other,
                jnp.where(same, low, group) * repeat,
                (jnp.where(same, high, group) + 1) * repeat,
            )

            @pl.when(whole)
            def _():
                conclude(other)

            return carry

        lax.fori_loop(low, high + 1, each, 0)

    def mates_here():
        for h in range(2):
            for wait in mate_waits[h]:
                wait()
            mate_waits[h] = []

    token_service(0)
    mates_here()
    arrive(g, g, g)
    weight_service(0)
    for t in range(chunks - 1):
        if t == chunks - 2:
            move(x_all, x_out)
        low, high = g - 1 - t, g + 1 + t
        has_low, has_high = low >= 0, high < chunks

        @pl.when(has_low)
        def _():
            arrive(low, low, jnp.minimum(g + t, chunks - 1))

        @pl.when(has_high & (low < 0))
        def _():
            arrive(high, 0, high)

        token_service(t + 1)
        weight_service(t + 1)

        @pl.when(has_high & has_low)
        def _():
            arrive(high, low, high)

        mates_here()
    for t in range(chunks, blocks + 1):
        weight_service(t)
    for wait in late:
        wait()
    own_out = pltpu.make_async_copy(o_send.at[g], o_out.at[g], here_sems.at[7])
    own_out.start()
    for one in here:
        one.wait()
    sibling = (s, c + 1 - 2 * turn)
    last_waits = []
    for piece in (
        w1_out.at[:, wide_at], w2_out.at[:, model_at], wo_out.at[:, model_at],
    ):
        last_waits.append(sender.copy(piece, piece, sibling))
    for wait in last_waits:
        wait()
    for d in range(1, chunks):
        group = lax.rem(g + d, chunks)
        pltpu.make_async_remote_copy(
            src_ref=o_send.at[g],
            dst_ref=o_out.at[group],
            send_sem=o_send_sems.at[g],
            recv_sem=o_recv_sems.at[group],
            device_id=(s, group * repeat + r),
            device_id_type=MESH,
        ).wait_recv()
        o_copy(group).wait_send()
    own_out.wait()
    sender.finish()


def advance(wq, wk, wv, wo, w1, w2, x, code, vec, chunks, heads):
    seqs, count = lax.axis_size("seq"), lax.axis_size("ctx")
    small_rows, model = wq.shape
    tall_rows, wide = w2.shape[0], w1.shape[1]
    rows = x.shape[0]
    mates = block_mates(small_rows)
    blocks, repeat = count // mates, count // chunks
    semaphores = (
        6 * (mates - 1) + 2 * (count - 1) + 2 * (seqs - 1) + 7 * (blocks - 1)
        + 3 * (seqs - 1) * (2 * blocks - 1) + 3 + 4 * (chunks - 1) + 2 * (2 * chunks - 1) * (repeat - 1)
    )
    devices = seqs * count
    width = heads * DH
    length, mine = count * rows, chunks * rows
    padded = -(-3 * width // LANES) * LANES
    shape = jax.ShapeDtypeStruct
    f32, bf16 = jnp.float32, jnp.bfloat16
    vmem, far = pl.BlockSpec(memory_space=pltpu.VMEM), pl.BlockSpec(memory_space=pl.ANY)
    block_rows, block_tall = mates * small_rows, mates * tall_rows
    dma = pltpu.SemaphoreType.DMA
    return pl.pallas_call(
        partial(advance_kernel, seqs, count, chunks, heads),
        out_shape=(
            shape((model, padded), bf16),
            shape((model, model), bf16),
            shape((model, wide), bf16),
            shape((tall_rows * devices, model), bf16),
            shape((length, model), bf16),
            shape((count, 1, rows), jnp.int32),
            shape((devices, 1, vec.shape[1]), f32),
            shape((heads, length + PAD, DH), bf16),
            shape((width, length), bf16),
            shape((width, mine), bf16),
            shape((width, mine), f32),
            shape((8, mine), f32),
            shape((chunks, width, rows), bf16),
        ),
        in_specs=[vmem] * 9,
        out_specs=(far,) * 7 + (vmem,) * 5 + (far,),
        scratch_shapes=[
            pltpu.VMEM((mates, 4, small_rows, model), f32),
            pltpu.VMEM((mates, small_rows, wide), f32),
            pltpu.VMEM((mates, tall_rows, model), f32),
            pltpu.VMEM((4, block_rows, model), f32),
            pltpu.VMEM((block_rows, wide), f32),
            pltpu.VMEM((block_tall, model), f32),
            pltpu.VMEM((block_rows, model), bf16),
            pltpu.VMEM((block_rows, wide), bf16),
            pltpu.VMEM((block_tall, model), bf16),
            pltpu.VMEM((chunks, block_rows, padded), bf16),
            pltpu.VMEM((model, padded), bf16),
            pltpu.VMEM((length, model), bf16),
            pltpu.VMEM((count, 1, rows), jnp.int32),
            pltpu.VMEM((devices, 1, vec.shape[1]), f32),
            pltpu.VMEM((padded, model), bf16),
            pltpu.VMEM((heads, length + PAD, 2 * DH + DOCS), bf16),
            pltpu.VMEM((heads, DH + 16, length + PAD), bf16),
            pltpu.VMEM((heads, 2 * DH + DOCS, mine), bf16),
            pltpu.VMEM((chunks, heads, 8, rows), f32),
            pltpu.VMEM((chunks, heads, DH + 16, rows), f32),
            pltpu.VMEM((heads, HALF, rows), f32),
            pltpu.VMEM((heads, HALF, rows), f32),
            pltpu.VMEM((chunks, width, rows), bf16),
            dma((semaphores,)),
            dma((semaphores,)),
            dma((8,)),
            dma((chunks,)),
            dma((chunks,)),
        ],
        compiler_params=pltpu.CompilerParams(
            vmem_limit_bytes=VMEM_LIMIT, collective_id=1, has_side_effects=True
        ),
        name="advance",
    )(wq, wk, wv, wo, w1, w2, x, code, vec)


def added(*parts):
    sum_of = parts[0].astype(jnp.float32)
    for part in parts[1:]:
        sum_of = sum_of + part.astype(jnp.float32)
    return sum_of


class Line:
    def __init__(self, sender, place, size, device, pieces, landing):
        self.sender, self.place, self.size, self.device = sender, place, size, device
        self.pieces, self.landing = pieces, landing
        self.waits = None

    def send(self, t):
        self.waits = []
        for way in range(2):
            rank = self.place if way == 0 else self.size - 1 - self.place
            mirror = (lambda d: d) if way == 0 else (lambda d: self.size - 1 - d)
            goal = jnp.clip(mirror(self.size - 1 - t + rank), 0, self.size - 1)
            sends = rank <= t
            receives = (rank >= 1) & (rank - 1 <= t)
            to = jnp.clip(self.place + (1 - 2 * way), 0, self.size - 1)
            waits = []
            for source, target in zip(self.pieces(goal), self.landing(way, t)):
                waits.append(self.sender.copy(source, target, self.device(to), sends, receives))
            self.waits.append((receives, mirror, rank, waits))

    def receive(self, t):
        for way, (receives, mirror, rank, waits) in enumerate(self.waits):
            goal = jnp.clip(mirror(self.size - 2 - t + rank), 0, self.size - 1)
            pieces, landing = self.pieces(goal), self.landing(way, t)
            for wait, piece, arrived in zip(waits, pieces, landing):
                wait()

                @pl.when(receives)
                def _():
                    piece[...] = added(piece[...], arrived[...]).astype(piece.dtype)


def settle_kernel(
    seqs, count, chunks,
    dx_ref, dw_ref, dwo_ref, dw1_ref, dw2_ref, dsmall_ref, db1_ref, db_ref,
    dx_out, dw_out, dwo_out, dw1_out, dw2_out, dsmall_out, db1_out,
    dx_sum, dx_in, dx_line, sum1, sum2, sum4, in1, in2, in4, cube1, cube2, cube4,
    line1, line2, line4, last1, last2, last4, w_mine, w_seq, w_block, w_mates, w_tmp,
    small_in, b1_in, b_in, vec_seq,
    send_sems, recv_sems, here_sems,
):
    s, c = lax.axis_index("seq"), lax.axis_index("ctx")
    bf16 = jnp.bfloat16
    rows, model = dx_out.shape
    wide = dw1_ref.shape[1]
    repeat = count // chunks
    mates = w_mates.shape[0]
    blocks = count // mates
    block_rows, block_tall = dwo_out.shape[0], dw2_out.shape[0]
    width = model // chunks
    b, i = c // mates, lax.rem(c, mates)
    g, r = c // repeat, lax.rem(c, repeat)
    turn = lax.rem(c, 2)
    half_wide, half_model = wide // 2, model // 2
    slab_rows, slab_tall = blocks * block_rows, blocks * block_tall
    sender = Sender(send_sems, recv_sems)
    here = []

    def move(source, target):
        one = pltpu.make_async_copy(source, target, here_sems.at[len(here)])
        one.start()
        here.append(one)

    greet(seqs, count)

    dx_waits = []
    for d in range(1, repeat):
        to = lax.rem(r + d, repeat)
        for k in range(chunks):
            dx_waits.append(
                sender.copy(dx_ref.at[k * repeat + to], dx_in.at[d - 1, k], (s, g * repeat + to))
            )
    for k in range(chunks):
        move(dx_ref.at[k * repeat + r], dx_sum.at[k])

    sibling = (s, c + 1 - 2 * turn)

    def column_half(which):
        wide_at = pl.ds(pl.multiple_of(which * half_wide, half_wide), half_wide)
        model_at = pl.ds(pl.multiple_of(which * half_model, half_model), half_model)
        return dw1_ref.at[:, wide_at], dw2_ref.at[:, model_at], dwo_ref.at[:, model_at]

    half_waits = [
        sender.copy(source, target, sibling)
        for source, target in zip(column_half(1 - turn), (in1, in2, in4))
    ]
    for source, target in zip(column_half(turn), (sum1, sum2, sum4)):
        move(source, target)

    w_waits = []
    for d in range(1, seqs):
        to = lax.rem(s + d, seqs)
        source = dw_ref.at[pl.ds(pl.multiple_of(to * slab_rows, slab_rows), slab_rows)]
        w_waits.append(sender.copy(source, w_seq.at[d - 1], (to, c)))
    move(dw_ref.at[pl.ds(pl.multiple_of(s * slab_rows, slab_rows), slab_rows)], w_mine)

    vec_waits = []
    for d in range(1, count):
        to = (s, lax.rem(c + d, count))
        for source, target in ((dsmall_ref, small_in), (db1_ref, b1_in), (db_ref, b_in)):
            vec_waits.append(sender.copy(source, target.at[c], to))
    small_in[c] = dsmall_ref[...]
    b1_in[c] = db1_ref[...]
    b_in[c] = db_ref[...]

    for one in here:
        one.wait()
    for wait in dx_waits:
        wait()
    for k in range(chunks):
        dx_sum[k] = added(dx_sum[k], *[dx_in[d, k] for d in range(repeat - 1)]).astype(bf16)
    half_rows = rows // 2
    token_lines = []
    for h in range(2):
        at = pl.ds(h * half_rows, half_rows)
        token_lines.append(
            Line(
                sender, g, chunks, lambda to: (s, to * repeat + r),
                lambda goal, at=at: (dx_sum.at[goal, at],),
                lambda way, t, at=at: (dx_line.at[way, t, at],),
            )
        )
    for line in token_lines:
        line.send(0)

    for wait in half_waits:
        wait()
    quarter = sum1.shape[0] // 4
    for k in range(4):
        at = slice(k * quarter, (k + 1) * quarter)
        sum1[at] = added(sum1[at], in1[at]).astype(bf16)
    quarter = sum2.shape[0] // 4
    for k in range(4):
        at = slice(k * quarter, (k + 1) * quarter)
        sum2[at] = added(sum2[at], in2[at]).astype(bf16)
    sum4[...] = added(sum4[...], in4[...]).astype(bf16)

    def slab(seq):
        at = pl.ds(pl.multiple_of(seq * slab_rows, slab_rows), slab_rows)
        tall = pl.ds(pl.multiple_of(seq * slab_tall, slab_tall), slab_tall)
        return sum1.at[at], sum2.at[tall], sum4.at[at]

    masks = cube_steps(seqs, turn)

    def family(seq, rest):
        found = [seq]
        for mask in rest:
            found = found + [across(one, mask) for one in found]
        return found

    cube_waits, used = [], 0

    def cube_send(j):
        nonlocal used
        partner = across(s, masks[j])
        cube_waits.clear()
        mine = family(s, masks[j + 1 :])
        for k, seq in enumerate(family(partner, masks[j + 1 :])):
            landing = cube1.at[used + k], cube2.at[used + k], cube4.at[used + k]
            waits = [
                sender.copy(source, target, (partner, c)) for source, target in zip(slab(seq), landing)
            ]
            cube_waits.append((mine[k], landing, waits))
        used += len(cube_waits)

    def cube_receive():
        for seq, landing, waits in cube_waits:
            for wait, target, arrived in zip(waits, slab(seq), landing):
                wait()
                target[...] = added(target[...], arrived[...]).astype(bf16)

    cube_send(0)

    for wait in w_waits:
        wait()
    w_mine[...] = added(w_mine[...], *[w_seq[d] for d in range(seqs - 1)]).astype(bf16)
    w_waits = []
    for d in range(1, blocks):
        to = lax.rem(b + d, blocks)
        source = w_mine.at[pl.ds(pl.multiple_of(to * block_rows, block_rows), block_rows)]
        w_waits.append(sender.copy(source, w_block.at[b], (s, to * mates + i)))
    w_block[b] = w_mine[pl.ds(pl.multiple_of(b * block_rows, block_rows), block_rows), :]

    for wait in vec_waits:
        wait()
    vec_waits = []
    small = small_in[0]
    tall = b1_in[0]
    for k in range(1, count):
        small = small + small_in[k]
        tall = tall + b1_in[k]
    pair = []
    for k in range(chunks):
        one = b_in[k * repeat]
        for d in range(1, repeat):
            one = one + b_in[k * repeat + d]
        pair.append(one)
    for m in range(2):
        joined = jnp.concatenate([one[0:1, m * width : (m + 1) * width] for one in pair], axis=1)
        dsmall_out[6 + m : 7 + m, :] = joined
    vec_seq[s, 0:6, 0:model] = small[0:6]
    vec_seq[s, 6:8, 0:model] = dsmall_out[6:8, :]
    vec_seq[s, :, model:] = tall
    for d in range(1, seqs):
        vec_waits.append(sender.copy(vec_seq.at[s], vec_seq.at[s], (lax.rem(s + d, seqs), c)))

    for wait in w_waits:
        wait()
    w_waits = []
    w_mates[i] = w_block[...]
    for d in range(1, mates):
        to = (s, b * mates + lax.rem(i + d, mates))
        w_waits.append(sender.copy(w_block, w_mates.at[i], to))

    def block_slab(goal):
        row = s * slab_rows + goal * block_rows
        tall = s * slab_tall + goal * block_tall
        at = pl.ds(pl.multiple_of(row, block_rows), block_rows)
        tall_at = pl.ds(pl.multiple_of(tall, block_tall), block_tall)
        return sum1.at[at], sum2.at[tall_at], sum4.at[at]

    weight_line = Line(
        sender, b, blocks, lambda to: (s, to * mates + i),
        block_slab, lambda way, t: (line1.at[way, t], line2.at[way, t], line4.at[way, t]),
    )
    steps = len(masks)
    token_steps, weight_steps = chunks - 1, blocks - 1
    for t in range(max(token_steps, steps + weight_steps)):
        if t < token_steps:
            for line in token_lines:
                line.receive(t)
                if t + 1 < token_steps:
                    line.send(t + 1)
        if t < steps:
            cube_receive()
            if t + 1 < steps:
                cube_send(t + 1)
            elif weight_steps:
                weight_line.send(0)
        elif t - steps < weight_steps:
            weight_line.receive(t - steps)
            if t - steps + 1 < weight_steps:
                weight_line.send(t - steps + 1)

    last_waits = []
    for source, target in zip(block_slab(b), (last1, last2, last4)):
        target[i] = source[...]
        for d in range(1, mates):
            to = (s, b * mates + lax.rem(i + d, mates))
            last_waits.append(sender.copy(source, target.at[i], to))
    dx_out[...] = dx_sum[g]
    for wait in w_waits + vec_waits + last_waits:
        wait()
    for target, source in ((dw1_out, last1), (dw2_out, last2), (dwo_out, last4)):
        size = target.shape[1] // 2
        for which in range(2):
            target[:, which * size : (which + 1) * size] = added(
                *[source[k] for k in range(which, mates, 2)]
            )
    for k in range(chunks):
        terms = [
            w_mates[p, q]
            for p in range(mates)
            for q in range(blocks)
            if (q * mates + p) // repeat == k
        ]
        dw_out[k] = added(*terms)
    vec = vec_seq[0]
    for d in range(1, seqs):
        vec = vec + vec_seq[d]
    dsmall_out[...] = vec[:, 0:model]
    db1_out[...] = vec[:, model:]
    sender.finish()


def settle(dx, dw, dwo, dw1, dw2, dsmall, db1, db, chunks):
    seqs, count = lax.axis_size("seq"), lax.axis_size("ctx")
    _, rows, model = dx.shape
    wide, tall = dw1.shape[1], dw2.shape[0]
    devices = seqs * count
    mates = block_mates(model // devices)
    blocks, repeat = count // mates, count // chunks
    block_rows, block_tall = mates * (model // devices), mates * (tall // devices)
    slab_rows, slab_tall = blocks * block_rows, blocks * block_tall
    padded = dw.shape[1]
    semaphores = (
        chunks * (repeat - 1) + 3 + (seqs - 1) + 3 * (count - 1) + 4 * (chunks - 1)
        + 3 * (seqs - 1) + (blocks - 1) + (seqs - 1) + (mates - 1) + 6 * (blocks - 1) + 3 * (mates - 1)
    )
    shape = jax.ShapeDtypeStruct
    f32, bf16 = jnp.float32, jnp.bfloat16
    vmem, far = pl.BlockSpec(memory_space=pltpu.VMEM), pl.BlockSpec(memory_space=pl.ANY)
    half_wide, half_model = wide // 2, model // 2
    triple = lambda lead, a, t: [
        pltpu.VMEM(lead + (a, half_wide), bf16),
        pltpu.VMEM(lead + (t, half_model), bf16),
        pltpu.VMEM(lead + (a, half_model), bf16),
    ]
    return pl.pallas_call(
        partial(settle_kernel, seqs, count, chunks),
        out_shape=(
            shape((rows, model), bf16),
            shape((chunks, block_rows, padded), f32),
            shape((block_rows, model), f32),
            shape((block_rows, wide), f32),
            shape((block_tall, model), f32),
            shape((8, model), f32),
            shape((8, wide), f32),
        ),
        in_specs=[far] * 5 + [vmem] * 3,
        out_specs=(vmem,) * 7,
        scratch_shapes=[
            pltpu.VMEM((chunks, rows, model), bf16),
            pltpu.VMEM((repeat - 1, chunks, rows, model), bf16),
            pltpu.VMEM((2, chunks - 1, rows, model), bf16),
        ]
        + triple((), model, tall)
        + triple((), model, tall)
        + triple((seqs - 1,), slab_rows, slab_tall)
        + triple((2, blocks - 1), block_rows, block_tall)
        + triple((mates,), block_rows, block_tall)
        + [
            pltpu.VMEM((slab_rows, padded), bf16),
            pltpu.VMEM((seqs - 1, slab_rows, padded), bf16),
            pltpu.VMEM((blocks, block_rows, padded), bf16),
            pltpu.VMEM((mates, blocks, block_rows, padded), bf16),
            pltpu.VMEM((8, 128), f32),
            pltpu.VMEM((count, 8, model), f32),
            pltpu.VMEM((count, 8, wide), f32),
            pltpu.VMEM((count, 8, db.shape[1]), f32),
            pltpu.VMEM((seqs, 8, model + wide), f32),
            pltpu.SemaphoreType.DMA((semaphores,)),
            pltpu.SemaphoreType.DMA((semaphores,)),
            pltpu.SemaphoreType.DMA((chunks + 4,)),
        ],
        compiler_params=pltpu.CompilerParams(
            vmem_limit_bytes=VMEM_LIMIT, collective_id=2, has_side_effects=True
        ),
        name="settle",
    )(dx, dw, dwo, dw1, dw2, dsmall, db1, db)


def swap_kernel(chunks, repeat, a_ref, a_out, send_sems, recv_sems, here_sem):
    s, c = lax.axis_index("seq"), lax.axis_index("ctx")
    g, r = c // repeat, lax.rem(c, repeat)
    place = lambda d: lax.rem(g + d, chunks)
    barrier = pltpu.get_barrier_semaphore()
    for d in range(1, chunks):
        pl.semaphore_signal(
            barrier, inc=1, device_id=(s, place(d) * repeat + r), device_id_type=MESH
        )
    pl.semaphore_wait(barrier, chunks - 1)
    sender = Sender(send_sems, recv_sems)
    here = pltpu.make_async_copy(a_ref.at[g], a_out.at[g], here_sem)
    here.start()
    waits = [
        sender.copy(a_ref.at[place(d)], a_out.at[g], (s, place(d) * repeat + r))
        for d in range(1, chunks)
    ]
    for wait in waits:
        wait()
    here.wait()
    sender.finish()


def swap(a):
    chunks = a.shape[0]
    far = pl.BlockSpec(memory_space=pl.ANY)
    return pl.pallas_call(
        partial(swap_kernel, chunks, lax.axis_size("ctx") // chunks),
        out_shape=jax.ShapeDtypeStruct(a.shape, a.dtype),
        in_specs=[far],
        out_specs=far,
        scratch_shapes=[
            pltpu.SemaphoreType.DMA((chunks - 1,)),
            pltpu.SemaphoreType.DMA((chunks - 1,)),
            pltpu.SemaphoreType.DMA,
        ],
        compiler_params=pltpu.CompilerParams(collective_id=3, has_side_effects=True),
        name="swap",
    )(a)


def pick(values, size, device):
    wide = values.shape[1]
    row = lax.broadcasted_iota(jnp.int32, (wide, size), 0)
    column = lax.broadcasted_iota(jnp.int32, (wide, size), 1)
    chosen = (row == column + device * size).astype(jnp.bfloat16)
    high = values.astype(jnp.bfloat16)
    rest = values - high.astype(jnp.float32)
    middle_part = rest.astype(jnp.bfloat16)
    low = (rest - middle_part.astype(jnp.float32)).astype(jnp.bfloat16)
    return nn(high, chosen) + nn(middle_part, chosen) + nn(low, chosen)


def finish_kernel(
    count, mates,
    e1_ref, dx_ref, dw_ref, dwo_ref, dw1_ref, dw2_ref, small_ref, b1_ref,
    dx_out, dwq_out, dwk_out, dwv_out, dwo_out, dw1_out, dw2_out, small_out, b1_out,
):
    s, c = lax.axis_index("seq"), lax.axis_index("ctx")
    dx_out[...] = e1_ref[...] + dx_ref[...].astype(jnp.float32)
    each, tall = dwo_out.shape[0], dw2_out.shape[0]
    chunks = dw_ref.shape[0]
    width = dwq_out.shape[1] // chunks
    i = lax.rem(c, mates)
    for p in range(mates):
        rows = slice(p * each, (p + 1) * each)

        @pl.when(i == p)
        def _():
            for m, out in enumerate((dwq_out, dwk_out, dwv_out)):
                parts = [dw_ref[k, rows, m * width : (m + 1) * width] for k in range(chunks)]
                out[...] = jnp.concatenate(parts, axis=1)
            dwo_out[...] = dwo_ref[rows, :]
            dw1_out[...] = dw1_ref[rows, :]
            dw2_out[...] = dw2_ref[p * tall : (p + 1) * tall, :]

    device = s * count + c
    small_out[...] = pick(small_ref[...], each, device)
    b1_out[...] = pick(b1_ref[...], tall, device)


def finish(e1, dx, dw, dwo, dw1, dw2, small, b1):
    count = lax.axis_size("ctx")
    devices = count * lax.axis_size("seq")
    model, wide = dwo.shape[1], dw1.shape[1]
    each, tall = model // devices, wide // devices
    shape = jax.ShapeDtypeStruct
    f32 = jnp.float32
    vmem = pl.BlockSpec(memory_space=pltpu.VMEM)
    return pl.pallas_call(
        partial(finish_kernel, count, block_mates(each)),
        out_shape=(shape(e1.shape, f32),)
        + (shape((each, model), f32),) * 4
        + (shape((each, wide), f32), shape((tall, model), f32), shape((8, each), f32), shape((8, tall), f32)),
        in_specs=[vmem] * 8,
        out_specs=(vmem,) * 9,
        compiler_params=pltpu.CompilerParams(vmem_limit_bytes=VMEM_LIMIT),
        name="finish",
    )(e1, dx, dw, dwo, dw1, dw2, small, b1)


def on_device(
    tokens, segment_ids, valid_tokens, query_weight, query_bias, key_weight, value_weight, value_bias,
    output_weight, output_bias, attn_norm_gain, attn_norm_shift, up_weight, up_bias, down_weight,
    down_bias, ffn_norm_gain, ffn_norm_shift, out_cotangent,
):
    count = lax.axis_size("ctx")
    chunks = math.gcd(H, count)
    heads = H // chunks
    x = tokens[0]
    vec = jnp.concatenate([
        output_bias, attn_norm_gain, attn_norm_shift, down_bias, ffn_norm_gain, ffn_norm_shift,
        query_bias, value_bias, up_bias,
    ])
    vec = jnp.pad(vec, (0, -vec.shape[0] % LANES))[None]
    w, wo, w1, w2, x_all, codes, vecs, k, v, q, o_float, lse, o = advance(
        query_weight, key_weight, value_weight, output_weight, up_weight, down_weight,
        x, segment_ids * 2 + valid_tokens, vec, chunks, heads,
    )
    codes = codes[:, 0]
    output, e1, do, dwo, dw1, dw2, dsmall, db1 = middle(
        o, x, out_cotangent[0], wo, w1, w2, vecs
    )
    dx, dw, db = retreat(x_all, w, k, v, q, o_float, lse, swap(do), codes, heads, chunks)
    summed = settle(dx, dw, dwo, dw1, dw2, dsmall, db1, db, chunks)
    grad, dwq, dwk, dwv, dwo, dw1, dw2, small, b1 = finish(e1, *summed)
    return (
        output[None], grad[None],
        dwq, small[6], dwk, dwv, small[7],
        dwo, small[0], small[1], small[2],
        dw1, b1[0], dw2, small[3], small[4], small[5],
    )


def solution(mesh):
    in_specs = (
        P("seq", "ctx", None),
        P("seq", "ctx"),
        P("seq", "ctx"),
        P(("seq", "ctx"), None),
        P(("seq", "ctx")),
        P(("seq", "ctx"), None),
        P(("seq", "ctx"), None),
        P(("seq", "ctx")),
        P(("seq", "ctx"), None),
        P(("seq", "ctx")),
        P(("seq", "ctx")),
        P(("seq", "ctx")),
        P(("seq", "ctx"), None),
        P(("seq", "ctx")),
        P(("seq", "ctx"), None),
        P(("seq", "ctx")),
        P(("seq", "ctx")),
        P(("seq", "ctx")),
        P("seq", "ctx", None),
    )
    out_specs = (
        P("seq", "ctx", None),
        P("seq", "ctx", None),
        P(("seq", "ctx"), None),
        P(("seq", "ctx")),
        P(("seq", "ctx"), None),
        P(("seq", "ctx"), None),
        P(("seq", "ctx")),
        P(("seq", "ctx"), None),
        P(("seq", "ctx")),
        P(("seq", "ctx")),
        P(("seq", "ctx")),
        P(("seq", "ctx"), None),
        P(("seq", "ctx")),
        P(("seq", "ctx"), None),
        P(("seq", "ctx")),
        P(("seq", "ctx")),
        P(("seq", "ctx")),
    )
    return jax.shard_map(
        on_device, mesh=mesh, in_specs=in_specs, out_specs=out_specs, check_vma=False
    )
```

```python
import math
from functools import partial

import jax
import jax.numpy as jnp
from jax import lax
from jax.experimental import pallas as pl
from jax.experimental.pallas import tpu as pltpu
from jax.sharding import PartitionSpec as P

H = 12
DH = 64
VMEM_LIMIT = 60 * 1024 * 1024

LOG2E = 1.4426950408889634
BQ = 512
BK = 512
HALF = BK // 2
PAD = BK + HALF
DOCS = 64
FAR = -(2.0**100)
LANES = 128


def nt(a, b):
    return lax.dot_general(a, b, (((1,), (1,)), ((), ())), preferred_element_type=jnp.float32)


def nn(a, b):
    return lax.dot_general(a, b, (((1,), (0,)), ((), ())), preferred_element_type=jnp.float32)


def unshard(vec, at, each):
    devices = vec.shape[0]
    shard = vec[:, at : at + each].astype(jnp.bfloat16)
    size = devices * each
    owner = lambda shape, axis: jnp.floor(
        (lax.broadcasted_iota(jnp.int32, shape, axis).astype(jnp.float32) + 0.5) / each
    )
    column = lax.broadcasted_iota(jnp.int32, (each, size), 1).astype(jnp.float32)
    inner = column - owner((each, size), 1) * each
    place = lax.broadcasted_iota(jnp.int32, (each, size), 0).astype(jnp.float32)
    repeated = nn(shard, (inner == place).astype(jnp.bfloat16))
    device = lax.broadcasted_iota(jnp.int32, (devices, size), 0).astype(jnp.float32)
    return jnp.sum(jnp.where(owner((devices, size), 1) == device, repeated, 0.0), axis=0, keepdims=True)


def tn(a, b):
    return lax.dot_general(a, b, (((0,), (0,)), ((), ())), preferred_element_type=jnp.float32)


def flip(a):
    return a.astype(jnp.float32).T.astype(a.dtype)


def three_parts(row):
    high = row.astype(jnp.bfloat16)
    rest = row - high.astype(jnp.float32)
    middle = rest.astype(jnp.bfloat16)
    low = (rest - middle.astype(jnp.float32)).astype(jnp.bfloat16)
    empty = jnp.zeros((13, row.shape[1]), jnp.float32)
    return jnp.concatenate(
        [high.astype(jnp.float32), middle.astype(jnp.float32), low.astype(jnp.float32), empty], axis=0
    )


EPSILON = 1e-12
FF_BLOCK = 512


def gelu_pair(u):
    z = jnp.abs(u) * (0.5**0.5)
    t = 1.0 / (1.0 + 0.3275911 * z)
    bell = jnp.exp(-z * z)
    poly = t * (
        0.254829592 + t * (-0.284496736 + t * (1.421413741 + t * (-1.453152027 + t * 1.061405429)))
    )
    half = 0.5 * poly * bell
    below = jnp.where(u < 0.0, half, 1.0 - half)
    return u * below, below + u * bell * 0.3989422804014327


def standard(hidden):
    centred = hidden - jnp.mean(hidden, axis=-1, keepdims=True)
    scale = lax.rsqrt(jnp.mean(centred * centred, axis=-1, keepdims=True) + EPSILON)
    return centred * scale, scale


def norm_back(grad, gain, normal, scale):
    t = grad * gain
    return scale * (
        t
        - jnp.mean(t, axis=-1, keepdims=True)
        - normal * jnp.mean(t * normal, axis=-1, keepdims=True)
    )


def middle_kernel(
    o_ref, x_ref, cot_ref, wo_ref, w1_ref, w2_ref, vec_ref,
    out_ref, e1_ref, do_ref, dwo_ref, dw1_ref, dw2_ref, dsmall_ref, db1_ref,
    act, slope, y1_ref, normal_ref, r2_ref, y1t_ref, grad_ref, small_ref, b1_ref,
):
    bf16 = jnp.bfloat16
    groups, width, rows = o_ref.shape
    hidden_width = w1_ref.shape[1]
    steps = hidden_width // FF_BLOCK
    vec = vec_ref[:, 0, :]
    each = x_ref.shape[1] // vec.shape[0]
    for i in range(6):
        small_ref[i : i + 1, :] = unshard(vec, i * each, each)
    b1_ref[0:1, :] = unshard(vec, 8 * each, hidden_width // vec.shape[0])
    row = lambda i: small_ref[i : i + 1, :]
    ones = jnp.ones((8, rows), bf16)
    o = o_ref[...].reshape(groups * width, rows)
    n1 = x_ref[...].astype(jnp.float32) + (tn(o, wo_ref[...]) + row(0))
    normal, scale_one = standard(n1)
    normal_ref[...] = normal
    y1 = normal * row(1) + row(2)
    y1_ref[...] = y1
    y1_low = y1.astype(bf16)
    y1t_ref[...] = y1.T.astype(bf16)
    grad_ref[...] = jnp.zeros(grad_ref.shape, jnp.float32)

    def forward(i, carry):
        at = pl.ds(pl.multiple_of(i * FF_BLOCK, FF_BLOCK), FF_BLOCK)
        u = nn(y1_low, w1_ref[:, at]) + b1_ref[0:1, at]
        value, gradient = gelu_pair(u)
        value = value.astype(bf16)
        act[:, at] = value
        slope[:, at] = gradient
        grad_ref[...] += nn(value, w2_ref[at, :])
        return carry

    lax.fori_loop(0, steps, forward, 0)
    normal_two, scale_two = standard(y1_ref[...] + (grad_ref[...] + row(3)))
    out_ref[...] = normal_two * row(4) + row(5)
    cot = cot_ref[...].astype(jnp.float32)
    dsmall_ref[4:5, :] = jnp.sum(cot * normal_two, axis=0, keepdims=True)
    dsmall_ref[5:6, :] = jnp.sum(cot, axis=0, keepdims=True)
    e2 = norm_back(cot, row(4), normal_two, scale_two)
    grad_ref[...] = e2
    r2 = e2.astype(bf16)
    r2_ref[...] = r2
    dsmall_ref[3:4, :] = nn(ones, r2)[0:1]

    def backward(i, carry):
        at = pl.ds(pl.multiple_of(i * FF_BLOCK, FF_BLOCK), FF_BLOCK)
        dw2_ref[at, :] = tn(act[:, at], r2_ref[...]).astype(bf16)
        du = (nt(r2_ref[...], w2_ref[at, :]) * slope[:, at]).astype(bf16)
        db1_ref[:, at] = nn(ones, du)[0:1]
        dw1_ref[:, at] = nn(y1t_ref[...], du).astype(bf16)
        grad_ref[...] += nt(du, w1_ref[:, at])
        return carry

    lax.fori_loop(0, steps, backward, 0)
    grad = grad_ref[...]
    normal = normal_ref[...]
    dsmall_ref[1:2, :] = jnp.sum(grad * normal, axis=0, keepdims=True)
    dsmall_ref[2:3, :] = jnp.sum(grad, axis=0, keepdims=True)
    e1 = norm_back(grad, row(1), normal, scale_one)
    e1_ref[...] = e1
    r1 = e1.astype(bf16)
    dsmall_ref[0:1, :] = nn(ones, r1)[0:1]
    dsmall_ref[6:8, :] = jnp.zeros((2, dsmall_ref.shape[1]), jnp.float32)
    dwo_ref[...] = nn(o, r1).astype(bf16)
    do_ref[...] = nt(wo_ref[...], r1).astype(bf16).reshape(groups, width, rows)


def middle(o, x, cot, wo, w1, w2, vec):
    groups, width, rows = o.shape
    model = x.shape[1]
    hidden_width = w1.shape[1]
    shape = jax.ShapeDtypeStruct
    whole = pl.BlockSpec(memory_space=pltpu.VMEM)
    f32, bf16 = jnp.float32, jnp.bfloat16
    return pl.pallas_call(
        middle_kernel,
        out_shape=(
            shape((rows, model), f32),
            shape((rows, model), f32),
            shape(o.shape, bf16),
            shape(wo.shape, bf16),
            shape(w1.shape, bf16),
            shape(w2.shape, bf16),
            shape((8, model), f32),
            shape((1, hidden_width), f32),
        ),
        in_specs=[whole] * 7,
        out_specs=(whole,) * 8,
        scratch_shapes=[
            pltpu.VMEM((rows, hidden_width), bf16),
            pltpu.VMEM((rows, hidden_width), f32),
            pltpu.VMEM((rows, model), f32),
            pltpu.VMEM((rows, model), f32),
            pltpu.VMEM((rows, model), bf16),
            pltpu.VMEM((model, rows), bf16),
            pltpu.VMEM((rows, model), f32),
            pltpu.VMEM((8, model), f32),
            pltpu.VMEM((8, hidden_width), f32),
        ],
        compiler_params=pltpu.CompilerParams(vmem_limit_bytes=VMEM_LIMIT),
        name="middle",
    )(o, x, cot, wo, w1, w2, vec)


MESH = pl.DeviceIdType.MESH


class Sender:
    def __init__(self, send_sems, recv_sems):
        self.send_sems, self.recv_sems, self.used, self.open = send_sems, recv_sems, 0, []

    def copy(self, source, target, device, when=None, until=None):
        index = self.used
        self.used += 1
        one = pltpu.make_async_remote_copy(
            src_ref=source,
            dst_ref=target,
            send_sem=self.send_sems.at[index],
            recv_sem=self.recv_sems.at[index],
            device_id=device,
            device_id_type=MESH,
        )
        if when is None:
            one.start()
        else:
            pl.when(when)(one.start)
        self.open.append((one, when))

        def arrive():
            if until is None:
                one.wait_recv()
            else:
                pl.when(until)(one.wait_recv)

        return arrive

    def finish(self):
        for one, when in self.open:
            if when is None:
                one.wait_send()
            else:
                pl.when(when)(one.wait_send)


def greet(seqs, count):
    s, c = lax.axis_index("seq"), lax.axis_index("ctx")
    barrier = pltpu.get_barrier_semaphore()
    for d in range(1, count):
        pl.semaphore_signal(barrier, inc=1, device_id=(s, lax.rem(c + d, count)), device_id_type=MESH)
    for d in range(1, seqs):
        pl.semaphore_signal(barrier, inc=1, device_id=(lax.rem(s + d, seqs), c), device_id_type=MESH)
    pl.semaphore_wait(barrier, count - 1 + seqs - 1)


def cube_steps(seqs, turn):
    bits = seqs.bit_length() - 1
    masks = []
    for j in range(bits):
        bit = lax.rem(j + turn, bits)
        mask = 0
        for k in range(bits):
            mask = mask + jnp.where(bit == k, 1 << k, 0)
        masks.append(mask)
    return masks


def across(s, mask):
    return s + mask * (1 - 2 * lax.rem(s // mask, 2))


def block_mates(rows):
    mates = 1
    while (mates * rows) % 16:
        mates *= 2
    return mates


def advance_kernel(
    seqs, count, chunks, heads,
    wq_ref, wk_ref, wv_ref, wo_ref, w1_ref, w2_ref, x_ref, code_ref, vec_ref,
    w_out, wo_out, wq_out, w1_out, w2_out, x_out, code_out, vec_out,
    k_out, v_out, q_out, of_out, lse_out, o_out,
    stage4, stage1, stage2, flat4, flat1, flat2, low4, lowq, low1, low2, share4,
    w_all, x_all, codes, vecs, wt, k_ext, v_ext, q_ext, top_ref, acc_ref, s_even, s_odd, o_send,
    send_sems, recv_sems, here_sems, o_send_sems, o_recv_sems,
):
    s, c = lax.axis_index("seq"), lax.axis_index("ctx")
    f32, bf16 = jnp.float32, jnp.bfloat16
    small_rows, model = wq_ref.shape
    tall_rows, wide = w2_ref.shape[0], w1_ref.shape[1]
    mates = block_mates(small_rows)
    blocks = count // mates
    b, i = c // mates, lax.rem(c, mates)
    turn = lax.rem(c, 2)
    repeat = count // chunks
    g, r = c // repeat, lax.rem(c, repeat)
    width = heads * DH
    rows = x_ref.shape[0]
    length = count * rows
    block_rows, block_tall = mates * small_rows, mates * tall_rows
    sender = Sender(send_sems, recv_sems)
    here = []

    def move(source, target):
        one = pltpu.make_async_copy(source, target, here_sems.at[len(here)])
        one.start()
        here.append(one)

    greet(seqs, count)

    def tokens_at(place, half):
        start = pl.multiple_of(place * rows + half * (rows // 2), rows // 2)
        return pl.ds(start, rows // 2)

    mate_waits = {}

    def to_mates(source, group, half, when=None):
        waits = mate_waits.setdefault(half, [])
        for d in range(1, repeat):
            other = (s, g * repeat + lax.rem(r + d, repeat))
            waits.append(sender.copy(source, x_all.at[tokens_at(group * repeat + r, half)], other, when, when))

    half_rows = [pl.ds(h * (rows // 2), rows // 2) for h in range(2)]
    above, below = jnp.minimum((g + 1) * repeat + r, count - 1), jnp.maximum((g - 1) * repeat + r, 0)

    def pass_on(t):
        waits = []
        low_group, high_group = jnp.maximum(g - t, 0), jnp.minimum(g + t, chunks - 1)
        low_at = [tokens_at(low_group * repeat + r, h) for h in range(2)]
        high_at = [tokens_at(high_group * repeat + r, h) for h in range(2)]
        for h in range(2):
            rise = x_ref.at[half_rows[h]] if t == 0 else x_all.at[low_at[h]]
            fall = x_ref.at[half_rows[h]] if t == 0 else x_all.at[high_at[h]]
            rising = (g - t >= 0) & (g + 1 < chunks)
            falling = (g + t < chunks) & (g >= 1)
            waits.append((
                sender.copy(rise, x_all.at[low_at[h]], (s, above), rising, g - 1 - t >= 0),
                sender.copy(fall, x_all.at[high_at[h]], (s, below), falling, g + 1 + t < chunks),
            ))
        return waits

    def received(t, waits):
        low_group, high_group = jnp.maximum(g - 1 - t, 0), jnp.minimum(g + 1 + t, chunks - 1)
        for h in range(2):
            waits[h][0]()
            to_mates(x_all.at[tokens_at(low_group * repeat + r, h)], low_group, h, g - 1 - t >= 0)
            waits[h][1]()
            to_mates(x_all.at[tokens_at(high_group * repeat + r, h)], high_group, h, g + 1 + t < chunks)

    x_waits = pass_on(0)
    for h in range(2):
        to_mates(x_ref.at[half_rows[h]], g, h)

    shards = []
    matrices = (wq_ref, wk_ref, wv_ref, wo_ref)
    for d in range(1, mates):
        other = (s, b * mates + lax.rem(i + d, mates))
        for m in range(4):
            shards.append(sender.copy(matrices[m], stage4.at[i, m], other))
        shards.append(sender.copy(w1_ref, stage1.at[i], other))
        shards.append(sender.copy(w2_ref, stage2.at[i], other))
    for m in range(4):
        stage4[i, m] = matrices[m][...]
    stage1[i] = w1_ref[...]
    stage2[i] = w2_ref[...]

    small_waits = []
    for d in range(1, count):
        other = (s, lax.rem(c + d, count))
        small_waits.append(sender.copy(code_ref, codes.at[c], other))
        small_waits.append(sender.copy(vec_ref, vecs.at[s * count + c], other))
    codes[c] = code_ref[...]
    vecs[s * count + c] = vec_ref[...]
    x_all[tokens_at(c, 0), :] = x_ref[0 : rows // 2, :]
    x_all[tokens_at(c, 1), :] = x_ref[rows // 2 :, :]

    for wait in shards:
        wait()
    for p in range(mates):
        for m in range(4):
            flat4[m, p * small_rows : (p + 1) * small_rows, :] = stage4[p, m]
        flat1[p * small_rows : (p + 1) * small_rows, :] = stage1[p]
        flat2[p * tall_rows : (p + 1) * tall_rows, :] = stage2[p]
    for k in range(chunks):
        part = slice(k * width, (k + 1) * width)
        pieces = [flat4[m, :, part] for m in range(3)]
        pieces.append(jnp.zeros((block_rows, w_out.shape[1] - 3 * width), f32))
        share4[k] = jnp.concatenate(pieces, axis=1).astype(bf16)

    def w_rows(seq, block, size):
        start = (seq * blocks + block) * block_rows
        return pl.ds(pl.multiple_of(start, block_rows), size * block_rows)

    columns = []
    for d in range(1, blocks):
        to = lax.rem(b + d, blocks) * mates + i
        columns.append(sender.copy(share4.at[to // repeat], w_all.at[w_rows(s, b, 1)], (s, to)))
    w_all[w_rows(s, b, 1), :] = share4[g]

    low4[...] = flat4[3].astype(bf16)
    lowq[...] = flat4[0].astype(bf16)
    low1[...] = flat1[...].astype(bf16)
    low2[...] = flat2[...].astype(bf16)

    half_wide, half_model = wide // 2, model // 2
    wide_at = pl.ds(pl.multiple_of(turn * half_wide, half_wide), half_wide)
    model_at = pl.ds(pl.multiple_of(turn * half_model, half_model), half_model)

    def tall_rows_at(seq, block, size):
        start = (seq * blocks + block) * block_tall
        return pl.ds(pl.multiple_of(start, block_tall), size * block_tall)

    def big(seq, block, size=1):
        return (
            w1_out.at[w_rows(seq, block, size), wide_at],
            w2_out.at[tall_rows_at(seq, block, size), model_at],
            wo_out.at[w_rows(seq, block, size), model_at],
            wq_out.at[w_rows(seq, block, size), model_at],
        )

    own = (low1.at[:, wide_at], low2.at[:, model_at], low4.at[:, model_at], lowq.at[:, model_at])
    for source, target in zip(own, big(s, b)):
        move(source, target)
    masks = cube_steps(seqs, turn)

    def families(seq):
        found = [(seq, -1)]
        for j, mask in enumerate(masks):
            found = found + [(across(one, mask), j) for one, _ in found]
        return found

    plane_waits = {}

    def spread(key, seq, step, block, sources, when):
        for j in range(step + 1, len(masks)):
            partner = (across(s, masks[j]), c)
            waits = plane_waits.setdefault((key, j), [])
            for source, target in zip(sources, big(seq, block)):
                waits.append((sender.copy(source, target, partner, when, when)))

    up, down = jnp.minimum((b + 1) * mates + i, count - 1), jnp.maximum((b - 1) * mates + i, 0)

    def line_send(t):
        waits = []
        low_block, high_block = jnp.maximum(b - t, 0), jnp.minimum(b + t, blocks - 1)
        rising = (b - t >= 0) & (b + 1 < blocks)
        falling = (b + t < blocks) & (b >= 1)
        rises = own if t == 0 else big(s, low_block)
        falls = own if t == 0 else big(s, high_block)
        for source, target in zip(rises, big(s, low_block)):
            waits.append(sender.copy(source, target, (s, up), rising, b - 1 - t >= 0))
        for source, target in zip(falls, big(s, high_block)):
            waits.append(sender.copy(source, target, (s, down), falling, b + 1 + t < blocks))
        return waits

    events = {("own",): (b, None)}
    for t in range(blocks - 1):
        events[(t, 0)] = (jnp.maximum(b - 1 - t, 0), b - 1 - t >= 0)
        events[(t, 1)] = (jnp.minimum(b + 1 + t, blocks - 1), b + 1 + t < blocks)

    spread(("own",), s, -1, b, own, None)
    line_waits = line_send(0)

    def token_service(t):
        nonlocal x_waits
        if t < chunks - 1:
            received(t, x_waits)
            if t + 1 < chunks - 1:
                x_waits = pass_on(t + 1)

    token_service(0)
    late = []

    def relay_event(key):
        block, when = events[key]
        queue = {j: list(plane_waits.get((key, j), [])) for j in range(len(masks))}
        for seq, j in families(s)[1:]:
            arriving, queue[j] = queue[j][: len(own)], queue[j][len(own) :]
            if j + 1 == len(masks):
                late.extend(arriving)
                continue
            for wait in arriving:
                wait()
            before = {k: len(plane_waits.get((key, k), [])) for k in range(j + 1, len(masks))}
            spread(key, seq, j, block, big(seq, block), when)
            for k in range(j + 1, len(masks)):
                queue[k] = queue[k] + plane_waits[(key, k)][before[k] :]

    def weight_service(t):
        nonlocal line_waits
        if t < blocks - 1:
            for wait in line_waits:
                wait()
            if t + 1 < blocks - 1:
                line_waits = line_send(t + 1)
            for way in range(2):
                block, when = events[(t, way)]
                spread((t, way), s, -1, block, big(s, block), when)
        if t == 0:
            relay_event(("own",))
        elif t - 1 < blocks - 1:
            relay_event((t - 1, 0))
            relay_event((t - 1, 1))

    for wait in columns:
        wait()
    columns = []
    for d in range(1, seqs):
        to = (lax.rem(s + d, seqs), c)
        slab = w_all.at[w_rows(s, 0, blocks)]
        columns.append(sender.copy(slab, slab, to))
    for wait in small_waits:
        wait()
    small_waits = []
    for d in range(1, seqs):
        to = (lax.rem(s + d, seqs), c)
        slab = vecs.at[pl.ds(s * count, count)]
        small_waits.append(sender.copy(slab, slab, to))

    top_ref[...] = jnp.full(top_ref.shape, FAR, f32)
    acc_ref[...] = jnp.zeros(acc_ref.shape, f32)
    k_ext[:, length:, :] = jnp.zeros((heads, PAD, k_ext.shape[2]), bf16)
    v_ext[:, 0:DH, length:] = jnp.zeros((heads, DH, PAD), bf16)
    v_ext[:, DH:, :] = jnp.ones((heads, 16, length + PAD), bf16)
    k_out[:, length:, :] = jnp.zeros((heads, PAD, DH), bf16)

    for wait in columns + small_waits:
        wait()
    move(w_all, w_out)
    move(vecs, vec_out)
    move(codes, code_out)
    wt[...] = w_all[...].astype(f32).T.astype(bf16)
    vec = vecs[:, 0, :]

    def bias_column(which):
        whole = unshard(vec, which * small_rows, small_rows)
        row = jnp.zeros((1, width), f32)
        for k in range(chunks):
            row = row + jnp.where(g == k, whole[:, k * width : (k + 1) * width], 0.0)
        extra = -width % LANES
        row = jnp.concatenate([row, jnp.zeros((1, extra), f32)], axis=1)
        return jnp.broadcast_to(row, (LANES, width + extra)).T[0:width, 0:1]

    bias_q, bias_v = bias_column(6), bias_column(7)

    def keys(chunk):
        at = pl.ds(pl.multiple_of(chunk * rows, rows), rows)
        x = x_all[at, :]
        k = nn(x, w_all[:, width : 2 * width]).astype(bf16)
        v = (nt(wt[2 * width : 3 * width, :], x) + bias_v).astype(bf16)
        v_out[:, at] = v
        code = codes[chunk].astype(f32)
        away = jnp.concatenate(
            [
                jnp.broadcast_to(code[:, j * LANES : (j + 1) * LANES], (LANES, LANES)).T[:, 0:DOCS]
                for j in range(rows // LANES)
            ],
            axis=0,
        )
        document = lax.broadcasted_iota(jnp.int32, (rows, DOCS), 1).astype(f32)
        away = jnp.where(away == 2.0 * document + 1.0, 0.0, 1.0).astype(bf16)
        for h in range(heads):
            one = k[:, h * DH : (h + 1) * DH]
            k_out[h, at, :] = one
            k_ext[h, at, :] = jnp.concatenate([one, one, away], axis=1)
            v_ext[h, 0:DH, at] = v[h * DH : (h + 1) * DH]

    def queries(group):
        chunk = group * repeat + r
        x = x_all[pl.ds(pl.multiple_of(chunk * rows, rows), rows), :]
        to = pl.ds(pl.multiple_of(group * rows, rows), rows)
        q = (nt(wt[0:width, :], x) + bias_q).astype(bf16)
        q_out[:, to] = q
        scaled = q.astype(f32) * (DH**-0.5 * LOG2E)
        high = scaled.astype(bf16)
        rest = (scaled - high.astype(f32)).astype(bf16)
        wanted = (codes[chunk] | 1).astype(f32)
        document = lax.broadcasted_iota(jnp.int32, (DOCS, rows), 0).astype(f32)
        away = jnp.where(wanted == 2.0 * document + 1.0, FAR, 0.0).astype(bf16)
        for h in range(heads):
            part = slice(h * DH, (h + 1) * DH)
            q_ext[h, :, to] = jnp.concatenate([high[part], rest[part], away], axis=0)

    def attend_to(group, first, last):
        at = pl.ds(pl.multiple_of(group * rows, rows), rows)

        def scores(slot, key_at):
            for h in range(heads):
                slot[h] = nn(k_ext[h, pl.ds(key_at, HALF), :], q_ext[h, :, at])

        def soften(slot, key_at):
            for h in range(heads):
                top = top_ref[group, h, 0:1, :]
                sc = slot[h]
                new = jnp.maximum(top, jnp.max(sc, axis=0, keepdims=True))
                p = jnp.exp2(sc - new).astype(bf16)
                acc_ref[group, h] = acc_ref[group, h] * jnp.exp2(top - new) + nn(
                    v_ext[h, :, pl.ds(key_at, HALF)], p
                )
                top_ref[group, h, 0:1, :] = new

        def step(j, carry):
            one = pl.multiple_of(j * BK, BK)
            two = pl.multiple_of(one + HALF, HALF)
            scores(s_odd, two)
            soften(s_even, one)
            scores(s_even, pl.multiple_of(one + BK, BK))
            soften(s_odd, two)
            return carry

        per = rows // BK
        scores(s_even, pl.multiple_of(first * rows, rows))
        lax.fori_loop(first * per, last * per, step, 0)

    def conclude(group):
        at = pl.ds(pl.multiple_of(group * rows, rows), rows)
        for h in range(heads):
            part = slice(h * DH, (h + 1) * DH)
            low = acc_ref[group, h, DH : DH + 1, :]
            out = acc_ref[group, h, 0:DH, :] / low
            of_out[part, at] = out
            o_send[group, part, :] = out.astype(bf16)
            lse_out[h : h + 1, at] = top_ref[group, h, 0:1, :] + jnp.log2(low)

        @pl.when(group != g)
        def _():
            o_copy(group).start()

    def o_copy(group):
        return pltpu.make_async_remote_copy(
            src_ref=o_send.at[group],
            dst_ref=o_out.at[g],
            send_sem=o_send_sems.at[group],
            recv_sem=o_recv_sems.at[g],
            device_id=(s, group * repeat + r),
            device_id_type=MESH,
        )

    def arrive(group, low, high):
        def make(j, carry):
            keys(group * repeat + j)
            return carry

        lax.fori_loop(0, repeat, make, 0)
        queries(group)
        whole = high - low + 1 == chunks

        def each(other, carry):
            same = other == group
            attend_to(
                other,
                jnp.where(same, low, group) * repeat,
                (jnp.where(same, high, group) + 1) * repeat,
            )

            @pl.when(whole)
            def _():
                conclude(other)

            return carry

        lax.fori_loop(low, high + 1, each, 0)

    def mates_here():
        for h in range(2):
            for wait in mate_waits[h]:
                wait()
            mate_waits[h] = []

    mates_here()
    arrive(g, g, g)
    weight_service(0)
    for t in range(chunks - 1):
        if t == chunks - 2:
            move(x_all, x_out)
        low, high = g - 1 - t, g + 1 + t
        has_low, has_high = low >= 0, high < chunks

        @pl.when(has_low)
        def _():
            arrive(low, low, jnp.minimum(g + t, chunks - 1))

        @pl.when(has_high & (low < 0))
        def _():
            arrive(high, 0, high)

        token_service(t + 1)
        weight_service(t + 1)

        @pl.when(has_high & has_low)
        def _():
            arrive(high, low, high)

        mates_here()
    for t in range(chunks, blocks + 1):
        weight_service(t)
    for wait in late:
        wait()
    own_out = pltpu.make_async_copy(o_send.at[g], o_out.at[g], here_sems.at[9])
    own_out.start()
    for one in here:
        one.wait()
    sibling = (s, c + 1 - 2 * turn)
    last_waits = []
    for piece in (
        w1_out.at[:, wide_at], w2_out.at[:, model_at], wo_out.at[:, model_at], wq_out.at[:, model_at],
    ):
        last_waits.append(sender.copy(piece, piece, sibling))
    for wait in last_waits:
        wait()
    for d in range(1, chunks):
        group = lax.rem(g + d, chunks)
        pltpu.make_async_remote_copy(
            src_ref=o_send.at[g],
            dst_ref=o_out.at[group],
            send_sem=o_send_sems.at[g],
            recv_sem=o_recv_sems.at[group],
            device_id=(s, group * repeat + r),
            device_id_type=MESH,
        ).wait_recv()
        o_copy(group).wait_send()
    own_out.wait()
    sender.finish()


def advance(wq, wk, wv, wo, w1, w2, x, code, vec, chunks, heads):
    seqs, count = lax.axis_size("seq"), lax.axis_size("ctx")
    small_rows, model = wq.shape
    tall_rows, wide = w2.shape[0], w1.shape[1]
    rows = x.shape[0]
    mates = block_mates(small_rows)
    blocks, repeat = count // mates, count // chunks
    semaphores = (
        6 * (mates - 1) + 2 * (count - 1) + 2 * (seqs - 1) + 9 * (blocks - 1)
        + 4 * (seqs - 1) * (2 * blocks - 1) + 4 + 4 * (chunks - 1) + 2 * (2 * chunks - 1) * (repeat - 1)
    )
    devices = seqs * count
    width = heads * DH
    length, mine = count * rows, chunks * rows
    padded = -(-3 * width // LANES) * LANES
    shape = jax.ShapeDtypeStruct
    f32, bf16 = jnp.float32, jnp.bfloat16
    vmem, far = pl.BlockSpec(memory_space=pltpu.VMEM), pl.BlockSpec(memory_space=pl.ANY)
    block_rows, block_tall = mates * small_rows, mates * tall_rows
    dma = pltpu.SemaphoreType.DMA
    return pl.pallas_call(
        partial(advance_kernel, seqs, count, chunks, heads),
        out_shape=(
            shape((model, padded), bf16),
            shape((model, model), bf16),
            shape((model, model), bf16),
            shape((model, wide), bf16),
            shape((tall_rows * devices, model), bf16),
            shape((length, model), bf16),
            shape((count, 1, rows), jnp.int32),
            shape((devices, 1, vec.shape[1]), f32),
            shape((heads, length + PAD, DH), bf16),
            shape((width, length), bf16),
            shape((width, mine), bf16),
            shape((width, mine), f32),
            shape((8, mine), f32),
            shape((chunks, width, rows), bf16),
        ),
        in_specs=[vmem] * 9,
        out_specs=(far,) * 8 + (vmem,) * 5 + (far,),
        scratch_shapes=[
            pltpu.VMEM((mates, 4, small_rows, model), f32),
            pltpu.VMEM((mates, small_rows, wide), f32),
            pltpu.VMEM((mates, tall_rows, model), f32),
            pltpu.VMEM((4, block_rows, model), f32),
            pltpu.VMEM((block_rows, wide), f32),
            pltpu.VMEM((block_tall, model), f32),
            pltpu.VMEM((block_rows, model), bf16),
            pltpu.VMEM((block_rows, model), bf16),
            pltpu.VMEM((block_rows, wide), bf16),
            pltpu.VMEM((block_tall, model), bf16),
            pltpu.VMEM((chunks, block_rows, padded), bf16),
            pltpu.VMEM((model, padded), bf16),
            pltpu.VMEM((length, model), bf16),
            pltpu.VMEM((count, 1, rows), jnp.int32),
            pltpu.VMEM((devices, 1, vec.shape[1]), f32),
            pltpu.VMEM((padded, model), bf16),
            pltpu.VMEM((heads, length + PAD, 2 * DH + DOCS), bf16),
            pltpu.VMEM((heads, DH + 16, length + PAD), bf16),
            pltpu.VMEM((heads, 2 * DH + DOCS, mine), bf16),
            pltpu.VMEM((chunks, heads, 8, rows), f32),
            pltpu.VMEM((chunks, heads, DH + 16, rows), f32),
            pltpu.VMEM((heads, HALF, rows), f32),
            pltpu.VMEM((heads, HALF, rows), f32),
            pltpu.VMEM((chunks, width, rows), bf16),
            dma((semaphores,)),
            dma((semaphores,)),
            dma((10,)),
            dma((chunks,)),
            dma((chunks,)),
        ],
        compiler_params=pltpu.CompilerParams(
            vmem_limit_bytes=VMEM_LIMIT, collective_id=1, has_side_effects=True
        ),
        name="advance",
    )(wq, wk, wv, wo, w1, w2, x, code, vec)


def added(*parts):
    sum_of = parts[0].astype(jnp.float32)
    for part in parts[1:]:
        sum_of = sum_of + part.astype(jnp.float32)
    return sum_of


class Line:
    def __init__(self, sender, place, size, device, pieces, landing):
        self.sender, self.place, self.size, self.device = sender, place, size, device
        self.pieces, self.landing = pieces, landing
        self.waits = None

    def send(self, t):
        self.waits = []
        for way in range(2):
            rank = self.place if way == 0 else self.size - 1 - self.place
            mirror = (lambda d: d) if way == 0 else (lambda d: self.size - 1 - d)
            goal = jnp.clip(mirror(self.size - 1 - t + rank), 0, self.size - 1)
            sends = rank <= t
            receives = (rank >= 1) & (rank - 1 <= t)
            to = jnp.clip(self.place + (1 - 2 * way), 0, self.size - 1)
            waits = []
            for source, target in zip(self.pieces(goal), self.landing(way, t)):
                waits.append(self.sender.copy(source, target, self.device(to), sends, receives))
            self.waits.append((receives, mirror, rank, waits))

    def receive(self, t):
        for way, (receives, mirror, rank, waits) in enumerate(self.waits):
            goal = jnp.clip(mirror(self.size - 2 - t + rank), 0, self.size - 1)
            pieces, landing = self.pieces(goal), self.landing(way, t)
            for wait, piece, arrived in zip(waits, pieces, landing):
                wait()

                @pl.when(receives)
                def _():
                    piece[...] = added(piece[...], arrived[...]).astype(piece.dtype)


def group_order(chunks):
    table = []
    for g in range(chunks):
        steps = [(chunks - 1 + g - d if d > g else chunks - 1 - g + d, d < g, d) for d in range(chunks) if d != g]
        table.append([d for _, _, d in sorted(steps)] + [g])
    return table


def retreat_kernel(
    seqs, count, chunks, heads,
    do_ref, x_ref, w_ref, wq_ref, k_ref, v_ref, q_ref, o_ref, lse_ref, code_ref,
    dwo_ref, dw1_ref, dw2_ref, dsmall_ref, db1_ref,
    dx_out, dw_out, dwo_out, dw1_out, dw2_out, dsmall_out, db1_out, in1, in2, in4, dx_in,
    do_in, q_ext, do_ext, dq, o_slot, k_slot, v_slot, x_slot, kt_ext, v_ext, dkv, dw, db,
    s_even, s_odd, g_even, g_odd, dx_send, dq_send, dq_in, w_full, wt,
    dx_sum, dx_line, sum1, sum2, sum4, part1, part2, cube1, cube2, cube4,
    line1, line2, line4, last1, last2, last4, w_mine, w_seq, w_block, w_mates,
    small_in, b1_in, b_in, vec_seq, bias_seq,
    send_sems, recv_sems, here_sems, fetch_sems, part_sems, own_sems, mate_send, mate_recv, dq_send_sems, dq_recv_sems,
):
    s, c = lax.axis_index("seq"), lax.axis_index("ctx")
    f32, bf16 = jnp.float32, jnp.bfloat16
    rows, model = dx_out.shape
    wide = dw1_ref.shape[1]
    repeat = count // chunks
    mates = w_mates.shape[0]
    blocks = count // mates
    block_rows, block_tall = dwo_out.shape[0], dw2_out.shape[0]
    width = heads * DH
    b, i = c // mates, lax.rem(c, mates)
    g, r = c // repeat, lax.rem(c, repeat)
    turn = lax.rem(c, 2)
    half_wide, half_model = wide // 2, model // 2
    slab_rows, slab_tall = blocks * block_rows, blocks * block_tall
    sender = Sender(send_sems, recv_sems)
    here = []

    def move(source, target):
        one = pltpu.make_async_copy(source, target, here_sems.at[len(here)])
        one.start()
        here.append(one)
        return one

    table = group_order(chunks)

    def group_at(index):
        found = table[chunks - 1][index]
        for k in range(chunks - 1):
            found = jnp.where(g == k, table[k][index], found)
        return found

    def fetch(chunk, slot):
        at = pl.ds(pl.multiple_of(chunk * rows, rows), rows)
        sems = fetch_sems.at[slot]
        return (
            pltpu.make_async_copy(k_ref.at[:, at, :], k_slot.at[slot], sems.at[0]),
            pltpu.make_async_copy(v_ref.at[:, at], v_slot.at[slot], sems.at[1]),
            pltpu.make_async_copy(x_ref.at[at], x_slot.at[slot], sems.at[2]),
        )

    for one in fetch(group_at(0) * repeat, 0):
        one.start()
    greet(seqs, count)

    do_waits = {}
    for d in range(1, chunks):
        to = lax.rem(g + d, chunks)
        do_waits[chunks - d] = sender.copy(do_ref.at[to], do_in.at[g], (s, to * repeat + r))
    own_do = move(do_ref.at[g], do_in.at[g])

    sibling = (s, c + 1 - 2 * turn)

    def column_half(which):
        wide_at = pl.ds(pl.multiple_of(which * half_wide, half_wide), half_wide)
        model_at = pl.ds(pl.multiple_of(which * half_model, half_model), half_model)
        return dw1_ref.at[:, wide_at], dw2_ref.at[:, model_at], dwo_ref.at[:, model_at]

    half_waits = [
        sender.copy(source, target, sibling)
        for source, target in zip(column_half(1 - turn), (in1, in2, in4))
    ]
    for source, target in zip(column_half(turn), (sum1, sum2, sum4)):
        move(source, target)
    vec_waits = []
    for d in range(1, count):
        to = (s, lax.rem(c + d, count))
        for source, target in ((dsmall_ref, small_in), (db1_ref, b1_in)):
            vec_waits.append(sender.copy(source, target.at[c], to))
    small_in[c] = dsmall_ref[...]
    b1_in[c] = db1_ref[...]

    wt[...] = w_ref[...].astype(f32).T.astype(bf16)
    dw[...] = jnp.zeros(dw.shape, f32)
    db[...] = jnp.zeros(db.shape, f32)
    dq[...] = jnp.zeros(dq.shape, f32)
    kt_ext[:, 2 * DH : 2 * DH + 16, :] = jnp.ones((heads, 16, rows), bf16)
    v_ext[:, DH:, :] = jnp.ones((heads, 16, rows), bf16)
    one_rows = jnp.ones((8, rows), bf16)

    def queries(group):
        at = pl.ds(pl.multiple_of(group * rows, rows), rows)
        load = pltpu.make_async_copy(o_ref.at[:, at], o_slot, own_sems.at[0])
        load.start()
        load.wait()
        wanted = (code_ref[group * repeat + r] | 1).astype(f32)
        document = lax.broadcasted_iota(jnp.int32, (DOCS, rows), 0).astype(f32)
        away = jnp.where(wanted == 2.0 * document + 1.0, FAR, 0.0)
        for h in range(heads):
            part = slice(h * DH, (h + 1) * DH)
            scaled = q_ref[part, at].astype(f32) * (DH**-0.5 * LOG2E)
            high = scaled.astype(bf16).astype(f32)
            extra = three_parts(-lse_ref[h : h + 1, at])
            full = jnp.concatenate([high, scaled - high, extra, away], axis=0)
            q_ext[h, at, :] = full.T.astype(bf16)
            grad = do_in[group, part, :].astype(f32)
            delta = jnp.sum(grad * o_slot[part, :], axis=0, keepdims=True)
            do_ext[h, at, :] = jnp.concatenate([grad, three_parts(-delta)], axis=0).T.astype(bf16)

    for one in here:
        one.wait()
    queries(g)

    for wait in half_waits:
        wait()
    loads = []
    for target, arrived, part, kind in ((sum1, in1, part1, 0), (sum2, in2, part2, 1), (sum4, in4, part2, 1)):
        size = part.shape[1]
        for k in range(target.shape[0] // size):
            loads.append((target, arrived, part, kind, k * size, size))
    used_slots = [0, 0]
    copies = []
    for target, arrived, part, kind, at, size in loads:
        slot = used_slots[kind] % 2
        used_slots[kind] += 1
        copies.append((
            pltpu.make_async_copy(arrived.at[pl.ds(at, size)], part.at[slot], part_sems.at[kind, slot]), slot
        ))
    copies[0][0].start()
    for n, (target, arrived, part, kind, at, size) in enumerate(loads):
        if n + 1 < len(loads):
            copies[n + 1][0].start()
        copies[n][0].wait()
        rows_at = slice(at, at + size)
        target[rows_at] = added(target[rows_at], part[copies[n][1]]).astype(bf16)

    def slab(seq):
        at = pl.ds(pl.multiple_of(seq * slab_rows, slab_rows), slab_rows)
        tall = pl.ds(pl.multiple_of(seq * slab_tall, slab_tall), slab_tall)
        return sum1.at[at], sum2.at[tall], sum4.at[at]

    masks = cube_steps(seqs, turn)

    def family(seq, rest):
        found = [seq]
        for mask in rest:
            found = found + [across(one, mask) for one in found]
        return found

    cube_waits, used = [], 0

    def cube_send(j):
        nonlocal used
        partner = across(s, masks[j])
        cube_waits.clear()
        mine = family(s, masks[j + 1 :])
        for k, seq in enumerate(family(partner, masks[j + 1 :])):
            landing = cube1.at[used + k], cube2.at[used + k], cube4.at[used + k]
            waits = [
                sender.copy(source, target, (partner, c)) for source, target in zip(slab(seq), landing)
            ]
            cube_waits.append((mine[k], landing, waits))
        used += len(cube_waits)

    def cube_receive():
        for seq, landing, waits in cube_waits:
            for wait, target, arrived in zip(waits, slab(seq), landing):
                wait()
                target[...] = added(target[...], arrived[...]).astype(bf16)

    cube_send(0)

    def block_slab(goal):
        row = s * slab_rows + goal * block_rows
        tall = s * slab_tall + goal * block_tall
        at = pl.ds(pl.multiple_of(row, block_rows), block_rows)
        tall_at = pl.ds(pl.multiple_of(tall, block_tall), block_tall)
        return sum1.at[at], sum2.at[tall_at], sum4.at[at]

    weight_line = Line(
        sender, b, blocks, lambda to: (s, to * mates + i),
        block_slab, lambda way, t: (line1.at[way, t], line2.at[way, t], line4.at[way, t]),
    )
    half_rows = rows // 2
    token_lines = []
    for h in range(2):
        at = pl.ds(h * half_rows, half_rows)
        token_lines.append(
            Line(
                sender, g, chunks, lambda to: (s, to * repeat + r),
                lambda goal, at=at: (dx_sum.at[goal, at],),
                lambda way, t, at=at: (dx_line.at[way, t, at],),
            )
        )

    for d in range(1, chunks):
        do_waits[d]()
        queries(lax.rem(g + d, chunks))

    for wait in vec_waits:
        wait()
    vec_waits = []
    small, tall = small_in[0], b1_in[0]
    for k in range(1, count):
        small = small + small_in[k]
        tall = tall + b1_in[k]
    vec_seq[s, 0:8, 0:model] = small
    vec_seq[s, 0:1, model:] = tall
    vec_seq[s, 1:8, model:] = jnp.zeros((7, wide), f32)
    for d in range(1, seqs):
        vec_waits.append(sender.copy(vec_seq.at[s], vec_seq.at[s], (lax.rem(s + d, seqs), c)))

    weight_steps = blocks - 1
    pending = []

    def cube_turn(j):
        cube_receive()
        if j + 1 < len(masks):
            cube_send(j + 1)
        elif weight_steps:
            weight_line.send(0)

    def line_turn(t):
        weight_line.receive(t)
        if t + 1 < weight_steps:
            weight_line.send(t + 1)

    pending += [partial(cube_turn, j) for j in range(len(masks))]
    pending += [partial(line_turn, t) for t in range(weight_steps)]

    def scores(s_slot, g_slot, group, half):
        at = pl.ds(pl.multiple_of(group * rows, rows), rows)
        key = pl.ds(half * HALF, HALF)
        for h in range(heads):
            s_slot[h] = nn(q_ext[h, at, :], kt_ext[h, :, key])
            g_slot[h] = nn(do_ext[h, at, :], v_ext[h, :, key])

    def absorb(s_slot, g_slot, slot, group, half):
        at = pl.ds(pl.multiple_of(group * rows, rows), rows)
        key = pl.ds(half * HALF, HALF)
        for h in range(heads):
            part = slice(h * DH, (h + 1) * DH)
            p = jnp.exp2(s_slot[h])
            ds = (p * g_slot[h]).astype(bf16)
            dkv[width + h * DH : width + (h + 1) * DH, key] += nn(do_in[group, part, :], p.astype(bf16))
            dkv[part, key] += nn(q_ref[part, at], ds)
            dq[h, at, :] += nn(ds, k_slot[slot, h, key, :])

    def next_group(p):
        return lax.rem(g + p, chunks)

    def one_chunk(chunk, following, slot, conclude):
        for one in fetch(chunk, slot):
            one.wait()
        if following is not None:
            for one in fetch(following, 1 - slot):
                one.start()
        document = lax.broadcasted_iota(jnp.int32, (DOCS, rows), 0).astype(f32)
        away = jnp.where(code_ref[chunk].astype(f32) == 2.0 * document + 1.0, 0.0, 1.0).astype(bf16)
        for h in range(heads):
            kt = flip(k_slot[slot, h])
            kt_ext[h, 0:DH, :] = kt
            kt_ext[h, DH : 2 * DH, :] = kt
            kt_ext[h, 2 * DH + 16 :, :] = away
            v_ext[h, 0:DH, :] = v_slot[slot, h * DH : (h + 1) * DH, :]
        dkv[...] = jnp.zeros(dkv.shape, f32)
        scores(s_even, g_even, next_group(1), 0)

        def turn_of(p, carry):
            group = next_group(p)
            scores(s_odd, g_odd, group, 1)
            absorb(s_even, g_even, slot, group, 0)
            scores(s_even, g_even, next_group(p + 1), 0)
            absorb(s_odd, g_odd, slot, group, 1)
            if conclude is not None:
                conclude(group)
            return carry

        lax.fori_loop(1, chunks + 1, turn_of, 0)

    def mate_copy(group, to, slot):
        return pltpu.make_async_remote_copy(
            src_ref=dx_send.at[slot],
            dst_ref=dx_in.at[slot, group],
            send_sem=mate_send.at[slot],
            recv_sem=mate_recv.at[slot, group],
            device_id=(s, g * repeat + to),
            device_id_type=MESH,
        )

    def keep(group, j, slot):
        dk = (dkv[0:width, :] * DH**-0.5).astype(bf16)
        dv = dkv[width:, :].astype(bf16)
        both = jnp.concatenate([dk, dv], axis=0)
        dx = tn(both, wt[width : 3 * width, :]).astype(bf16)
        dw[width : 3 * width, :] += nn(both, x_slot[slot])
        db[0:8, width:] += nt(one_rows, dv)

        @pl.when(j == r)
        def _():
            dx_sum[group] = dx

        @pl.when(j != r)
        def _():
            to = lax.rem(j - r + repeat, repeat) - 1
            dx_send[to] = dx
            mate_copy(group, j, to).start()

    spare = chunks * repeat % 2

    def conclude(group):
        at = pl.ds(pl.multiple_of(group * rows, rows), rows)
        from_x = pl.ds(pl.multiple_of((group * repeat + r) * rows, rows), rows)
        load = pltpu.make_async_copy(x_ref.at[from_x], x_slot.at[spare], own_sems.at[1])
        load.start()
        grad = jnp.concatenate([dq[h, at, :] for h in range(heads)], axis=1) * DH**-0.5
        dq_send[group] = grad.T.astype(bf16)

        @pl.when(group != g)
        def _():
            dq_copy(group).start()

        low = grad.astype(bf16)
        db[0:8, 0:width] += nn(one_rows, low)
        load.wait()
        dw[0:width, :] += tn(low, x_slot[spare])

    def dq_copy(group):
        return pltpu.make_async_remote_copy(
            src_ref=dq_send.at[group],
            dst_ref=dq_in.at[g],
            send_sem=dq_send_sems.at[group],
            recv_sem=dq_recv_sems.at[g],
            device_id=(s, group * repeat + r),
            device_id_type=MESH,
        )

    def gather_mates(group):
        for d in range(1, repeat):
            mate_copy(group, lax.rem(r + d, repeat), d - 1).wait()
        loads = [
            pltpu.make_async_copy(dx_in.at[d, group], dx_send.at[d], mate_send.at[d]) for d in range(repeat - 1)
        ]
        for load in loads:
            load.start()
        for load in loads:
            load.wait()
        terms = [dx_send[d] for d in range(repeat - 1)]
        dx_sum[group] = added(dx_sum[group], *terms).astype(bf16)

    for index in range(chunks):
        group = group_at(index)
        for j in range(repeat):
            position = index * repeat + j
            slot = position % 2
            final = position + 1 == chunks * repeat
            if j + 1 < repeat:
                following = group * repeat + j + 1
            elif not final:
                following = group_at(index + 1) * repeat
            else:
                following = None
            one_chunk(group * repeat + j, following, slot, conclude if final else None)
            keep(group, j, slot)
            if j == 0 and index == chunks - 1 and pending:
                pending.pop(0)()
        gather_mates(group)
        if index >= 1:
            for line in token_lines:
                line.receive(index - 1)
        if index < chunks - 1:
            for line in token_lines:
                line.send(index)
            if pending:
                pending.pop(0)()

    w_full[...] = dw[...].T.astype(bf16)
    w_waits = []
    for d in range(1, seqs):
        to = lax.rem(s + d, seqs)
        source = w_full.at[pl.ds(pl.multiple_of(to * slab_rows, slab_rows), slab_rows)]
        w_waits.append(sender.copy(source, w_seq.at[d - 1], (to, c)))
    b_waits = []
    b_in[c] = db[0:1, :]
    for d in range(1, count):
        b_waits.append(sender.copy(b_in.at[c], b_in.at[c], (s, lax.rem(c + d, count))))
    while pending:
        pending.pop(0)()
    last_waits = []
    for source, target in zip(block_slab(b), (last1, last2, last4)):
        target[i] = source[...]
        for d in range(1, mates):
            to = (s, b * mates + lax.rem(i + d, mates))
            last_waits.append(sender.copy(source, target.at[i], to))
    for wait in b_waits:
        wait()
    b_waits = []
    pair = []
    for k in range(chunks):
        one = b_in[k * repeat]
        for d in range(1, repeat):
            one = one + b_in[k * repeat + d]
        pair.append(one)
    for m in range(2):
        joined = jnp.concatenate([one[:, m * width : (m + 1) * width] for one in pair], axis=1)
        bias_seq[s, m : m + 1, :] = joined
    bias_seq[s, 2:8, :] = jnp.zeros((6, model), f32)
    for d in range(1, seqs):
        b_waits.append(sender.copy(bias_seq.at[s], bias_seq.at[s], (lax.rem(s + d, seqs), c)))
    for wait in w_waits:
        wait()
    w_mine[...] = added(
        w_full[pl.ds(pl.multiple_of(s * slab_rows, slab_rows), slab_rows), :],
        *[w_seq[d] for d in range(seqs - 1)],
    ).astype(bf16)
    w_waits = []
    for d in range(1, blocks):
        to = lax.rem(b + d, blocks)
        source = w_mine.at[pl.ds(pl.multiple_of(to * block_rows, block_rows), block_rows)]
        w_waits.append(sender.copy(source, w_block.at[b], (s, to * mates + i)))
    w_block[b] = w_mine[pl.ds(pl.multiple_of(b * block_rows, block_rows), block_rows), :]

    dq_in[g] = dq_send[g]
    for d in range(1, chunks):
        group = lax.rem(g + d, chunks)
        pltpu.make_async_remote_copy(
            src_ref=dq_send.at[g],
            dst_ref=dq_in.at[group],
            send_sem=dq_send_sems.at[g],
            recv_sem=dq_recv_sems.at[group],
            device_id=(s, group * repeat + r),
            device_id_type=MESH,
        ).wait_recv()
        dq_copy(group).wait_send()
    part = nn(wq_ref[...], dq_in[...].reshape(chunks * width, rows))
    dx_out[...] = dx_sum[g].astype(f32) + part.T

    for wait in w_waits:
        wait()
    w_waits = []
    w_mates[i] = w_block[...]
    for d in range(1, mates):
        to = (s, b * mates + lax.rem(i + d, mates))
        w_waits.append(sender.copy(w_block, w_mates.at[i], to))
    for wait in vec_waits + b_waits + last_waits:
        wait()
    for target, source in ((dw1_out, last1), (dw2_out, last2), (dwo_out, last4)):
        size = target.shape[1] // 2
        for which in range(2):
            target[:, which * size : (which + 1) * size] = added(
                *[source[k] for k in range(which, mates, 2)]
            )
    vec, bias = vec_seq[0], bias_seq[0]
    for d in range(1, seqs):
        vec = vec + vec_seq[d]
        bias = bias + bias_seq[d]
    dsmall_out[0:6, :] = vec[0:6, 0:model]
    dsmall_out[6:8, :] = bias[0:2]
    db1_out[...] = vec[:, model:]
    for wait in w_waits:
        wait()
    for k in range(chunks):
        terms = [
            w_mates[p, q]
            for p in range(mates)
            for q in range(blocks)
            if (q * mates + p) // repeat == k
        ]
        dw_out[k] = added(*terms)
    sender.finish()


def retreat(do, x, w, wq, k, v, q, o, lse, codes, dwo, dw1, dw2, dsmall, db1, heads):
    seqs, count = lax.axis_size("seq"), lax.axis_size("ctx")
    chunks, width, rows = do.shape
    model = x.shape[1]
    wide, tall = dw1.shape[1], dw2.shape[0]
    devices = seqs * count
    mates = block_mates(model // devices)
    blocks, repeat = count // mates, count // chunks
    block_rows, block_tall = mates * (model // devices), mates * (tall // devices)
    slab_rows, slab_tall = blocks * block_rows, blocks * block_tall
    padded = w.shape[1]
    mine = chunks * rows
    semaphores = (
        (chunks - 1) + 3 + 2 * (count - 1) + (seqs - 1) + 3 * (seqs - 1) + 6 * (blocks - 1)
        + 4 * (chunks - 1) + (seqs - 1) + (count - 1) + 3 * (mates - 1) + (seqs - 1) + (blocks - 1) + (mates - 1)
    )
    shape = jax.ShapeDtypeStruct
    f32, bf16 = jnp.float32, jnp.bfloat16
    vmem, far = pl.BlockSpec(memory_space=pltpu.VMEM), pl.BlockSpec(memory_space=pl.ANY)
    half_wide, half_model = wide // 2, model // 2
    triple = lambda lead, a, t: [
        pltpu.VMEM(lead + (a, half_wide), bf16),
        pltpu.VMEM(lead + (t, half_model), bf16),
        pltpu.VMEM(lead + (a, half_model), bf16),
    ]
    dma = pltpu.SemaphoreType.DMA
    return pl.pallas_call(
        partial(retreat_kernel, seqs, count, chunks, heads),
        out_shape=(
            shape((rows, model), f32),
            shape((chunks, block_rows, padded), f32),
            shape((block_rows, model), f32),
            shape((block_rows, wide), f32),
            shape((block_tall, model), f32),
            shape((8, model), f32),
            shape((8, wide), f32),
            shape((model, half_wide), bf16),
            shape((tall, half_model), bf16),
            shape((model, half_model), bf16),
            shape((repeat - 1, chunks, rows, model), bf16),
        ),
        in_specs=[far, far, vmem, vmem, far, far, vmem, far, vmem, vmem, far, far, far, vmem, vmem],
        out_specs=(vmem,) * 7 + (far,) * 4,
        scratch_shapes=[
            pltpu.VMEM((chunks, width, rows), bf16),
            pltpu.VMEM((heads, mine, 2 * DH + 16 + DOCS), bf16),
            pltpu.VMEM((heads, mine, DH + 16), bf16),
            pltpu.VMEM((heads, mine, DH), f32),
            pltpu.VMEM((width, rows), f32),
            pltpu.VMEM((2, heads, rows, DH), bf16),
            pltpu.VMEM((2, width, rows), bf16),
            pltpu.VMEM((2, rows, model), bf16),
            pltpu.VMEM((heads, 2 * DH + 16 + DOCS, rows), bf16),
            pltpu.VMEM((heads, DH + 16, rows), bf16),
            pltpu.VMEM((2 * width, rows), f32),
            pltpu.VMEM((padded, model), f32),
            pltpu.VMEM((8, 2 * width), f32),
        ]
        + [pltpu.VMEM((heads, rows, HALF), f32)] * 4
        + [
            pltpu.VMEM((repeat - 1, rows, model), bf16),
            pltpu.VMEM((chunks, width, rows), bf16),
            pltpu.VMEM((chunks, width, rows), bf16),
            pltpu.VMEM((model, padded), bf16),
            pltpu.VMEM((padded, model), bf16),
            pltpu.VMEM((chunks, rows, model), bf16),
            pltpu.VMEM((2, chunks - 1, rows, model), bf16),
        ]
        + triple((), model, tall)
        + [pltpu.VMEM((2, model // 8, half_wide), bf16), pltpu.VMEM((2, model // 2, half_model), bf16)]
        + triple((seqs - 1,), slab_rows, slab_tall)
        + triple((2, blocks - 1), block_rows, block_tall)
        + triple((mates,), block_rows, block_tall)
        + [
            pltpu.VMEM((slab_rows, padded), bf16),
            pltpu.VMEM((seqs - 1, slab_rows, padded), bf16),
            pltpu.VMEM((blocks, block_rows, padded), bf16),
            pltpu.VMEM((mates, blocks, block_rows, padded), bf16),
            pltpu.VMEM((count, 8, model), f32),
            pltpu.VMEM((count, 1, wide), f32),
            pltpu.VMEM((count, 1, 2 * width), f32),
            pltpu.VMEM((seqs, 8, model + wide), f32),
            pltpu.VMEM((seqs, 8, model), f32),
            dma((semaphores,)),
            dma((semaphores,)),
            dma((8,)),
            dma((2, 3)),
            dma((2, 2)),
            dma((2,)),
            dma((repeat - 1,)),
            dma((repeat - 1, chunks)),
            dma((chunks,)),
            dma((chunks,)),
        ],
        compiler_params=pltpu.CompilerParams(
            vmem_limit_bytes=63 * 1024 * 1024, collective_id=2, has_side_effects=True
        ),
        name="retreat",
    )(do, x, w, wq, k, v, q, o, lse, codes, dwo, dw1, dw2, dsmall, db1)


def pick(values, size, device):
    wide = values.shape[1]
    row = lax.broadcasted_iota(jnp.int32, (wide, size), 0)
    column = lax.broadcasted_iota(jnp.int32, (wide, size), 1)
    chosen = (row == column + device * size).astype(jnp.bfloat16)
    high = values.astype(jnp.bfloat16)
    rest = values - high.astype(jnp.float32)
    middle_part = rest.astype(jnp.bfloat16)
    low = (rest - middle_part.astype(jnp.float32)).astype(jnp.bfloat16)
    return nn(high, chosen) + nn(middle_part, chosen) + nn(low, chosen)


def finish_kernel(
    count, mates,
    e1_ref, dx_ref, dw_ref, dwo_ref, dw1_ref, dw2_ref, small_ref, b1_ref,
    dx_out, dwq_out, dwk_out, dwv_out, dwo_out, dw1_out, dw2_out, small_out, b1_out,
):
    s, c = lax.axis_index("seq"), lax.axis_index("ctx")
    dx_out[...] = e1_ref[...] + dx_ref[...].astype(jnp.float32)
    each, tall = dwo_out.shape[0], dw2_out.shape[0]
    chunks = dw_ref.shape[0]
    width = dwq_out.shape[1] // chunks
    i = lax.rem(c, mates)
    for p in range(mates):
        rows = slice(p * each, (p + 1) * each)

        @pl.when(i == p)
        def _():
            for m, out in enumerate((dwq_out, dwk_out, dwv_out)):
                parts = [dw_ref[k, rows, m * width : (m + 1) * width] for k in range(chunks)]
                out[...] = jnp.concatenate(parts, axis=1)
            dwo_out[...] = dwo_ref[rows, :]
            dw1_out[...] = dw1_ref[rows, :]
            dw2_out[...] = dw2_ref[p * tall : (p + 1) * tall, :]

    device = s * count + c
    small_out[...] = pick(small_ref[...], each, device)
    b1_out[...] = pick(b1_ref[...], tall, device)


def finish(e1, dx, dw, dwo, dw1, dw2, small, b1):
    count = lax.axis_size("ctx")
    devices = count * lax.axis_size("seq")
    model, wide = dwo.shape[1], dw1.shape[1]
    each, tall = model // devices, wide // devices
    shape = jax.ShapeDtypeStruct
    f32 = jnp.float32
    vmem = pl.BlockSpec(memory_space=pltpu.VMEM)
    return pl.pallas_call(
        partial(finish_kernel, count, block_mates(each)),
        out_shape=(shape(e1.shape, f32),)
        + (shape((each, model), f32),) * 4
        + (shape((each, wide), f32), shape((tall, model), f32), shape((8, each), f32), shape((8, tall), f32)),
        in_specs=[vmem] * 8,
        out_specs=(vmem,) * 9,
        compiler_params=pltpu.CompilerParams(vmem_limit_bytes=VMEM_LIMIT),
        name="finish",
    )(e1, dx, dw, dwo, dw1, dw2, small, b1)


def on_device(
    tokens, segment_ids, valid_tokens, query_weight, query_bias, key_weight, value_weight, value_bias,
    output_weight, output_bias, attn_norm_gain, attn_norm_shift, up_weight, up_bias, down_weight,
    down_bias, ffn_norm_gain, ffn_norm_shift, out_cotangent,
):
    count = lax.axis_size("ctx")
    chunks = math.gcd(H, count)
    heads = H // chunks
    x = tokens[0]
    vec = jnp.concatenate([
        output_bias, attn_norm_gain, attn_norm_shift, down_bias, ffn_norm_gain, ffn_norm_shift,
        query_bias, value_bias, up_bias,
    ])
    vec = jnp.pad(vec, (0, -vec.shape[0] % LANES))[None]
    w, wo, wq, w1, w2, x_all, codes, vecs, k, v, q, o_float, lse, o = advance(
        query_weight, key_weight, value_weight, output_weight, up_weight, down_weight,
        x, segment_ids * 2 + valid_tokens, vec, chunks, heads,
    )
    output, e1, do, dwo, dw1, dw2, dsmall, db1 = middle(
        o, x, out_cotangent[0], wo, w1, w2, vecs
    )
    summed = retreat(
        do, x_all, w, wq, k, v, q, o_float, lse, codes, dwo, dw1, dw2, dsmall, db1, heads
    )[:7]
    grad, dwq, dwk, dwv, dwo, dw1, dw2, small, b1 = finish(e1, *summed)
    return (
        output[None], grad[None],
        dwq, small[6], dwk, dwv, small[7],
        dwo, small[0], small[1], small[2],
        dw1, b1[0], dw2, small[3], small[4], small[5],
    )


def solution(mesh):
    in_specs = (
        P("seq", "ctx", None),
        P("seq", "ctx"),
        P("seq", "ctx"),
        P(("seq", "ctx"), None),
        P(("seq", "ctx")),
        P(("seq", "ctx"), None),
        P(("seq", "ctx"), None),
        P(("seq", "ctx")),
        P(("seq", "ctx"), None),
        P(("seq", "ctx")),
        P(("seq", "ctx")),
        P(("seq", "ctx")),
        P(("seq", "ctx"), None),
        P(("seq", "ctx")),
        P(("seq", "ctx"), None),
        P(("seq", "ctx")),
        P(("seq", "ctx")),
        P(("seq", "ctx")),
        P("seq", "ctx", None),
    )
    out_specs = (
        P("seq", "ctx", None),
        P("seq", "ctx", None),
        P(("seq", "ctx"), None),
        P(("seq", "ctx")),
        P(("seq", "ctx"), None),
        P(("seq", "ctx"), None),
        P(("seq", "ctx")),
        P(("seq", "ctx"), None),
        P(("seq", "ctx")),
        P(("seq", "ctx")),
        P(("seq", "ctx")),
        P(("seq", "ctx"), None),
        P(("seq", "ctx")),
        P(("seq", "ctx"), None),
        P(("seq", "ctx")),
        P(("seq", "ctx")),
        P(("seq", "ctx")),
    )
    return jax.shard_map(
        on_device, mesh=mesh, in_specs=in_specs, out_specs=out_specs, check_vma=False
    )
```

```python
import math
from functools import partial

import jax
import jax.numpy as jnp
from jax import lax
from jax.experimental import pallas as pl
from jax.experimental.pallas import tpu as pltpu
from jax.sharding import PartitionSpec as P

H = 12
DH = 64
VMEM_LIMIT = 60 * 1024 * 1024

LOG2E = 1.4426950408889634
BQ = 512
BK = 512
HALF = BK // 2
PAD = BK + HALF
DOCS = 64
FAR = -(2.0**100)
LANES = 128


def nt(a, b):
    return lax.dot_general(a, b, (((1,), (1,)), ((), ())), preferred_element_type=jnp.float32)


def nn(a, b):
    return lax.dot_general(a, b, (((1,), (0,)), ((), ())), preferred_element_type=jnp.float32)


def unshard(vec, at, each):
    devices = vec.shape[0]
    shard = vec[:, at : at + each].astype(jnp.bfloat16)
    size = devices * each
    owner = lambda shape, axis: jnp.floor(
        (lax.broadcasted_iota(jnp.int32, shape, axis).astype(jnp.float32) + 0.5) / each
    )
    column = lax.broadcasted_iota(jnp.int32, (each, size), 1).astype(jnp.float32)
    inner = column - owner((each, size), 1) * each
    place = lax.broadcasted_iota(jnp.int32, (each, size), 0).astype(jnp.float32)
    repeated = nn(shard, (inner == place).astype(jnp.bfloat16))
    device = lax.broadcasted_iota(jnp.int32, (devices, size), 0).astype(jnp.float32)
    return jnp.sum(jnp.where(owner((devices, size), 1) == device, repeated, 0.0), axis=0, keepdims=True)


def tn(a, b):
    return lax.dot_general(a, b, (((0,), (0,)), ((), ())), preferred_element_type=jnp.float32)


def flip(a):
    return a.astype(jnp.float32).T.astype(a.dtype)


def three_parts(row):
    high = row.astype(jnp.bfloat16)
    rest = row - high.astype(jnp.float32)
    middle = rest.astype(jnp.bfloat16)
    low = (rest - middle.astype(jnp.float32)).astype(jnp.bfloat16)
    empty = jnp.zeros((13, row.shape[1]), jnp.float32)
    return jnp.concatenate(
        [high.astype(jnp.float32), middle.astype(jnp.float32), low.astype(jnp.float32), empty], axis=0
    )


EPSILON = 1e-12
FF_BLOCK = 512


def gelu_pair(u):
    z = jnp.abs(u) * (0.5**0.5)
    t = 1.0 / (1.0 + 0.3275911 * z)
    bell = jnp.exp(-z * z)
    poly = t * (
        0.254829592 + t * (-0.284496736 + t * (1.421413741 + t * (-1.453152027 + t * 1.061405429)))
    )
    half = 0.5 * poly * bell
    below = jnp.where(u < 0.0, half, 1.0 - half)
    return u * below, below + u * bell * 0.3989422804014327


def standard(hidden):
    centred = hidden - jnp.mean(hidden, axis=-1, keepdims=True)
    scale = lax.rsqrt(jnp.mean(centred * centred, axis=-1, keepdims=True) + EPSILON)
    return centred * scale, scale


def norm_back(grad, gain, normal, scale):
    t = grad * gain
    return scale * (
        t
        - jnp.mean(t, axis=-1, keepdims=True)
        - normal * jnp.mean(t * normal, axis=-1, keepdims=True)
    )


def middle_kernel(
    o_ref, x_ref, cot_ref, wo_ref, w1_ref, w2_ref, vec_ref,
    out_ref, e1_ref, do_ref, dwo_ref, dw1_ref, dw2_ref, dsmall_ref, db1_ref,
    act, slope, y1_ref, normal_ref, r2_ref, y1t_ref, grad_ref, small_ref, b1_ref,
    wo, w1, w2, out1, out2, y1low_ref, even, odd, wo_sem, in_sems, out_sems,
):
    bf16 = jnp.bfloat16
    load = pltpu.make_async_copy(wo_ref, wo, wo_sem)
    load.start()

    def fetch(i):
        at = pl.ds(pl.multiple_of(i * FF_BLOCK, FF_BLOCK), FF_BLOCK)
        return (
            pltpu.make_async_copy(w1_ref.at[:, at], w1.at[:, at], in_sems.at[0, i]),
            pltpu.make_async_copy(w2_ref.at[at], w2.at[at], in_sems.at[1, i]),
        )

    def deliver(i):
        at = pl.ds(pl.multiple_of(i * FF_BLOCK, FF_BLOCK), FF_BLOCK)
        slot = lax.rem(i, 2)
        return (
            pltpu.make_async_copy(out1.at[slot], dw1_ref.at[:, at], out_sems.at[0, slot]),
            pltpu.make_async_copy(out2.at[slot], dw2_ref.at[at], out_sems.at[1, slot]),
        )

    for i in range(w1_ref.shape[1] // FF_BLOCK):
        for one in fetch(i):
            one.start()
    groups, width, rows = o_ref.shape
    hidden_width = w1_ref.shape[1]
    steps = hidden_width // FF_BLOCK
    vec = vec_ref[:, 0, :]
    each = x_ref.shape[1] // vec.shape[0]
    for i in range(6):
        small_ref[i : i + 1, :] = unshard(vec, i * each, each)
    b1_ref[0:1, :] = unshard(vec, 8 * each, hidden_width // vec.shape[0])
    row = lambda i: small_ref[i : i + 1, :]
    ones = jnp.ones((8, rows), bf16)
    load.wait()
    o = o_ref[...].reshape(groups * width, rows)
    n1 = x_ref[...].astype(jnp.float32) + (tn(o, wo[...]) + row(0))
    normal, scale_one = standard(n1)
    normal_ref[...] = normal
    y1 = normal * row(1) + row(2)
    y1_ref[...] = y1
    y1_low = y1.astype(bf16)
    y1t_ref[...] = y1.T.astype(bf16)
    grad_ref[...] = jnp.zeros(grad_ref.shape, jnp.float32)

    def rise(slot, i):
        for one in fetch(i):
            one.wait()
        at = pl.ds(pl.multiple_of(i * FF_BLOCK, FF_BLOCK), FF_BLOCK)
        slot[...] = nn(y1low_ref[...], w1[:, at]) + b1_ref[0:1, at]

    def activate(slot, i):
        at = pl.ds(pl.multiple_of(i * FF_BLOCK, FF_BLOCK), FF_BLOCK)
        value, gradient = gelu_pair(slot[...])
        value = value.astype(bf16)
        act[:, at] = value
        slope[:, at] = gradient
        grad_ref[...] += nn(value, w2[at, :])

    y1low_ref[...] = y1_low
    rise(even, 0)

    def forward(k, carry):
        rise(odd, 2 * k + 1)
        activate(even, 2 * k)
        rise(even, 2 * k + 2)
        activate(odd, 2 * k + 1)
        return carry

    lax.fori_loop(0, steps // 2 - 1, forward, 0)
    rise(odd, steps - 1)
    activate(even, steps - 2)
    activate(odd, steps - 1)
    normal_two, scale_two = standard(y1_ref[...] + (grad_ref[...] + row(3)))
    out_ref[...] = normal_two * row(4) + row(5)
    cot = cot_ref[...].astype(jnp.float32)
    dsmall_ref[4:5, :] = jnp.sum(cot * normal_two, axis=0, keepdims=True)
    dsmall_ref[5:6, :] = jnp.sum(cot, axis=0, keepdims=True)
    e2 = norm_back(cot, row(4), normal_two, scale_two)
    grad_ref[...] = e2
    r2 = e2.astype(bf16)
    r2_ref[...] = r2
    dsmall_ref[3:4, :] = nn(ones, r2)[0:1]

    def backward(i, carry):
        at = pl.ds(pl.multiple_of(i * FF_BLOCK, FF_BLOCK), FF_BLOCK)
        slot = lax.rem(i, 2)

        @pl.when(i >= 2)
        def _():
            for one in deliver(i - 2):
                one.wait()

        out2[slot] = tn(act[:, at], r2_ref[...]).astype(bf16)
        du = (nt(r2_ref[...], w2[at, :]) * slope[:, at]).astype(bf16)
        db1_ref[:, at] = nn(ones, du)[0:1]
        out1[slot] = nn(y1t_ref[...], du).astype(bf16)
        for one in deliver(i):
            one.start()
        grad_ref[...] += nt(du, w1[:, at])
        return carry

    lax.fori_loop(0, steps, backward, 0)
    grad = grad_ref[...]
    normal = normal_ref[...]
    dsmall_ref[1:2, :] = jnp.sum(grad * normal, axis=0, keepdims=True)
    dsmall_ref[2:3, :] = jnp.sum(grad, axis=0, keepdims=True)
    e1 = norm_back(grad, row(1), normal, scale_one)
    e1_ref[...] = e1
    r1 = e1.astype(bf16)
    dsmall_ref[0:1, :] = nn(ones, r1)[0:1]
    dsmall_ref[6:8, :] = jnp.zeros((2, dsmall_ref.shape[1]), jnp.float32)
    dwo_ref[...] = nn(o, r1).astype(bf16)
    for i in (steps - 2, steps - 1):
        for one in deliver(i):
            one.wait()
    do_ref[...] = nt(wo[...], r1).astype(bf16).reshape(groups, width, rows)


def middle(o, x, cot, wo, w1, w2, vec):
    groups, width, rows = o.shape
    model = x.shape[1]
    hidden_width = w1.shape[1]
    shape = jax.ShapeDtypeStruct
    whole, far = pl.BlockSpec(memory_space=pltpu.VMEM), pl.BlockSpec(memory_space=pl.ANY)
    f32, bf16 = jnp.float32, jnp.bfloat16
    return pl.pallas_call(
        middle_kernel,
        out_shape=(
            shape((rows, model), f32),
            shape((rows, model), f32),
            shape(o.shape, bf16),
            shape(wo.shape, bf16),
            shape(w1.shape, bf16),
            shape(w2.shape, bf16),
            shape((8, model), f32),
            shape((1, hidden_width), f32),
        ),
        in_specs=[whole] * 3 + [far] * 3 + [whole],
        out_specs=(whole,) * 4 + (far,) * 2 + (whole,) * 2,
        scratch_shapes=[
            pltpu.VMEM((rows, hidden_width), bf16),
            pltpu.VMEM((rows, hidden_width), f32),
            pltpu.VMEM((rows, model), f32),
            pltpu.VMEM((rows, model), f32),
            pltpu.VMEM((rows, model), bf16),
            pltpu.VMEM((model, rows), bf16),
            pltpu.VMEM((rows, model), f32),
            pltpu.VMEM((8, model), f32),
            pltpu.VMEM((8, hidden_width), f32),
            pltpu.VMEM(wo.shape, bf16),
            pltpu.VMEM(w1.shape, bf16),
            pltpu.VMEM(w2.shape, bf16),
            pltpu.VMEM((2, model, FF_BLOCK), bf16),
            pltpu.VMEM((2, FF_BLOCK, model), bf16),
            pltpu.VMEM((rows, model), bf16),
            pltpu.VMEM((rows, FF_BLOCK), f32),
            pltpu.VMEM((rows, FF_BLOCK), f32),
            pltpu.SemaphoreType.DMA,
            pltpu.SemaphoreType.DMA((2, hidden_width // FF_BLOCK)),
            pltpu.SemaphoreType.DMA((2, 2)),
        ],
        compiler_params=pltpu.CompilerParams(vmem_limit_bytes=VMEM_LIMIT),
        name="middle",
    )(o, x, cot, wo, w1, w2, vec)


MESH = pl.DeviceIdType.MESH


class Sender:
    def __init__(self, send_sems, recv_sems):
        self.send_sems, self.recv_sems, self.used, self.open = send_sems, recv_sems, 0, []

    def copy(self, source, target, device, when=None, until=None):
        index = self.used
        self.used += 1
        one = pltpu.make_async_remote_copy(
            src_ref=source,
            dst_ref=target,
            send_sem=self.send_sems.at[index],
            recv_sem=self.recv_sems.at[index],
            device_id=device,
            device_id_type=MESH,
        )
        if when is None:
            one.start()
        else:
            pl.when(when)(one.start)
        self.open.append((one, when))

        def arrive():
            if until is None:
                one.wait_recv()
            else:
                pl.when(until)(one.wait_recv)

        return arrive

    def finish(self):
        for one, when in self.open:
            if when is None:
                one.wait_send()
            else:
                pl.when(when)(one.wait_send)


def greet(seqs, count):
    s, c = lax.axis_index("seq"), lax.axis_index("ctx")
    barrier = pltpu.get_barrier_semaphore()
    for d in range(1, count):
        pl.semaphore_signal(barrier, inc=1, device_id=(s, lax.rem(c + d, count)), device_id_type=MESH)
    for d in range(1, seqs):
        pl.semaphore_signal(barrier, inc=1, device_id=(lax.rem(s + d, seqs), c), device_id_type=MESH)
    pl.semaphore_wait(barrier, count - 1 + seqs - 1)


def cube_steps(seqs, turn):
    bits = seqs.bit_length() - 1
    masks = []
    for j in range(bits):
        bit = lax.rem(j + turn, bits)
        mask = 0
        for k in range(bits):
            mask = mask + jnp.where(bit == k, 1 << k, 0)
        masks.append(mask)
    return masks


def across(s, mask):
    return s + mask * (1 - 2 * lax.rem(s // mask, 2))


def block_mates(rows):
    mates = 1
    while (mates * rows) % 16:
        mates *= 2
    return mates


def advance_kernel(
    seqs, count, chunks, heads,
    wq_ref, wk_ref, wv_ref, wo_ref, w1_ref, w2_ref, x_ref, code_ref, vec_ref,
    w_out, wo_out, wq_out, w1_out, w2_out, x_out, code_out, vec_out,
    k_out, v_out, q_out, of_out, lse_out, o_out,
    stage4, stage1, stage2, flat4, flat1, flat2, low4, lowq, low1, low2, share4,
    w_all, x_all, codes, vecs, wt, k_ext, v_ext, q_ext, top_ref, acc_ref, s_even, s_odd, o_send,
    send_sems, recv_sems, here_sems, o_send_sems, o_recv_sems,
):
    s, c = lax.axis_index("seq"), lax.axis_index("ctx")
    f32, bf16 = jnp.float32, jnp.bfloat16
    small_rows, model = wq_ref.shape
    tall_rows, wide = w2_ref.shape[0], w1_ref.shape[1]
    mates = block_mates(small_rows)
    blocks = count // mates
    b, i = c // mates, lax.rem(c, mates)
    turn = lax.rem(c, 2)
    repeat = count // chunks
    g, r = c // repeat, lax.rem(c, repeat)
    width = heads * DH
    rows = x_ref.shape[0]
    length = count * rows
    block_rows, block_tall = mates * small_rows, mates * tall_rows
    sender = Sender(send_sems, recv_sems)
    here = []

    def move(source, target):
        one = pltpu.make_async_copy(source, target, here_sems.at[len(here)])
        one.start()
        here.append(one)

    greet(seqs, count)

    def tokens_at(place, half):
        start = pl.multiple_of(place * rows + half * (rows // 2), rows // 2)
        return pl.ds(start, rows // 2)

    mate_waits = {}

    def to_mates(source, group, half, when=None):
        waits = mate_waits.setdefault(half, [])
        for d in range(1, repeat):
            other = (s, g * repeat + lax.rem(r + d, repeat))
            waits.append(sender.copy(source, x_all.at[tokens_at(group * repeat + r, half)], other, when, when))

    half_rows = [pl.ds(h * (rows // 2), rows // 2) for h in range(2)]
    above, below = jnp.minimum((g + 1) * repeat + r, count - 1), jnp.maximum((g - 1) * repeat + r, 0)

    def pass_on(t):
        waits = []
        low_group, high_group = jnp.maximum(g - t, 0), jnp.minimum(g + t, chunks - 1)
        low_at = [tokens_at(low_group * repeat + r, h) for h in range(2)]
        high_at = [tokens_at(high_group * repeat + r, h) for h in range(2)]
        for h in range(2):
            rise = x_ref.at[half_rows[h]] if t == 0 else x_all.at[low_at[h]]
            fall = x_ref.at[half_rows[h]] if t == 0 else x_all.at[high_at[h]]
            rising = (g - t >= 0) & (g + 1 < chunks)
            falling = (g + t < chunks) & (g >= 1)
            waits.append((
                sender.copy(rise, x_all.at[low_at[h]], (s, above), rising, g - 1 - t >= 0),
                sender.copy(fall, x_all.at[high_at[h]], (s, below), falling, g + 1 + t < chunks),
            ))
        return waits

    def received(t, waits):
        low_group, high_group = jnp.maximum(g - 1 - t, 0), jnp.minimum(g + 1 + t, chunks - 1)
        for h in range(2):
            waits[h][0]()
            to_mates(x_all.at[tokens_at(low_group * repeat + r, h)], low_group, h, g - 1 - t >= 0)
            waits[h][1]()
            to_mates(x_all.at[tokens_at(high_group * repeat + r, h)], high_group, h, g + 1 + t < chunks)

    x_waits = pass_on(0)
    for h in range(2):
        to_mates(x_ref.at[half_rows[h]], g, h)

    shards = []
    matrices = (wq_ref, wk_ref, wv_ref, wo_ref)
    for d in range(1, mates):
        other = (s, b * mates + lax.rem(i + d, mates))
        for m in range(4):
            shards.append(sender.copy(matrices[m], stage4.at[i, m], other))
        shards.append(sender.copy(w1_ref, stage1.at[i], other))
        shards.append(sender.copy(w2_ref, stage2.at[i], other))
    for m in range(4):
        stage4[i, m] = matrices[m][...]
    stage1[i] = w1_ref[...]
    stage2[i] = w2_ref[...]

    small_waits = []
    for d in range(1, count):
        other = (s, lax.rem(c + d, count))
        small_waits.append(sender.copy(code_ref, codes.at[c], other))
        small_waits.append(sender.copy(vec_ref, vecs.at[s * count + c], other))
    codes[c] = code_ref[...]
    vecs[s * count + c] = vec_ref[...]
    x_all[tokens_at(c, 0), :] = x_ref[0 : rows // 2, :]
    x_all[tokens_at(c, 1), :] = x_ref[rows // 2 :, :]

    for wait in shards:
        wait()
    for p in range(mates):
        for m in range(4):
            flat4[m, p * small_rows : (p + 1) * small_rows, :] = stage4[p, m]
        flat1[p * small_rows : (p + 1) * small_rows, :] = stage1[p]
        flat2[p * tall_rows : (p + 1) * tall_rows, :] = stage2[p]
    for k in range(chunks):
        part = slice(k * width, (k + 1) * width)
        pieces = [flat4[m, :, part] for m in range(3)]
        pieces.append(jnp.zeros((block_rows, w_out.shape[1] - 3 * width), f32))
        share4[k] = jnp.concatenate(pieces, axis=1).astype(bf16)

    def w_rows(seq, block, size):
        start = (seq * blocks + block) * block_rows
        return pl.ds(pl.multiple_of(start, block_rows), size * block_rows)

    columns = []
    for d in range(1, blocks):
        to = lax.rem(b + d, blocks) * mates + i
        columns.append(sender.copy(share4.at[to // repeat], w_all.at[w_rows(s, b, 1)], (s, to)))
    w_all[w_rows(s, b, 1), :] = share4[g]

    low4[...] = flat4[3].astype(bf16)
    lowq[...] = flat4[0].astype(bf16)
    low1[...] = flat1[...].astype(bf16)
    low2[...] = flat2[...].astype(bf16)

    half_wide, half_model = wide // 2, model // 2
    wide_at = pl.ds(pl.multiple_of(turn * half_wide, half_wide), half_wide)
    model_at = pl.ds(pl.multiple_of(turn * half_model, half_model), half_model)

    def tall_rows_at(seq, block, size):
        start = (seq * blocks + block) * block_tall
        return pl.ds(pl.multiple_of(start, block_tall), size * block_tall)

    def big(seq, block, size=1):
        return (
            w1_out.at[w_rows(seq, block, size), wide_at],
            w2_out.at[tall_rows_at(seq, block, size), model_at],
            wo_out.at[w_rows(seq, block, size), model_at],
            wq_out.at[w_rows(seq, block, size), model_at],
        )

    own = (low1.at[:, wide_at], low2.at[:, model_at], low4.at[:, model_at], lowq.at[:, model_at])
    move(low1, w1_out.at[w_rows(s, b, 1)])
    move(low2, w2_out.at[tall_rows_at(s, b, 1)])
    move(low4, wo_out.at[w_rows(s, b, 1)])
    move(lowq, wq_out.at[w_rows(s, b, 1)])
    sibling = (s, c + 1 - 2 * turn)
    sibling_waits = []

    def to_sibling(seq, block, when):
        for piece in big(seq, block):
            sibling_waits.append(sender.copy(piece, piece, sibling, when, when))

    masks = cube_steps(seqs, turn)

    def families(seq):
        found = [(seq, -1)]
        for j, mask in enumerate(masks):
            found = found + [(across(one, mask), j) for one, _ in found]
        return found

    plane_waits = {}

    def spread(key, seq, step, block, sources, when):
        for j in range(step + 1, len(masks)):
            partner = (across(s, masks[j]), c)
            waits = plane_waits.setdefault((key, j), [])
            for source, target in zip(sources, big(seq, block)):
                waits.append((sender.copy(source, target, partner, when, when)))

    up, down = jnp.minimum((b + 1) * mates + i, count - 1), jnp.maximum((b - 1) * mates + i, 0)

    def line_send(t):
        waits = []
        low_block, high_block = jnp.maximum(b - t, 0), jnp.minimum(b + t, blocks - 1)
        rising = (b - t >= 0) & (b + 1 < blocks)
        falling = (b + t < blocks) & (b >= 1)
        rises = own if t == 0 else big(s, low_block)
        falls = own if t == 0 else big(s, high_block)
        for source, target in zip(rises, big(s, low_block)):
            waits.append(sender.copy(source, target, (s, up), rising, b - 1 - t >= 0))
        for source, target in zip(falls, big(s, high_block)):
            waits.append(sender.copy(source, target, (s, down), falling, b + 1 + t < blocks))
        return waits

    events = {("own",): (b, None)}
    for t in range(blocks - 1):
        events[(t, 0)] = (jnp.maximum(b - 1 - t, 0), b - 1 - t >= 0)
        events[(t, 1)] = (jnp.minimum(b + 1 + t, blocks - 1), b + 1 + t < blocks)

    spread(("own",), s, -1, b, own, None)
    line_waits = line_send(0)

    def token_service(t):
        nonlocal x_waits
        if t < chunks - 1:
            received(t, x_waits)
            if t + 1 < chunks - 1:
                x_waits = pass_on(t + 1)

    token_service(0)
    late = []

    def settle_late():
        for arriving, seq, block, when in late:
            for wait in arriving:
                wait()
            to_sibling(seq, block, when)
        late.clear()

    def relay_event(key):
        block, when = events[key]
        queue = {j: list(plane_waits.get((key, j), [])) for j in range(len(masks))}
        for seq, j in families(s)[1:]:
            arriving, queue[j] = queue[j][: len(own)], queue[j][len(own) :]
            if j + 1 == len(masks):
                late.append((arriving, seq, block, when))
                continue
            for wait in arriving:
                wait()
            to_sibling(seq, block, when)
            before = {k: len(plane_waits.get((key, k), [])) for k in range(j + 1, len(masks))}
            spread(key, seq, j, block, big(seq, block), when)
            for k in range(j + 1, len(masks)):
                queue[k] = queue[k] + plane_waits[(key, k)][before[k] :]

    def weight_service(t):
        nonlocal line_waits
        if t < blocks - 1:
            for wait in line_waits:
                wait()
            if t + 1 < blocks - 1:
                line_waits = line_send(t + 1)
            for way in range(2):
                block, when = events[(t, way)]
                spread((t, way), s, -1, block, big(s, block), when)
                to_sibling(s, block, when)
        settle_late()
        if t == 0:
            relay_event(("own",))
        elif t - 1 < blocks - 1:
            relay_event((t - 1, 0))
            relay_event((t - 1, 1))

    for wait in columns:
        wait()
    columns = []
    for d in range(1, seqs):
        to = (lax.rem(s + d, seqs), c)
        slab = w_all.at[w_rows(s, 0, blocks)]
        columns.append(sender.copy(slab, slab, to))
    for wait in small_waits:
        wait()
    small_waits = []
    for d in range(1, seqs):
        to = (lax.rem(s + d, seqs), c)
        slab = vecs.at[pl.ds(s * count, count)]
        small_waits.append(sender.copy(slab, slab, to))

    top_ref[...] = jnp.full(top_ref.shape, FAR, f32)
    acc_ref[...] = jnp.zeros(acc_ref.shape, f32)
    k_ext[:, length:, :] = jnp.zeros((heads, PAD, k_ext.shape[2]), bf16)
    v_ext[:, 0:DH, length:] = jnp.zeros((heads, DH, PAD), bf16)
    v_ext[:, DH:, :] = jnp.ones((heads, 16, length + PAD), bf16)
    k_out[:, length:, :] = jnp.zeros((heads, PAD, DH), bf16)

    for wait in columns + small_waits:
        wait()
    move(w_all, w_out)
    move(vecs, vec_out)
    move(codes, code_out)
    wt[...] = w_all[...].astype(f32).T.astype(bf16)
    vec = vecs[:, 0, :]

    def bias_column(which):
        whole = unshard(vec, which * small_rows, small_rows)
        row = jnp.zeros((1, width), f32)
        for k in range(chunks):
            row = row + jnp.where(g == k, whole[:, k * width : (k + 1) * width], 0.0)
        extra = -width % LANES
        row = jnp.concatenate([row, jnp.zeros((1, extra), f32)], axis=1)
        return jnp.broadcast_to(row, (LANES, width + extra)).T[0:width, 0:1]

    bias_q, bias_v = bias_column(6), bias_column(7)

    def keys(chunk):
        at = pl.ds(pl.multiple_of(chunk * rows, rows), rows)
        x = x_all[at, :]
        k = nn(x, w_all[:, width : 2 * width]).astype(bf16)
        v = (nt(wt[2 * width : 3 * width, :], x) + bias_v).astype(bf16)
        v_out[:, at] = v
        code = codes[chunk].astype(f32)
        away = jnp.concatenate(
            [
                jnp.broadcast_to(code[:, j * LANES : (j + 1) * LANES], (LANES, LANES)).T[:, 0:DOCS]
                for j in range(rows // LANES)
            ],
            axis=0,
        )
        document = lax.broadcasted_iota(jnp.int32, (rows, DOCS), 1).astype(f32)
        away = jnp.where(away == 2.0 * document + 1.0, 0.0, 1.0).astype(bf16)
        for h in range(heads):
            one = k[:, h * DH : (h + 1) * DH]
            k_out[h, at, :] = one
            k_ext[h, at, :] = jnp.concatenate([one, one, away], axis=1)
            v_ext[h, 0:DH, at] = v[h * DH : (h + 1) * DH]

    def queries(group):
        chunk = group * repeat + r
        x = x_all[pl.ds(pl.multiple_of(chunk * rows, rows), rows), :]
        to = pl.ds(pl.multiple_of(group * rows, rows), rows)
        q = (nt(wt[0:width, :], x) + bias_q).astype(bf16)
        q_out[:, to] = q
        scaled = q.astype(f32) * (DH**-0.5 * LOG2E)
        high = scaled.astype(bf16)
        rest = (scaled - high.astype(f32)).astype(bf16)
        wanted = (codes[chunk] | 1).astype(f32)
        document = lax.broadcasted_iota(jnp.int32, (DOCS, rows), 0).astype(f32)
        away = jnp.where(wanted == 2.0 * document + 1.0, FAR, 0.0).astype(bf16)
        for h in range(heads):
            part = slice(h * DH, (h + 1) * DH)
            q_ext[h, :, to] = jnp.concatenate([high[part], rest[part], away], axis=0)

    def attend_to(group, first, last):
        at = pl.ds(pl.multiple_of(group * rows, rows), rows)

        def scores(slot, key_at):
            for h in range(heads):
                slot[h] = nn(k_ext[h, pl.ds(key_at, HALF), :], q_ext[h, :, at])

        def soften(slot, key_at):
            for h in range(heads):
                top = top_ref[group, h, 0:1, :]
                sc = slot[h]
                new = jnp.maximum(top, jnp.max(sc, axis=0, keepdims=True))
                p = jnp.exp2(sc - new).astype(bf16)
                acc_ref[group, h] = acc_ref[group, h] * jnp.exp2(top - new) + nn(
                    v_ext[h, :, pl.ds(key_at, HALF)], p
                )
                top_ref[group, h, 0:1, :] = new

        def step(j, carry):
            one = pl.multiple_of(j * BK, BK)
            two = pl.multiple_of(one + HALF, HALF)
            scores(s_odd, two)
            soften(s_even, one)
            scores(s_even, pl.multiple_of(one + BK, BK))
            soften(s_odd, two)
            return carry

        per = rows // BK
        scores(s_even, pl.multiple_of(first * rows, rows))
        lax.fori_loop(first * per, last * per, step, 0)

    def conclude(group):
        at = pl.ds(pl.multiple_of(group * rows, rows), rows)
        for h in range(heads):
            part = slice(h * DH, (h + 1) * DH)
            low = acc_ref[group, h, DH : DH + 1, :]
            out = acc_ref[group, h, 0:DH, :] / low
            of_out[part, at] = out
            o_send[group, part, :] = out.astype(bf16)
            lse_out[h : h + 1, at] = top_ref[group, h, 0:1, :] + jnp.log2(low)

        @pl.when(group != g)
        def _():
            o_copy(group).start()

    def o_copy(group):
        return pltpu.make_async_remote_copy(
            src_ref=o_send.at[group],
            dst_ref=o_out.at[g],
            send_sem=o_send_sems.at[group],
            recv_sem=o_recv_sems.at[g],
            device_id=(s, group * repeat + r),
            device_id_type=MESH,
        )

    def arrive(group, low, high):
        def make(j, carry):
            keys(group * repeat + j)
            return carry

        lax.fori_loop(0, repeat, make, 0)
        queries(group)
        whole = high - low + 1 == chunks

        def each(other, carry):
            same = other == group
            attend_to(
                other,
                jnp.where(same, low, group) * repeat,
                (jnp.where(same, high, group) + 1) * repeat,
            )

            @pl.when(whole)
            def _():
                conclude(other)

            return carry

        lax.fori_loop(low, high + 1, each, 0)

    def mates_here():
        for h in range(2):
            for wait in mate_waits[h]:
                wait()
            mate_waits[h] = []

    mates_here()
    arrive(g, g, g)
    weight_service(0)
    for t in range(chunks - 1):
        if t == chunks - 2:
            move(x_all, x_out)
        low, high = g - 1 - t, g + 1 + t
        has_low, has_high = low >= 0, high < chunks

        @pl.when(has_low)
        def _():
            arrive(low, low, jnp.minimum(g + t, chunks - 1))

        @pl.when(has_high & (low < 0))
        def _():
            arrive(high, 0, high)

        token_service(t + 1)
        weight_service(t + 1)

        @pl.when(has_high & has_low)
        def _():
            arrive(high, low, high)

        mates_here()
    for t in range(chunks, blocks + 1):
        weight_service(t)
    settle_late()
    own_out = pltpu.make_async_copy(o_send.at[g], o_out.at[g], here_sems.at[9])
    own_out.start()
    for one in here:
        one.wait()
    for wait in sibling_waits:
        wait()
    for d in range(1, chunks):
        group = lax.rem(g + d, chunks)
        pltpu.make_async_remote_copy(
            src_ref=o_send.at[g],
            dst_ref=o_out.at[group],
            send_sem=o_send_sems.at[g],
            recv_sem=o_recv_sems.at[group],
            device_id=(s, group * repeat + r),
            device_id_type=MESH,
        ).wait_recv()
        o_copy(group).wait_send()
    own_out.wait()
    sender.finish()


def advance(wq, wk, wv, wo, w1, w2, x, code, vec, chunks, heads):
    seqs, count = lax.axis_size("seq"), lax.axis_size("ctx")
    small_rows, model = wq.shape
    tall_rows, wide = w2.shape[0], w1.shape[1]
    rows = x.shape[0]
    mates = block_mates(small_rows)
    blocks, repeat = count // mates, count // chunks
    semaphores = (
        6 * (mates - 1) + 2 * (count - 1) + 2 * (seqs - 1) + 9 * (blocks - 1)
        + 4 * (seqs - 1) * (2 * blocks - 1) + 4 * (seqs * (2 * blocks - 1) - 1) + 4 * (chunks - 1) + 2 * (2 * chunks - 1) * (repeat - 1)
    )
    devices = seqs * count
    width = heads * DH
    length, mine = count * rows, chunks * rows
    padded = -(-3 * width // LANES) * LANES
    shape = jax.ShapeDtypeStruct
    f32, bf16 = jnp.float32, jnp.bfloat16
    vmem, far = pl.BlockSpec(memory_space=pltpu.VMEM), pl.BlockSpec(memory_space=pl.ANY)
    block_rows, block_tall = mates * small_rows, mates * tall_rows
    dma = pltpu.SemaphoreType.DMA
    return pl.pallas_call(
        partial(advance_kernel, seqs, count, chunks, heads),
        out_shape=(
            shape((model, padded), bf16),
            shape((model, model), bf16),
            shape((model, model), bf16),
            shape((model, wide), bf16),
            shape((tall_rows * devices, model), bf16),
            shape((length, model), bf16),
            shape((count, 1, rows), jnp.int32),
            shape((devices, 1, vec.shape[1]), f32),
            shape((heads, length + PAD, DH), bf16),
            shape((width, length), bf16),
            shape((width, mine), bf16),
            shape((width, mine), f32),
            shape((8, mine), f32),
            shape((chunks, width, rows), bf16),
        ),
        in_specs=[vmem] * 9,
        out_specs=(far,) * 8 + (vmem,) * 5 + (far,),
        scratch_shapes=[
            pltpu.VMEM((mates, 4, small_rows, model), f32),
            pltpu.VMEM((mates, small_rows, wide), f32),
            pltpu.VMEM((mates, tall_rows, model), f32),
            pltpu.VMEM((4, block_rows, model), f32),
            pltpu.VMEM((block_rows, wide), f32),
            pltpu.VMEM((block_tall, model), f32),
            pltpu.VMEM((block_rows, model), bf16),
            pltpu.VMEM((block_rows, model), bf16),
            pltpu.VMEM((block_rows, wide), bf16),
            pltpu.VMEM((block_tall, model), bf16),
            pltpu.VMEM((chunks, block_rows, padded), bf16),
            pltpu.VMEM((model, padded), bf16),
            pltpu.VMEM((length, model), bf16),
            pltpu.VMEM((count, 1, rows), jnp.int32),
            pltpu.VMEM((devices, 1, vec.shape[1]), f32),
            pltpu.VMEM((padded, model), bf16),
            pltpu.VMEM((heads, length + PAD, 2 * DH + DOCS), bf16),
            pltpu.VMEM((heads, DH + 16, length + PAD), bf16),
            pltpu.VMEM((heads, 2 * DH + DOCS, mine), bf16),
            pltpu.VMEM((chunks, heads, 8, rows), f32),
            pltpu.VMEM((chunks, heads, DH + 16, rows), f32),
            pltpu.VMEM((heads, HALF, rows), f32),
            pltpu.VMEM((heads, HALF, rows), f32),
            pltpu.VMEM((chunks, width, rows), bf16),
            dma((semaphores,)),
            dma((semaphores,)),
            dma((10,)),
            dma((chunks,)),
            dma((chunks,)),
        ],
        compiler_params=pltpu.CompilerParams(
            vmem_limit_bytes=VMEM_LIMIT, collective_id=1, has_side_effects=True
        ),
        name="advance",
    )(wq, wk, wv, wo, w1, w2, x, code, vec)


def added(*parts):
    sum_of = parts[0].astype(jnp.float32)
    for part in parts[1:]:
        sum_of = sum_of + part.astype(jnp.float32)
    return sum_of


class Line:
    def __init__(self, sender, place, size, device, pieces, landing):
        self.sender, self.place, self.size, self.device = sender, place, size, device
        self.pieces, self.landing = pieces, landing
        self.waits = None

    def send(self, t):
        self.waits = []
        for way in range(2):
            rank = self.place if way == 0 else self.size - 1 - self.place
            mirror = (lambda d: d) if way == 0 else (lambda d: self.size - 1 - d)
            goal = jnp.clip(mirror(self.size - 1 - t + rank), 0, self.size - 1)
            sends = rank <= t
            receives = (rank >= 1) & (rank - 1 <= t)
            to = jnp.clip(self.place + (1 - 2 * way), 0, self.size - 1)
            waits = []
            for source, target in zip(self.pieces(goal), self.landing(way, t)):
                waits.append(self.sender.copy(source, target, self.device(to), sends, receives))
            self.waits.append((receives, mirror, rank, waits))

    def receive(self, t):
        for way, (receives, mirror, rank, waits) in enumerate(self.waits):
            goal = jnp.clip(mirror(self.size - 2 - t + rank), 0, self.size - 1)
            pieces, landing = self.pieces(goal), self.landing(way, t)
            for wait, piece, arrived in zip(waits, pieces, landing):
                wait()

                @pl.when(receives)
                def _():
                    piece[...] = added(piece[...], arrived[...]).astype(piece.dtype)


def group_order(chunks):
    table = []
    for g in range(chunks):
        steps = [(chunks - 1 + g - d if d > g else chunks - 1 - g + d, d < g, d) for d in range(chunks) if d != g]
        table.append([d for _, _, d in sorted(steps)] + [g])
    return table


def retreat_kernel(
    seqs, count, chunks, heads,
    do_ref, x_ref, w_ref, wq_ref, k_ref, v_ref, q_ref, o_ref, lse_ref, code_ref,
    dwo_ref, dw1_ref, dw2_ref, dsmall_ref, db1_ref,
    dx_out, dw_out, dwo_out, dw1_out, dw2_out, dsmall_out, db1_out, in1, in2, in4, dx_in,
    do_in, q_ext, do_ext, dq, o_slot, k_slot, v_slot, x_slot, kt_ext, v_ext, dkv, dw, db,
    s_even, s_odd, g_even, g_odd, dx_send, dq_send, dq_in, w_full, wt,
    dx_sum, dx_line, sum1, sum2, sum4, part1, part2, cube1, cube2, cube4,
    line1, line2, line4, last1, last2, last4, w_mine, w_seq, w_block, w_mates,
    small_in, b1_in, b_in, vec_seq, bias_seq,
    send_sems, recv_sems, here_sems, fetch_sems, part_sems, own_sems, mate_send, mate_recv, dq_send_sems, dq_recv_sems,
):
    s, c = lax.axis_index("seq"), lax.axis_index("ctx")
    f32, bf16 = jnp.float32, jnp.bfloat16
    rows, model = dx_out.shape
    wide = dw1_ref.shape[1]
    repeat = count // chunks
    mates = w_mates.shape[0]
    blocks = count // mates
    block_rows, block_tall = dwo_out.shape[0], dw2_out.shape[0]
    width = heads * DH
    b, i = c // mates, lax.rem(c, mates)
    g, r = c // repeat, lax.rem(c, repeat)
    turn = lax.rem(c, 2)
    half_wide, half_model = wide // 2, model // 2
    slab_rows, slab_tall = blocks * block_rows, blocks * block_tall
    sender = Sender(send_sems, recv_sems)
    here = []

    def move(source, target):
        one = pltpu.make_async_copy(source, target, here_sems.at[len(here)])
        one.start()
        here.append(one)
        return one

    table = group_order(chunks)

    def group_at(index):
        found = table[chunks - 1][index]
        for k in range(chunks - 1):
            found = jnp.where(g == k, table[k][index], found)
        return found

    def fetch(chunk, slot):
        at = pl.ds(pl.multiple_of(chunk * rows, rows), rows)
        sems = fetch_sems.at[slot]
        return (
            pltpu.make_async_copy(k_ref.at[:, at, :], k_slot.at[slot], sems.at[0]),
            pltpu.make_async_copy(v_ref.at[:, at], v_slot.at[slot], sems.at[1]),
            pltpu.make_async_copy(x_ref.at[at], x_slot.at[slot], sems.at[2]),
        )

    for one in fetch(group_at(0) * repeat, 0):
        one.start()
    greet(seqs, count)

    do_waits = {}
    for d in range(1, chunks):
        to = lax.rem(g + d, chunks)
        do_waits[chunks - d] = sender.copy(do_ref.at[to], do_in.at[g], (s, to * repeat + r))
    own_do = move(do_ref.at[g], do_in.at[g])

    sibling = (s, c + 1 - 2 * turn)

    def column_half(which):
        wide_at = pl.ds(pl.multiple_of(which * half_wide, half_wide), half_wide)
        model_at = pl.ds(pl.multiple_of(which * half_model, half_model), half_model)
        return dw1_ref.at[:, wide_at], dw2_ref.at[:, model_at], dwo_ref.at[:, model_at]

    half_waits = [
        sender.copy(source, target, sibling)
        for source, target in zip(column_half(1 - turn), (in1, in2, in4))
    ]
    for source, target in zip(column_half(turn), (sum1, sum2, sum4)):
        move(source, target)
    vec_waits = []
    for d in range(1, count):
        to = (s, lax.rem(c + d, count))
        for source, target in ((dsmall_ref, small_in), (db1_ref, b1_in)):
            vec_waits.append(sender.copy(source, target.at[c], to))
    small_in[c] = dsmall_ref[...]
    b1_in[c] = db1_ref[...]

    wt[...] = w_ref[...].astype(f32).T.astype(bf16)
    dw[...] = jnp.zeros(dw.shape, f32)
    db[...] = jnp.zeros(db.shape, f32)
    dq[...] = jnp.zeros(dq.shape, f32)
    kt_ext[:, 2 * DH : 2 * DH + 16, :] = jnp.ones((heads, 16, rows), bf16)
    v_ext[:, DH:, :] = jnp.ones((heads, 16, rows), bf16)
    one_rows = jnp.ones((8, rows), bf16)

    def queries(group):
        at = pl.ds(pl.multiple_of(group * rows, rows), rows)
        load = pltpu.make_async_copy(o_ref.at[:, at], o_slot, own_sems.at[0])
        load.start()
        load.wait()
        wanted = (code_ref[group * repeat + r] | 1).astype(f32)
        document = lax.broadcasted_iota(jnp.int32, (DOCS, rows), 0).astype(f32)
        away = jnp.where(wanted == 2.0 * document + 1.0, FAR, 0.0)
        for h in range(heads):
            part = slice(h * DH, (h + 1) * DH)
            scaled = q_ref[part, at].astype(f32) * (DH**-0.5 * LOG2E)
            high = scaled.astype(bf16).astype(f32)
            extra = three_parts(-lse_ref[h : h + 1, at])
            full = jnp.concatenate([high, scaled - high, extra, away], axis=0)
            q_ext[h, at, :] = full.T.astype(bf16)
            grad = do_in[group, part, :].astype(f32)
            delta = jnp.sum(grad * o_slot[part, :], axis=0, keepdims=True)
            do_ext[h, at, :] = jnp.concatenate([grad, three_parts(-delta)], axis=0).T.astype(bf16)

    for one in here:
        one.wait()
    queries(g)

    for wait in half_waits:
        wait()
    loads = []
    for target, arrived, part, kind in ((sum1, in1, part1, 0), (sum2, in2, part2, 1), (sum4, in4, part2, 1)):
        size = part.shape[1]
        for k in range(target.shape[0] // size):
            loads.append((target, arrived, part, kind, k * size, size))
    used_slots = [0, 0]
    copies = []
    for target, arrived, part, kind, at, size in loads:
        slot = used_slots[kind] % 2
        used_slots[kind] += 1
        copies.append((
            pltpu.make_async_copy(arrived.at[pl.ds(at, size)], part.at[slot], part_sems.at[kind, slot]), slot
        ))
    copies[0][0].start()
    for n, (target, arrived, part, kind, at, size) in enumerate(loads):
        if n + 1 < len(loads):
            copies[n + 1][0].start()
        copies[n][0].wait()
        rows_at = slice(at, at + size)
        target[rows_at] = added(target[rows_at], part[copies[n][1]]).astype(bf16)

    def slab(seq):
        at = pl.ds(pl.multiple_of(seq * slab_rows, slab_rows), slab_rows)
        tall = pl.ds(pl.multiple_of(seq * slab_tall, slab_tall), slab_tall)
        return sum1.at[at], sum2.at[tall], sum4.at[at]

    masks = cube_steps(seqs, turn)

    def family(seq, rest):
        found = [seq]
        for mask in rest:
            found = found + [across(one, mask) for one in found]
        return found

    cube_waits, used = [], 0

    def cube_send(j):
        nonlocal used
        partner = across(s, masks[j])
        cube_waits.clear()
        mine = family(s, masks[j + 1 :])
        for k, seq in enumerate(family(partner, masks[j + 1 :])):
            landing = cube1.at[used + k], cube2.at[used + k], cube4.at[used + k]
            waits = [
                sender.copy(source, target, (partner, c)) for source, target in zip(slab(seq), landing)
            ]
            cube_waits.append((mine[k], landing, waits))
        used += len(cube_waits)

    def cube_receive():
        for seq, landing, waits in cube_waits:
            for wait, target, arrived in zip(waits, slab(seq), landing):
                wait()
                target[...] = added(target[...], arrived[...]).astype(bf16)

    cube_send(0)

    def block_slab(goal):
        row = s * slab_rows + goal * block_rows
        tall = s * slab_tall + goal * block_tall
        at = pl.ds(pl.multiple_of(row, block_rows), block_rows)
        tall_at = pl.ds(pl.multiple_of(tall, block_tall), block_tall)
        return sum1.at[at], sum2.at[tall_at], sum4.at[at]

    weight_line = Line(
        sender, b, blocks, lambda to: (s, to * mates + i),
        block_slab, lambda way, t: (line1.at[way, t], line2.at[way, t], line4.at[way, t]),
    )
    half_rows = rows // 2
    token_lines = []
    for h in range(2):
        at = pl.ds(h * half_rows, half_rows)
        token_lines.append(
            Line(
                sender, g, chunks, lambda to: (s, to * repeat + r),
                lambda goal, at=at: (dx_sum.at[goal, at],),
                lambda way, t, at=at: (dx_line.at[way, t, at],),
            )
        )

    for d in range(1, chunks):
        do_waits[d]()
        queries(lax.rem(g + d, chunks))

    for wait in vec_waits:
        wait()
    vec_waits = []
    small, tall = small_in[0], b1_in[0]
    for k in range(1, count):
        small = small + small_in[k]
        tall = tall + b1_in[k]
    vec_seq[s, 0:8, 0:model] = small
    vec_seq[s, 0:1, model:] = tall
    vec_seq[s, 1:8, model:] = jnp.zeros((7, wide), f32)
    for d in range(1, seqs):
        vec_waits.append(sender.copy(vec_seq.at[s], vec_seq.at[s], (lax.rem(s + d, seqs), c)))

    weight_steps = blocks - 1
    pending = []

    def cube_turn(j):
        cube_receive()
        if j + 1 < len(masks):
            cube_send(j + 1)
        elif weight_steps:
            weight_line.send(0)

    def line_turn(t):
        weight_line.receive(t)
        if t + 1 < weight_steps:
            weight_line.send(t + 1)

    pending += [partial(cube_turn, j) for j in range(len(masks))]
    pending += [partial(line_turn, t) for t in range(weight_steps)]

    def scores(s_slot, g_slot, group, half):
        at = pl.ds(pl.multiple_of(group * rows, rows), rows)
        key = pl.ds(half * HALF, HALF)
        for h in range(heads):
            s_slot[h] = nn(q_ext[h, at, :], kt_ext[h, :, key])
            g_slot[h] = nn(do_ext[h, at, :], v_ext[h, :, key])

    def absorb(s_slot, g_slot, slot, group, half):
        at = pl.ds(pl.multiple_of(group * rows, rows), rows)
        key = pl.ds(half * HALF, HALF)
        for h in range(heads):
            part = slice(h * DH, (h + 1) * DH)
            p = jnp.exp2(s_slot[h])
            ds = (p * g_slot[h]).astype(bf16)
            dkv[width + h * DH : width + (h + 1) * DH, key] += nn(do_in[group, part, :], p.astype(bf16))
            dkv[part, key] += nn(q_ref[part, at], ds)
            dq[h, at, :] += nn(ds, k_slot[slot, h, key, :])

    def next_group(p):
        return lax.rem(g + p, chunks)

    def one_chunk(chunk, following, slot, conclude):
        for one in fetch(chunk, slot):
            one.wait()
        if following is not None:
            for one in fetch(following, 1 - slot):
                one.start()
        document = lax.broadcasted_iota(jnp.int32, (DOCS, rows), 0).astype(f32)
        away = jnp.where(code_ref[chunk].astype(f32) == 2.0 * document + 1.0, 0.0, 1.0).astype(bf16)
        for h in range(heads):
            kt = flip(k_slot[slot, h])
            kt_ext[h, 0:DH, :] = kt
            kt_ext[h, DH : 2 * DH, :] = kt
            kt_ext[h, 2 * DH + 16 :, :] = away
            v_ext[h, 0:DH, :] = v_slot[slot, h * DH : (h + 1) * DH, :]
        dkv[...] = jnp.zeros(dkv.shape, f32)
        scores(s_even, g_even, next_group(1), 0)

        def turn_of(p, carry):
            group = next_group(p)
            scores(s_odd, g_odd, group, 1)
            absorb(s_even, g_even, slot, group, 0)
            scores(s_even, g_even, next_group(p + 1), 0)
            absorb(s_odd, g_odd, slot, group, 1)
            if conclude is not None:
                conclude(group)
            return carry

        lax.fori_loop(1, chunks + 1, turn_of, 0)

    def mate_copy(group, to, slot):
        return pltpu.make_async_remote_copy(
            src_ref=dx_send.at[slot],
            dst_ref=dx_in.at[slot, group],
            send_sem=mate_send.at[slot],
            recv_sem=mate_recv.at[slot, group],
            device_id=(s, g * repeat + to),
            device_id_type=MESH,
        )

    def keep(group, j, slot):
        dk = (dkv[0:width, :] * DH**-0.5).astype(bf16)
        dv = dkv[width:, :].astype(bf16)
        both = jnp.concatenate([dk, dv], axis=0)
        dx = tn(both, wt[width : 3 * width, :]).astype(bf16)
        dw[width : 3 * width, :] += nn(both, x_slot[slot])
        db[0:8, width:] += nt(one_rows, dv)

        @pl.when(j == r)
        def _():
            dx_sum[group] = dx

        @pl.when(j != r)
        def _():
            to = lax.rem(j - r + repeat, repeat) - 1
            dx_send[to] = dx
            mate_copy(group, j, to).start()

    spare = chunks * repeat % 2

    def conclude(group):
        at = pl.ds(pl.multiple_of(group * rows, rows), rows)
        from_x = pl.ds(pl.multiple_of((group * repeat + r) * rows, rows), rows)
        load = pltpu.make_async_copy(x_ref.at[from_x], x_slot.at[spare], own_sems.at[1])
        load.start()
        grad = jnp.concatenate([dq[h, at, :] for h in range(heads)], axis=1) * DH**-0.5
        dq_send[group] = grad.T.astype(bf16)

        @pl.when(group != g)
        def _():
            dq_copy(group).start()

        low = grad.astype(bf16)
        db[0:8, 0:width] += nn(one_rows, low)
        load.wait()
        dw[0:width, :] += tn(low, x_slot[spare])

    def dq_copy(group):
        return pltpu.make_async_remote_copy(
            src_ref=dq_send.at[group],
            dst_ref=dq_in.at[g],
            send_sem=dq_send_sems.at[group],
            recv_sem=dq_recv_sems.at[g],
            device_id=(s, group * repeat + r),
            device_id_type=MESH,
        )

    def gather_mates(group):
        for d in range(1, repeat):
            mate_copy(group, lax.rem(r + d, repeat), d - 1).wait()
        loads = [
            pltpu.make_async_copy(dx_in.at[d, group], dx_send.at[d], mate_send.at[d]) for d in range(repeat - 1)
        ]
        for load in loads:
            load.start()
        for load in loads:
            load.wait()
        terms = [dx_send[d] for d in range(repeat - 1)]
        dx_sum[group] = added(dx_sum[group], *terms).astype(bf16)

    for index in range(chunks):
        group = group_at(index)
        for j in range(repeat):
            position = index * repeat + j
            slot = position % 2
            final = position + 1 == chunks * repeat
            if j + 1 < repeat:
                following = group * repeat + j + 1
            elif not final:
                following = group_at(index + 1) * repeat
            else:
                following = None
            one_chunk(group * repeat + j, following, slot, conclude if final else None)
            keep(group, j, slot)
            if j == 0 and index == chunks - 1 and pending:
                pending.pop(0)()
        gather_mates(group)
        if index >= 1:
            for line in token_lines:
                line.receive(index - 1)
        if index < chunks - 1:
            for line in token_lines:
                line.send(index)
            if pending:
                pending.pop(0)()

    w_full[...] = dw[...].T.astype(bf16)
    w_waits = []
    for d in range(1, seqs):
        to = lax.rem(s + d, seqs)
        source = w_full.at[pl.ds(pl.multiple_of(to * slab_rows, slab_rows), slab_rows)]
        w_waits.append(sender.copy(source, w_seq.at[d - 1], (to, c)))
    b_waits = []
    b_in[c] = db[0:1, :]
    for d in range(1, count):
        b_waits.append(sender.copy(b_in.at[c], b_in.at[c], (s, lax.rem(c + d, count))))
    while pending:
        pending.pop(0)()
    last_waits = []
    for source, target in zip(block_slab(b), (last1, last2, last4)):
        target[i] = source[...]
        for d in range(1, mates):
            to = (s, b * mates + lax.rem(i + d, mates))
            last_waits.append(sender.copy(source, target.at[i], to))
    for wait in b_waits:
        wait()
    b_waits = []
    pair = []
    for k in range(chunks):
        one = b_in[k * repeat]
        for d in range(1, repeat):
            one = one + b_in[k * repeat + d]
        pair.append(one)
    for m in range(2):
        joined = jnp.concatenate([one[:, m * width : (m + 1) * width] for one in pair], axis=1)
        bias_seq[s, m : m + 1, :] = joined
    bias_seq[s, 2:8, :] = jnp.zeros((6, model), f32)
    for d in range(1, seqs):
        b_waits.append(sender.copy(bias_seq.at[s], bias_seq.at[s], (lax.rem(s + d, seqs), c)))
    for wait in w_waits:
        wait()
    w_mine[...] = added(
        w_full[pl.ds(pl.multiple_of(s * slab_rows, slab_rows), slab_rows), :],
        *[w_seq[d] for d in range(seqs - 1)],
    ).astype(bf16)
    w_waits = []
    for d in range(1, blocks):
        to = lax.rem(b + d, blocks)
        source = w_mine.at[pl.ds(pl.multiple_of(to * block_rows, block_rows), block_rows)]
        w_waits.append(sender.copy(source, w_block.at[b], (s, to * mates + i)))
    w_block[b] = w_mine[pl.ds(pl.multiple_of(b * block_rows, block_rows), block_rows), :]

    dq_in[g] = dq_send[g]
    for d in range(1, chunks):
        group = lax.rem(g + d, chunks)
        pltpu.make_async_remote_copy(
            src_ref=dq_send.at[g],
            dst_ref=dq_in.at[group],
            send_sem=dq_send_sems.at[g],
            recv_sem=dq_recv_sems.at[group],
            device_id=(s, group * repeat + r),
            device_id_type=MESH,
        ).wait_recv()
        dq_copy(group).wait_send()
    part = nn(wq_ref[...], dq_in[...].reshape(chunks * width, rows))
    dx_out[...] = dx_sum[g].astype(f32) + part.T

    for wait in w_waits:
        wait()
    w_waits = []
    w_mates[i] = w_block[...]
    for d in range(1, mates):
        to = (s, b * mates + lax.rem(i + d, mates))
        w_waits.append(sender.copy(w_block, w_mates.at[i], to))
    for wait in vec_waits + b_waits + last_waits:
        wait()
    for target, source in ((dw1_out, last1), (dw2_out, last2), (dwo_out, last4)):
        size = target.shape[1] // 2
        for which in range(2):
            target[:, which * size : (which + 1) * size] = added(
                *[source[k] for k in range(which, mates, 2)]
            )
    vec, bias = vec_seq[0], bias_seq[0]
    for d in range(1, seqs):
        vec = vec + vec_seq[d]
        bias = bias + bias_seq[d]
    dsmall_out[0:6, :] = vec[0:6, 0:model]
    dsmall_out[6:8, :] = bias[0:2]
    db1_out[...] = vec[:, model:]
    for wait in w_waits:
        wait()
    for k in range(chunks):
        terms = [
            w_mates[p, q]
            for p in range(mates)
            for q in range(blocks)
            if (q * mates + p) // repeat == k
        ]
        dw_out[k] = added(*terms)
    sender.finish()


def retreat(do, x, w, wq, k, v, q, o, lse, codes, dwo, dw1, dw2, dsmall, db1, heads):
    seqs, count = lax.axis_size("seq"), lax.axis_size("ctx")
    chunks, width, rows = do.shape
    model = x.shape[1]
    wide, tall = dw1.shape[1], dw2.shape[0]
    devices = seqs * count
    mates = block_mates(model // devices)
    blocks, repeat = count // mates, count // chunks
    block_rows, block_tall = mates * (model // devices), mates * (tall // devices)
    slab_rows, slab_tall = blocks * block_rows, blocks * block_tall
    padded = w.shape[1]
    mine = chunks * rows
    semaphores = (
        (chunks - 1) + 3 + 2 * (count - 1) + (seqs - 1) + 3 * (seqs - 1) + 6 * (blocks - 1)
        + 4 * (chunks - 1) + (seqs - 1) + (count - 1) + 3 * (mates - 1) + (seqs - 1) + (blocks - 1) + (mates - 1)
    )
    shape = jax.ShapeDtypeStruct
    f32, bf16 = jnp.float32, jnp.bfloat16
    vmem, far = pl.BlockSpec(memory_space=pltpu.VMEM), pl.BlockSpec(memory_space=pl.ANY)
    half_wide, half_model = wide // 2, model // 2
    triple = lambda lead, a, t: [
        pltpu.VMEM(lead + (a, half_wide), bf16),
        pltpu.VMEM(lead + (t, half_model), bf16),
        pltpu.VMEM(lead + (a, half_model), bf16),
    ]
    dma = pltpu.SemaphoreType.DMA
    return pl.pallas_call(
        partial(retreat_kernel, seqs, count, chunks, heads),
        out_shape=(
            shape((rows, model), f32),
            shape((chunks, block_rows, padded), f32),
            shape((block_rows, model), f32),
            shape((block_rows, wide), f32),
            shape((block_tall, model), f32),
            shape((8, model), f32),
            shape((8, wide), f32),
            shape((model, half_wide), bf16),
            shape((tall, half_model), bf16),
            shape((model, half_model), bf16),
            shape((repeat - 1, chunks, rows, model), bf16),
        ),
        in_specs=[far, far, vmem, vmem, far, far, vmem, far, vmem, vmem, far, far, far, vmem, vmem],
        out_specs=(vmem,) * 7 + (far,) * 4,
        scratch_shapes=[
            pltpu.VMEM((chunks, width, rows), bf16),
            pltpu.VMEM((heads, mine, 2 * DH + 16 + DOCS), bf16),
            pltpu.VMEM((heads, mine, DH + 16), bf16),
            pltpu.VMEM((heads, mine, DH), f32),
            pltpu.VMEM((width, rows), f32),
            pltpu.VMEM((2, heads, rows, DH), bf16),
            pltpu.VMEM((2, width, rows), bf16),
            pltpu.VMEM((2, rows, model), bf16),
            pltpu.VMEM((heads, 2 * DH + 16 + DOCS, rows), bf16),
            pltpu.VMEM((heads, DH + 16, rows), bf16),
            pltpu.VMEM((2 * width, rows), f32),
            pltpu.VMEM((padded, model), f32),
            pltpu.VMEM((8, 2 * width), f32),
        ]
        + [pltpu.VMEM((heads, rows, HALF), f32)] * 4
        + [
            pltpu.VMEM((repeat - 1, rows, model), bf16),
            pltpu.VMEM((chunks, width, rows), bf16),
            pltpu.VMEM((chunks, width, rows), bf16),
            pltpu.VMEM((model, padded), bf16),
            pltpu.VMEM((padded, model), bf16),
            pltpu.VMEM((chunks, rows, model), bf16),
            pltpu.VMEM((2, chunks - 1, rows, model), bf16),
        ]
        + triple((), model, tall)
        + [pltpu.VMEM((2, model // 8, half_wide), bf16), pltpu.VMEM((2, model // 2, half_model), bf16)]
        + triple((seqs - 1,), slab_rows, slab_tall)
        + triple((2, blocks - 1), block_rows, block_tall)
        + triple((mates,), block_rows, block_tall)
        + [
            pltpu.VMEM((slab_rows, padded), bf16),
            pltpu.VMEM((seqs - 1, slab_rows, padded), bf16),
            pltpu.VMEM((blocks, block_rows, padded), bf16),
            pltpu.VMEM((mates, blocks, block_rows, padded), bf16),
            pltpu.VMEM((count, 8, model), f32),
            pltpu.VMEM((count, 1, wide), f32),
            pltpu.VMEM((count, 1, 2 * width), f32),
            pltpu.VMEM((seqs, 8, model + wide), f32),
            pltpu.VMEM((seqs, 8, model), f32),
            dma((semaphores,)),
            dma((semaphores,)),
            dma((8,)),
            dma((2, 3)),
            dma((2, 2)),
            dma((2,)),
            dma((repeat - 1,)),
            dma((repeat - 1, chunks)),
            dma((chunks,)),
            dma((chunks,)),
        ],
        compiler_params=pltpu.CompilerParams(
            vmem_limit_bytes=63 * 1024 * 1024, collective_id=2, has_side_effects=True
        ),
        name="retreat",
    )(do, x, w, wq, k, v, q, o, lse, codes, dwo, dw1, dw2, dsmall, db1)


def pick(values, size, device):
    wide = values.shape[1]
    row = lax.broadcasted_iota(jnp.int32, (wide, size), 0)
    column = lax.broadcasted_iota(jnp.int32, (wide, size), 1)
    chosen = (row == column + device * size).astype(jnp.bfloat16)
    high = values.astype(jnp.bfloat16)
    rest = values - high.astype(jnp.float32)
    middle_part = rest.astype(jnp.bfloat16)
    low = (rest - middle_part.astype(jnp.float32)).astype(jnp.bfloat16)
    return nn(high, chosen) + nn(middle_part, chosen) + nn(low, chosen)


def finish_kernel(
    count, mates,
    e1_ref, dx_ref, dw_ref, dwo_ref, dw1_ref, dw2_ref, small_ref, b1_ref,
    dx_out, dwq_out, dwk_out, dwv_out, dwo_out, dw1_out, dw2_out, small_out, b1_out,
):
    s, c = lax.axis_index("seq"), lax.axis_index("ctx")
    dx_out[...] = e1_ref[...] + dx_ref[...].astype(jnp.float32)
    each, tall = dwo_out.shape[0], dw2_out.shape[0]
    chunks = dw_ref.shape[0]
    width = dwq_out.shape[1] // chunks
    i = lax.rem(c, mates)
    for p in range(mates):
        rows = slice(p * each, (p + 1) * each)

        @pl.when(i == p)
        def _():
            for m, out in enumerate((dwq_out, dwk_out, dwv_out)):
                parts = [dw_ref[k, rows, m * width : (m + 1) * width] for k in range(chunks)]
                out[...] = jnp.concatenate(parts, axis=1)
            dwo_out[...] = dwo_ref[rows, :]
            dw1_out[...] = dw1_ref[rows, :]
            dw2_out[...] = dw2_ref[p * tall : (p + 1) * tall, :]

    device = s * count + c
    small_out[...] = pick(small_ref[...], each, device)
    b1_out[...] = pick(b1_ref[...], tall, device)


def finish(e1, dx, dw, dwo, dw1, dw2, small, b1):
    count = lax.axis_size("ctx")
    devices = count * lax.axis_size("seq")
    model, wide = dwo.shape[1], dw1.shape[1]
    each, tall = model // devices, wide // devices
    shape = jax.ShapeDtypeStruct
    f32 = jnp.float32
    vmem = pl.BlockSpec(memory_space=pltpu.VMEM)
    return pl.pallas_call(
        partial(finish_kernel, count, block_mates(each)),
        out_shape=(shape(e1.shape, f32),)
        + (shape((each, model), f32),) * 4
        + (shape((each, wide), f32), shape((tall, model), f32), shape((8, each), f32), shape((8, tall), f32)),
        in_specs=[vmem] * 8,
        out_specs=(vmem,) * 9,
        compiler_params=pltpu.CompilerParams(vmem_limit_bytes=VMEM_LIMIT),
        name="finish",
    )(e1, dx, dw, dwo, dw1, dw2, small, b1)


def on_device(
    tokens, segment_ids, valid_tokens, query_weight, query_bias, key_weight, value_weight, value_bias,
    output_weight, output_bias, attn_norm_gain, attn_norm_shift, up_weight, up_bias, down_weight,
    down_bias, ffn_norm_gain, ffn_norm_shift, out_cotangent,
):
    count = lax.axis_size("ctx")
    chunks = math.gcd(H, count)
    heads = H // chunks
    x = tokens[0]
    vec = jnp.concatenate([
        output_bias, attn_norm_gain, attn_norm_shift, down_bias, ffn_norm_gain, ffn_norm_shift,
        query_bias, value_bias, up_bias,
    ])
    vec = jnp.pad(vec, (0, -vec.shape[0] % LANES))[None]
    w, wo, wq, w1, w2, x_all, codes, vecs, k, v, q, o_float, lse, o = advance(
        query_weight, key_weight, value_weight, output_weight, up_weight, down_weight,
        x, segment_ids * 2 + valid_tokens, vec, chunks, heads,
    )
    output, e1, do, dwo, dw1, dw2, dsmall, db1 = middle(
        o, x, out_cotangent[0], wo, w1, w2, vecs
    )
    summed = retreat(
        do, x_all, w, wq, k, v, q, o_float, lse, codes, dwo, dw1, dw2, dsmall, db1, heads
    )[:7]
    grad, dwq, dwk, dwv, dwo, dw1, dw2, small, b1 = finish(e1, *summed)
    return (
        output[None], grad[None],
        dwq, small[6], dwk, dwv, small[7],
        dwo, small[0], small[1], small[2],
        dw1, b1[0], dw2, small[3], small[4], small[5],
    )


def solution(mesh):
    in_specs = (
        P("seq", "ctx", None),
        P("seq", "ctx"),
        P("seq", "ctx"),
        P(("seq", "ctx"), None),
        P(("seq", "ctx")),
        P(("seq", "ctx"), None),
        P(("seq", "ctx"), None),
        P(("seq", "ctx")),
        P(("seq", "ctx"), None),
        P(("seq", "ctx")),
        P(("seq", "ctx")),
        P(("seq", "ctx")),
        P(("seq", "ctx"), None),
        P(("seq", "ctx")),
        P(("seq", "ctx"), None),
        P(("seq", "ctx")),
        P(("seq", "ctx")),
        P(("seq", "ctx")),
        P("seq", "ctx", None),
    )
    out_specs = (
        P("seq", "ctx", None),
        P("seq", "ctx", None),
        P(("seq", "ctx"), None),
        P(("seq", "ctx")),
        P(("seq", "ctx"), None),
        P(("seq", "ctx"), None),
        P(("seq", "ctx")),
        P(("seq", "ctx"), None),
        P(("seq", "ctx")),
        P(("seq", "ctx")),
        P(("seq", "ctx")),
        P(("seq", "ctx"), None),
        P(("seq", "ctx")),
        P(("seq", "ctx"), None),
        P(("seq", "ctx")),
        P(("seq", "ctx")),
        P(("seq", "ctx")),
    )
    return jax.shard_map(
        on_device, mesh=mesh, in_specs=in_specs, out_specs=out_specs, check_vma=False
    )
```

```python
import math
from functools import partial

import jax
import jax.numpy as jnp
from jax import lax
from jax.experimental import pallas as pl
from jax.experimental.pallas import tpu as pltpu
from jax.sharding import PartitionSpec as P

H = 12
DH = 64
VMEM_LIMIT = 60 * 1024 * 1024

LOG2E = 1.4426950408889634
BQ = 512
BK = 512
HALF = BK // 2
PAD = BK + HALF
DOCS = 64
FAR = -(2.0**100)
LANES = 128


def nt(a, b):
    return lax.dot_general(a, b, (((1,), (1,)), ((), ())), preferred_element_type=jnp.float32)


def nn(a, b):
    return lax.dot_general(a, b, (((1,), (0,)), ((), ())), preferred_element_type=jnp.float32)


def unshard(vec, at, each):
    devices = vec.shape[0]
    shard = vec[:, at : at + each].astype(jnp.bfloat16)
    size = devices * each
    owner = lambda shape, axis: jnp.floor(
        (lax.broadcasted_iota(jnp.int32, shape, axis).astype(jnp.float32) + 0.5) / each
    )
    column = lax.broadcasted_iota(jnp.int32, (each, size), 1).astype(jnp.float32)
    inner = column - owner((each, size), 1) * each
    place = lax.broadcasted_iota(jnp.int32, (each, size), 0).astype(jnp.float32)
    repeated = nn(shard, (inner == place).astype(jnp.bfloat16))
    device = lax.broadcasted_iota(jnp.int32, (devices, size), 0).astype(jnp.float32)
    return jnp.sum(jnp.where(owner((devices, size), 1) == device, repeated, 0.0), axis=0, keepdims=True)


def tn(a, b):
    return lax.dot_general(a, b, (((0,), (0,)), ((), ())), preferred_element_type=jnp.float32)


def three_parts(row):
    high = row.astype(jnp.bfloat16)
    rest = row - high.astype(jnp.float32)
    middle = rest.astype(jnp.bfloat16)
    low = (rest - middle.astype(jnp.float32)).astype(jnp.bfloat16)
    empty = jnp.zeros((13, row.shape[1]), jnp.float32)
    return jnp.concatenate(
        [high.astype(jnp.float32), middle.astype(jnp.float32), low.astype(jnp.float32), empty], axis=0
    )


EPSILON = 1e-12
FF_BLOCK = 512


def gelu_pair(u):
    z = jnp.abs(u) * (0.5**0.5)
    t = 1.0 / (1.0 + 0.3275911 * z)
    bell = jnp.exp(-z * z)
    poly = t * (
        0.254829592 + t * (-0.284496736 + t * (1.421413741 + t * (-1.453152027 + t * 1.061405429)))
    )
    half = 0.5 * poly * bell
    below = jnp.where(u < 0.0, half, 1.0 - half)
    return u * below, below + u * bell * 0.3989422804014327


def standard(hidden):
    centred = hidden - jnp.mean(hidden, axis=-1, keepdims=True)
    scale = lax.rsqrt(jnp.mean(centred * centred, axis=-1, keepdims=True) + EPSILON)
    return centred * scale, scale


def norm_back(grad, gain, normal, scale):
    t = grad * gain
    return scale * (
        t
        - jnp.mean(t, axis=-1, keepdims=True)
        - normal * jnp.mean(t * normal, axis=-1, keepdims=True)
    )


def middle_kernel(
    o_ref, x_ref, cot_ref, wo_ref, w1_ref, w2_ref, vec_ref,
    out_ref, e1_ref, do_ref, dwo_ref, dw1_ref, dw2_ref, dsmall_ref, db1_ref,
    act, slope, y1_ref, normal_ref, r2_ref, y1t_ref, grad_ref, small_ref, b1_ref,
    wo, w1, w2, out1, out2, y1low_ref, even, odd, wo_sem, in_sems, out_sems,
):
    bf16 = jnp.bfloat16
    load = pltpu.make_async_copy(wo_ref, wo, wo_sem)
    load.start()

    def fetch(i):
        at = pl.ds(pl.multiple_of(i * FF_BLOCK, FF_BLOCK), FF_BLOCK)
        return (
            pltpu.make_async_copy(w1_ref.at[:, at], w1.at[:, at], in_sems.at[0, i]),
            pltpu.make_async_copy(w2_ref.at[at], w2.at[at], in_sems.at[1, i]),
        )

    def deliver(i):
        at = pl.ds(pl.multiple_of(i * FF_BLOCK, FF_BLOCK), FF_BLOCK)
        slot = lax.rem(i, 2)
        return (
            pltpu.make_async_copy(out1.at[slot], dw1_ref.at[:, at], out_sems.at[0, slot]),
            pltpu.make_async_copy(out2.at[slot], dw2_ref.at[at], out_sems.at[1, slot]),
        )

    for i in range(w1_ref.shape[1] // FF_BLOCK):
        for one in fetch(i):
            one.start()
    groups, width, rows = o_ref.shape
    hidden_width = w1_ref.shape[1]
    steps = hidden_width // FF_BLOCK
    vec = vec_ref[:, 0, :]
    each = x_ref.shape[1] // vec.shape[0]
    for i in range(6):
        small_ref[i : i + 1, :] = unshard(vec, i * each, each)
    b1_ref[0:1, :] = unshard(vec, 8 * each, hidden_width // vec.shape[0])
    row = lambda i: small_ref[i : i + 1, :]
    ones = jnp.ones((8, rows), bf16)
    load.wait()
    o = o_ref[...].reshape(groups * width, rows)
    n1 = x_ref[...].astype(jnp.float32) + (tn(o, wo[...]) + row(0))
    normal, scale_one = standard(n1)
    normal_ref[...] = normal
    y1 = normal * row(1) + row(2)
    y1_ref[...] = y1
    y1_low = y1.astype(bf16)
    y1t_ref[...] = y1.T.astype(bf16)
    grad_ref[...] = jnp.zeros(grad_ref.shape, jnp.float32)

    def rise(slot, i):
        for one in fetch(i):
            one.wait()
        at = pl.ds(pl.multiple_of(i * FF_BLOCK, FF_BLOCK), FF_BLOCK)
        slot[...] = nn(y1low_ref[...], w1[:, at]) + b1_ref[0:1, at]

    def activate(slot, i):
        at = pl.ds(pl.multiple_of(i * FF_BLOCK, FF_BLOCK), FF_BLOCK)
        value, gradient = gelu_pair(slot[...])
        value = value.astype(bf16)
        act[:, at] = value
        slope[:, at] = gradient
        grad_ref[...] += nn(value, w2[at, :])

    y1low_ref[...] = y1_low
    rise(even, 0)

    def forward(k, carry):
        rise(odd, 2 * k + 1)
        activate(even, 2 * k)
        rise(even, 2 * k + 2)
        activate(odd, 2 * k + 1)
        return carry

    lax.fori_loop(0, steps // 2 - 1, forward, 0)
    rise(odd, steps - 1)
    activate(even, steps - 2)
    activate(odd, steps - 1)
    normal_two, scale_two = standard(y1_ref[...] + (grad_ref[...] + row(3)))
    out_ref[...] = normal_two * row(4) + row(5)
    cot = cot_ref[...].astype(jnp.float32)
    dsmall_ref[4:5, :] = jnp.sum(cot * normal_two, axis=0, keepdims=True)
    dsmall_ref[5:6, :] = jnp.sum(cot, axis=0, keepdims=True)
    e2 = norm_back(cot, row(4), normal_two, scale_two)
    grad_ref[...] = e2
    r2 = e2.astype(bf16)
    r2_ref[...] = r2
    dsmall_ref[3:4, :] = nn(ones, r2)[0:1]

    def backward(i, carry):
        at = pl.ds(pl.multiple_of(i * FF_BLOCK, FF_BLOCK), FF_BLOCK)
        slot = lax.rem(i, 2)

        @pl.when(i >= 2)
        def _():
            for one in deliver(i - 2):
                one.wait()

        out2[slot] = tn(act[:, at], r2_ref[...]).astype(bf16)
        du = (nt(r2_ref[...], w2[at, :]) * slope[:, at]).astype(bf16)
        db1_ref[:, at] = nn(ones, du)[0:1]
        out1[slot] = nn(y1t_ref[...], du).astype(bf16)
        for one in deliver(i):
            one.start()
        grad_ref[...] += nt(du, w1[:, at])
        return carry

    lax.fori_loop(0, steps, backward, 0)
    grad = grad_ref[...]
    normal = normal_ref[...]
    dsmall_ref[1:2, :] = jnp.sum(grad * normal, axis=0, keepdims=True)
    dsmall_ref[2:3, :] = jnp.sum(grad, axis=0, keepdims=True)
    e1 = norm_back(grad, row(1), normal, scale_one)
    e1_ref[...] = e1
    r1 = e1.astype(bf16)
    dsmall_ref[0:1, :] = nn(ones, r1)[0:1]
    dsmall_ref[6:8, :] = jnp.zeros((2, dsmall_ref.shape[1]), jnp.float32)
    dwo_ref[...] = nn(o, r1).astype(bf16)
    for i in (steps - 2, steps - 1):
        for one in deliver(i):
            one.wait()
    do_ref[...] = nt(wo[...], r1).astype(bf16).reshape(groups, width, rows)


def middle(o, x, cot, wo, w1, w2, vec):
    groups, width, rows = o.shape
    model = x.shape[1]
    hidden_width = w1.shape[1]
    shape = jax.ShapeDtypeStruct
    whole, far = pl.BlockSpec(memory_space=pltpu.VMEM), pl.BlockSpec(memory_space=pl.ANY)
    f32, bf16 = jnp.float32, jnp.bfloat16
    return pl.pallas_call(
        middle_kernel,
        out_shape=(
            shape((rows, model), f32),
            shape((rows, model), f32),
            shape(o.shape, bf16),
            shape(wo.shape, bf16),
            shape(w1.shape, bf16),
            shape(w2.shape, bf16),
            shape((8, model), f32),
            shape((1, hidden_width), f32),
        ),
        in_specs=[whole] * 3 + [far] * 3 + [whole],
        out_specs=(whole,) * 4 + (far,) * 2 + (whole,) * 2,
        scratch_shapes=[
            pltpu.VMEM((rows, hidden_width), bf16),
            pltpu.VMEM((rows, hidden_width), f32),
            pltpu.VMEM((rows, model), f32),
            pltpu.VMEM((rows, model), f32),
            pltpu.VMEM((rows, model), bf16),
            pltpu.VMEM((model, rows), bf16),
            pltpu.VMEM((rows, model), f32),
            pltpu.VMEM((8, model), f32),
            pltpu.VMEM((8, hidden_width), f32),
            pltpu.VMEM(wo.shape, bf16),
            pltpu.VMEM(w1.shape, bf16),
            pltpu.VMEM(w2.shape, bf16),
            pltpu.VMEM((2, model, FF_BLOCK), bf16),
            pltpu.VMEM((2, FF_BLOCK, model), bf16),
            pltpu.VMEM((rows, model), bf16),
            pltpu.VMEM((rows, FF_BLOCK), f32),
            pltpu.VMEM((rows, FF_BLOCK), f32),
            pltpu.SemaphoreType.DMA,
            pltpu.SemaphoreType.DMA((2, hidden_width // FF_BLOCK)),
            pltpu.SemaphoreType.DMA((2, 2)),
        ],
        compiler_params=pltpu.CompilerParams(vmem_limit_bytes=VMEM_LIMIT),
        name="middle",
    )(o, x, cot, wo, w1, w2, vec)


MESH = pl.DeviceIdType.MESH


class Sender:
    def __init__(self, send_sems, recv_sems):
        self.send_sems, self.recv_sems, self.used, self.open = send_sems, recv_sems, 0, []

    def copy(self, source, target, device, when=None, until=None):
        index = self.used
        self.used += 1
        one = pltpu.make_async_remote_copy(
            src_ref=source,
            dst_ref=target,
            send_sem=self.send_sems.at[index],
            recv_sem=self.recv_sems.at[index],
            device_id=device,
            device_id_type=MESH,
        )
        if when is None:
            one.start()
        else:
            pl.when(when)(one.start)
        self.open.append((one, when))

        def arrive():
            if until is None:
                one.wait_recv()
            else:
                pl.when(until)(one.wait_recv)

        return arrive

    def finish(self):
        for one, when in self.open:
            if when is None:
                one.wait_send()
            else:
                pl.when(when)(one.wait_send)


def greet(seqs, count):
    s, c = lax.axis_index("seq"), lax.axis_index("ctx")
    barrier = pltpu.get_barrier_semaphore()
    for d in range(1, count):
        pl.semaphore_signal(barrier, inc=1, device_id=(s, lax.rem(c + d, count)), device_id_type=MESH)
    for d in range(1, seqs):
        pl.semaphore_signal(barrier, inc=1, device_id=(lax.rem(s + d, seqs), c), device_id_type=MESH)
    pl.semaphore_wait(barrier, count - 1 + seqs - 1)


def cube_steps(seqs, turn):
    bits = seqs.bit_length() - 1
    masks = []
    for j in range(bits):
        bit = lax.rem(j + turn, bits)
        mask = 0
        for k in range(bits):
            mask = mask + jnp.where(bit == k, 1 << k, 0)
        masks.append(mask)
    return masks


def across(s, mask):
    return s + mask * (1 - 2 * lax.rem(s // mask, 2))


def block_mates(rows):
    mates = 1
    while (mates * rows) % 16:
        mates *= 2
    return mates


def advance_kernel(
    seqs, count, chunks, heads,
    wq_ref, wk_ref, wv_ref, wo_ref, w1_ref, w2_ref, x_ref, code_ref, vec_ref,
    w_out, wo_out, wq_out, w1_out, w2_out, x_out, code_out, vec_out,
    k_out, kt_out, v_out, q_out, of_out, lse_out, o_out,
    stage4, stage1, stage2, flat4, flat1, flat2, low4, lowq, low1, low2, share4,
    w_all, x_all, codes, vecs, wt, k_ext, v_ext, q_ext, top_ref, acc_ref, s_even, s_odd, o_send,
    send_sems, recv_sems, here_sems, o_send_sems, o_recv_sems,
):
    s, c = lax.axis_index("seq"), lax.axis_index("ctx")
    f32, bf16 = jnp.float32, jnp.bfloat16
    small_rows, model = wq_ref.shape
    tall_rows, wide = w2_ref.shape[0], w1_ref.shape[1]
    mates = block_mates(small_rows)
    blocks = count // mates
    b, i = c // mates, lax.rem(c, mates)
    turn = lax.rem(c, 2)
    repeat = count // chunks
    g, r = c // repeat, lax.rem(c, repeat)
    width = heads * DH
    rows = x_ref.shape[0]
    length = count * rows
    block_rows, block_tall = mates * small_rows, mates * tall_rows
    sender = Sender(send_sems, recv_sems)
    here = []

    def move(source, target):
        one = pltpu.make_async_copy(source, target, here_sems.at[len(here)])
        one.start()
        here.append(one)

    greet(seqs, count)

    def tokens_at(place, half):
        start = pl.multiple_of(place * rows + half * (rows // 2), rows // 2)
        return pl.ds(start, rows // 2)

    mate_waits = {}

    def to_mates(source, group, half, when=None):
        waits = mate_waits.setdefault(half, [])
        for d in range(1, repeat):
            other = (s, g * repeat + lax.rem(r + d, repeat))
            waits.append(sender.copy(source, x_all.at[tokens_at(group * repeat + r, half)], other, when, when))

    half_rows = [pl.ds(h * (rows // 2), rows // 2) for h in range(2)]
    above, below = jnp.minimum((g + 1) * repeat + r, count - 1), jnp.maximum((g - 1) * repeat + r, 0)

    def pass_on(t):
        waits = []
        low_group, high_group = jnp.maximum(g - t, 0), jnp.minimum(g + t, chunks - 1)
        low_at = [tokens_at(low_group * repeat + r, h) for h in range(2)]
        high_at = [tokens_at(high_group * repeat + r, h) for h in range(2)]
        for h in range(2):
            rise = x_ref.at[half_rows[h]] if t == 0 else x_all.at[low_at[h]]
            fall = x_ref.at[half_rows[h]] if t == 0 else x_all.at[high_at[h]]
            rising = (g - t >= 0) & (g + 1 < chunks)
            falling = (g + t < chunks) & (g >= 1)
            waits.append((
                sender.copy(rise, x_all.at[low_at[h]], (s, above), rising, g - 1 - t >= 0),
                sender.copy(fall, x_all.at[high_at[h]], (s, below), falling, g + 1 + t < chunks),
            ))
        return waits

    def received(t, waits):
        low_group, high_group = jnp.maximum(g - 1 - t, 0), jnp.minimum(g + 1 + t, chunks - 1)
        for h in range(2):
            waits[h][0]()
            to_mates(x_all.at[tokens_at(low_group * repeat + r, h)], low_group, h, g - 1 - t >= 0)
            waits[h][1]()
            to_mates(x_all.at[tokens_at(high_group * repeat + r, h)], high_group, h, g + 1 + t < chunks)

    x_waits = pass_on(0)
    for h in range(2):
        to_mates(x_ref.at[half_rows[h]], g, h)

    shards = []
    matrices = (wq_ref, wk_ref, wv_ref, wo_ref)
    for d in range(1, mates):
        other = (s, b * mates + lax.rem(i + d, mates))
        for m in range(4):
            shards.append(sender.copy(matrices[m], stage4.at[i, m], other))
        shards.append(sender.copy(w1_ref, stage1.at[i], other))
        shards.append(sender.copy(w2_ref, stage2.at[i], other))
    for m in range(4):
        stage4[i, m] = matrices[m][...]
    stage1[i] = w1_ref[...]
    stage2[i] = w2_ref[...]

    small_waits = []
    for d in range(1, count):
        other = (s, lax.rem(c + d, count))
        small_waits.append(sender.copy(code_ref, codes.at[c], other))
        small_waits.append(sender.copy(vec_ref, vecs.at[s * count + c], other))
    codes[c] = code_ref[...]
    vecs[s * count + c] = vec_ref[...]
    x_all[tokens_at(c, 0), :] = x_ref[0 : rows // 2, :]
    x_all[tokens_at(c, 1), :] = x_ref[rows // 2 :, :]

    for wait in shards:
        wait()
    for p in range(mates):
        for m in range(4):
            flat4[m, p * small_rows : (p + 1) * small_rows, :] = stage4[p, m]
        flat1[p * small_rows : (p + 1) * small_rows, :] = stage1[p]
        flat2[p * tall_rows : (p + 1) * tall_rows, :] = stage2[p]
    for k in range(chunks):
        part = slice(k * width, (k + 1) * width)
        pieces = [flat4[m, :, part] for m in range(3)]
        pieces.append(jnp.zeros((block_rows, w_out.shape[1] - 3 * width), f32))
        share4[k] = jnp.concatenate(pieces, axis=1).astype(bf16)

    def w_rows(seq, block, size):
        start = (seq * blocks + block) * block_rows
        return pl.ds(pl.multiple_of(start, block_rows), size * block_rows)

    columns = []
    for d in range(1, blocks):
        to = lax.rem(b + d, blocks) * mates + i
        columns.append(sender.copy(share4.at[to // repeat], w_all.at[w_rows(s, b, 1)], (s, to)))
    w_all[w_rows(s, b, 1), :] = share4[g]

    low4[...] = flat4[3].astype(bf16)
    lowq[...] = flat4[0].astype(bf16)
    low1[...] = flat1[...].astype(bf16)
    low2[...] = flat2[...].astype(bf16)

    half_wide, half_model = wide // 2, model // 2
    wide_at = pl.ds(pl.multiple_of(turn * half_wide, half_wide), half_wide)
    model_at = pl.ds(pl.multiple_of(turn * half_model, half_model), half_model)

    def tall_rows_at(seq, block, size):
        start = (seq * blocks + block) * block_tall
        return pl.ds(pl.multiple_of(start, block_tall), size * block_tall)

    def big(seq, block, size=1):
        return (
            w1_out.at[w_rows(seq, block, size), wide_at],
            w2_out.at[tall_rows_at(seq, block, size), model_at],
            wo_out.at[w_rows(seq, block, size), model_at],
            wq_out.at[w_rows(seq, block, size), model_at],
        )

    own = (low1.at[:, wide_at], low2.at[:, model_at], low4.at[:, model_at], lowq.at[:, model_at])
    move(low1, w1_out.at[w_rows(s, b, 1)])
    move(low2, w2_out.at[tall_rows_at(s, b, 1)])
    move(low4, wo_out.at[w_rows(s, b, 1)])
    move(lowq, wq_out.at[w_rows(s, b, 1)])
    sibling = (s, c + 1 - 2 * turn)
    sibling_waits = []

    def to_sibling(seq, block, when):
        for piece in big(seq, block):
            sibling_waits.append(sender.copy(piece, piece, sibling, when, when))

    masks = cube_steps(seqs, turn)

    def families(seq):
        found = [(seq, -1)]
        for j, mask in enumerate(masks):
            found = found + [(across(one, mask), j) for one, _ in found]
        return found

    plane_waits = {}

    def spread(key, seq, step, block, sources, when):
        for j in range(step + 1, len(masks)):
            partner = (across(s, masks[j]), c)
            waits = plane_waits.setdefault((key, j), [])
            for source, target in zip(sources, big(seq, block)):
                waits.append((sender.copy(source, target, partner, when, when)))

    up, down = jnp.minimum((b + 1) * mates + i, count - 1), jnp.maximum((b - 1) * mates + i, 0)

    def line_send(t):
        waits = []
        low_block, high_block = jnp.maximum(b - t, 0), jnp.minimum(b + t, blocks - 1)
        rising = (b - t >= 0) & (b + 1 < blocks)
        falling = (b + t < blocks) & (b >= 1)
        rises = own if t == 0 else big(s, low_block)
        falls = own if t == 0 else big(s, high_block)
        for source, target in zip(rises, big(s, low_block)):
            waits.append(sender.copy(source, target, (s, up), rising, b - 1 - t >= 0))
        for source, target in zip(falls, big(s, high_block)):
            waits.append(sender.copy(source, target, (s, down), falling, b + 1 + t < blocks))
        return waits

    events = {("own",): (b, None)}
    for t in range(blocks - 1):
        events[(t, 0)] = (jnp.maximum(b - 1 - t, 0), b - 1 - t >= 0)
        events[(t, 1)] = (jnp.minimum(b + 1 + t, blocks - 1), b + 1 + t < blocks)

    spread(("own",), s, -1, b, own, None)
    line_waits = line_send(0)

    def token_service(t):
        nonlocal x_waits
        if t < chunks - 1:
            received(t, x_waits)
            if t + 1 < chunks - 1:
                x_waits = pass_on(t + 1)

    token_service(0)
    late = []

    def settle_late():
        for arriving, seq, block, when in late:
            for wait in arriving:
                wait()
            to_sibling(seq, block, when)
        late.clear()

    def relay_event(key):
        block, when = events[key]
        queue = {j: list(plane_waits.get((key, j), [])) for j in range(len(masks))}
        for seq, j in families(s)[1:]:
            arriving, queue[j] = queue[j][: len(own)], queue[j][len(own) :]
            if j + 1 == len(masks):
                late.append((arriving, seq, block, when))
                continue
            for wait in arriving:
                wait()
            to_sibling(seq, block, when)
            before = {k: len(plane_waits.get((key, k), [])) for k in range(j + 1, len(masks))}
            spread(key, seq, j, block, big(seq, block), when)
            for k in range(j + 1, len(masks)):
                queue[k] = queue[k] + plane_waits[(key, k)][before[k] :]

    def weight_service(t):
        nonlocal line_waits
        if t < blocks - 1:
            for wait in line_waits:
                wait()
            if t + 1 < blocks - 1:
                line_waits = line_send(t + 1)
            for way in range(2):
                block, when = events[(t, way)]
                spread((t, way), s, -1, block, big(s, block), when)
                to_sibling(s, block, when)
        settle_late()
        if t == 0:
            relay_event(("own",))
        elif t - 1 < blocks - 1:
            relay_event((t - 1, 0))
            relay_event((t - 1, 1))

    for wait in columns:
        wait()
    columns = []
    for d in range(1, seqs):
        to = (lax.rem(s + d, seqs), c)
        slab = w_all.at[w_rows(s, 0, blocks)]
        columns.append(sender.copy(slab, slab, to))
    for wait in small_waits:
        wait()
    small_waits = []
    for d in range(1, seqs):
        to = (lax.rem(s + d, seqs), c)
        slab = vecs.at[pl.ds(s * count, count)]
        small_waits.append(sender.copy(slab, slab, to))

    top_ref[...] = jnp.full(top_ref.shape, FAR, f32)
    acc_ref[...] = jnp.zeros(acc_ref.shape, f32)
    k_ext[:, length:, :] = jnp.zeros((heads, PAD, k_ext.shape[2]), bf16)
    v_ext[:, 0:DH, length:] = jnp.zeros((heads, DH, PAD), bf16)
    v_ext[:, DH:, :] = jnp.ones((heads, 16, length + PAD), bf16)
    k_out[:, length:, :] = jnp.zeros((heads, PAD, DH), bf16)

    for wait in columns + small_waits:
        wait()
    move(w_all, w_out)
    move(vecs, vec_out)
    move(codes, code_out)
    wt[...] = w_all[...].astype(f32).T.astype(bf16)
    vec = vecs[:, 0, :]

    def bias_column(which):
        whole = unshard(vec, which * small_rows, small_rows)
        row = jnp.zeros((1, width), f32)
        for k in range(chunks):
            row = row + jnp.where(g == k, whole[:, k * width : (k + 1) * width], 0.0)
        extra = -width % LANES
        row = jnp.concatenate([row, jnp.zeros((1, extra), f32)], axis=1)
        return jnp.broadcast_to(row, (LANES, width + extra)).T[0:width, 0:1]

    bias_q, bias_v = bias_column(6), bias_column(7)

    def keys(chunk):
        at = pl.ds(pl.multiple_of(chunk * rows, rows), rows)
        x = x_all[at, :]
        k = nn(x, w_all[:, width : 2 * width]).astype(bf16)
        v = (nt(wt[2 * width : 3 * width, :], x) + bias_v).astype(bf16)
        v_out[:, at] = v
        kt_out[:, at] = nt(wt[width : 2 * width, :], x).astype(bf16)
        code = codes[chunk].astype(f32)
        away = jnp.concatenate(
            [
                jnp.broadcast_to(code[:, j * LANES : (j + 1) * LANES], (LANES, LANES)).T[:, 0:DOCS]
                for j in range(rows // LANES)
            ],
            axis=0,
        )
        document = lax.broadcasted_iota(jnp.int32, (rows, DOCS), 1).astype(f32)
        away = jnp.where(away == 2.0 * document + 1.0, 0.0, 1.0).astype(bf16)
        for h in range(heads):
            one = k[:, h * DH : (h + 1) * DH]
            k_out[h, at, :] = one
            k_ext[h, at, :] = jnp.concatenate([one, one, away], axis=1)
            v_ext[h, 0:DH, at] = v[h * DH : (h + 1) * DH]

    def queries(group):
        chunk = group * repeat + r
        x = x_all[pl.ds(pl.multiple_of(chunk * rows, rows), rows), :]
        to = pl.ds(pl.multiple_of(group * rows, rows), rows)
        q = (nt(wt[0:width, :], x) + bias_q).astype(bf16)
        q_out[:, to] = q
        scaled = q.astype(f32) * (DH**-0.5 * LOG2E)
        high = scaled.astype(bf16)
        rest = (scaled - high.astype(f32)).astype(bf16)
        wanted = (codes[chunk] | 1).astype(f32)
        document = lax.broadcasted_iota(jnp.int32, (DOCS, rows), 0).astype(f32)
        away = jnp.where(wanted == 2.0 * document + 1.0, FAR, 0.0).astype(bf16)
        for h in range(heads):
            part = slice(h * DH, (h + 1) * DH)
            q_ext[h, :, to] = jnp.concatenate([high[part], rest[part], away], axis=0)

    def attend_to(group, first, last):
        at = pl.ds(pl.multiple_of(group * rows, rows), rows)

        def scores(slot, key_at):
            for h in range(heads):
                slot[h] = nn(k_ext[h, pl.ds(key_at, HALF), :], q_ext[h, :, at])

        def soften(slot, key_at):
            for h in range(heads):
                top = top_ref[group, h, 0:1, :]
                sc = slot[h]
                new = jnp.maximum(top, jnp.max(sc, axis=0, keepdims=True))
                p = jnp.exp2(sc - new).astype(bf16)
                acc_ref[group, h] = acc_ref[group, h] * jnp.exp2(top - new) + nn(
                    v_ext[h, :, pl.ds(key_at, HALF)], p
                )
                top_ref[group, h, 0:1, :] = new

        def step(j, carry):
            one = pl.multiple_of(j * BK, BK)
            two = pl.multiple_of(one + HALF, HALF)
            scores(s_odd, two)
            soften(s_even, one)
            scores(s_even, pl.multiple_of(one + BK, BK))
            soften(s_odd, two)
            return carry

        per = rows // BK
        scores(s_even, pl.multiple_of(first * rows, rows))
        lax.fori_loop(first * per, last * per, step, 0)

    def conclude(group):
        at = pl.ds(pl.multiple_of(group * rows, rows), rows)
        for h in range(heads):
            part = slice(h * DH, (h + 1) * DH)
            low = acc_ref[group, h, DH : DH + 1, :]
            out = acc_ref[group, h, 0:DH, :] / low
            of_out[part, at] = out
            o_send[group, part, :] = out.astype(bf16)
            lse_out[h : h + 1, at] = top_ref[group, h, 0:1, :] + jnp.log2(low)

        @pl.when(group != g)
        def _():
            o_copy(group).start()

    def o_copy(group):
        return pltpu.make_async_remote_copy(
            src_ref=o_send.at[group],
            dst_ref=o_out.at[g],
            send_sem=o_send_sems.at[group],
            recv_sem=o_recv_sems.at[g],
            device_id=(s, group * repeat + r),
            device_id_type=MESH,
        )

    def arrive(group, low, high):
        def make(j, carry):
            keys(group * repeat + j)
            return carry

        lax.fori_loop(0, repeat, make, 0)
        queries(group)
        whole = high - low + 1 == chunks

        def each(other, carry):
            same = other == group
            attend_to(
                other,
                jnp.where(same, low, group) * repeat,
                (jnp.where(same, high, group) + 1) * repeat,
            )

            @pl.when(whole)
            def _():
                conclude(other)

            return carry

        lax.fori_loop(low, high + 1, each, 0)

    def mates_here():
        for h in range(2):
            for wait in mate_waits[h]:
                wait()
            mate_waits[h] = []

    mates_here()
    arrive(g, g, g)
    weight_service(0)
    for t in range(chunks - 1):
        if t == chunks - 2:
            move(x_all, x_out)
        low, high = g - 1 - t, g + 1 + t
        has_low, has_high = low >= 0, high < chunks

        @pl.when(has_low)
        def _():
            arrive(low, low, jnp.minimum(g + t, chunks - 1))

        @pl.when(has_high & (low < 0))
        def _():
            arrive(high, 0, high)

        token_service(t + 1)
        weight_service(t + 1)

        @pl.when(has_high & has_low)
        def _():
            arrive(high, low, high)

        mates_here()
    for t in range(chunks, blocks + 1):
        weight_service(t)
    settle_late()
    own_out = pltpu.make_async_copy(o_send.at[g], o_out.at[g], here_sems.at[9])
    own_out.start()
    for one in here:
        one.wait()
    for wait in sibling_waits:
        wait()
    for d in range(1, chunks):
        group = lax.rem(g + d, chunks)
        pltpu.make_async_remote_copy(
            src_ref=o_send.at[g],
            dst_ref=o_out.at[group],
            send_sem=o_send_sems.at[g],
            recv_sem=o_recv_sems.at[group],
            device_id=(s, group * repeat + r),
            device_id_type=MESH,
        ).wait_recv()
        o_copy(group).wait_send()
    own_out.wait()
    sender.finish()


def advance(wq, wk, wv, wo, w1, w2, x, code, vec, chunks, heads):
    seqs, count = lax.axis_size("seq"), lax.axis_size("ctx")
    small_rows, model = wq.shape
    tall_rows, wide = w2.shape[0], w1.shape[1]
    rows = x.shape[0]
    mates = block_mates(small_rows)
    blocks, repeat = count // mates, count // chunks
    semaphores = (
        6 * (mates - 1) + 2 * (count - 1) + 2 * (seqs - 1) + 9 * (blocks - 1)
        + 4 * (seqs - 1) * (2 * blocks - 1) + 4 * (seqs * (2 * blocks - 1) - 1) + 4 * (chunks - 1) + 2 * (2 * chunks - 1) * (repeat - 1)
    )
    devices = seqs * count
    width = heads * DH
    length, mine = count * rows, chunks * rows
    padded = -(-3 * width // LANES) * LANES
    shape = jax.ShapeDtypeStruct
    f32, bf16 = jnp.float32, jnp.bfloat16
    vmem, far = pl.BlockSpec(memory_space=pltpu.VMEM), pl.BlockSpec(memory_space=pl.ANY)
    block_rows, block_tall = mates * small_rows, mates * tall_rows
    dma = pltpu.SemaphoreType.DMA
    return pl.pallas_call(
        partial(advance_kernel, seqs, count, chunks, heads),
        out_shape=(
            shape((model, padded), bf16),
            shape((model, model), bf16),
            shape((model, model), bf16),
            shape((model, wide), bf16),
            shape((tall_rows * devices, model), bf16),
            shape((length, model), bf16),
            shape((count, 1, rows), jnp.int32),
            shape((devices, 1, vec.shape[1]), f32),
            shape((heads, length + PAD, DH), bf16),
            shape((width, length), bf16),
            shape((width, length), bf16),
            shape((width, mine), bf16),
            shape((width, mine), f32),
            shape((8, mine), f32),
            shape((chunks, width, rows), bf16),
        ),
        in_specs=[vmem] * 9,
        out_specs=(far,) * 8 + (vmem,) * 6 + (far,),
        scratch_shapes=[
            pltpu.VMEM((mates, 4, small_rows, model), f32),
            pltpu.VMEM((mates, small_rows, wide), f32),
            pltpu.VMEM((mates, tall_rows, model), f32),
            pltpu.VMEM((4, block_rows, model), f32),
            pltpu.VMEM((block_rows, wide), f32),
            pltpu.VMEM((block_tall, model), f32),
            pltpu.VMEM((block_rows, model), bf16),
            pltpu.VMEM((block_rows, model), bf16),
            pltpu.VMEM((block_rows, wide), bf16),
            pltpu.VMEM((block_tall, model), bf16),
            pltpu.VMEM((chunks, block_rows, padded), bf16),
            pltpu.VMEM((model, padded), bf16),
            pltpu.VMEM((length, model), bf16),
            pltpu.VMEM((count, 1, rows), jnp.int32),
            pltpu.VMEM((devices, 1, vec.shape[1]), f32),
            pltpu.VMEM((padded, model), bf16),
            pltpu.VMEM((heads, length + PAD, 2 * DH + DOCS), bf16),
            pltpu.VMEM((heads, DH + 16, length + PAD), bf16),
            pltpu.VMEM((heads, 2 * DH + DOCS, mine), bf16),
            pltpu.VMEM((chunks, heads, 8, rows), f32),
            pltpu.VMEM((chunks, heads, DH + 16, rows), f32),
            pltpu.VMEM((heads, HALF, rows), f32),
            pltpu.VMEM((heads, HALF, rows), f32),
            pltpu.VMEM((chunks, width, rows), bf16),
            dma((semaphores,)),
            dma((semaphores,)),
            dma((10,)),
            dma((chunks,)),
            dma((chunks,)),
        ],
        compiler_params=pltpu.CompilerParams(
            vmem_limit_bytes=63 * 1024 * 1024, collective_id=1, has_side_effects=True
        ),
        name="advance",
    )(wq, wk, wv, wo, w1, w2, x, code, vec)


def added(*parts):
    sum_of = parts[0].astype(jnp.float32)
    for part in parts[1:]:
        sum_of = sum_of + part.astype(jnp.float32)
    return sum_of


class Line:
    def __init__(self, sender, place, size, device, pieces, landing):
        self.sender, self.place, self.size, self.device = sender, place, size, device
        self.pieces, self.landing = pieces, landing
        self.waits = None

    def send(self, t):
        self.waits = []
        for way in range(2):
            rank = self.place if way == 0 else self.size - 1 - self.place
            mirror = (lambda d: d) if way == 0 else (lambda d: self.size - 1 - d)
            goal = jnp.clip(mirror(self.size - 1 - t + rank), 0, self.size - 1)
            sends = rank <= t
            receives = (rank >= 1) & (rank - 1 <= t)
            to = jnp.clip(self.place + (1 - 2 * way), 0, self.size - 1)
            waits = []
            for source, target in zip(self.pieces(goal), self.landing(way, t)):
                waits.append(self.sender.copy(source, target, self.device(to), sends, receives))
            self.waits.append((receives, mirror, rank, waits))

    def receive(self, t):
        for way, (receives, mirror, rank, waits) in enumerate(self.waits):
            goal = jnp.clip(mirror(self.size - 2 - t + rank), 0, self.size - 1)
            pieces, landing = self.pieces(goal), self.landing(way, t)
            for wait, piece, arrived in zip(waits, pieces, landing):
                wait()

                @pl.when(receives)
                def _():
                    piece[...] = added(piece[...], arrived[...]).astype(piece.dtype)


def group_order(chunks):
    table = []
    for g in range(chunks):
        steps = [(chunks - 1 + g - d if d > g else chunks - 1 - g + d, d < g, d) for d in range(chunks) if d != g]
        table.append([d for _, _, d in sorted(steps)] + [g])
    return table


def retreat_kernel(
    seqs, count, chunks, heads,
    do_ref, x_ref, w_ref, wq_ref, k_ref, kt_ref, v_ref, q_ref, o_ref, lse_ref, code_ref,
    dwo_ref, dw1_ref, dw2_ref, dsmall_ref, db1_ref,
    dx_out, dw_out, dwo_out, dw1_out, dw2_out, dsmall_out, db1_out, in1, in2, in4, dx_in,
    do_in, q_ext, do_ext, dq, o_slot, k_slot, x_slot, kt_ext, v_ext, dkv, dw, db,
    s_even, s_odd, g_even, g_odd, dx_send, dq_send, dq_in, w_full, wt,
    dx_sum, dx_line, sum1, sum2, sum4, part1, part2, cube1, cube2, cube4,
    line1, line2, line4, last1, last2, last4, w_mine, w_seq, w_block, w_mates,
    small_in, b1_in, b_in, vec_seq, bias_seq,
    send_sems, recv_sems, here_sems, fetch_sems, part_sems, own_sems, mate_send, mate_recv, dq_send_sems, dq_recv_sems,
):
    s, c = lax.axis_index("seq"), lax.axis_index("ctx")
    f32, bf16 = jnp.float32, jnp.bfloat16
    rows, model = dx_out.shape
    wide = dw1_ref.shape[1]
    repeat = count // chunks
    mates = w_mates.shape[0]
    blocks = count // mates
    block_rows, block_tall = dwo_out.shape[0], dw2_out.shape[0]
    width = heads * DH
    b, i = c // mates, lax.rem(c, mates)
    g, r = c // repeat, lax.rem(c, repeat)
    turn = lax.rem(c, 2)
    half_wide, half_model = wide // 2, model // 2
    slab_rows, slab_tall = blocks * block_rows, blocks * block_tall
    sender = Sender(send_sems, recv_sems)
    here = []

    def move(source, target):
        one = pltpu.make_async_copy(source, target, here_sems.at[len(here)])
        one.start()
        here.append(one)
        return one

    table = group_order(chunks)

    def group_at(index):
        found = table[chunks - 1][index]
        for k in range(chunks - 1):
            found = jnp.where(g == k, table[k][index], found)
        return found

    def fetch(chunk, slot):
        at = pl.ds(pl.multiple_of(chunk * rows, rows), rows)
        sems = fetch_sems.at[slot]
        copies = [
            pltpu.make_async_copy(k_ref.at[:, at, :], k_slot.at[slot], sems.at[0]),
            pltpu.make_async_copy(x_ref.at[at], x_slot.at[slot], sems.at[1]),
        ]
        for h in range(heads):
            part = pl.ds(h * DH, DH)
            for m, (source, target) in enumerate((
                (kt_ref, kt_ext.at[slot, h, pl.ds(0, DH)]),
                (kt_ref, kt_ext.at[slot, h, pl.ds(DH, DH)]),
                (v_ref, v_ext.at[slot, h, pl.ds(0, DH)]),
            )):
                copies.append(pltpu.make_async_copy(source.at[part, at], target, sems.at[2 + 3 * h + m]))
        return copies

    kt_ext[:, :, 2 * DH : 2 * DH + 16, :] = jnp.ones((2, heads, 16, rows), bf16)
    v_ext[:, :, DH:, :] = jnp.ones((2, heads, 16, rows), bf16)
    for one in fetch(group_at(0) * repeat, 0):
        one.start()
    greet(seqs, count)

    do_waits = {}
    for d in range(1, chunks):
        to = lax.rem(g + d, chunks)
        do_waits[chunks - d] = sender.copy(do_ref.at[to], do_in.at[g], (s, to * repeat + r))
    own_do = move(do_ref.at[g], do_in.at[g])

    sibling = (s, c + 1 - 2 * turn)

    def column_half(which):
        wide_at = pl.ds(pl.multiple_of(which * half_wide, half_wide), half_wide)
        model_at = pl.ds(pl.multiple_of(which * half_model, half_model), half_model)
        return dw1_ref.at[:, wide_at], dw2_ref.at[:, model_at], dwo_ref.at[:, model_at]

    half_waits = [
        sender.copy(source, target, sibling)
        for source, target in zip(column_half(1 - turn), (in1, in2, in4))
    ]
    for source, target in zip(column_half(turn), (sum1, sum2, sum4)):
        move(source, target)
    vec_waits = []
    for d in range(1, count):
        to = (s, lax.rem(c + d, count))
        for source, target in ((dsmall_ref, small_in), (db1_ref, b1_in)):
            vec_waits.append(sender.copy(source, target.at[c], to))
    small_in[c] = dsmall_ref[...]
    b1_in[c] = db1_ref[...]

    wt[...] = w_ref[...].astype(f32).T.astype(bf16)
    dw[...] = jnp.zeros(dw.shape, f32)
    db[...] = jnp.zeros(db.shape, f32)
    dq[...] = jnp.zeros(dq.shape, f32)
    one_rows = jnp.ones((8, rows), bf16)

    def queries(group):
        at = pl.ds(pl.multiple_of(group * rows, rows), rows)
        load = pltpu.make_async_copy(o_ref.at[:, at], o_slot, own_sems.at[0])
        load.start()
        load.wait()
        wanted = (code_ref[group * repeat + r] | 1).astype(f32)
        document = lax.broadcasted_iota(jnp.int32, (DOCS, rows), 0).astype(f32)
        away = jnp.where(wanted == 2.0 * document + 1.0, FAR, 0.0)
        for h in range(heads):
            part = slice(h * DH, (h + 1) * DH)
            scaled = q_ref[part, at].astype(f32) * (DH**-0.5 * LOG2E)
            high = scaled.astype(bf16).astype(f32)
            extra = three_parts(-lse_ref[h : h + 1, at])
            full = jnp.concatenate([high, scaled - high, extra, away], axis=0)
            q_ext[h, at, :] = full.T.astype(bf16)
            grad = do_in[group, part, :].astype(f32)
            delta = jnp.sum(grad * o_slot[part, :], axis=0, keepdims=True)
            do_ext[h, at, :] = jnp.concatenate([grad, three_parts(-delta)], axis=0).T.astype(bf16)

    for one in here:
        one.wait()
    queries(g)

    for wait in half_waits:
        wait()
    loads = []
    for target, arrived, part, kind in ((sum1, in1, part1, 0), (sum2, in2, part2, 1), (sum4, in4, part2, 1)):
        size = part.shape[1]
        for k in range(target.shape[0] // size):
            loads.append((target, arrived, part, kind, k * size, size))
    used_slots = [0, 0]
    copies = []
    for target, arrived, part, kind, at, size in loads:
        slot = used_slots[kind] % 2
        used_slots[kind] += 1
        copies.append((
            pltpu.make_async_copy(arrived.at[pl.ds(at, size)], part.at[slot], part_sems.at[kind, slot]), slot
        ))
    copies[0][0].start()
    for n, (target, arrived, part, kind, at, size) in enumerate(loads):
        if n + 1 < len(loads):
            copies[n + 1][0].start()
        copies[n][0].wait()
        rows_at = slice(at, at + size)
        target[rows_at] = added(target[rows_at], part[copies[n][1]]).astype(bf16)

    def slab(seq):
        at = pl.ds(pl.multiple_of(seq * slab_rows, slab_rows), slab_rows)
        tall = pl.ds(pl.multiple_of(seq * slab_tall, slab_tall), slab_tall)
        return sum1.at[at], sum2.at[tall], sum4.at[at]

    masks = cube_steps(seqs, turn)

    def family(seq, rest):
        found = [seq]
        for mask in rest:
            found = found + [across(one, mask) for one in found]
        return found

    cube_waits, used = [], 0

    def cube_send(j):
        nonlocal used
        partner = across(s, masks[j])
        cube_waits.clear()
        mine = family(s, masks[j + 1 :])
        for k, seq in enumerate(family(partner, masks[j + 1 :])):
            landing = cube1.at[used + k], cube2.at[used + k], cube4.at[used + k]
            waits = [
                sender.copy(source, target, (partner, c)) for source, target in zip(slab(seq), landing)
            ]
            cube_waits.append((mine[k], landing, waits))
        used += len(cube_waits)

    def cube_receive():
        for seq, landing, waits in cube_waits:
            for wait, target, arrived in zip(waits, slab(seq), landing):
                wait()
                target[...] = added(target[...], arrived[...]).astype(bf16)

    cube_send(0)

    def block_slab(goal):
        row = s * slab_rows + goal * block_rows
        tall = s * slab_tall + goal * block_tall
        at = pl.ds(pl.multiple_of(row, block_rows), block_rows)
        tall_at = pl.ds(pl.multiple_of(tall, block_tall), block_tall)
        return sum1.at[at], sum2.at[tall_at], sum4.at[at]

    weight_line = Line(
        sender, b, blocks, lambda to: (s, to * mates + i),
        block_slab, lambda way, t: (line1.at[way, t], line2.at[way, t], line4.at[way, t]),
    )
    half_rows = rows // 2
    token_lines = []
    for h in range(2):
        at = pl.ds(h * half_rows, half_rows)
        token_lines.append(
            Line(
                sender, g, chunks, lambda to: (s, to * repeat + r),
                lambda goal, at=at: (dx_sum.at[goal, at],),
                lambda way, t, at=at: (dx_line.at[way, t, at],),
            )
        )

    for d in range(1, chunks):
        do_waits[d]()
        queries(lax.rem(g + d, chunks))

    for wait in vec_waits:
        wait()
    vec_waits = []
    small, tall = small_in[0], b1_in[0]
    for k in range(1, count):
        small = small + small_in[k]
        tall = tall + b1_in[k]
    vec_seq[s, 0:8, 0:model] = small
    vec_seq[s, 0:1, model:] = tall
    vec_seq[s, 1:8, model:] = jnp.zeros((7, wide), f32)
    for d in range(1, seqs):
        vec_waits.append(sender.copy(vec_seq.at[s], vec_seq.at[s], (lax.rem(s + d, seqs), c)))

    weight_steps = blocks - 1
    pending = []

    def cube_turn(j):
        cube_receive()
        if j + 1 < len(masks):
            cube_send(j + 1)
        elif weight_steps:
            weight_line.send(0)

    def line_turn(t):
        weight_line.receive(t)
        if t + 1 < weight_steps:
            weight_line.send(t + 1)

    pending += [partial(cube_turn, j) for j in range(len(masks))]
    pending += [partial(line_turn, t) for t in range(weight_steps)]

    def scores(s_slot, g_slot, slot, group, half):
        at = pl.ds(pl.multiple_of(group * rows, rows), rows)
        key = pl.ds(half * HALF, HALF)
        for h in range(heads):
            s_slot[h] = nn(q_ext[h, at, :], kt_ext[slot, h, :, key])
            g_slot[h] = nn(do_ext[h, at, :], v_ext[slot, h, :, key])

    def absorb(s_slot, g_slot, slot, group, half):
        at = pl.ds(pl.multiple_of(group * rows, rows), rows)
        key = pl.ds(half * HALF, HALF)
        for h in range(heads):
            part = slice(h * DH, (h + 1) * DH)
            p = jnp.exp2(s_slot[h])
            ds = (p * g_slot[h]).astype(bf16)
            dkv[width + h * DH : width + (h + 1) * DH, key] += nn(do_in[group, part, :], p.astype(bf16))
            dkv[part, key] += nn(q_ref[part, at], ds)
            dq[h, at, :] += nn(ds, k_slot[slot, h, key, :])

    def next_group(p):
        return lax.rem(g + p, chunks)

    def one_chunk(chunk, following, slot, conclude):
        for one in fetch(chunk, slot):
            one.wait()
        if following is not None:
            for one in fetch(following, 1 - slot):
                one.start()
        document = lax.broadcasted_iota(jnp.int32, (DOCS, rows), 0).astype(f32)
        away = jnp.where(code_ref[chunk].astype(f32) == 2.0 * document + 1.0, 0.0, 1.0).astype(bf16)
        for h in range(heads):
            kt_ext[slot, h, 2 * DH + 16 :, :] = away
        dkv[...] = jnp.zeros(dkv.shape, f32)
        scores(s_even, g_even, slot, next_group(1), 0)

        def turn_of(p, carry):
            group = next_group(p)
            absorb(s_even, g_even, slot, group, 0)
            scores(s_odd, g_odd, slot, group, 1)
            absorb(s_odd, g_odd, slot, group, 1)
            scores(s_even, g_even, slot, next_group(p + 1), 0)
            if conclude is not None:
                conclude(group)
            return carry

        lax.fori_loop(1, chunks + 1, turn_of, 0)

    def mate_copy(group, to, slot):
        return pltpu.make_async_remote_copy(
            src_ref=dx_send.at[slot],
            dst_ref=dx_in.at[slot, group],
            send_sem=mate_send.at[slot],
            recv_sem=mate_recv.at[slot, group],
            device_id=(s, g * repeat + to),
            device_id_type=MESH,
        )

    def keep(group, j, slot):
        dk = (dkv[0:width, :] * DH**-0.5).astype(bf16)
        dv = dkv[width:, :].astype(bf16)
        both = jnp.concatenate([dk, dv], axis=0)
        dx = tn(both, wt[width : 3 * width, :]).astype(bf16)
        dw[width : 3 * width, :] += nn(both, x_slot[slot])
        db[0:8, width:] += nt(one_rows, dv)

        @pl.when(j == r)
        def _():
            dx_sum[group] = dx

        @pl.when(j != r)
        def _():
            to = lax.rem(j - r + repeat, repeat) - 1
            dx_send[to] = dx
            mate_copy(group, j, to).start()

    spare = chunks * repeat % 2

    def conclude(group):
        at = pl.ds(pl.multiple_of(group * rows, rows), rows)
        from_x = pl.ds(pl.multiple_of((group * repeat + r) * rows, rows), rows)
        load = pltpu.make_async_copy(x_ref.at[from_x], x_slot.at[spare], own_sems.at[1])
        load.start()
        grad = jnp.concatenate([dq[h, at, :] for h in range(heads)], axis=1) * DH**-0.5
        dq_send[group] = grad.T.astype(bf16)

        @pl.when(group != g)
        def _():
            dq_copy(group).start()

        low = grad.astype(bf16)
        db[0:8, 0:width] += nn(one_rows, low)
        load.wait()
        dw[0:width, :] += nn(dq_send[group], x_slot[spare])

    def dq_copy(group):
        return pltpu.make_async_remote_copy(
            src_ref=dq_send.at[group],
            dst_ref=dq_in.at[g],
            send_sem=dq_send_sems.at[group],
            recv_sem=dq_recv_sems.at[g],
            device_id=(s, group * repeat + r),
            device_id_type=MESH,
        )

    def gather_mates(group):
        for d in range(1, repeat):
            mate_copy(group, lax.rem(r + d, repeat), d - 1).wait()
        loads = [
            pltpu.make_async_copy(dx_in.at[d, group], dx_send.at[d], mate_send.at[d]) for d in range(repeat - 1)
        ]
        for load in loads:
            load.start()
        for load in loads:
            load.wait()
        terms = [dx_send[d] for d in range(repeat - 1)]
        dx_sum[group] = added(dx_sum[group], *terms).astype(bf16)

    for index in range(chunks):
        group = group_at(index)
        for j in range(repeat):
            position = index * repeat + j
            slot = position % 2
            final = position + 1 == chunks * repeat
            if j + 1 < repeat:
                following = group * repeat + j + 1
            elif not final:
                following = group_at(index + 1) * repeat
            else:
                following = None
            one_chunk(group * repeat + j, following, slot, conclude if final else None)
            keep(group, j, slot)
            if j == 0 and index == chunks - 1 and pending:
                pending.pop(0)()
        gather_mates(group)
        if index >= 1:
            for line in token_lines:
                line.receive(index - 1)
        if index < chunks - 1:
            for line in token_lines:
                line.send(index)
            if pending:
                pending.pop(0)()

    w_full[...] = dw[...].T.astype(bf16)
    w_waits = []
    for d in range(1, seqs):
        to = lax.rem(s + d, seqs)
        source = w_full.at[pl.ds(pl.multiple_of(to * slab_rows, slab_rows), slab_rows)]
        w_waits.append(sender.copy(source, w_seq.at[d - 1], (to, c)))
    b_waits = []
    b_in[c] = db[0:1, :]
    for d in range(1, count):
        b_waits.append(sender.copy(b_in.at[c], b_in.at[c], (s, lax.rem(c + d, count))))
    while pending:
        pending.pop(0)()
    last_waits = []
    for source, target in zip(block_slab(b), (last1, last2, last4)):
        target[i] = source[...]
        for d in range(1, mates):
            to = (s, b * mates + lax.rem(i + d, mates))
            last_waits.append(sender.copy(source, target.at[i], to))
    for wait in b_waits:
        wait()
    b_waits = []
    pair = []
    for k in range(chunks):
        one = b_in[k * repeat]
        for d in range(1, repeat):
            one = one + b_in[k * repeat + d]
        pair.append(one)
    for m in range(2):
        joined = jnp.concatenate([one[:, m * width : (m + 1) * width] for one in pair], axis=1)
        bias_seq[s, m : m + 1, :] = joined
    bias_seq[s, 2:8, :] = jnp.zeros((6, model), f32)
    for d in range(1, seqs):
        b_waits.append(sender.copy(bias_seq.at[s], bias_seq.at[s], (lax.rem(s + d, seqs), c)))
    for wait in w_waits:
        wait()
    w_mine[...] = added(
        w_full[pl.ds(pl.multiple_of(s * slab_rows, slab_rows), slab_rows), :],
        *[w_seq[d] for d in range(seqs - 1)],
    ).astype(bf16)
    w_waits = []
    for d in range(1, blocks):
        to = lax.rem(b + d, blocks)
        source = w_mine.at[pl.ds(pl.multiple_of(to * block_rows, block_rows), block_rows)]
        w_waits.append(sender.copy(source, w_block.at[b], (s, to * mates + i)))
    w_block[b] = w_mine[pl.ds(pl.multiple_of(b * block_rows, block_rows), block_rows), :]

    dq_in[g] = dq_send[g]
    for d in range(1, chunks):
        group = lax.rem(g + d, chunks)
        pltpu.make_async_remote_copy(
            src_ref=dq_send.at[g],
            dst_ref=dq_in.at[group],
            send_sem=dq_send_sems.at[g],
            recv_sem=dq_recv_sems.at[group],
            device_id=(s, group * repeat + r),
            device_id_type=MESH,
        ).wait_recv()
        dq_copy(group).wait_send()
    part = nn(wq_ref[...], dq_in[...].reshape(chunks * width, rows))
    dx_out[...] = dx_sum[g].astype(f32) + part.T

    for wait in w_waits:
        wait()
    w_waits = []
    w_mates[i] = w_block[...]
    for d in range(1, mates):
        to = (s, b * mates + lax.rem(i + d, mates))
        w_waits.append(sender.copy(w_block, w_mates.at[i], to))
    for wait in vec_waits + b_waits + last_waits:
        wait()
    for target, source in ((dw1_out, last1), (dw2_out, last2), (dwo_out, last4)):
        size = target.shape[1] // 2
        for which in range(2):
            target[:, which * size : (which + 1) * size] = added(
                *[source[k] for k in range(which, mates, 2)]
            )
    vec, bias = vec_seq[0], bias_seq[0]
    for d in range(1, seqs):
        vec = vec + vec_seq[d]
        bias = bias + bias_seq[d]
    dsmall_out[0:6, :] = vec[0:6, 0:model]
    dsmall_out[6:8, :] = bias[0:2]
    db1_out[...] = vec[:, model:]
    for wait in w_waits:
        wait()
    for k in range(chunks):
        terms = [
            w_mates[p, q]
            for p in range(mates)
            for q in range(blocks)
            if (q * mates + p) // repeat == k
        ]
        dw_out[k] = added(*terms)
    sender.finish()


def retreat(do, x, w, wq, k, kt, v, q, o, lse, codes, dwo, dw1, dw2, dsmall, db1, heads):
    seqs, count = lax.axis_size("seq"), lax.axis_size("ctx")
    chunks, width, rows = do.shape
    model = x.shape[1]
    wide, tall = dw1.shape[1], dw2.shape[0]
    devices = seqs * count
    mates = block_mates(model // devices)
    blocks, repeat = count // mates, count // chunks
    block_rows, block_tall = mates * (model // devices), mates * (tall // devices)
    slab_rows, slab_tall = blocks * block_rows, blocks * block_tall
    padded = w.shape[1]
    mine = chunks * rows
    semaphores = (
        (chunks - 1) + 3 + 2 * (count - 1) + (seqs - 1) + 3 * (seqs - 1) + 6 * (blocks - 1)
        + 4 * (chunks - 1) + (seqs - 1) + (count - 1) + 3 * (mates - 1) + (seqs - 1) + (blocks - 1) + (mates - 1)
    )
    shape = jax.ShapeDtypeStruct
    f32, bf16 = jnp.float32, jnp.bfloat16
    vmem, far = pl.BlockSpec(memory_space=pltpu.VMEM), pl.BlockSpec(memory_space=pl.ANY)
    half_wide, half_model = wide // 2, model // 2
    triple = lambda lead, a, t: [
        pltpu.VMEM(lead + (a, half_wide), bf16),
        pltpu.VMEM(lead + (t, half_model), bf16),
        pltpu.VMEM(lead + (a, half_model), bf16),
    ]
    dma = pltpu.SemaphoreType.DMA
    return pl.pallas_call(
        partial(retreat_kernel, seqs, count, chunks, heads),
        out_shape=(
            shape((rows, model), f32),
            shape((chunks, block_rows, padded), f32),
            shape((block_rows, model), f32),
            shape((block_rows, wide), f32),
            shape((block_tall, model), f32),
            shape((8, model), f32),
            shape((8, wide), f32),
            shape((model, half_wide), bf16),
            shape((tall, half_model), bf16),
            shape((model, half_model), bf16),
            shape((repeat - 1, chunks, rows, model), bf16),
        ),
        in_specs=[far, far, vmem, vmem, far, far, far, vmem, far, vmem, vmem, far, far, far, vmem, vmem],
        out_specs=(vmem,) * 7 + (far,) * 4,
        scratch_shapes=[
            pltpu.VMEM((chunks, width, rows), bf16),
            pltpu.VMEM((heads, mine, 2 * DH + 16 + DOCS), bf16),
            pltpu.VMEM((heads, mine, DH + 16), bf16),
            pltpu.VMEM((heads, mine, DH), f32),
            pltpu.VMEM((width, rows), f32),
            pltpu.VMEM((2, heads, rows, DH), bf16),
            pltpu.VMEM((2, rows, model), bf16),
            pltpu.VMEM((2, heads, 2 * DH + 16 + DOCS, rows), bf16),
            pltpu.VMEM((2, heads, DH + 16, rows), bf16),
            pltpu.VMEM((2 * width, rows), f32),
            pltpu.VMEM((padded, model), f32),
            pltpu.VMEM((8, 2 * width), f32),
        ]
        + [pltpu.VMEM((heads, rows, HALF), f32)] * 4
        + [
            pltpu.VMEM((repeat - 1, rows, model), bf16),
            pltpu.VMEM((chunks, width, rows), bf16),
            pltpu.VMEM((chunks, width, rows), bf16),
            pltpu.VMEM((model, padded), bf16),
            pltpu.VMEM((padded, model), bf16),
            pltpu.VMEM((chunks, rows, model), bf16),
            pltpu.VMEM((2, chunks - 1, rows, model), bf16),
        ]
        + triple((), model, tall)
        + [pltpu.VMEM((2, model // 8, half_wide), bf16), pltpu.VMEM((2, model // 2, half_model), bf16)]
        + triple((seqs - 1,), slab_rows, slab_tall)
        + triple((2, blocks - 1), block_rows, block_tall)
        + triple((mates,), block_rows, block_tall)
        + [
            pltpu.VMEM((slab_rows, padded), bf16),
            pltpu.VMEM((seqs - 1, slab_rows, padded), bf16),
            pltpu.VMEM((blocks, block_rows, padded), bf16),
            pltpu.VMEM((mates, blocks, block_rows, padded), bf16),
            pltpu.VMEM((count, 8, model), f32),
            pltpu.VMEM((count, 1, wide), f32),
            pltpu.VMEM((count, 1, 2 * width), f32),
            pltpu.VMEM((seqs, 8, model + wide), f32),
            pltpu.VMEM((seqs, 8, model), f32),
            dma((semaphores,)),
            dma((semaphores,)),
            dma((8,)),
            dma((2, 2 + 3 * heads)),
            dma((2, 2)),
            dma((2,)),
            dma((repeat - 1,)),
            dma((repeat - 1, chunks)),
            dma((chunks,)),
            dma((chunks,)),
        ],
        compiler_params=pltpu.CompilerParams(
            vmem_limit_bytes=63 * 1024 * 1024, collective_id=2, has_side_effects=True
        ),
        name="retreat",
    )(do, x, w, wq, k, kt, v, q, o, lse, codes, dwo, dw1, dw2, dsmall, db1)


def pick(values, size, device):
    wide = values.shape[1]
    row = lax.broadcasted_iota(jnp.int32, (wide, size), 0)
    column = lax.broadcasted_iota(jnp.int32, (wide, size), 1)
    chosen = (row == column + device * size).astype(jnp.bfloat16)
    high = values.astype(jnp.bfloat16)
    rest = values - high.astype(jnp.float32)
    middle_part = rest.astype(jnp.bfloat16)
    low = (rest - middle_part.astype(jnp.float32)).astype(jnp.bfloat16)
    return nn(high, chosen) + nn(middle_part, chosen) + nn(low, chosen)


def finish_kernel(
    count, mates,
    e1_ref, dx_ref, dw_ref, dwo_ref, dw1_ref, dw2_ref, small_ref, b1_ref,
    dx_out, dwq_out, dwk_out, dwv_out, dwo_out, dw1_out, dw2_out, small_out, b1_out,
):
    s, c = lax.axis_index("seq"), lax.axis_index("ctx")
    dx_out[...] = e1_ref[...] + dx_ref[...].astype(jnp.float32)
    each, tall = dwo_out.shape[0], dw2_out.shape[0]
    chunks = dw_ref.shape[0]
    width = dwq_out.shape[1] // chunks
    i = lax.rem(c, mates)
    for p in range(mates):
        rows = slice(p * each, (p + 1) * each)

        @pl.when(i == p)
        def _():
            for m, out in enumerate((dwq_out, dwk_out, dwv_out)):
                parts = [dw_ref[k, rows, m * width : (m + 1) * width] for k in range(chunks)]
                out[...] = jnp.concatenate(parts, axis=1)
            dwo_out[...] = dwo_ref[rows, :]
            dw1_out[...] = dw1_ref[rows, :]
            dw2_out[...] = dw2_ref[p * tall : (p + 1) * tall, :]

    device = s * count + c
    small_out[...] = pick(small_ref[...], each, device)
    b1_out[...] = pick(b1_ref[...], tall, device)


def finish(e1, dx, dw, dwo, dw1, dw2, small, b1):
    count = lax.axis_size("ctx")
    devices = count * lax.axis_size("seq")
    model, wide = dwo.shape[1], dw1.shape[1]
    each, tall = model // devices, wide // devices
    shape = jax.ShapeDtypeStruct
    f32 = jnp.float32
    vmem = pl.BlockSpec(memory_space=pltpu.VMEM)
    return pl.pallas_call(
        partial(finish_kernel, count, block_mates(each)),
        out_shape=(shape(e1.shape, f32),)
        + (shape((each, model), f32),) * 4
        + (shape((each, wide), f32), shape((tall, model), f32), shape((8, each), f32), shape((8, tall), f32)),
        in_specs=[vmem] * 8,
        out_specs=(vmem,) * 9,
        compiler_params=pltpu.CompilerParams(vmem_limit_bytes=VMEM_LIMIT),
        name="finish",
    )(e1, dx, dw, dwo, dw1, dw2, small, b1)


def on_device(
    tokens, segment_ids, valid_tokens, query_weight, query_bias, key_weight, value_weight, value_bias,
    output_weight, output_bias, attn_norm_gain, attn_norm_shift, up_weight, up_bias, down_weight,
    down_bias, ffn_norm_gain, ffn_norm_shift, out_cotangent,
):
    count = lax.axis_size("ctx")
    chunks = math.gcd(H, count)
    heads = H // chunks
    x = tokens[0]
    vec = jnp.concatenate([
        output_bias, attn_norm_gain, attn_norm_shift, down_bias, ffn_norm_gain, ffn_norm_shift,
        query_bias, value_bias, up_bias,
    ])
    vec = jnp.pad(vec, (0, -vec.shape[0] % LANES))[None]
    w, wo, wq, w1, w2, x_all, codes, vecs, k, kt, v, q, o_float, lse, o = advance(
        query_weight, key_weight, value_weight, output_weight, up_weight, down_weight,
        x, segment_ids * 2 + valid_tokens, vec, chunks, heads,
    )
    output, e1, do, dwo, dw1, dw2, dsmall, db1 = middle(
        o, x, out_cotangent[0], wo, w1, w2, vecs
    )
    summed = retreat(
        do, x_all, w, wq, k, kt, v, q, o_float, lse, codes, dwo, dw1, dw2, dsmall, db1, heads
    )[:7]
    grad, dwq, dwk, dwv, dwo, dw1, dw2, small, b1 = finish(e1, *summed)
    return (
        output[None], grad[None],
        dwq, small[6], dwk, dwv, small[7],
        dwo, small[0], small[1], small[2],
        dw1, b1[0], dw2, small[3], small[4], small[5],
    )


def solution(mesh):
    in_specs = (
        P("seq", "ctx", None),
        P("seq", "ctx"),
        P("seq", "ctx"),
        P(("seq", "ctx"), None),
        P(("seq", "ctx")),
        P(("seq", "ctx"), None),
        P(("seq", "ctx"), None),
        P(("seq", "ctx")),
        P(("seq", "ctx"), None),
        P(("seq", "ctx")),
        P(("seq", "ctx")),
        P(("seq", "ctx")),
        P(("seq", "ctx"), None),
        P(("seq", "ctx")),
        P(("seq", "ctx"), None),
        P(("seq", "ctx")),
        P(("seq", "ctx")),
        P(("seq", "ctx")),
        P("seq", "ctx", None),
    )
    out_specs = (
        P("seq", "ctx", None),
        P("seq", "ctx", None),
        P(("seq", "ctx"), None),
        P(("seq", "ctx")),
        P(("seq", "ctx"), None),
        P(("seq", "ctx"), None),
        P(("seq", "ctx")),
        P(("seq", "ctx"), None),
        P(("seq", "ctx")),
        P(("seq", "ctx")),
        P(("seq", "ctx")),
        P(("seq", "ctx"), None),
        P(("seq", "ctx")),
        P(("seq", "ctx"), None),
        P(("seq", "ctx")),
        P(("seq", "ctx")),
        P(("seq", "ctx")),
    )
    return jax.shard_map(
        on_device, mesh=mesh, in_specs=in_specs, out_specs=out_specs, check_vma=False
    )
```

```python
import math
from functools import partial

import jax
import jax.numpy as jnp
from jax import lax
from jax.experimental import pallas as pl
from jax.experimental.pallas import tpu as pltpu
from jax.sharding import PartitionSpec as P

H = 12
DH = 64
VMEM_LIMIT = 60 * 1024 * 1024

LOG2E = 1.4426950408889634
BQ = 512
BK = 512
HALF = BK // 2
PAD = BK + HALF
DOCS = 64
FAR = -(2.0**100)
LANES = 128


def nt(a, b):
    return lax.dot_general(a, b, (((1,), (1,)), ((), ())), preferred_element_type=jnp.float32)


def nn(a, b):
    return lax.dot_general(a, b, (((1,), (0,)), ((), ())), preferred_element_type=jnp.float32)


def unshard(vec, at, each):
    devices = vec.shape[0]
    shard = vec[:, at : at + each].astype(jnp.bfloat16)
    size = devices * each
    owner = lambda shape, axis: jnp.floor(
        (lax.broadcasted_iota(jnp.int32, shape, axis).astype(jnp.float32) + 0.5) / each
    )
    column = lax.broadcasted_iota(jnp.int32, (each, size), 1).astype(jnp.float32)
    inner = column - owner((each, size), 1) * each
    place = lax.broadcasted_iota(jnp.int32, (each, size), 0).astype(jnp.float32)
    repeated = nn(shard, (inner == place).astype(jnp.bfloat16))
    device = lax.broadcasted_iota(jnp.int32, (devices, size), 0).astype(jnp.float32)
    return jnp.sum(jnp.where(owner((devices, size), 1) == device, repeated, 0.0), axis=0, keepdims=True)


def tn(a, b):
    return lax.dot_general(a, b, (((0,), (0,)), ((), ())), preferred_element_type=jnp.float32)


def three_parts(row):
    high = row.astype(jnp.bfloat16)
    rest = row - high.astype(jnp.float32)
    middle = rest.astype(jnp.bfloat16)
    low = (rest - middle.astype(jnp.float32)).astype(jnp.bfloat16)
    empty = jnp.zeros((13, row.shape[1]), jnp.float32)
    return jnp.concatenate(
        [high.astype(jnp.float32), middle.astype(jnp.float32), low.astype(jnp.float32), empty], axis=0
    )


EPSILON = 1e-12
FF_BLOCK = 512


def gelu_pair(u):
    z = jnp.abs(u) * (0.5**0.5)
    t = 1.0 / (1.0 + 0.3275911 * z)
    bell = jnp.exp(-z * z)
    poly = t * (
        0.254829592 + t * (-0.284496736 + t * (1.421413741 + t * (-1.453152027 + t * 1.061405429)))
    )
    half = 0.5 * poly * bell
    below = jnp.where(u < 0.0, half, 1.0 - half)
    return u * below, below + u * bell * 0.3989422804014327


def standard(hidden):
    centred = hidden - jnp.mean(hidden, axis=-1, keepdims=True)
    scale = lax.rsqrt(jnp.mean(centred * centred, axis=-1, keepdims=True) + EPSILON)
    return centred * scale, scale


def norm_back(grad, gain, normal, scale):
    t = grad * gain
    return scale * (
        t
        - jnp.mean(t, axis=-1, keepdims=True)
        - normal * jnp.mean(t * normal, axis=-1, keepdims=True)
    )


def middle_kernel(
    o_ref, x_ref, cot_ref, wo_ref, w1_ref, w2_ref, vec_ref,
    out_ref, e1_ref, do_ref, dwo_ref, dw1_ref, dw2_ref, dsmall_ref, db1_ref,
    act, slope, y1_ref, normal_ref, r2_ref, y1t_ref, grad_ref, small_ref, b1_ref,
    wo, w1, w2, out1, out2, y1low_ref, even, odd, wo_sem, in_sems, out_sems,
):
    bf16 = jnp.bfloat16
    load = pltpu.make_async_copy(wo_ref, wo, wo_sem)
    load.start()

    def fetch(i):
        at = pl.ds(pl.multiple_of(i * FF_BLOCK, FF_BLOCK), FF_BLOCK)
        return (
            pltpu.make_async_copy(w1_ref.at[:, at], w1.at[:, at], in_sems.at[0, i]),
            pltpu.make_async_copy(w2_ref.at[at], w2.at[at], in_sems.at[1, i]),
        )

    def deliver(i):
        at = pl.ds(pl.multiple_of(i * FF_BLOCK, FF_BLOCK), FF_BLOCK)
        slot = lax.rem(i, 2)
        return (
            pltpu.make_async_copy(out1.at[slot], dw1_ref.at[:, at], out_sems.at[0, slot]),
            pltpu.make_async_copy(out2.at[slot], dw2_ref.at[at], out_sems.at[1, slot]),
        )

    for i in range(w1_ref.shape[1] // FF_BLOCK):
        for one in fetch(i):
            one.start()
    groups, width, rows = o_ref.shape
    hidden_width = w1_ref.shape[1]
    steps = hidden_width // FF_BLOCK
    vec = vec_ref[:, 0, :]
    each = x_ref.shape[1] // vec.shape[0]
    for i in range(6):
        small_ref[i : i + 1, :] = unshard(vec, i * each, each)
    b1_ref[0:1, :] = unshard(vec, 8 * each, hidden_width // vec.shape[0])
    row = lambda i: small_ref[i : i + 1, :]
    ones = jnp.ones((8, rows), bf16)
    load.wait()
    o = o_ref[...].reshape(groups * width, rows)
    n1 = x_ref[...].astype(jnp.float32) + (tn(o, wo[...]) + row(0))
    normal, scale_one = standard(n1)
    normal_ref[...] = normal
    y1 = normal * row(1) + row(2)
    y1_ref[...] = y1
    y1_low = y1.astype(bf16)
    y1t_ref[...] = y1.T.astype(bf16)
    grad_ref[...] = jnp.zeros(grad_ref.shape, jnp.float32)

    def rise(slot, i):
        for one in fetch(i):
            one.wait()
        at = pl.ds(pl.multiple_of(i * FF_BLOCK, FF_BLOCK), FF_BLOCK)
        slot[...] = nn(y1low_ref[...], w1[:, at]) + b1_ref[0:1, at]

    def activate(slot, i):
        at = pl.ds(pl.multiple_of(i * FF_BLOCK, FF_BLOCK), FF_BLOCK)
        value, gradient = gelu_pair(slot[...])
        value = value.astype(bf16)
        act[:, at] = value
        slope[:, at] = gradient
        grad_ref[...] += nn(value, w2[at, :])

    y1low_ref[...] = y1_low
    rise(even, 0)

    def forward(k, carry):
        rise(odd, 2 * k + 1)
        activate(even, 2 * k)
        rise(even, 2 * k + 2)
        activate(odd, 2 * k + 1)
        return carry

    lax.fori_loop(0, steps // 2 - 1, forward, 0)
    rise(odd, steps - 1)
    activate(even, steps - 2)
    activate(odd, steps - 1)
    normal_two, scale_two = standard(y1_ref[...] + (grad_ref[...] + row(3)))
    out_ref[...] = normal_two * row(4) + row(5)
    cot = cot_ref[...].astype(jnp.float32)
    dsmall_ref[4:5, :] = jnp.sum(cot * normal_two, axis=0, keepdims=True)
    dsmall_ref[5:6, :] = jnp.sum(cot, axis=0, keepdims=True)
    e2 = norm_back(cot, row(4), normal_two, scale_two)
    grad_ref[...] = e2
    r2 = e2.astype(bf16)
    r2_ref[...] = r2
    dsmall_ref[3:4, :] = nn(ones, r2)[0:1]

    def backward(i, carry):
        at = pl.ds(pl.multiple_of(i * FF_BLOCK, FF_BLOCK), FF_BLOCK)
        slot = lax.rem(i, 2)

        @pl.when(i >= 2)
        def _():
            for one in deliver(i - 2):
                one.wait()

        out2[slot] = tn(act[:, at], r2_ref[...]).astype(bf16)
        du = (nt(r2_ref[...], w2[at, :]) * slope[:, at]).astype(bf16)
        db1_ref[:, at] = nn(ones, du)[0:1]
        out1[slot] = nn(y1t_ref[...], du).astype(bf16)
        for one in deliver(i):
            one.start()
        grad_ref[...] += nt(du, w1[:, at])
        return carry

    lax.fori_loop(0, steps, backward, 0)
    grad = grad_ref[...]
    normal = normal_ref[...]
    dsmall_ref[1:2, :] = jnp.sum(grad * normal, axis=0, keepdims=True)
    dsmall_ref[2:3, :] = jnp.sum(grad, axis=0, keepdims=True)
    e1 = norm_back(grad, row(1), normal, scale_one)
    e1_ref[...] = e1
    r1 = e1.astype(bf16)
    dsmall_ref[0:1, :] = nn(ones, r1)[0:1]
    dsmall_ref[6:8, :] = jnp.zeros((2, dsmall_ref.shape[1]), jnp.float32)
    dwo_ref[...] = nn(o, r1).astype(bf16)
    for i in (steps - 2, steps - 1):
        for one in deliver(i):
            one.wait()
    do_ref[...] = nt(wo[...], r1).astype(bf16).reshape(groups, width, rows)


def middle(o, x, cot, wo, w1, w2, vec):
    groups, width, rows = o.shape
    model = x.shape[1]
    hidden_width = w1.shape[1]
    shape = jax.ShapeDtypeStruct
    whole, far = pl.BlockSpec(memory_space=pltpu.VMEM), pl.BlockSpec(memory_space=pl.ANY)
    f32, bf16 = jnp.float32, jnp.bfloat16
    return pl.pallas_call(
        middle_kernel,
        out_shape=(
            shape((rows, model), f32),
            shape((rows, model), f32),
            shape(o.shape, bf16),
            shape(wo.shape, bf16),
            shape(w1.shape, bf16),
            shape(w2.shape, bf16),
            shape((8, model), f32),
            shape((1, hidden_width), f32),
        ),
        in_specs=[whole] * 3 + [far] * 3 + [whole],
        out_specs=(whole,) * 4 + (far,) * 2 + (whole,) * 2,
        scratch_shapes=[
            pltpu.VMEM((rows, hidden_width), bf16),
            pltpu.VMEM((rows, hidden_width), f32),
            pltpu.VMEM((rows, model), f32),
            pltpu.VMEM((rows, model), f32),
            pltpu.VMEM((rows, model), bf16),
            pltpu.VMEM((model, rows), bf16),
            pltpu.VMEM((rows, model), f32),
            pltpu.VMEM((8, model), f32),
            pltpu.VMEM((8, hidden_width), f32),
            pltpu.VMEM(wo.shape, bf16),
            pltpu.VMEM(w1.shape, bf16),
            pltpu.VMEM(w2.shape, bf16),
            pltpu.VMEM((2, model, FF_BLOCK), bf16),
            pltpu.VMEM((2, FF_BLOCK, model), bf16),
            pltpu.VMEM((rows, model), bf16),
            pltpu.VMEM((rows, FF_BLOCK), f32),
            pltpu.VMEM((rows, FF_BLOCK), f32),
            pltpu.SemaphoreType.DMA,
            pltpu.SemaphoreType.DMA((2, hidden_width // FF_BLOCK)),
            pltpu.SemaphoreType.DMA((2, 2)),
        ],
        compiler_params=pltpu.CompilerParams(vmem_limit_bytes=VMEM_LIMIT),
        name="middle",
    )(o, x, cot, wo, w1, w2, vec)


MESH = pl.DeviceIdType.MESH


class Sender:
    def __init__(self, send_sems, recv_sems):
        self.send_sems, self.recv_sems, self.used, self.open = send_sems, recv_sems, 0, []

    def copy(self, source, target, device, when=None, until=None):
        index = self.used
        self.used += 1
        one = pltpu.make_async_remote_copy(
            src_ref=source,
            dst_ref=target,
            send_sem=self.send_sems.at[index],
            recv_sem=self.recv_sems.at[index],
            device_id=device,
            device_id_type=MESH,
        )
        if when is None:
            one.start()
        else:
            pl.when(when)(one.start)
        self.open.append((one, when))

        def arrive():
            if until is None:
                one.wait_recv()
            else:
                pl.when(until)(one.wait_recv)

        return arrive

    def finish(self):
        for one, when in self.open:
            if when is None:
                one.wait_send()
            else:
                pl.when(when)(one.wait_send)


def greet(seqs, count):
    s, c = lax.axis_index("seq"), lax.axis_index("ctx")
    barrier = pltpu.get_barrier_semaphore()
    for d in range(1, count):
        pl.semaphore_signal(barrier, inc=1, device_id=(s, lax.rem(c + d, count)), device_id_type=MESH)
    for d in range(1, seqs):
        pl.semaphore_signal(barrier, inc=1, device_id=(lax.rem(s + d, seqs), c), device_id_type=MESH)
    pl.semaphore_wait(barrier, count - 1 + seqs - 1)


def cube_steps(seqs, turn):
    bits = seqs.bit_length() - 1
    masks = []
    for j in range(bits):
        bit = lax.rem(j + turn, bits)
        mask = 0
        for k in range(bits):
            mask = mask + jnp.where(bit == k, 1 << k, 0)
        masks.append(mask)
    return masks


def across(s, mask):
    return s + mask * (1 - 2 * lax.rem(s // mask, 2))


def block_mates(rows):
    mates = 1
    while (mates * rows) % 16:
        mates *= 2
    return mates


def advance_kernel(
    seqs, count, chunks, heads,
    wq_ref, wk_ref, wv_ref, wo_ref, w1_ref, w2_ref, x_ref, seg_ref, val_ref, vec_ref,
    w_out, wo_out, wq_out, w1_out, w2_out, x_out, code_out, vec_out,
    k_out, kt_out, v_out, q_out, of_out, lse_out, o_out,
    stage4, stage1, stage2, flat4, flat1, flat2, low4, lowq, low1, low2, share4,
    w_all, x_all, codes, vecs, wt, k_ext, v_ext, q_ext, top_ref, acc_ref, s_even, s_odd, o_send,
    send_sems, recv_sems, here_sems, o_send_sems, o_recv_sems,
):
    s, c = lax.axis_index("seq"), lax.axis_index("ctx")
    f32, bf16 = jnp.float32, jnp.bfloat16
    small_rows, model = wq_ref.shape
    tall_rows, wide = w2_ref.shape[0], w1_ref.shape[1]
    mates = block_mates(small_rows)
    blocks = count // mates
    b, i = c // mates, lax.rem(c, mates)
    turn = lax.rem(c, 2)
    repeat = count // chunks
    g, r = c // repeat, lax.rem(c, repeat)
    width = heads * DH
    rows = x_ref.shape[0]
    length = count * rows
    block_rows, block_tall = mates * small_rows, mates * tall_rows
    sender = Sender(send_sems, recv_sems)
    here = []

    def move(source, target):
        one = pltpu.make_async_copy(source, target, here_sems.at[len(here)])
        one.start()
        here.append(one)

    greet(seqs, count)

    def tokens_at(place, half):
        start = pl.multiple_of(place * rows + half * (rows // 2), rows // 2)
        return pl.ds(start, rows // 2)

    mate_waits = {}

    def to_mates(source, group, half, when=None):
        waits = mate_waits.setdefault(half, [])
        for d in range(1, repeat):
            other = (s, g * repeat + lax.rem(r + d, repeat))
            waits.append(sender.copy(source, x_all.at[tokens_at(group * repeat + r, half)], other, when, when))

    half_rows = [pl.ds(h * (rows // 2), rows // 2) for h in range(2)]
    above, below = jnp.minimum((g + 1) * repeat + r, count - 1), jnp.maximum((g - 1) * repeat + r, 0)

    def pass_on(t):
        waits = []
        low_group, high_group = jnp.maximum(g - t, 0), jnp.minimum(g + t, chunks - 1)
        low_at = [tokens_at(low_group * repeat + r, h) for h in range(2)]
        high_at = [tokens_at(high_group * repeat + r, h) for h in range(2)]
        for h in range(2):
            rise = x_ref.at[half_rows[h]] if t == 0 else x_all.at[low_at[h]]
            fall = x_ref.at[half_rows[h]] if t == 0 else x_all.at[high_at[h]]
            rising = (g - t >= 0) & (g + 1 < chunks)
            falling = (g + t < chunks) & (g >= 1)
            waits.append((
                sender.copy(rise, x_all.at[low_at[h]], (s, above), rising, g - 1 - t >= 0),
                sender.copy(fall, x_all.at[high_at[h]], (s, below), falling, g + 1 + t < chunks),
            ))
        return waits

    def received(t, waits):
        low_group, high_group = jnp.maximum(g - 1 - t, 0), jnp.minimum(g + 1 + t, chunks - 1)
        for h in range(2):
            waits[h][0]()
            to_mates(x_all.at[tokens_at(low_group * repeat + r, h)], low_group, h, g - 1 - t >= 0)
            waits[h][1]()
            to_mates(x_all.at[tokens_at(high_group * repeat + r, h)], high_group, h, g + 1 + t < chunks)

    x_waits = pass_on(0)
    for h in range(2):
        to_mates(x_ref.at[half_rows[h]], g, h)

    shards = []
    matrices = (wq_ref, wk_ref, wv_ref, wo_ref)
    for d in range(1, mates):
        other = (s, b * mates + lax.rem(i + d, mates))
        for m in range(4):
            shards.append(sender.copy(matrices[m], stage4.at[i, m], other))
        shards.append(sender.copy(w1_ref, stage1.at[i], other))
        shards.append(sender.copy(w2_ref, stage2.at[i], other))
    for m in range(4):
        stage4[i, m] = matrices[m][...]
    stage1[i] = w1_ref[...]
    stage2[i] = w2_ref[...]

    codes[c] = seg_ref[...] * 2 + val_ref[...]
    small_waits = []
    for d in range(1, count):
        other = (s, lax.rem(c + d, count))
        small_waits.append(sender.copy(codes.at[c], codes.at[c], other))
        small_waits.append(sender.copy(vec_ref, vecs.at[s * count + c], other))
    vecs[s * count + c] = vec_ref[...]
    x_all[tokens_at(c, 0), :] = x_ref[0 : rows // 2, :]
    x_all[tokens_at(c, 1), :] = x_ref[rows // 2 :, :]

    for wait in shards:
        wait()
    for p in range(mates):
        for m in range(4):
            flat4[m, p * small_rows : (p + 1) * small_rows, :] = stage4[p, m]
        flat1[p * small_rows : (p + 1) * small_rows, :] = stage1[p]
        flat2[p * tall_rows : (p + 1) * tall_rows, :] = stage2[p]
    for k in range(chunks):
        part = slice(k * width, (k + 1) * width)
        pieces = [flat4[m, :, part] for m in range(3)]
        pieces.append(jnp.zeros((block_rows, w_out.shape[1] - 3 * width), f32))
        share4[k] = jnp.concatenate(pieces, axis=1).astype(bf16)

    def w_rows(seq, block, size):
        start = (seq * blocks + block) * block_rows
        return pl.ds(pl.multiple_of(start, block_rows), size * block_rows)

    columns = []
    for d in range(1, blocks):
        to = lax.rem(b + d, blocks) * mates + i
        columns.append(sender.copy(share4.at[to // repeat], w_all.at[w_rows(s, b, 1)], (s, to)))
    w_all[w_rows(s, b, 1), :] = share4[g]

    low4[...] = flat4[3].astype(bf16)
    lowq[...] = flat4[0].astype(bf16)
    low1[...] = flat1[...].astype(bf16)
    low2[...] = flat2[...].astype(bf16)

    half_wide, half_model = wide // 2, model // 2
    wide_at = pl.ds(pl.multiple_of(turn * half_wide, half_wide), half_wide)
    model_at = pl.ds(pl.multiple_of(turn * half_model, half_model), half_model)

    def tall_rows_at(seq, block, size):
        start = (seq * blocks + block) * block_tall
        return pl.ds(pl.multiple_of(start, block_tall), size * block_tall)

    def big(seq, block, size=1):
        return (
            w1_out.at[w_rows(seq, block, size), wide_at],
            w2_out.at[tall_rows_at(seq, block, size), model_at],
            wo_out.at[w_rows(seq, block, size), model_at],
            wq_out.at[w_rows(seq, block, size), model_at],
        )

    own = (low1.at[:, wide_at], low2.at[:, model_at], low4.at[:, model_at], lowq.at[:, model_at])
    move(low1, w1_out.at[w_rows(s, b, 1)])
    move(low2, w2_out.at[tall_rows_at(s, b, 1)])
    move(low4, wo_out.at[w_rows(s, b, 1)])
    move(lowq, wq_out.at[w_rows(s, b, 1)])
    sibling = (s, c + 1 - 2 * turn)
    sibling_waits = []

    def to_sibling(seq, block, when):
        for piece in big(seq, block):
            sibling_waits.append(sender.copy(piece, piece, sibling, when, when))

    masks = cube_steps(seqs, turn)

    def families(seq):
        found = [(seq, -1)]
        for j, mask in enumerate(masks):
            found = found + [(across(one, mask), j) for one, _ in found]
        return found

    plane_waits = {}

    def spread(key, seq, step, block, sources, when):
        for j in range(step + 1, len(masks)):
            partner = (across(s, masks[j]), c)
            waits = plane_waits.setdefault((key, j), [])
            for source, target in zip(sources, big(seq, block)):
                waits.append((sender.copy(source, target, partner, when, when)))

    up, down = jnp.minimum((b + 1) * mates + i, count - 1), jnp.maximum((b - 1) * mates + i, 0)

    def line_send(t):
        waits = []
        low_block, high_block = jnp.maximum(b - t, 0), jnp.minimum(b + t, blocks - 1)
        rising = (b - t >= 0) & (b + 1 < blocks)
        falling = (b + t < blocks) & (b >= 1)
        rises = own if t == 0 else big(s, low_block)
        falls = own if t == 0 else big(s, high_block)
        for source, target in zip(rises, big(s, low_block)):
            waits.append(sender.copy(source, target, (s, up), rising, b - 1 - t >= 0))
        for source, target in zip(falls, big(s, high_block)):
            waits.append(sender.copy(source, target, (s, down), falling, b + 1 + t < blocks))
        return waits

    events = {("own",): (b, None)}
    for t in range(blocks - 1):
        events[(t, 0)] = (jnp.maximum(b - 1 - t, 0), b - 1 - t >= 0)
        events[(t, 1)] = (jnp.minimum(b + 1 + t, blocks - 1), b + 1 + t < blocks)

    spread(("own",), s, -1, b, own, None)
    line_waits = line_send(0)

    def token_service(t):
        nonlocal x_waits
        if t < chunks - 1:
            received(t, x_waits)
            if t + 1 < chunks - 1:
                x_waits = pass_on(t + 1)

    token_service(0)
    late = []

    def settle_late():
        for arriving, seq, block, when in late:
            for wait in arriving:
                wait()
            to_sibling(seq, block, when)
        late.clear()

    def relay_event(key):
        block, when = events[key]
        queue = {j: list(plane_waits.get((key, j), [])) for j in range(len(masks))}
        for seq, j in families(s)[1:]:
            arriving, queue[j] = queue[j][: len(own)], queue[j][len(own) :]
            if j + 1 == len(masks):
                late.append((arriving, seq, block, when))
                continue
            for wait in arriving:
                wait()
            to_sibling(seq, block, when)
            before = {k: len(plane_waits.get((key, k), [])) for k in range(j + 1, len(masks))}
            spread(key, seq, j, block, big(seq, block), when)
            for k in range(j + 1, len(masks)):
                queue[k] = queue[k] + plane_waits[(key, k)][before[k] :]

    def weight_service(t):
        nonlocal line_waits
        if t < blocks - 1:
            for wait in line_waits:
                wait()
            if t + 1 < blocks - 1:
                line_waits = line_send(t + 1)
            for way in range(2):
                block, when = events[(t, way)]
                spread((t, way), s, -1, block, big(s, block), when)
                to_sibling(s, block, when)
        settle_late()
        if t == 0:
            relay_event(("own",))
        elif t - 1 < blocks - 1:
            relay_event((t - 1, 0))
            relay_event((t - 1, 1))

    for wait in columns:
        wait()
    columns = []
    for d in range(1, seqs):
        to = (lax.rem(s + d, seqs), c)
        slab = w_all.at[w_rows(s, 0, blocks)]
        columns.append(sender.copy(slab, slab, to))
    for wait in small_waits:
        wait()
    small_waits = []
    for d in range(1, seqs):
        to = (lax.rem(s + d, seqs), c)
        slab = vecs.at[pl.ds(s * count, count)]
        small_waits.append(sender.copy(slab, slab, to))

    top_ref[...] = jnp.full(top_ref.shape, FAR, f32)
    acc_ref[...] = jnp.zeros(acc_ref.shape, f32)
    k_ext[:, length:, :] = jnp.zeros((heads, PAD, k_ext.shape[2]), bf16)
    v_ext[:, 0:DH, length:] = jnp.zeros((heads, DH, PAD), bf16)
    v_ext[:, DH:, :] = jnp.ones((heads, 16, length + PAD), bf16)
    k_out[:, length:, :] = jnp.zeros((heads, PAD, DH), bf16)

    for wait in columns + small_waits:
        wait()
    move(w_all, w_out)
    move(vecs, vec_out)
    move(codes, code_out)
    wt[...] = w_all[...].astype(f32).T.astype(bf16)
    vec = vecs[:, 0, :]

    def bias_column(which):
        whole = unshard(vec, which * small_rows, small_rows)
        row = jnp.zeros((1, width), f32)
        for k in range(chunks):
            row = row + jnp.where(g == k, whole[:, k * width : (k + 1) * width], 0.0)
        extra = -width % LANES
        row = jnp.concatenate([row, jnp.zeros((1, extra), f32)], axis=1)
        return jnp.broadcast_to(row, (LANES, width + extra)).T[0:width, 0:1]

    bias_q, bias_v = bias_column(6), bias_column(7)

    def keys(chunk):
        at = pl.ds(pl.multiple_of(chunk * rows, rows), rows)
        x = x_all[at, :]
        k = nn(x, w_all[:, width : 2 * width]).astype(bf16)
        v = (nt(wt[2 * width : 3 * width, :], x) + bias_v).astype(bf16)
        v_out[:, at] = v
        kt_out[:, at] = nt(wt[width : 2 * width, :], x).astype(bf16)
        code = codes[chunk].astype(f32)
        away = jnp.concatenate(
            [
                jnp.broadcast_to(code[:, j * LANES : (j + 1) * LANES], (LANES, LANES)).T[:, 0:DOCS]
                for j in range(rows // LANES)
            ],
            axis=0,
        )
        document = lax.broadcasted_iota(jnp.int32, (rows, DOCS), 1).astype(f32)
        away = jnp.where(away == 2.0 * document + 1.0, 0.0, 1.0).astype(bf16)
        for h in range(heads):
            one = k[:, h * DH : (h + 1) * DH]
            k_out[h, at, :] = one
            k_ext[h, at, :] = jnp.concatenate([one, one, away], axis=1)
            v_ext[h, 0:DH, at] = v[h * DH : (h + 1) * DH]

    def queries(group):
        chunk = group * repeat + r
        x = x_all[pl.ds(pl.multiple_of(chunk * rows, rows), rows), :]
        to = pl.ds(pl.multiple_of(group * rows, rows), rows)
        q = (nt(wt[0:width, :], x) + bias_q).astype(bf16)
        q_out[:, to] = q
        scaled = q.astype(f32) * (DH**-0.5 * LOG2E)
        high = scaled.astype(bf16)
        rest = (scaled - high.astype(f32)).astype(bf16)
        wanted = (codes[chunk] | 1).astype(f32)
        document = lax.broadcasted_iota(jnp.int32, (DOCS, rows), 0).astype(f32)
        away = jnp.where(wanted == 2.0 * document + 1.0, FAR, 0.0).astype(bf16)
        for h in range(heads):
            part = slice(h * DH, (h + 1) * DH)
            q_ext[h, :, to] = jnp.concatenate([high[part], rest[part], away], axis=0)

    def attend_to(group, first, last):
        at = pl.ds(pl.multiple_of(group * rows, rows), rows)

        def scores(slot, key_at):
            for h in range(heads):
                slot[h] = nn(k_ext[h, pl.ds(key_at, HALF), :], q_ext[h, :, at])

        def soften(slot, key_at):
            for h in range(heads):
                top = top_ref[group, h, 0:1, :]
                sc = slot[h]
                new = jnp.maximum(top, jnp.max(sc, axis=0, keepdims=True))
                p = jnp.exp2(sc - new).astype(bf16)
                acc_ref[group, h] = acc_ref[group, h] * jnp.exp2(top - new) + nn(
                    v_ext[h, :, pl.ds(key_at, HALF)], p
                )
                top_ref[group, h, 0:1, :] = new

        def step(j, carry):
            one = pl.multiple_of(j * BK, BK)
            two = pl.multiple_of(one + HALF, HALF)
            scores(s_odd, two)
            soften(s_even, one)
            scores(s_even, pl.multiple_of(one + BK, BK))
            soften(s_odd, two)
            return carry

        per = rows // BK
        scores(s_even, pl.multiple_of(first * rows, rows))
        lax.fori_loop(first * per, last * per, step, 0)

    def conclude(group):
        at = pl.ds(pl.multiple_of(group * rows, rows), rows)
        for h in range(heads):
            part = slice(h * DH, (h + 1) * DH)
            low = acc_ref[group, h, DH : DH + 1, :]
            out = acc_ref[group, h, 0:DH, :] / low
            of_out[part, at] = out
            o_send[group, part, :] = out.astype(bf16)
            lse_out[h : h + 1, at] = top_ref[group, h, 0:1, :] + jnp.log2(low)

        @pl.when(group != g)
        def _():
            o_copy(group).start()

    def o_copy(group):
        return pltpu.make_async_remote_copy(
            src_ref=o_send.at[group],
            dst_ref=o_out.at[g],
            send_sem=o_send_sems.at[group],
            recv_sem=o_recv_sems.at[g],
            device_id=(s, group * repeat + r),
            device_id_type=MESH,
        )

    def arrive(group, low, high):
        def make(j, carry):
            keys(group * repeat + j)
            return carry

        lax.fori_loop(0, repeat, make, 0)
        queries(group)
        whole = high - low + 1 == chunks

        def each(other, carry):
            same = other == group
            attend_to(
                other,
                jnp.where(same, low, group) * repeat,
                (jnp.where(same, high, group) + 1) * repeat,
            )

            @pl.when(whole)
            def _():
                conclude(other)

            return carry

        lax.fori_loop(low, high + 1, each, 0)

    def mates_here():
        for h in range(2):
            for wait in mate_waits[h]:
                wait()
            mate_waits[h] = []

    mates_here()
    arrive(g, g, g)
    weight_service(0)
    for t in range(chunks - 1):
        if t == chunks - 2:
            move(x_all, x_out)
        low, high = g - 1 - t, g + 1 + t
        has_low, has_high = low >= 0, high < chunks

        @pl.when(has_low)
        def _():
            arrive(low, low, jnp.minimum(g + t, chunks - 1))

        @pl.when(has_high & (low < 0))
        def _():
            arrive(high, 0, high)

        token_service(t + 1)
        weight_service(t + 1)

        @pl.when(has_high & has_low)
        def _():
            arrive(high, low, high)

        mates_here()
    for t in range(chunks, blocks + 1):
        weight_service(t)
    settle_late()
    own_out = pltpu.make_async_copy(o_send.at[g], o_out.at[g], here_sems.at[9])
    own_out.start()
    for one in here:
        one.wait()
    for wait in sibling_waits:
        wait()
    for d in range(1, chunks):
        group = lax.rem(g + d, chunks)
        pltpu.make_async_remote_copy(
            src_ref=o_send.at[g],
            dst_ref=o_out.at[group],
            send_sem=o_send_sems.at[g],
            recv_sem=o_recv_sems.at[group],
            device_id=(s, group * repeat + r),
            device_id_type=MESH,
        ).wait_recv()
        o_copy(group).wait_send()
    own_out.wait()
    sender.finish()


def advance(wq, wk, wv, wo, w1, w2, x, seg, val, vec, chunks, heads):
    seqs, count = lax.axis_size("seq"), lax.axis_size("ctx")
    small_rows, model = wq.shape
    tall_rows, wide = w2.shape[0], w1.shape[1]
    rows = x.shape[0]
    mates = block_mates(small_rows)
    blocks, repeat = count // mates, count // chunks
    semaphores = (
        6 * (mates - 1) + 2 * (count - 1) + 2 * (seqs - 1) + 9 * (blocks - 1)
        + 4 * (seqs - 1) * (2 * blocks - 1) + 4 * (seqs * (2 * blocks - 1) - 1) + 4 * (chunks - 1) + 2 * (2 * chunks - 1) * (repeat - 1)
    )
    devices = seqs * count
    width = heads * DH
    length, mine = count * rows, chunks * rows
    padded = -(-3 * width // LANES) * LANES
    shape = jax.ShapeDtypeStruct
    f32, bf16 = jnp.float32, jnp.bfloat16
    vmem, far = pl.BlockSpec(memory_space=pltpu.VMEM), pl.BlockSpec(memory_space=pl.ANY)
    block_rows, block_tall = mates * small_rows, mates * tall_rows
    dma = pltpu.SemaphoreType.DMA
    return pl.pallas_call(
        partial(advance_kernel, seqs, count, chunks, heads),
        out_shape=(
            shape((model, padded), bf16),
            shape((model, model), bf16),
            shape((model, model), bf16),
            shape((model, wide), bf16),
            shape((tall_rows * devices, model), bf16),
            shape((length, model), bf16),
            shape((count, 1, rows), jnp.int32),
            shape((devices, 1, vec.shape[1]), f32),
            shape((heads, length + PAD, DH), bf16),
            shape((width, length), bf16),
            shape((width, length), bf16),
            shape((width, mine), bf16),
            shape((width, mine), f32),
            shape((8, mine), f32),
            shape((chunks, width, rows), bf16),
        ),
        in_specs=[vmem] * 10,
        out_specs=(far,) * 8 + (vmem,) * 6 + (far,),
        scratch_shapes=[
            pltpu.VMEM((mates, 4, small_rows, model), f32),
            pltpu.VMEM((mates, small_rows, wide), f32),
            pltpu.VMEM((mates, tall_rows, model), f32),
            pltpu.VMEM((4, block_rows, model), f32),
            pltpu.VMEM((block_rows, wide), f32),
            pltpu.VMEM((block_tall, model), f32),
            pltpu.VMEM((block_rows, model), bf16),
            pltpu.VMEM((block_rows, model), bf16),
            pltpu.VMEM((block_rows, wide), bf16),
            pltpu.VMEM((block_tall, model), bf16),
            pltpu.VMEM((chunks, block_rows, padded), bf16),
            pltpu.VMEM((model, padded), bf16),
            pltpu.VMEM((length, model), bf16),
            pltpu.VMEM((count, 1, rows), jnp.int32),
            pltpu.VMEM((devices, 1, vec.shape[1]), f32),
            pltpu.VMEM((padded, model), bf16),
            pltpu.VMEM((heads, length + PAD, 2 * DH + DOCS), bf16),
            pltpu.VMEM((heads, DH + 16, length + PAD), bf16),
            pltpu.VMEM((heads, 2 * DH + DOCS, mine), bf16),
            pltpu.VMEM((chunks, heads, 8, rows), f32),
            pltpu.VMEM((chunks, heads, DH + 16, rows), f32),
            pltpu.VMEM((heads, HALF, rows), f32),
            pltpu.VMEM((heads, HALF, rows), f32),
            pltpu.VMEM((chunks, width, rows), bf16),
            dma((semaphores,)),
            dma((semaphores,)),
            dma((10,)),
            dma((chunks,)),
            dma((chunks,)),
        ],
        compiler_params=pltpu.CompilerParams(
            vmem_limit_bytes=63 * 1024 * 1024, collective_id=1, has_side_effects=True
        ),
        name="advance",
    )(wq, wk, wv, wo, w1, w2, x, seg, val, vec)


def added(*parts):
    sum_of = parts[0].astype(jnp.float32)
    for part in parts[1:]:
        sum_of = sum_of + part.astype(jnp.float32)
    return sum_of


class Line:
    def __init__(self, sender, place, size, device, pieces, landing):
        self.sender, self.place, self.size, self.device = sender, place, size, device
        self.pieces, self.landing = pieces, landing
        self.waits = None

    def send(self, t):
        self.waits = []
        for way in range(2):
            rank = self.place if way == 0 else self.size - 1 - self.place
            mirror = (lambda d: d) if way == 0 else (lambda d: self.size - 1 - d)
            goal = jnp.clip(mirror(self.size - 1 - t + rank), 0, self.size - 1)
            sends = rank <= t
            receives = (rank >= 1) & (rank - 1 <= t)
            to = jnp.clip(self.place + (1 - 2 * way), 0, self.size - 1)
            waits = []
            for source, target in zip(self.pieces(goal), self.landing(way, t)):
                waits.append(self.sender.copy(source, target, self.device(to), sends, receives))
            self.waits.append((receives, mirror, rank, waits))

    def receive(self, t):
        for way, (receives, mirror, rank, waits) in enumerate(self.waits):
            goal = jnp.clip(mirror(self.size - 2 - t + rank), 0, self.size - 1)
            pieces, landing = self.pieces(goal), self.landing(way, t)
            for wait, piece, arrived in zip(waits, pieces, landing):
                wait()

                @pl.when(receives)
                def _():
                    piece[...] = added(piece[...], arrived[...]).astype(piece.dtype)


def group_order(chunks):
    table = []
    for g in range(chunks):
        steps = [(chunks - 1 + g - d if d > g else chunks - 1 - g + d, d < g, d) for d in range(chunks) if d != g]
        table.append([d for _, _, d in sorted(steps)] + [g])
    return table


def retreat_kernel(
    seqs, count, chunks, heads,
    do_ref, x_ref, w_ref, wq_ref, k_ref, kt_ref, v_ref, q_ref, o_ref, lse_ref, code_ref,
    dwo_ref, dw1_ref, dw2_ref, dsmall_ref, db1_ref,
    dx_out, dw_out, dwo_out, dw1_out, dw2_out, dsmall_out, db1_out, in1, in2, in4, dx_in,
    do_in, q_ext, do_ext, dq, o_slot, k_slot, x_slot, kt_ext, v_ext, dkv, dw, db,
    s_even, s_odd, g_even, g_odd, dx_send, dq_send, dq_in, w_full, wt,
    dx_sum, dx_line, sum1, sum2, sum4, part1, part2, cube1, cube2, cube4,
    line1, line2, line4, last1, last2, last4, w_mine, w_seq, w_block, w_mates,
    small_in, b1_in, b_in, vec_seq, bias_seq,
    send_sems, recv_sems, here_sems, fetch_sems, part_sems, own_sems, mate_send, mate_recv, dq_send_sems, dq_recv_sems,
):
    s, c = lax.axis_index("seq"), lax.axis_index("ctx")
    f32, bf16 = jnp.float32, jnp.bfloat16
    rows, model = dx_out.shape
    wide = dw1_ref.shape[1]
    repeat = count // chunks
    mates = w_mates.shape[0]
    blocks = count // mates
    block_rows, block_tall = dwo_out.shape[0], dw2_out.shape[0]
    width = heads * DH
    b, i = c // mates, lax.rem(c, mates)
    g, r = c // repeat, lax.rem(c, repeat)
    turn = lax.rem(c, 2)
    half_wide, half_model = wide // 2, model // 2
    slab_rows, slab_tall = blocks * block_rows, blocks * block_tall
    sender = Sender(send_sems, recv_sems)
    here = []

    def move(source, target):
        one = pltpu.make_async_copy(source, target, here_sems.at[len(here)])
        one.start()
        here.append(one)
        return one

    table = group_order(chunks)

    def group_at(index):
        found = table[chunks - 1][index]
        for k in range(chunks - 1):
            found = jnp.where(g == k, table[k][index], found)
        return found

    def fetch(chunk, slot):
        at = pl.ds(pl.multiple_of(chunk * rows, rows), rows)
        sems = fetch_sems.at[slot]
        copies = [
            pltpu.make_async_copy(k_ref.at[:, at, :], k_slot.at[slot], sems.at[0]),
            pltpu.make_async_copy(x_ref.at[at], x_slot.at[slot], sems.at[1]),
        ]
        for h in range(heads):
            part = pl.ds(h * DH, DH)
            for m, (source, target) in enumerate((
                (kt_ref, kt_ext.at[slot, h, pl.ds(0, DH)]),
                (kt_ref, kt_ext.at[slot, h, pl.ds(DH, DH)]),
                (v_ref, v_ext.at[slot, h, pl.ds(0, DH)]),
            )):
                copies.append(pltpu.make_async_copy(source.at[part, at], target, sems.at[2 + 3 * h + m]))
        return copies

    kt_ext[:, :, 2 * DH : 2 * DH + 16, :] = jnp.ones((2, heads, 16, rows), bf16)
    v_ext[:, :, DH:, :] = jnp.ones((2, heads, 16, rows), bf16)
    for one in fetch(group_at(0) * repeat, 0):
        one.start()
    greet(seqs, count)

    do_waits = {}
    for d in range(1, chunks):
        to = lax.rem(g + d, chunks)
        do_waits[chunks - d] = sender.copy(do_ref.at[to], do_in.at[g], (s, to * repeat + r))
    own_do = move(do_ref.at[g], do_in.at[g])

    sibling = (s, c + 1 - 2 * turn)

    def column_half(which):
        wide_at = pl.ds(pl.multiple_of(which * half_wide, half_wide), half_wide)
        model_at = pl.ds(pl.multiple_of(which * half_model, half_model), half_model)
        return dw1_ref.at[:, wide_at], dw2_ref.at[:, model_at], dwo_ref.at[:, model_at]

    half_waits = [
        sender.copy(source, target, sibling)
        for source, target in zip(column_half(1 - turn), (in1, in2, in4))
    ]
    for source, target in zip(column_half(turn), (sum1, sum2, sum4)):
        move(source, target)
    vec_waits = []
    for d in range(1, count):
        to = (s, lax.rem(c + d, count))
        for source, target in ((dsmall_ref, small_in), (db1_ref, b1_in)):
            vec_waits.append(sender.copy(source, target.at[c], to))
    small_in[c] = dsmall_ref[...]
    b1_in[c] = db1_ref[...]

    wt[...] = w_ref[...].astype(f32).T.astype(bf16)
    dw[...] = jnp.zeros(dw.shape, f32)
    db[...] = jnp.zeros(db.shape, f32)
    dq[...] = jnp.zeros(dq.shape, f32)
    one_rows = jnp.ones((8, rows), bf16)

    def queries(group):
        at = pl.ds(pl.multiple_of(group * rows, rows), rows)
        load = pltpu.make_async_copy(o_ref.at[:, at], o_slot, own_sems.at[0])
        load.start()
        load.wait()
        wanted = (code_ref[group * repeat + r] | 1).astype(f32)
        document = lax.broadcasted_iota(jnp.int32, (DOCS, rows), 0).astype(f32)
        away = jnp.where(wanted == 2.0 * document + 1.0, FAR, 0.0)
        for h in range(heads):
            part = slice(h * DH, (h + 1) * DH)
            scaled = q_ref[part, at].astype(f32) * (DH**-0.5 * LOG2E)
            high = scaled.astype(bf16).astype(f32)
            extra = three_parts(-lse_ref[h : h + 1, at])
            full = jnp.concatenate([high, scaled - high, extra, away], axis=0)
            q_ext[h, at, :] = full.T.astype(bf16)
            grad = do_in[group, part, :].astype(f32)
            delta = jnp.sum(grad * o_slot[part, :], axis=0, keepdims=True)
            do_ext[h, at, :] = jnp.concatenate([grad, three_parts(-delta)], axis=0).T.astype(bf16)

    for one in here:
        one.wait()
    queries(g)

    for wait in half_waits:
        wait()
    loads = []
    for target, arrived, part, kind in ((sum1, in1, part1, 0), (sum2, in2, part2, 1), (sum4, in4, part2, 1)):
        size = part.shape[1]
        for k in range(target.shape[0] // size):
            loads.append((target, arrived, part, kind, k * size, size))
    used_slots = [0, 0]
    copies = []
    for target, arrived, part, kind, at, size in loads:
        slot = used_slots[kind] % 2
        used_slots[kind] += 1
        copies.append((
            pltpu.make_async_copy(arrived.at[pl.ds(at, size)], part.at[slot], part_sems.at[kind, slot]), slot
        ))
    copies[0][0].start()
    for n, (target, arrived, part, kind, at, size) in enumerate(loads):
        if n + 1 < len(loads):
            copies[n + 1][0].start()
        copies[n][0].wait()
        rows_at = slice(at, at + size)
        target[rows_at] = added(target[rows_at], part[copies[n][1]]).astype(bf16)

    def slab(seq):
        at = pl.ds(pl.multiple_of(seq * slab_rows, slab_rows), slab_rows)
        tall = pl.ds(pl.multiple_of(seq * slab_tall, slab_tall), slab_tall)
        return sum1.at[at], sum2.at[tall], sum4.at[at]

    masks = cube_steps(seqs, turn)

    def family(seq, rest):
        found = [seq]
        for mask in rest:
            found = found + [across(one, mask) for one in found]
        return found

    cube_waits, used = [], 0

    def cube_send(j):
        nonlocal used
        partner = across(s, masks[j])
        cube_waits.clear()
        mine = family(s, masks[j + 1 :])
        for k, seq in enumerate(family(partner, masks[j + 1 :])):
            landing = cube1.at[used + k], cube2.at[used + k], cube4.at[used + k]
            waits = [
                sender.copy(source, target, (partner, c)) for source, target in zip(slab(seq), landing)
            ]
            cube_waits.append((mine[k], landing, waits))
        used += len(cube_waits)

    def cube_receive():
        for seq, landing, waits in cube_waits:
            for wait, target, arrived in zip(waits, slab(seq), landing):
                wait()
                target[...] = added(target[...], arrived[...]).astype(bf16)

    cube_send(0)

    def block_slab(goal):
        row = s * slab_rows + goal * block_rows
        tall = s * slab_tall + goal * block_tall
        at = pl.ds(pl.multiple_of(row, block_rows), block_rows)
        tall_at = pl.ds(pl.multiple_of(tall, block_tall), block_tall)
        return sum1.at[at], sum2.at[tall_at], sum4.at[at]

    weight_line = Line(
        sender, b, blocks, lambda to: (s, to * mates + i),
        block_slab, lambda way, t: (line1.at[way, t], line2.at[way, t], line4.at[way, t]),
    )
    half_rows = rows // 2
    token_lines = []
    for h in range(2):
        at = pl.ds(h * half_rows, half_rows)
        token_lines.append(
            Line(
                sender, g, chunks, lambda to: (s, to * repeat + r),
                lambda goal, at=at: (dx_sum.at[goal, at],),
                lambda way, t, at=at: (dx_line.at[way, t, at],),
            )
        )

    for d in range(1, chunks):
        do_waits[d]()
        queries(lax.rem(g + d, chunks))

    for wait in vec_waits:
        wait()
    vec_waits = []
    small, tall = small_in[0], b1_in[0]
    for k in range(1, count):
        small = small + small_in[k]
        tall = tall + b1_in[k]
    vec_seq[s, 0:8, 0:model] = small
    vec_seq[s, 0:1, model:] = tall
    vec_seq[s, 1:8, model:] = jnp.zeros((7, wide), f32)
    for d in range(1, seqs):
        vec_waits.append(sender.copy(vec_seq.at[s], vec_seq.at[s], (lax.rem(s + d, seqs), c)))

    weight_steps = blocks - 1
    pending = []

    def cube_turn(j):
        cube_receive()
        if j + 1 < len(masks):
            cube_send(j + 1)
        elif weight_steps:
            weight_line.send(0)

    def line_turn(t):
        weight_line.receive(t)
        if t + 1 < weight_steps:
            weight_line.send(t + 1)

    pending += [partial(cube_turn, j) for j in range(len(masks))]
    pending += [partial(line_turn, t) for t in range(weight_steps)]

    def scores(s_slot, g_slot, slot, group, half):
        at = pl.ds(pl.multiple_of(group * rows, rows), rows)
        key = pl.ds(half * HALF, HALF)
        for h in range(heads):
            s_slot[h] = nn(q_ext[h, at, :], kt_ext[slot, h, :, key])
            g_slot[h] = nn(do_ext[h, at, :], v_ext[slot, h, :, key])

    def absorb(s_slot, g_slot, slot, group, half):
        at = pl.ds(pl.multiple_of(group * rows, rows), rows)
        key = pl.ds(half * HALF, HALF)
        for h in range(heads):
            part = slice(h * DH, (h + 1) * DH)
            p = jnp.exp2(s_slot[h])
            ds = (p * g_slot[h]).astype(bf16)
            dkv[width + h * DH : width + (h + 1) * DH, key] += nn(do_in[group, part, :], p.astype(bf16))
            dkv[part, key] += nn(q_ref[part, at], ds)
            dq[h, at, :] += nn(ds, k_slot[slot, h, key, :])

    def next_group(p):
        return lax.rem(g + p, chunks)

    def one_chunk(chunk, following, slot, conclude):
        for one in fetch(chunk, slot):
            one.wait()
        if following is not None:
            for one in fetch(following, 1 - slot):
                one.start()
        document = lax.broadcasted_iota(jnp.int32, (DOCS, rows), 0).astype(f32)
        away = jnp.where(code_ref[chunk].astype(f32) == 2.0 * document + 1.0, 0.0, 1.0).astype(bf16)
        for h in range(heads):
            kt_ext[slot, h, 2 * DH + 16 :, :] = away
        dkv[...] = jnp.zeros(dkv.shape, f32)
        scores(s_even, g_even, slot, next_group(1), 0)

        def turn_of(p, carry):
            group = next_group(p)
            absorb(s_even, g_even, slot, group, 0)
            scores(s_odd, g_odd, slot, group, 1)
            absorb(s_odd, g_odd, slot, group, 1)
            scores(s_even, g_even, slot, next_group(p + 1), 0)
            if conclude is not None:
                conclude(group)
            return carry

        lax.fori_loop(1, chunks + 1, turn_of, 0)

    def mate_copy(group, to, slot):
        return pltpu.make_async_remote_copy(
            src_ref=dx_send.at[slot],
            dst_ref=dx_in.at[slot, group],
            send_sem=mate_send.at[slot],
            recv_sem=mate_recv.at[slot, group],
            device_id=(s, g * repeat + to),
            device_id_type=MESH,
        )

    def keep(group, j, slot):
        dk = (dkv[0:width, :] * DH**-0.5).astype(bf16)
        dv = dkv[width:, :].astype(bf16)
        both = jnp.concatenate([dk, dv], axis=0)
        dx = tn(both, wt[width : 3 * width, :]).astype(bf16)
        dw[width : 3 * width, :] += nn(both, x_slot[slot])
        db[0:8, width:] += nt(one_rows, dv)

        @pl.when(j == r)
        def _():
            dx_sum[group] = dx

        @pl.when(j != r)
        def _():
            to = lax.rem(j - r + repeat, repeat) - 1
            dx_send[to] = dx
            mate_copy(group, j, to).start()

    spare = chunks * repeat % 2

    def conclude(group):
        at = pl.ds(pl.multiple_of(group * rows, rows), rows)
        from_x = pl.ds(pl.multiple_of((group * repeat + r) * rows, rows), rows)
        load = pltpu.make_async_copy(x_ref.at[from_x], x_slot.at[spare], own_sems.at[1])
        load.start()
        grad = jnp.concatenate([dq[h, at, :] for h in range(heads)], axis=1) * DH**-0.5
        dq_send[group] = grad.T.astype(bf16)

        @pl.when(group != g)
        def _():
            dq_copy(group).start()

        low = grad.astype(bf16)
        db[0:8, 0:width] += nn(one_rows, low)
        load.wait()
        dw[0:width, :] += nn(dq_send[group], x_slot[spare])

    def dq_copy(group):
        return pltpu.make_async_remote_copy(
            src_ref=dq_send.at[group],
            dst_ref=dq_in.at[g],
            send_sem=dq_send_sems.at[group],
            recv_sem=dq_recv_sems.at[g],
            device_id=(s, group * repeat + r),
            device_id_type=MESH,
        )

    def gather_mates(group):
        for d in range(1, repeat):
            mate_copy(group, lax.rem(r + d, repeat), d - 1).wait()
        loads = [
            pltpu.make_async_copy(dx_in.at[d, group], dx_send.at[d], mate_send.at[d]) for d in range(repeat - 1)
        ]
        for load in loads:
            load.start()
        for load in loads:
            load.wait()
        terms = [dx_send[d] for d in range(repeat - 1)]
        dx_sum[group] = added(dx_sum[group], *terms).astype(bf16)

    for index in range(chunks):
        group = group_at(index)
        for j in range(repeat):
            position = index * repeat + j
            slot = position % 2
            final = position + 1 == chunks * repeat
            if j + 1 < repeat:
                following = group * repeat + j + 1
            elif not final:
                following = group_at(index + 1) * repeat
            else:
                following = None
            one_chunk(group * repeat + j, following, slot, conclude if final else None)
            keep(group, j, slot)
            if j == 0 and index == chunks - 1 and pending:
                pending.pop(0)()
        gather_mates(group)
        if index >= 1:
            for line in token_lines:
                line.receive(index - 1)
        if index < chunks - 1:
            for line in token_lines:
                line.send(index)
            if pending:
                pending.pop(0)()

    w_full[...] = dw[...].T.astype(bf16)
    w_waits = []
    for d in range(1, seqs):
        to = lax.rem(s + d, seqs)
        source = w_full.at[pl.ds(pl.multiple_of(to * slab_rows, slab_rows), slab_rows)]
        w_waits.append(sender.copy(source, w_seq.at[d - 1], (to, c)))
    b_waits = []
    b_in[c] = db[0:1, :]
    for d in range(1, count):
        b_waits.append(sender.copy(b_in.at[c], b_in.at[c], (s, lax.rem(c + d, count))))
    while pending:
        pending.pop(0)()
    last_waits = []
    for source, target in zip(block_slab(b), (last1, last2, last4)):
        target[i] = source[...]
        for d in range(1, mates):
            to = (s, b * mates + lax.rem(i + d, mates))
            last_waits.append(sender.copy(source, target.at[i], to))
    for wait in b_waits:
        wait()
    b_waits = []
    pair = []
    for k in range(chunks):
        one = b_in[k * repeat]
        for d in range(1, repeat):
            one = one + b_in[k * repeat + d]
        pair.append(one)
    for m in range(2):
        joined = jnp.concatenate([one[:, m * width : (m + 1) * width] for one in pair], axis=1)
        bias_seq[s, m : m + 1, :] = joined
    bias_seq[s, 2:8, :] = jnp.zeros((6, model), f32)
    for d in range(1, seqs):
        b_waits.append(sender.copy(bias_seq.at[s], bias_seq.at[s], (lax.rem(s + d, seqs), c)))
    for wait in w_waits:
        wait()
    w_mine[...] = added(
        w_full[pl.ds(pl.multiple_of(s * slab_rows, slab_rows), slab_rows), :],
        *[w_seq[d] for d in range(seqs - 1)],
    ).astype(bf16)
    w_waits = []
    for d in range(1, blocks):
        to = lax.rem(b + d, blocks)
        source = w_mine.at[pl.ds(pl.multiple_of(to * block_rows, block_rows), block_rows)]
        w_waits.append(sender.copy(source, w_block.at[b], (s, to * mates + i)))
    w_block[b] = w_mine[pl.ds(pl.multiple_of(b * block_rows, block_rows), block_rows), :]

    dq_in[g] = dq_send[g]
    for d in range(1, chunks):
        group = lax.rem(g + d, chunks)
        pltpu.make_async_remote_copy(
            src_ref=dq_send.at[g],
            dst_ref=dq_in.at[group],
            send_sem=dq_send_sems.at[g],
            recv_sem=dq_recv_sems.at[group],
            device_id=(s, group * repeat + r),
            device_id_type=MESH,
        ).wait_recv()
        dq_copy(group).wait_send()
    part = nn(wq_ref[...], dq_in[...].reshape(chunks * width, rows))
    dx_out[...] = dx_sum[g].astype(f32) + part.T

    for wait in w_waits:
        wait()
    w_waits = []
    w_mates[i] = w_block[...]
    for d in range(1, mates):
        to = (s, b * mates + lax.rem(i + d, mates))
        w_waits.append(sender.copy(w_block, w_mates.at[i], to))
    for wait in vec_waits + b_waits + last_waits:
        wait()
    for target, source in ((dw1_out, last1), (dw2_out, last2), (dwo_out, last4)):
        size = target.shape[1] // 2
        for which in range(2):
            target[:, which * size : (which + 1) * size] = added(
                *[source[k] for k in range(which, mates, 2)]
            )
    vec, bias = vec_seq[0], bias_seq[0]
    for d in range(1, seqs):
        vec = vec + vec_seq[d]
        bias = bias + bias_seq[d]
    dsmall_out[0:6, :] = vec[0:6, 0:model]
    dsmall_out[6:8, :] = bias[0:2]
    db1_out[...] = vec[:, model:]
    for wait in w_waits:
        wait()
    for k in range(chunks):
        terms = [
            w_mates[p, q]
            for p in range(mates)
            for q in range(blocks)
            if (q * mates + p) // repeat == k
        ]
        dw_out[k] = added(*terms)
    sender.finish()


def retreat(do, x, w, wq, k, kt, v, q, o, lse, codes, dwo, dw1, dw2, dsmall, db1, heads):
    seqs, count = lax.axis_size("seq"), lax.axis_size("ctx")
    chunks, width, rows = do.shape
    model = x.shape[1]
    wide, tall = dw1.shape[1], dw2.shape[0]
    devices = seqs * count
    mates = block_mates(model // devices)
    blocks, repeat = count // mates, count // chunks
    block_rows, block_tall = mates * (model // devices), mates * (tall // devices)
    slab_rows, slab_tall = blocks * block_rows, blocks * block_tall
    padded = w.shape[1]
    mine = chunks * rows
    semaphores = (
        (chunks - 1) + 3 + 2 * (count - 1) + (seqs - 1) + 3 * (seqs - 1) + 6 * (blocks - 1)
        + 4 * (chunks - 1) + (seqs - 1) + (count - 1) + 3 * (mates - 1) + (seqs - 1) + (blocks - 1) + (mates - 1)
    )
    shape = jax.ShapeDtypeStruct
    f32, bf16 = jnp.float32, jnp.bfloat16
    vmem, far = pl.BlockSpec(memory_space=pltpu.VMEM), pl.BlockSpec(memory_space=pl.ANY)
    half_wide, half_model = wide // 2, model // 2
    triple = lambda lead, a, t: [
        pltpu.VMEM(lead + (a, half_wide), bf16),
        pltpu.VMEM(lead + (t, half_model), bf16),
        pltpu.VMEM(lead + (a, half_model), bf16),
    ]
    dma = pltpu.SemaphoreType.DMA
    return pl.pallas_call(
        partial(retreat_kernel, seqs, count, chunks, heads),
        out_shape=(
            shape((rows, model), f32),
            shape((chunks, block_rows, padded), f32),
            shape((block_rows, model), f32),
            shape((block_rows, wide), f32),
            shape((block_tall, model), f32),
            shape((8, model), f32),
            shape((8, wide), f32),
            shape((model, half_wide), bf16),
            shape((tall, half_model), bf16),
            shape((model, half_model), bf16),
            shape((repeat - 1, chunks, rows, model), bf16),
        ),
        in_specs=[far, far, vmem, vmem, far, far, far, vmem, far, vmem, vmem, far, far, far, vmem, vmem],
        out_specs=(vmem,) * 7 + (far,) * 4,
        scratch_shapes=[
            pltpu.VMEM((chunks, width, rows), bf16),
            pltpu.VMEM((heads, mine, 2 * DH + 16 + DOCS), bf16),
            pltpu.VMEM((heads, mine, DH + 16), bf16),
            pltpu.VMEM((heads, mine, DH), f32),
            pltpu.VMEM((width, rows), f32),
            pltpu.VMEM((2, heads, rows, DH), bf16),
            pltpu.VMEM((2, rows, model), bf16),
            pltpu.VMEM((2, heads, 2 * DH + 16 + DOCS, rows), bf16),
            pltpu.VMEM((2, heads, DH + 16, rows), bf16),
            pltpu.VMEM((2 * width, rows), f32),
            pltpu.VMEM((padded, model), f32),
            pltpu.VMEM((8, 2 * width), f32),
        ]
        + [pltpu.VMEM((heads, rows, HALF), f32)] * 4
        + [
            pltpu.VMEM((repeat - 1, rows, model), bf16),
            pltpu.VMEM((chunks, width, rows), bf16),
            pltpu.VMEM((chunks, width, rows), bf16),
            pltpu.VMEM((model, padded), bf16),
            pltpu.VMEM((padded, model), bf16),
            pltpu.VMEM((chunks, rows, model), bf16),
            pltpu.VMEM((2, chunks - 1, rows, model), bf16),
        ]
        + triple((), model, tall)
        + [pltpu.VMEM((2, model // 8, half_wide), bf16), pltpu.VMEM((2, model // 2, half_model), bf16)]
        + triple((seqs - 1,), slab_rows, slab_tall)
        + triple((2, blocks - 1), block_rows, block_tall)
        + triple((mates,), block_rows, block_tall)
        + [
            pltpu.VMEM((slab_rows, padded), bf16),
            pltpu.VMEM((seqs - 1, slab_rows, padded), bf16),
            pltpu.VMEM((blocks, block_rows, padded), bf16),
            pltpu.VMEM((mates, blocks, block_rows, padded), bf16),
            pltpu.VMEM((count, 8, model), f32),
            pltpu.VMEM((count, 1, wide), f32),
            pltpu.VMEM((count, 1, 2 * width), f32),
            pltpu.VMEM((seqs, 8, model + wide), f32),
            pltpu.VMEM((seqs, 8, model), f32),
            dma((semaphores,)),
            dma((semaphores,)),
            dma((8,)),
            dma((2, 2 + 3 * heads)),
            dma((2, 2)),
            dma((2,)),
            dma((repeat - 1,)),
            dma((repeat - 1, chunks)),
            dma((chunks,)),
            dma((chunks,)),
        ],
        compiler_params=pltpu.CompilerParams(
            vmem_limit_bytes=63 * 1024 * 1024, collective_id=2, has_side_effects=True
        ),
        name="retreat",
    )(do, x, w, wq, k, kt, v, q, o, lse, codes, dwo, dw1, dw2, dsmall, db1)


def pick(values, size, device):
    wide = values.shape[1]
    row = lax.broadcasted_iota(jnp.int32, (wide, size), 0)
    column = lax.broadcasted_iota(jnp.int32, (wide, size), 1)
    chosen = (row == column + device * size).astype(jnp.bfloat16)
    high = values.astype(jnp.bfloat16)
    rest = values - high.astype(jnp.float32)
    middle_part = rest.astype(jnp.bfloat16)
    low = (rest - middle_part.astype(jnp.float32)).astype(jnp.bfloat16)
    return nn(high, chosen) + nn(middle_part, chosen) + nn(low, chosen)


def finish_kernel(
    count, mates,
    e1_ref, dx_ref, dw_ref, dwo_ref, dw1_ref, dw2_ref, small_ref, b1_ref,
    dx_out, dwq_out, dwk_out, dwv_out, dwo_out, dw1_out, dw2_out, small_out, b1_out,
):
    s, c = lax.axis_index("seq"), lax.axis_index("ctx")
    dx_out[...] = e1_ref[...] + dx_ref[...].astype(jnp.float32)
    each, tall = dwo_out.shape[0], dw2_out.shape[0]
    chunks = dw_ref.shape[0]
    width = dwq_out.shape[1] // chunks
    i = lax.rem(c, mates)
    for p in range(mates):
        rows = slice(p * each, (p + 1) * each)

        @pl.when(i == p)
        def _():
            for m, out in enumerate((dwq_out, dwk_out, dwv_out)):
                parts = [dw_ref[k, rows, m * width : (m + 1) * width] for k in range(chunks)]
                out[...] = jnp.concatenate(parts, axis=1)
            dwo_out[...] = dwo_ref[rows, :]
            dw1_out[...] = dw1_ref[rows, :]
            dw2_out[...] = dw2_ref[p * tall : (p + 1) * tall, :]

    device = s * count + c
    small_out[...] = pick(small_ref[...], each, device)
    b1_out[...] = pick(b1_ref[...], tall, device)


def finish(e1, dx, dw, dwo, dw1, dw2, small, b1):
    count = lax.axis_size("ctx")
    devices = count * lax.axis_size("seq")
    model, wide = dwo.shape[1], dw1.shape[1]
    each, tall = model // devices, wide // devices
    shape = jax.ShapeDtypeStruct
    f32 = jnp.float32
    vmem = pl.BlockSpec(memory_space=pltpu.VMEM)
    return pl.pallas_call(
        partial(finish_kernel, count, block_mates(each)),
        out_shape=(shape(e1.shape, f32),)
        + (shape((each, model), f32),) * 4
        + (shape((each, wide), f32), shape((tall, model), f32), shape((8, each), f32), shape((8, tall), f32)),
        in_specs=[vmem] * 8,
        out_specs=(vmem,) * 9,
        compiler_params=pltpu.CompilerParams(vmem_limit_bytes=VMEM_LIMIT),
        name="finish",
    )(e1, dx, dw, dwo, dw1, dw2, small, b1)


def on_device(
    tokens, segment_ids, valid_tokens, query_weight, query_bias, key_weight, value_weight, value_bias,
    output_weight, output_bias, attn_norm_gain, attn_norm_shift, up_weight, up_bias, down_weight,
    down_bias, ffn_norm_gain, ffn_norm_shift, out_cotangent,
):
    count = lax.axis_size("ctx")
    chunks = math.gcd(H, count)
    heads = H // chunks
    x = tokens[0]
    vec = jnp.concatenate([
        output_bias, attn_norm_gain, attn_norm_shift, down_bias, ffn_norm_gain, ffn_norm_shift,
        query_bias, value_bias, up_bias,
    ])
    vec = jnp.pad(vec, (0, -vec.shape[0] % LANES))[None]
    w, wo, wq, w1, w2, x_all, codes, vecs, k, kt, v, q, o_float, lse, o = advance(
        query_weight, key_weight, value_weight, output_weight, up_weight, down_weight,
        x, segment_ids, valid_tokens, vec, chunks, heads,
    )
    output, e1, do, dwo, dw1, dw2, dsmall, db1 = middle(
        o, x, out_cotangent[0], wo, w1, w2, vecs
    )
    summed = retreat(
        do, x_all, w, wq, k, kt, v, q, o_float, lse, codes, dwo, dw1, dw2, dsmall, db1, heads
    )[:7]
    grad, dwq, dwk, dwv, dwo, dw1, dw2, small, b1 = finish(e1, *summed)
    return (
        output[None], grad[None],
        dwq, small[6], dwk, dwv, small[7],
        dwo, small[0], small[1], small[2],
        dw1, b1[0], dw2, small[3], small[4], small[5],
    )


def solution(mesh):
    in_specs = (
        P("seq", "ctx", None),
        P("seq", "ctx"),
        P("seq", "ctx"),
        P(("seq", "ctx"), None),
        P(("seq", "ctx")),
        P(("seq", "ctx"), None),
        P(("seq", "ctx"), None),
        P(("seq", "ctx")),
        P(("seq", "ctx"), None),
        P(("seq", "ctx")),
        P(("seq", "ctx")),
        P(("seq", "ctx")),
        P(("seq", "ctx"), None),
        P(("seq", "ctx")),
        P(("seq", "ctx"), None),
        P(("seq", "ctx")),
        P(("seq", "ctx")),
        P(("seq", "ctx")),
        P("seq", "ctx", None),
    )
    out_specs = (
        P("seq", "ctx", None),
        P("seq", "ctx", None),
        P(("seq", "ctx"), None),
        P(("seq", "ctx")),
        P(("seq", "ctx"), None),
        P(("seq", "ctx"), None),
        P(("seq", "ctx")),
        P(("seq", "ctx"), None),
        P(("seq", "ctx")),
        P(("seq", "ctx")),
        P(("seq", "ctx")),
        P(("seq", "ctx"), None),
        P(("seq", "ctx")),
        P(("seq", "ctx"), None),
        P(("seq", "ctx")),
        P(("seq", "ctx")),
        P(("seq", "ctx")),
    )
    return jax.shard_map(
        on_device, mesh=mesh, in_specs=in_specs, out_specs=out_specs, check_vma=False
    )
```
